32 devices in a mesh: ep: 8 (over z, x), tp: 4 (over y, core).
Axes of the slice: x: 2, y: 2, z: 4, core: 2. Of those that a mesh axis runs over, the one named last changes fastest.
Arguments:
- data_rows: bfloat16 [16, 3072, 512], P('ep', 'tp'), may hold values from -6 to 6
- prompt_rows: bfloat16 [1024, 512], P('tp'), may hold values from -6 to 6
- context_rows: int32 [16], P('ep'), may hold values from 100 to 3000, as said below
- test_rows: int32 [16], P('ep'), may hold values from 1 to 2972, as said below
- qkv_weight: bfloat16 [3, 512, 512], P(None, None, 'tp'), may hold values from -0.25 to 0.25
- out_bias: bfloat16 [512], replicated, may hold values from -3 to 3
- out_weight: bfloat16 [512, 512], P('tp'), may hold values from -6 to 6
- attn_gain: bfloat16 [512], replicated, may hold values from 0.5 to 1.5
- attn_shift: bfloat16 [512], replicated, may hold values from -3 to 3
- up_weight: bfloat16 [512, 1024], P(None, 'tp'), may hold values from -0.25 to 0.25
- up_bias: bfloat16 [1024], P('tp'), may hold values from -3 to 3
- down_weight: bfloat16 [1024, 512], P('tp'), may hold values from -0.1875 to 0.1875
- down_bias: bfloat16 [512], replicated, may hold values from -3 to 3
- mlp_gain: bfloat16 [512], replicated, may hold values from 0.5 to 1.5
- mlp_shift: bfloat16 [512], replicated, may hold values from -3 to 3
- data_cotangent: bfloat16 [16, 3072, 512], P('ep', 'tp'), may hold values from -6 to 6
- prompt_cotangent: bfloat16 [16, 1024, 512], P('ep', 'tp'), may hold values from -6 to 6
Outputs:
- data_output: bfloat16 [16, 3072, 512], P('ep', 'tp')
- prompt_output: bfloat16 [16, 1024, 512], P('ep', 'tp')
- data_grad: bfloat16 [16, 3072, 512], P('ep', 'tp')
- prompt_grad: float32 [1024, 512], P('tp')
- qkv_weight_grad: float32 [3, 512, 512], P(None, None, 'tp')
- out_bias_grad: float32 [512], replicated
- out_weight_grad: float32 [512, 512], P('tp')
- attn_gain_grad: float32 [512], replicated
- attn_shift_grad: float32 [512], replicated
- up_weight_grad: float32 [512, 1024], P(None, 'tp')
- up_bias_grad: float32 [1024], P('tp')
- down_weight_grad: float32 [1024, 512], P('tp')
- down_bias_grad: float32 [512], replicated
- mlp_gain_grad: float32 [512], replicated
- mlp_shift_grad: float32 [512], replicated
The draws below stay inside these ranges and needn't reach their ends.
Inputs may be any that keep to these rules, and one draw needn't show every extreme that they name: `context_rows`: in the 2 episodes of each index of ep one has more than 2304 context rows. context_rows + test_rows of an episode is at most 3072.
All inputs are finite; a program needn't handle non-finite values.
Results may differ from the reference program's by a relative error of at most 0.02.
Values may be sent and summed in bfloat16 or wider, within the bound.
No kernel may reach another device: no remote copies, remote signals or barrier semaphores. Data moves between devices by JAX's collectives and lax.ppermute only.
A program may use at most 320 MiB of HBM per device.

```python
import math
import jax
import jax.numpy as jnp
from jax import lax

D = 512
HEADS = 4
HEAD_DIM = 128
FF = 1024
PROMPT = 1024
DATA = 3072
CTX_MIN = 100
CTX_MAX = 3000
EPI_DEV = 2
EPISODES = 16


def episode_counts(key):
    subkeys = jax.random.split(key, 6)
    groups = EPISODES // EPI_DEV
    context = jax.random.randint(subkeys[0], (EPISODES,), CTX_MIN, CTX_MAX + 1)
    chosen = jax.random.randint(subkeys[1], (groups,), 0, EPI_DEV)
    span_ends = jax.random.randint(subkeys[2], (groups,), 3 * DATA // 4 + 1, CTX_MAX + 1)
    longest = jnp.arange(groups) * EPI_DEV + chosen
    context = context.at[longest].set(span_ends)
    top_group = jax.random.randint(subkeys[3], (), 0, groups)
    context = context.at[longest[top_group]].set(CTX_MAX)
    low_group = jax.random.randint(subkeys[4], (), 0, groups)
    shortest = low_group * EPI_DEV + (chosen[low_group] + 1) % EPI_DEV
    context = context.at[shortest].set(CTX_MIN)
    test_counts = jax.random.randint(subkeys[5], (EPISODES,), 1, DATA - context + 1)
    test_counts = test_counts.at[shortest].set(DATA - CTX_MIN)
    return (context.astype(jnp.int32), test_counts.astype(jnp.int32))


def draw_context_rows(key, part):
    return episode_counts(key)[0]


def draw_test_rows(key, part):
    return episode_counts(key)[1]


def levels(own_key, extent, shards, least, top_value):
    gain = 1.0
    for dim, blocks in shards:
        steps = jax.random.uniform(jax.random.fold_in(jax.random.fold_in(own_key, 6), dim), (blocks,), jnp.float32, least / len(shards), top_value / len(shards))
        gain = gain * jnp.repeat(jnp.exp(steps), extent[dim] // blocks).reshape((-1,) + (1,) * (len(extent) - 1 - dim))
    return gain


def normal_values(rng, dims, scale, bound, shards=(), held_as=jnp.bfloat16):
    result = jax.random.normal(rng, dims, jnp.float32) * scale
    if len(shards) > 0:
        result = levels(rng, dims, shards, -0.22, 0.18) * result
    return jnp.clip(result, min=-bound, max=bound).astype(held_as)


def setup_inputs(seed: int = 0) -> dict:
    key_of = jax.random.split(jax.random.key(seed), 18)
    data_rows = normal_values(key_of[0], (EPISODES, DATA, D), 1.0, 6.0, ((0, 8), (1, 4)))
    prompt_rows = normal_values(key_of[1], (PROMPT, D), 1.0, 6.0, ((0, 4),))
    context_rows = draw_context_rows(jax.random.fold_in(key_of[17], 71), 0)
    test_rows = draw_test_rows(jax.random.fold_in(key_of[17], 71), 0)
    qkv_weight = normal_values(key_of[4], (3, D, D), D ** -0.5, 0.25, ((2, 4),))
    out_bias = normal_values(key_of[5], (D,), 0.3, 3.0)
    out_weight = normal_values(key_of[6], (D, D), 1 ** -0.5, 6.0, ((0, 4),))
    attn_gain = jnp.clip(1.0 + 0.1 * jax.random.normal(key_of[7], (D,), jnp.float32), 0.5, 1.5).astype(jnp.bfloat16)
    attn_shift = normal_values(key_of[8], (D,), 0.3, 3.0)
    up_weight = normal_values(key_of[9], (D, FF), D ** -0.5, 0.25, ((1, 4),))
    up_bias = normal_values(key_of[10], (FF,), 0.3, 3.0, ((0, 4),))
    down_weight = normal_values(key_of[11], (FF, D), FF ** -0.5, 0.1875, ((0, 4),))
    down_bias = normal_values(key_of[12], (D,), 0.3, 3.0)
    mlp_gain = jnp.clip(1.0 + 0.1 * jax.random.normal(key_of[13], (D,), jnp.float32), 0.5, 1.5).astype(jnp.bfloat16)
    mlp_shift = normal_values(key_of[14], (D,), 0.3, 3.0)
    data_cotangent = normal_values(key_of[15], (EPISODES, DATA, D), 1.0, 6.0, ((0, 8), (1, 4)))
    prompt_cotangent = normal_values(key_of[16], (EPISODES, PROMPT, D), 1.0, 6.0, ((0, 8), (1, 4)))
    return dict(data_rows=data_rows, prompt_rows=prompt_rows, context_rows=context_rows, test_rows=test_rows, qkv_weight=qkv_weight, out_bias=out_bias, out_weight=out_weight, attn_gain=attn_gain, attn_shift=attn_shift, up_weight=up_weight, up_bias=up_bias, down_weight=down_weight, down_bias=down_bias, mlp_gain=mlp_gain, mlp_shift=mlp_shift, data_cotangent=data_cotangent, prompt_cotangent=prompt_cotangent)


@jax.custom_vjp
def low(v):
    return lax.optimization_barrier(v.astype(jnp.bfloat16)).astype(jnp.float32)

@jax.custom_vjp
def low_back(v):
    return v

def low_keep(v):
    return (low(v), None)

def low_pass(kept, grad):
    return (grad,)

def back_keep(v):
    return (v, None)

def back_low(kept, grad):
    return (low(grad),)
low.defvjp(low_keep, low_pass)
low_back.defvjp(back_keep, back_low)
epsilon = 1e-05
big_negative = -1e+30
highest = lax.Precision.HIGHEST

def product(left, right):
    return jnp.dot(left, right, precision=highest, preferred_element_type=jnp.float32)

def layer_norm(values, gain_row, shift_row):
    row_mean = lax.optimization_barrier(jnp.mean(values, axis=-1, keepdims=True))
    centered = values - row_mean
    variance = lax.optimization_barrier(jnp.mean(centered * centered, axis=-1, keepdims=True))
    return centered * lax.rsqrt(variance + epsilon) * gain_row + shift_row

def head_attention(queries, key_rows, value_rows, key_bias):
    seq_len = queries.shape[0]
    block_rows = math.gcd(seq_len, 512)
    score_scale = 1.0 / math.sqrt(HEAD_DIM)

    @jax.checkpoint
    def one_block(query_block):
        raw_scores = low_back(product(query_block, key_rows.T))
        scores = raw_scores * score_scale + key_bias[None, :]
        row_top = lax.optimization_barrier(jnp.max(scores, axis=-1, keepdims=True))
        weights = jnp.exp(scores - row_top)
        probability = weights / lax.optimization_barrier(jnp.sum(weights, axis=-1, keepdims=True))
        return product(low(probability), value_rows)
    blocks = lax.map(one_block, queries.reshape(seq_len // block_rows, block_rows, HEAD_DIM))
    return blocks.reshape(seq_len, HEAD_DIM)

def forward(params, prompt_in, data_in, key_bias):
    qkv_weight, out_bias, out_weight, attn_gain, attn_shift, up_weight, up_bias, down_weight, down_bias, mlp_gain, mlp_shift = params
    inputs = jnp.concatenate([prompt_in, data_in], axis=0)
    projected = [low_back(low(product(inputs, qkv_weight[which]))) for which in range(3)]
    head_outputs = []
    for head_index in range(HEADS):
        columns = slice(head_index * HEAD_DIM, (head_index + 1) * HEAD_DIM)
        head_outputs.append(head_attention(projected[0][:, columns], projected[1][:, columns], projected[2][:, columns], key_bias))
    attended = low_back(low(jnp.concatenate(head_outputs, axis=1)))
    branch = low_back(product(attended, out_weight)) + out_bias
    hidden = layer_norm(inputs + branch, attn_gain, attn_shift)
    pre_act = low_back(product(low(hidden), up_weight) + up_bias)
    activated = low(jax.nn.gelu(pre_act, approximate=False))
    mlp_branch = low_back(product(activated, down_weight)) + down_bias
    return layer_norm(hidden + mlp_branch, mlp_gain, mlp_shift)

def reference(data_rows, prompt_rows, context_rows, test_rows, qkv_weight, out_bias, out_weight, attn_gain, attn_shift, up_weight, up_bias, down_weight, down_bias, mlp_gain, mlp_shift, data_cotangent, prompt_cotangent):
    params = tuple((item.astype(jnp.float32) for item in (qkv_weight, out_bias, out_weight, attn_gain, attn_shift, up_weight, up_bias, down_weight, down_bias, mlp_gain, mlp_shift)))
    prompt_full = prompt_rows.astype(jnp.float32)
    data_pos = jnp.arange(DATA, dtype=jnp.int32)

    def episode(running, pieces):
        rows_here, context, test_count, data_cot, prompt_cot = pieces
        key_ok = jnp.concatenate([jnp.ones((PROMPT,), jnp.bool_), data_pos < context])
        key_bias = jnp.where(key_ok, jnp.float32(0.0), jnp.float32(big_negative))
        live_rows = (data_pos < context + test_count).astype(jnp.float32)[:, None]

        def layer(param_set, prompt_in, data_in):
            return forward(param_set, prompt_in, data_in, key_bias)
        outputs, pull_back = jax.vjp(layer, params, prompt_full, rows_here.astype(jnp.float32))
        cotangent = jnp.concatenate([prompt_cot.astype(jnp.float32), data_cot.astype(jnp.float32) * live_rows], axis=0)
        param_grads, prompt_part, data_part = pull_back(cotangent)
        summed = jax.tree.map(jnp.add, running, (param_grads, prompt_part))
        return (summed, (outputs[:PROMPT].astype(jnp.bfloat16), outputs[PROMPT:].astype(jnp.bfloat16), data_part.astype(jnp.bfloat16)))
    start = jax.tree.map(jnp.zeros_like, (params, prompt_full))
    totals, stacked = lax.scan(episode, start, (data_rows, context_rows, test_rows, data_cotangent, prompt_cotangent))
    grads, prompt_grad = totals
    prompt_output, data_output, data_grad = stacked
    return (data_output, prompt_output, data_grad, prompt_grad, grads[0], grads[1], grads[2], grads[3], grads[4], grads[5], grads[6], grads[7], grads[8], grads[9], grads[10])
```

```python
from functools import partial
import math

import jax
import jax.numpy as jnp
from jax import lax
from jax.experimental import pallas as pl
from jax.experimental.pallas import tpu as pltpu
from jax.sharding import PartitionSpec as P

HEAD_DIM = 128
ROWS = 256
EPS = 1e-05
MASKED = -1e30
LOG2E = math.log2(math.e)
LIMIT = 2.0**60
VMEM = 60 * 1024 * 1024
F32 = jnp.float32
BF16 = jnp.bfloat16
NN = (((1,), (0,)), ((), ()))
NT = (((1,), (1,)), ((), ()))
TN = (((0,), (0,)), ((), ()))


def mm(left, right, dims=NN):
    return lax.dot_general(left, right, dims, preferred_element_type=F32)


def relative_slot(t, j):
    return t ^ ((j & 1) * 2 + (j >> 1))


def global_block(t, i, prompt_blocks, data_blocks):
    per_slot = prompt_blocks + data_blocks
    slot = relative_slot(t, i // per_slot)
    inner = i % per_slot
    return jnp.where(
        inner < prompt_blocks,
        slot * prompt_blocks + inner,
        4 * prompt_blocks + slot * data_blocks + inner - prompt_blocks,
    )


def params(**more):
    return pltpu.CompilerParams(vmem_limit_bytes=VMEM, **more)


def cost(flops, nbytes, trans=0):
    return pl.CostEstimate(
        flops=int(flops), bytes_accessed=int(nbytes), transcendentals=int(trans)
    )


def once(shape):
    return pl.BlockSpec(shape, lambda *_: (0,) * len(shape), pipeline_mode=pl.Buffered(1))


def extra_rows(values, count):
    width = values[0].shape[1]
    row = lax.broadcasted_iota(jnp.int32, (count, width), 0)
    out = jnp.zeros((count, width), F32)
    for index, value in enumerate(values):
        out = jnp.where(row == index, value, out)
    return out.astype(BF16)


def three_parts(row):
    high = row.astype(BF16).astype(F32)
    middle = (row - high).astype(BF16).astype(F32)
    return high, middle, row - high - middle


def project_kernel(shape, meta, x_ref, w_ref, qt_ref, q_ref, ka_ref, kt_ref, va_ref, vt_ref):
    prompt_blocks, data_blocks = shape
    i = pl.program_id(0)
    g = global_block(meta[0], i, prompt_blocks, data_blocks)
    z = mm(x_ref[...], w_ref[...]).astype(BF16)
    lane = lax.broadcasted_iota(jnp.int32, (ROWS, HEAD_DIM), 1)
    row = lax.broadcasted_iota(jnp.int32, (ROWS, HEAD_DIM), 0)
    position = (g - 4 * prompt_blocks) * ROWS + row
    bias = jnp.where(position < meta[1], F32(0.0), F32(MASKED))
    ones = jnp.where(lane < 4, F32(1.0), F32(0.0))
    key_extra = jnp.where(lane == 0, bias, ones).astype(BF16)
    value_extra = ones.astype(BF16)
    factor = F32(LOG2E / math.sqrt(HEAD_DIM))
    for h in range(2):
        lo = h * HEAD_DIM
        q = (z[:, lo : lo + HEAD_DIM].astype(F32) * factor).astype(BF16)
        k = z[:, 256 + lo : 256 + lo + HEAD_DIM]
        v = z[:, 512 + lo : 512 + lo + HEAD_DIM]
        q_ref[h] = q
        qt_ref[h] = q.T
        ka_ref[h, :, :HEAD_DIM] = k
        ka_ref[h, :, HEAD_DIM:] = key_extra
        kt_ref[h] = k.T
        va_ref[h, :, :HEAD_DIM] = v
        va_ref[h, :, HEAD_DIM:] = value_extra
        vt_ref[h] = v.T


def project(meta, x, w, prompt_blocks, data_blocks):
    rows, width = x.shape
    n = rows // ROWS

    def place(i, meta):
        return global_block(meta[0], i, prompt_blocks, data_blocks)

    flat = lambda cols: jax.ShapeDtypeStruct((2, rows, cols), BF16)
    tall = jax.ShapeDtypeStruct((2, HEAD_DIM, rows), BF16)
    return pl.pallas_call(
        partial(project_kernel, (prompt_blocks, data_blocks)),
        out_shape=[tall, flat(HEAD_DIM), flat(256), tall, flat(256), tall],
        grid_spec=pltpu.PrefetchScalarGridSpec(
            num_scalar_prefetch=1,
            grid=(n,),
            in_specs=[
                pl.BlockSpec((ROWS, width), lambda i, meta: (i, 0)),
                once(w.shape),
            ],
            out_specs=[
                pl.BlockSpec((2, HEAD_DIM, ROWS), lambda i, meta: (0, 0, i)),
                pl.BlockSpec((2, ROWS, HEAD_DIM), lambda i, meta: (0, i, 0)),
                pl.BlockSpec((2, ROWS, 256), lambda i, meta: (0, place(i, meta), 0)),
                pl.BlockSpec((2, HEAD_DIM, ROWS), lambda i, meta: (0, 0, place(i, meta))),
                pl.BlockSpec((2, ROWS, 256), lambda i, meta: (0, place(i, meta), 0)),
                pl.BlockSpec((2, HEAD_DIM, ROWS), lambda i, meta: (0, 0, place(i, meta))),
            ],
        ),
        compiler_params=params(),
        cost_estimate=cost(2 * rows * width * 768, 4 * rows * width * 2 * 2),
        name="project",
    )(meta, x, w)


def attend_kernel(chunk, qt_ref, ka_ref, vt_ref, pt_ref, o_ref, stat_ref, m_ref, l_ref):
    seq = ka_ref.shape[1]
    width = qt_ref.shape[2]

    def scores(h, qa, start):
        return mm(ka_ref[h, pl.ds(start, chunk), :], qa)

    def shifted(h, top):
        high, middle, low = three_parts(top)
        one = jnp.ones_like(top)
        extra = extra_rows([one, -high, -middle, -low], HEAD_DIM)
        return jnp.concatenate([qt_ref[h], extra], axis=0)

    def part(h, qa, start):
        weight = jnp.exp2(scores(h, qa, start))
        total = jnp.sum(weight.reshape(chunk // 8, 8, width), axis=0)
        low = weight.astype(BF16)
        pt_ref[0, h, pl.ds(start, chunk), :] = low
        return total, mm(vt_ref[h, :, pl.ds(start, chunk)], low)

    def finish(h, total, acc):
        total = jnp.sum(total, axis=0, keepdims=True)
        inverse = 1.0 / total
        l_ref[h : h + 1, :] = total
        stat_ref[0, h : h + 1, :] = inverse
        o_ref[:, h * HEAD_DIM : (h + 1) * HEAD_DIM] = (acc * inverse).T.astype(BF16)

    for h in range(2):
        top = jnp.max(mm(ka_ref[h, :ROWS, :HEAD_DIM], qt_ref[h]), axis=0, keepdims=True)
        qa = shifted(h, top)
        total = jnp.zeros((8, width), F32)
        acc = jnp.zeros((HEAD_DIM, width), F32)
        for start in range(0, seq, chunk):
            more, product = part(h, qa, start)
            total, acc = total + more, acc + product
        finish(h, total, acc)

    @pl.when(jnp.logical_not(jnp.max(l_ref[0:2, :]) <= LIMIT))
    def _():
        for h in range(2):
            qa = shifted(h, jnp.zeros((1, width), F32))

            def step(j, top):
                found = scores(h, qa, pl.multiple_of(j * chunk, chunk))
                return jnp.maximum(top, jnp.max(found, axis=0, keepdims=True))

            m_ref[0:1, :] = lax.fori_loop(
                0, seq // chunk, step, jnp.full((1, width), MASKED, F32)
            )
            qa = shifted(h, m_ref[0:1, :])

            def again(j, state):
                more, product = part(h, qa, pl.multiple_of(j * chunk, chunk))
                return state[0] + more, state[1] + product

            total, acc = lax.fori_loop(
                0,
                seq // chunk,
                again,
                (jnp.zeros((8, width), F32), jnp.zeros((HEAD_DIM, width), F32)),
            )
            finish(h, total, acc)


def attend(qt, ka, vt):
    rows = qt.shape[2]
    seq = ka.shape[1]
    n = rows // ROWS
    chunk = 512
    return pl.pallas_call(
        partial(attend_kernel, chunk),
        out_shape=[
            jax.ShapeDtypeStruct((n, 2, seq, ROWS), BF16),
            jax.ShapeDtypeStruct((rows, 256), BF16),
            jax.ShapeDtypeStruct((n, 8, ROWS), F32),
        ],
        grid=(n,),
        in_specs=[
            pl.BlockSpec((2, HEAD_DIM, ROWS), lambda i: (0, 0, i)),
            once(ka.shape),
            once(vt.shape),
        ],
        out_specs=[
            pl.BlockSpec((1, 2, seq, ROWS), lambda i: (i, 0, 0, 0)),
            pl.BlockSpec((ROWS, 256), lambda i: (i, 0)),
            pl.BlockSpec((1, 8, ROWS), lambda i: (i, 0, 0)),
        ],
        scratch_shapes=[pltpu.VMEM((8, ROWS), F32), pltpu.VMEM((8, ROWS), F32)],
        compiler_params=params(),
        cost_estimate=cost(
            2 * 2 * 2 * rows * seq * HEAD_DIM, 2 * rows * seq * 2, 2 * rows * seq
        ),
        name="attend",
    )(qt, ka, vt)


def attend_back_kernel(
    chunk, do_ref, o_ref, stat_ref, pt_ref, q_ref, va_ref, kt_ref, dq_ref, dk_ref, dv_ref,
    key_acc, value_acc,
):
    seq = va_ref.shape[1]
    i = pl.program_id(0)

    @pl.when(i == 0)
    def _():
        key_acc[...] = jnp.zeros_like(key_acc)
        value_acc[...] = jnp.zeros_like(value_acc)

    for h in range(2):
        cols = slice(h * HEAD_DIM, (h + 1) * HEAD_DIM)
        dot_t = do_ref[:, cols].astype(F32).T
        o_t = o_ref[:, cols].astype(F32).T
        inverse = stat_ref[0, h : h + 1, :]
        delta = jnp.sum(dot_t * o_t, axis=0, keepdims=True) * inverse
        scaled = dot_t * inverse
        high, middle, low = three_parts(delta)
        zero = jnp.zeros_like(delta)
        extra = extra_rows([zero, -high, -middle, -low], HEAD_DIM)
        da = jnp.concatenate([scaled.astype(BF16), extra], axis=0)
        d_rows = scaled.T.astype(BF16)
        q_rows = q_ref[h]
        query_acc = jnp.zeros((HEAD_DIM, ROWS), F32)
        for start in range(0, seq, chunk):
            here = slice(start, start + chunk)
            prob = pt_ref[0, h, here, :]
            grad = mm(va_ref[h, here, :], da)
            score = (prob.astype(F32) * grad).astype(BF16)
            value_acc[h, here, :] += mm(prob, d_rows)
            key_acc[h, here, :] += mm(score, q_rows)
            query_acc = query_acc + mm(kt_ref[h, :, here], score)
        query_acc = query_acc * F32(1.0 / math.sqrt(HEAD_DIM))
        dq_ref[:, cols] = query_acc.T.astype(BF16)

    @pl.when(i == pl.num_programs(0) - 1)
    def _():
        for h in range(2):
            cols = slice(h * HEAD_DIM, (h + 1) * HEAD_DIM)
            dk_ref[:, cols] = (key_acc[h] * F32(1.0 / LOG2E)).astype(BF16)
            dv_ref[:, cols] = value_acc[h].astype(BF16)


def attend_back(do, o, stat, pt, q, va, kt):
    rows = do.shape[0]
    seq = va.shape[1]
    n = rows // ROWS
    whole = jax.ShapeDtypeStruct((seq, 256), BF16)
    return pl.pallas_call(
        partial(attend_back_kernel, 512),
        out_shape=[jax.ShapeDtypeStruct((rows, 256), BF16), whole, whole],
        grid=(n,),
        in_specs=[
            pl.BlockSpec((ROWS, 256), lambda i: (i, 0)),
            pl.BlockSpec((ROWS, 256), lambda i: (i, 0)),
            pl.BlockSpec((1, 8, ROWS), lambda i: (i, 0, 0)),
            pl.BlockSpec((1, 2, seq, ROWS), lambda i: (i, 0, 0, 0)),
            pl.BlockSpec((2, ROWS, HEAD_DIM), lambda i: (0, i, 0)),
            once(va.shape),
            once(kt.shape),
        ],
        out_specs=[
            pl.BlockSpec((ROWS, 256), lambda i: (i, 0)),
            once(whole.shape),
            once(whole.shape),
        ],
        scratch_shapes=[
            pltpu.VMEM((2, seq, HEAD_DIM), F32),
            pltpu.VMEM((2, seq, HEAD_DIM), F32),
        ],
        compiler_params=params(),
        cost_estimate=cost(4 * 2 * 2 * rows * seq * HEAD_DIM, 2 * rows * seq * 2),
        name="attend_back",
    )(do, o, stat, pt, q, va, kt)


def mean(values):
    return jnp.mean(values, axis=-1, keepdims=True)


def norm(values):
    centered = values - mean(values)
    inverse = lax.rsqrt(mean(centered * centered) + EPS)
    return centered * inverse, inverse


def norm_back(incoming, normed, inverse, gain):
    scaled = incoming * gain
    return inverse * (scaled - mean(scaled) - normed * mean(scaled * normed))


def gelu_parts(v):
    bell = jnp.exp2(v * v * F32(-0.5 * LOG2E))
    t = 1.0 / (1.0 + F32(0.3275911 / math.sqrt(2.0)) * jnp.abs(v))
    series = t * (
        F32(0.5 * 0.254829592)
        + t
        * (
            F32(0.5 * -0.284496736)
            + t
            * (
                F32(0.5 * 1.421413741)
                + t * (F32(0.5 * -1.453152027) + t * F32(0.5 * 1.061405429))
            )
        )
    )
    tail = series * bell
    return bell * F32(1.0 / math.sqrt(2.0 * math.pi)), jnp.where(v >= 0, 1.0 - tail, tail)


def fold_rows(values):
    return jnp.sum(values.reshape(values.shape[0] // 8, 8, values.shape[1]), axis=0)


def rows_kernel(
    sizes, meta, x_ref, oa_ref, ob_ref, cot_ref, wo_ref, up_ref, down_ref, vec_ref, bias_ref,
    out_ref, resid_ref, da_ref, db_ref, mine_ref, theirs_ref, sums_ref,
    grad_acc, vec_acc, bias_acc,
):
    prompt_local, data_local = sizes
    i = pl.program_id(0)
    rows = x_ref.shape[0]
    slot_rows = prompt_local + data_local
    quarter = up_ref.shape[1] // 4

    @pl.when(i == 0)
    def _():
        grad_acc[...] = jnp.zeros_like(grad_acc)
        vec_acc[...] = jnp.zeros_like(vec_acc)
        bias_acc[...] = jnp.zeros_like(bias_acc)

    per_slot = slot_rows // rows
    slot = relative_slot(meta[0], i // per_slot)
    inner = (i % per_slot) * rows + lax.broadcasted_iota(jnp.int32, (rows, 1), 0)
    index = inner - prompt_local
    live = jnp.logical_or(index < 0, slot * data_local + index < meta[2])

    out_bias, attn_gain, attn_shift = vec_ref[0:1, :], vec_ref[1:2, :], vec_ref[2:3, :]
    down_bias, mlp_gain, mlp_shift = vec_ref[3:4, :], vec_ref[4:5, :], vec_ref[5:6, :]
    attended = jnp.concatenate([oa_ref[...], ob_ref[...]], axis=1)
    normed_one, inverse_one = norm(
        x_ref[...].astype(F32) + (mm(attended, wo_ref[...]) + out_bias)
    )
    hidden = normed_one * attn_gain + attn_shift
    hidden_low = hidden.astype(BF16)
    pre = mm(hidden_low, up_ref[...]) + bias_ref[0:1, :]
    density, share = gelu_parts(pre)
    activated = (pre * share).astype(BF16)
    slope = share + pre * density
    mixed = hidden + (mm(activated, down_ref[...]) + down_bias)
    normed_two, inverse_two = norm(mixed)
    out_ref[...] = (normed_two * mlp_gain + mlp_shift).astype(BF16)

    cotangent = jnp.where(live, cot_ref[...].astype(F32), 0.0)
    mixed_grad = norm_back(cotangent, normed_two, inverse_two, mlp_gain)
    mixed_low = mixed_grad.astype(BF16)
    pre_grad = (mm(mixed_low, down_ref[...], NT) * slope).astype(BF16)
    hidden_grad = mixed_grad + mm(pre_grad, up_ref[...], NT)
    resid_grad = norm_back(hidden_grad, normed_one, inverse_one, attn_gain)
    resid_ref[...] = resid_grad
    resid_low = resid_grad.astype(BF16)
    attended_grad = mm(resid_low, wo_ref[...], NT).astype(BF16)
    da_ref[...] = attended_grad[:, :256]
    db_ref[...] = attended_grad[:, 256:]

    up_grad = mm(hidden_low, pre_grad, TN)
    down_grad = mm(mixed_low, activated, TN)
    out_grad = mm(resid_low, attended, TN)
    for j in range(4):
        cols = slice(j * quarter, (j + 1) * quarter)
        grad_acc[j, :, :quarter] += up_grad[:, cols]
        grad_acc[j, :, quarter : 2 * quarter] += down_grad[:, cols]
        grad_acc[j, :, 2 * quarter :] += out_grad[:, j * HEAD_DIM : (j + 1) * HEAD_DIM]
    bias_acc[...] += fold_rows(pre_grad.astype(F32))
    for place, value in enumerate(
        (
            resid_grad,
            hidden_grad * normed_one,
            hidden_grad,
            mixed_grad,
            cotangent * normed_two,
            cotangent,
        )
    ):
        vec_acc[place] += fold_rows(value)

    @pl.when(i == pl.num_programs(0) - 1)
    def _():
        depth = grad_acc.shape[1]
        bias_grad = jnp.sum(bias_acc[...], axis=0, keepdims=True)
        for j in range(4):
            target = mine_ref if j < 2 else theirs_ref
            kind = target.dtype
            target[j % 2, :depth, :] = grad_acc[j].astype(kind)
            target[j % 2, depth:, :] = jnp.zeros((16, grad_acc.shape[2]), kind)
            target[j % 2, depth:, :quarter] = jnp.broadcast_to(
                bias_grad[:, j * quarter : (j + 1) * quarter], (16, quarter)
            ).astype(kind)
        for place in range(6):
            sums_ref[place : place + 1, :] = jnp.sum(vec_acc[place], axis=0, keepdims=True)
        sums_ref[6:8, :] = jnp.zeros((2, depth), F32)


def row_work(meta, x, oa, ob, cot, wo, up, down, vec, bias, sizes):
    rows, width = cot.shape
    step = 512
    n = rows // step
    hidden = up.shape[1]
    quarter = hidden // 4
    wide = 2 * quarter + HEAD_DIM
    row = lambda cols: pl.BlockSpec((step, cols), lambda i, meta: (i, 0))
    return pl.pallas_call(
        partial(rows_kernel, sizes),
        out_shape=[
            jax.ShapeDtypeStruct((rows, width), BF16),
            jax.ShapeDtypeStruct((rows, width), F32),
            jax.ShapeDtypeStruct((rows, 256), BF16),
            jax.ShapeDtypeStruct((rows, 256), BF16),
            jax.ShapeDtypeStruct((2, width + 16, wide), F32),
            jax.ShapeDtypeStruct((2, width + 16, wide), BF16),
            jax.ShapeDtypeStruct((8, width), F32),
        ],
        grid_spec=pltpu.PrefetchScalarGridSpec(
            num_scalar_prefetch=1,
            grid=(n,),
            in_specs=[
                row(width),
                row(256),
                row(256),
                row(width),
                once(wo.shape),
                once(up.shape),
                once(down.shape),
                once(vec.shape),
                once(bias.shape),
            ],
            out_specs=[
                row(width),
                row(width),
                row(256),
                row(256),
                once((2, width + 16, wide)),
                once((2, width + 16, wide)),
                once((8, width)),
            ],
            scratch_shapes=[
                pltpu.VMEM((4, width, wide), F32),
                pltpu.VMEM((6, 8, width), F32),
                pltpu.VMEM((8, hidden), F32),
            ],
        ),
        compiler_params=params(),
        cost_estimate=cost(
            3 * 2 * rows * width * (width + 2 * hidden), 12 * rows * width, 2 * rows * hidden
        ),
        name="row_work",
    )(meta, x, oa, ob, cot, wo, up, down, vec, bias)


def project_back_kernel(meta, x_ref, dq_ref, dk_ref, dv_ref, w_ref, resid_ref, own_ref, sib_ref,
                        wg_ref, acc):
    i = pl.program_id(0)
    half = pl.num_programs(0) // 2

    @pl.when(i == 0)
    def _():
        acc[...] = jnp.zeros_like(acc)

    dz = jnp.concatenate([dq_ref[...], dk_ref[...], dv_ref[...]], axis=1)
    acc[...] += mm(x_ref[...], dz, TN)
    part = mm(dz, w_ref[...], NT)

    @pl.when(i < half)
    def _():
        sib_ref[...] = part.astype(BF16)

    @pl.when(i >= half)
    def _():
        own_ref[...] = part + resid_ref[...]

    @pl.when(i == pl.num_programs(0) - 1)
    def _():
        wg_ref[...] = acc[...]


def project_back(meta, x, dq, dk, dv, w, resid, prompt_blocks, data_blocks):
    rows, width = x.shape
    n = rows // ROWS
    half = n // 2

    def turn(i):
        return (i + half) % n

    def place(i, meta):
        return global_block(meta[0], turn(i), prompt_blocks, data_blocks)

    return pl.pallas_call(
        project_back_kernel,
        out_shape=[
            jax.ShapeDtypeStruct((rows // 2, width), F32),
            jax.ShapeDtypeStruct((rows // 2, width), BF16),
            jax.ShapeDtypeStruct(w.shape, F32),
        ],
        grid_spec=pltpu.PrefetchScalarGridSpec(
            num_scalar_prefetch=1,
            grid=(n,),
            in_specs=[
                pl.BlockSpec((ROWS, width), lambda i, meta: (turn(i), 0)),
                pl.BlockSpec((ROWS, 256), lambda i, meta: (turn(i), 0)),
                pl.BlockSpec((ROWS, 256), lambda i, meta: (place(i, meta), 0)),
                pl.BlockSpec((ROWS, 256), lambda i, meta: (place(i, meta), 0)),
                once(w.shape),
                pl.BlockSpec((ROWS, width), lambda i, meta: (jnp.maximum(i - half, 0), 0)),
            ],
            out_specs=[
                pl.BlockSpec((ROWS, width), lambda i, meta: (jnp.maximum(i - half, 0), 0)),
                pl.BlockSpec((ROWS, width), lambda i, meta: (jnp.minimum(i, half - 1), 0)),
                once(w.shape),
            ],
            scratch_shapes=[pltpu.VMEM(w.shape, F32)],
        ),
        compiler_params=params(),
        cost_estimate=cost(4 * rows * width * 768, 6 * rows * width * 2),
        name="project_back",
    )(meta, x, dq, dk, dv, w, resid)


def on_device(
    data_rows,
    prompt_rows,
    context_rows,
    test_rows,
    qkv_weight,
    out_bias,
    out_weight,
    attn_gain,
    attn_shift,
    up_weight,
    up_bias,
    down_weight,
    down_bias,
    mlp_gain,
    mlp_shift,
    data_cotangent,
    prompt_cotangent,
):
    data_local = data_rows.shape[1]
    prompt_local = prompt_rows.shape[0]
    width = prompt_rows.shape[1]
    prompt_blocks, data_blocks = prompt_local // ROWS, data_local // ROWS
    slot_rows = prompt_local + data_local
    t = lax.axis_index("tp")
    mine = t >> 1
    other = 1 - mine

    def across(value):
        return lax.ppermute(value, "tp", [(i, i ^ 2) for i in range(4)])

    def beside(value):
        return lax.ppermute(value, "tp", [(i, i ^ 1) for i in range(4)])

    def pick(values, which):
        return lax.dynamic_index_in_dim(values, which, axis=0, keepdims=False)

    def stack(prompt_part, data_part):
        return jnp.concatenate([prompt_part, data_part], axis=0)

    x_here = stack(prompt_rows, pick(data_rows, mine))
    x_there = across(stack(prompt_rows, pick(data_rows, other)))
    w_there = across(qkv_weight)
    x = jnp.concatenate([x_here, x_there, beside(x_here), beside(x_there)], axis=0)
    w = jnp.concatenate(
        [part for which in range(3) for part in (qkv_weight[which], w_there[which])], axis=1
    )
    context = pick(context_rows, mine)
    live = context + pick(test_rows, mine)
    meta = jnp.stack([t, context, live]).astype(jnp.int32)

    qt, q, ka, kt, va, vt = project(meta, x, w, prompt_blocks, data_blocks)
    pt, attended, stat = attend(qt, ka, vt)

    cot_here = stack(pick(prompt_cotangent, mine), pick(data_cotangent, mine))
    cot_there = across(stack(pick(prompt_cotangent, other), pick(data_cotangent, other)))
    cot = jnp.concatenate([cot_here, cot_there], axis=0)

    def spread(value, axis):
        pair = jnp.concatenate([value, across(value)], axis=axis)
        return jnp.concatenate([pair, beside(pair)], axis=axis)

    wo, up, down = spread(out_weight, 0), spread(up_weight, 1), spread(down_weight, 0)
    bias = spread(jnp.broadcast_to(up_bias.astype(F32)[None, :], (8, up_bias.shape[0])), 1)
    vec = jnp.stack(
        [out_bias, attn_gain, attn_shift, down_bias, mlp_gain, mlp_shift, mlp_shift, mlp_shift]
    ).astype(F32)
    attended_there = beside(attended[2 * slot_rows :])
    out, resid, da, db, grads_mine, grads_theirs, sums = row_work(
        meta, x, attended, attended_there, cot, wo, up, down, vec, bias,
        (prompt_local, data_local),
    )

    do = jnp.concatenate([da, beside(db)], axis=0)
    dq, dk, dv = attend_back(do, attended, stat, pt, q, va, kt)
    dx_own, dx_sib, qkv_grad = project_back(
        meta, x, dq, dk, dv, w, resid, prompt_blocks, data_blocks
    )

    def by_episode(own, received):
        first = mine == 0
        return jnp.stack([jnp.where(first, own, received), jnp.where(first, received, own)])

    out_back = across(out[slot_rows:])
    data_output = by_episode(out[prompt_local:slot_rows], out_back[prompt_local:])
    prompt_output = by_episode(out[:prompt_local], out_back[:prompt_local])

    pair = grads_mine + beside(grads_theirs).astype(F32)
    total = pair[0] + across(pair[1].astype(BF16)).astype(F32)
    total = lax.psum(total.astype(BF16), "ep").astype(F32)
    quarter = up_weight.shape[1]
    up_grad = total[:width, :quarter]
    down_grad = total[:width, quarter : 2 * quarter].T
    out_grad = total[:width, 2 * quarter :].T
    bias_grad = total[width, :quarter]
    sums = lax.psum(sums, ("ep", "tp"))

    split = qkv_grad.reshape(width, 3, 2, HEAD_DIM).transpose(2, 1, 0, 3)
    qkv_sum = split[0] + across(split[1].astype(BF16)).astype(F32)
    qkv_total = lax.psum(qkv_sum.astype(BF16), "ep").astype(F32)

    input_grad = dx_own + beside(dx_sib).astype(F32)
    there = across(input_grad[slot_rows:].astype(BF16))
    data_grad = by_episode(input_grad[prompt_local:slot_rows].astype(BF16), there[prompt_local:])
    prompt_sum = input_grad[:prompt_local] + there[:prompt_local].astype(F32)
    prompt_grad = lax.psum(prompt_sum.astype(BF16), "ep").astype(F32)

    return (
        data_output,
        prompt_output,
        data_grad,
        prompt_grad,
        qkv_total,
        sums[0],
        out_grad,
        sums[1],
        sums[2],
        up_grad,
        bias_grad,
        down_grad,
        sums[3],
        sums[4],
        sums[5],
    )


def solution(mesh):
    return jax.shard_map(
        on_device,
        mesh=mesh,
        in_specs=(
            P("ep", "tp", None),
            P("tp", None),
            P("ep"),
            P("ep"),
            P(None, None, "tp"),
            P(),
            P("tp", None),
            P(),
            P(),
            P(None, "tp"),
            P("tp"),
            P("tp", None),
            P(),
            P(),
            P(),
            P("ep", "tp", None),
            P("ep", "tp", None),
        ),
        out_specs=(
            P("ep", "tp", None),
            P("ep", "tp", None),
            P("ep", "tp", None),
            P("tp", None),
            P(None, None, "tp"),
            P(),
            P("tp", None),
            P(),
            P(),
            P(None, "tp"),
            P("tp"),
            P("tp", None),
            P(),
            P(),
            P(),
        ),
        check_vma=False,
    )
```

```python
from functools import partial
import math

import jax
import jax.numpy as jnp
from jax import lax
from jax.experimental import pallas as pl
from jax.experimental.pallas import tpu as pltpu
from jax.sharding import PartitionSpec as P

HEAD_DIM = 128
ROWS = 256
EPS = 1e-05
MASKED = -1e30
LOG2E = math.log2(math.e)
LIMIT = 2.0**60
VMEM = 60 * 1024 * 1024
F32 = jnp.float32
BF16 = jnp.bfloat16
NN = (((1,), (0,)), ((), ()))
NT = (((1,), (1,)), ((), ()))
TN = (((0,), (0,)), ((), ()))


def mm(left, right, dims=NN):
    return lax.dot_general(left, right, dims, preferred_element_type=F32)


def params(**more):
    return pltpu.CompilerParams(vmem_limit_bytes=VMEM, **more)


def cost(flops, nbytes, trans=0):
    return pl.CostEstimate(
        flops=int(flops), bytes_accessed=int(nbytes), transcendentals=int(trans)
    )


def once(shape):
    return pl.BlockSpec(shape, lambda *_: (0,) * len(shape), pipeline_mode=pl.Buffered(1))


def extra_rows(values, count):
    width = values[0].shape[1]
    row = lax.broadcasted_iota(jnp.int32, (count, width), 0)
    out = jnp.zeros((count, width), F32)
    for index, value in enumerate(values):
        out = jnp.where(row == index, value, out)
    return out.astype(BF16)


def three_parts(row):
    high = row.astype(BF16).astype(F32)
    middle = (row - high).astype(BF16).astype(F32)
    return high, middle, row - high - middle


def clamp(i, low, high):
    return jnp.minimum(jnp.maximum(i, low), high)


def project_kernel(sizes, flip, meta, xa_ref, xb_ref, wa_ref, wb_ref, qt_ref, k_ref, kx_ref,
                   kt_ref, v_ref, vt_ref, w_ref, wt_ref):
    prompt_local, data_local = sizes
    i = pl.program_id(0)
    per_slot = pl.num_programs(0) // 2
    rows = xa_ref.shape[0]

    @pl.when(i == 0)
    def _():
        for which in range(3):
            for h, source in enumerate((wa_ref, wb_ref)):
                cols = slice(which * 256 + h * HEAD_DIM, which * 256 + (h + 1) * HEAD_DIM)
                w_ref[:, cols] = source[which]
                wt_ref[cols, :] = source[which].T

    x = jnp.where(i < per_slot, xa_ref[...], xb_ref[...])
    slot = jnp.where(i < per_slot, meta[0] ^ flip, meta[0] ^ flip ^ 1)
    row = lax.broadcasted_iota(jnp.int32, (rows, HEAD_DIM), 0)
    lane = lax.broadcasted_iota(jnp.int32, (rows, HEAD_DIM), 1)
    index = (i % per_slot) * rows + row - prompt_local
    attended = jnp.logical_or(index < 0, slot * data_local + index < meta[1])
    bias = jnp.where(attended, F32(0.0), F32(MASKED))
    ones = jnp.where(lane < 4, F32(1.0), F32(0.0))
    kx_ref[...] = jnp.where(lane == 0, bias, ones).astype(BF16)
    z = mm(x, w_ref[:, 256:]).astype(BF16)
    k_ref[...] = z[:, :256]
    v_ref[...] = z[:, 256:]
    zt = mm(wt_ref[...], x, NT)
    factor = F32(LOG2E / math.sqrt(HEAD_DIM))
    qt_ref[...] = (zt[:256] * factor).astype(BF16)
    kt_ref[...] = zt[256:512].astype(BF16)
    vt_ref[...] = zt[512:].astype(BF16)


def project(meta, xa, xb, wa, wb, sizes, flip):
    rows, width = xa.shape
    step = 512
    n = rows // step
    flat = jax.ShapeDtypeStruct((2 * rows, 256), BF16)
    tall = jax.ShapeDtypeStruct((256, 2 * rows), BF16)
    row = pl.BlockSpec((step, 256), lambda i, meta: (i, 0))
    col = pl.BlockSpec((256, step), lambda i, meta: (0, i))
    return pl.pallas_call(
        partial(project_kernel, sizes, flip),
        out_shape=[
            tall,
            flat,
            jax.ShapeDtypeStruct((2 * rows, HEAD_DIM), BF16),
            tall,
            flat,
            tall,
            jax.ShapeDtypeStruct((width, 768), BF16),
        ],
        grid_spec=pltpu.PrefetchScalarGridSpec(
            num_scalar_prefetch=1,
            grid=(2 * n,),
            in_specs=[
                pl.BlockSpec((step, width), lambda i, meta: (jnp.minimum(i, n - 1), 0)),
                pl.BlockSpec((step, width), lambda i, meta: (jnp.maximum(i - n, 0), 0)),
                once(wa.shape),
                once(wb.shape),
            ],
            out_specs=[
                col,
                row,
                pl.BlockSpec((step, HEAD_DIM), lambda i, meta: (i, 0)),
                col,
                row,
                col,
                once((width, 768)),
            ],
            scratch_shapes=[pltpu.VMEM((768, width), BF16)],
        ),
        compiler_params=params(),
        cost_estimate=cost(4 * 2 * rows * width * 768, 2 * rows * width * 8),
        name="project",
    )(meta, xa, xb, wa, wb)


def head_rows(h):
    return slice(h * HEAD_DIM, (h + 1) * HEAD_DIM)


def with_shift(qt, top):
    high, middle, low = three_parts(top)
    extra = extra_rows([jnp.ones_like(top), -high, -middle, -low], HEAD_DIM)
    return jnp.concatenate([qt, extra], axis=0)


def half_weights(chunk, h, qa, start, k_ref, kx_ref):
    here = pl.ds(start, chunk)
    keys = jnp.concatenate([k_ref[here, head_rows(h)], kx_ref[here, :]], axis=1)
    return mm(keys, qa)


def half_part(chunk, h, qa, start, k_ref, kx_ref, vt_ref, pt_ref):
    weight = jnp.exp2(half_weights(chunk, h, qa, start, k_ref, kx_ref))
    total = jnp.sum(weight.reshape(chunk // 8, 8, weight.shape[1]), axis=0)
    low = weight.astype(BF16)
    pt_ref[0, h, pl.ds(start, chunk), :] = low
    return total, mm(vt_ref[head_rows(h), pl.ds(start, chunk)], low)


def half_attend(chunk, h, qt, k_ref, kx_ref, vt_ref, pt_ref):
    width = qt.shape[1]
    top = jnp.max(mm(k_ref[:ROWS, head_rows(h)], qt), axis=0, keepdims=True)
    qa = with_shift(qt, top)
    total = jnp.zeros((8, width), F32)
    acc = jnp.zeros((HEAD_DIM, width), F32)
    for start in range(0, k_ref.shape[0], chunk):
        more, product = half_part(chunk, h, qa, start, k_ref, kx_ref, vt_ref, pt_ref)
        total, acc = total + more, acc + product
    return top, jnp.sum(total, axis=0, keepdims=True), acc


def half_attend_exact(chunk, h, qt, k_ref, kx_ref, vt_ref, pt_ref):
    width = qt.shape[1]
    count = k_ref.shape[0] // chunk
    qa = with_shift(qt, jnp.zeros((1, width), F32))

    def find(j, top):
        found = half_weights(chunk, h, qa, pl.multiple_of(j * chunk, chunk), k_ref, kx_ref)
        return jnp.maximum(top, jnp.max(found, axis=0, keepdims=True))

    top = lax.fori_loop(0, count, find, jnp.full((1, width), MASKED, F32))
    qa = with_shift(qt, top)

    def add(j, state):
        start = pl.multiple_of(j * chunk, chunk)
        more, product = half_part(chunk, h, qa, start, k_ref, kx_ref, vt_ref, pt_ref)
        return state[0] + more, state[1] + product

    total, acc = lax.fori_loop(
        0, count, add, (jnp.zeros((8, width), F32), jnp.zeros((HEAD_DIM, width), F32))
    )
    return top, jnp.sum(total, axis=0, keepdims=True), acc


def merge(states):
    top = states[0][0]
    for state in states[1:]:
        top = jnp.maximum(top, state[0])
    scales = [jnp.exp2(state[0] - top) for state in states]
    total = sum(state[1] * scale for state, scale in zip(states, scales))
    factors = [scale / total for scale in scales]
    return factors, sum(state[2] * factor for state, factor in zip(states, factors))


def attend_kernel(chunk, halves, state_in, state_out, *refs):
    refs = list(refs)
    qt_ref = refs.pop(0)
    keys = [[refs.pop(0) for _ in range(3)] for _ in range(halves)]
    if state_in:
        old_ref, old_acc_ref = refs.pop(0), refs.pop(0)
    pts = [refs.pop(0) for _ in range(halves)]
    if state_out:
        new_ref, new_acc_ref = refs
    else:
        mine_ref, theirs_ref, stat_ref = refs
    i = pl.program_id(0)
    half_steps = pl.num_programs(0) // 2

    def run(attend_half):
        worst = None
        for h in range(2):
            qt = qt_ref[head_rows(h), :]
            states = []
            if state_in:
                states.append(
                    (old_ref[0, h : h + 1, :], old_ref[0, 2 + h : 3 + h, :],
                     old_acc_ref[head_rows(h), :])
                )
            for key_refs, pt_ref in zip(keys, pts):
                state = attend_half(chunk, h, qt, *key_refs, pt_ref)
                worst = state[1] if worst is None else jnp.maximum(worst, state[1])
                states.append(state)
            if state_out:
                new_ref[0, h : h + 1, :] = states[0][0]
                new_ref[0, 2 + h : 3 + h, :] = states[0][1]
                new_acc_ref[head_rows(h), :] = states[0][2]
            else:
                factors, result = merge(states)
                stat_ref[0, h : h + 1, :] = factors[0]
                stat_ref[0, 2 + h : 3 + h, :] = factors[1]
                low = result.T.astype(BF16)

                @pl.when(i < half_steps)
                def _():
                    mine_ref[:, head_rows(h)] = low

                @pl.when(i >= half_steps)
                def _():
                    theirs_ref[:, head_rows(h)] = low

        return worst

    worst = run(half_attend)

    @pl.when(jnp.logical_not(jnp.max(worst) <= LIMIT))
    def _():
        run(half_attend_exact)


def attend(qt, keys, state, last):
    rows = qt.shape[1]
    seq = keys[0][0].shape[0]
    n = rows // ROWS
    half = n // 2
    col = pl.BlockSpec((256, ROWS), lambda i: (0, i))
    stat = pl.BlockSpec((1, 8, ROWS), lambda i: (i, 0, 0))
    stat_shape = jax.ShapeDtypeStruct((n, 8, ROWS), F32)
    in_specs = [col]
    args = [qt]
    for key in keys:
        in_specs += [once(item.shape) for item in key]
        args += list(key)
    if state is not None:
        in_specs += [stat, col]
        args += list(state)
    out_specs = [pl.BlockSpec((1, 2, seq, ROWS), lambda i: (i, 0, 0, 0))] * len(keys)
    out_shape = [jax.ShapeDtypeStruct((n, 2, seq, ROWS), BF16)] * len(keys)
    if last:
        out_specs += [
            pl.BlockSpec((ROWS, 256), lambda i: (jnp.minimum(i, half - 1), 0)),
            pl.BlockSpec((ROWS, 256), lambda i: (jnp.maximum(i - half, 0), 0)),
            stat,
        ]
        out_shape += [jax.ShapeDtypeStruct((rows // 2, 256), BF16)] * 2 + [stat_shape]
    else:
        out_specs += [stat, col]
        out_shape += [stat_shape, jax.ShapeDtypeStruct((256, rows), F32)]
    pairs = 2 * rows * seq * len(keys)
    return pl.pallas_call(
        partial(attend_kernel, 512, len(keys), state is not None, not last),
        out_shape=out_shape,
        grid=(n,),
        in_specs=in_specs,
        out_specs=out_specs,
        compiler_params=params(),
        cost_estimate=cost(4 * pairs * HEAD_DIM * 2, 2 * pairs, pairs),
        name="attend",
    )(*args)


def back_weights(do, o, factor):
    dot_t = do.astype(F32).T
    delta = jnp.sum(dot_t * o.astype(F32).T, axis=0, keepdims=True) * factor
    high, middle, low = three_parts(delta)
    extra = extra_rows([jnp.zeros_like(delta), -high, -middle, -low], HEAD_DIM)
    return jnp.concatenate([(dot_t * factor).astype(BF16), extra], axis=0)


def back_half(chunk, h, da, qt, pt_ref, v_ref, kt_ref, key_acc, value_acc):
    ones = jnp.where(
        lax.broadcasted_iota(jnp.int32, (chunk, HEAD_DIM), 1) < 4, F32(1.0), F32(0.0)
    ).astype(BF16)
    query_grad = jnp.zeros((HEAD_DIM, qt.shape[1]), F32)
    for start in range(0, v_ref.shape[0], chunk):
        here = slice(start, start + chunk)
        prob = pt_ref[0, h, here, :]
        values = jnp.concatenate([v_ref[here, head_rows(h)], ones], axis=1)
        grad = mm(values, da)
        score = (prob.astype(F32) * grad).astype(BF16)
        value_acc[h, here, :] += mm(prob, da[:HEAD_DIM], NT)
        key_acc[h, here, :] += mm(score, qt, NT)
        query_grad = query_grad + mm(kt_ref[head_rows(h), here], score)
    return query_grad


def store_keys(key_acc, value_acc, dk_ref, dv_ref):
    for h in range(2):
        dk_ref[:, head_rows(h)] = (key_acc[h] * F32(1.0 / LOG2E)).astype(BF16)
        dv_ref[:, head_rows(h)] = value_acc[h].astype(BF16)


SCORE_SCALE = 1.0 / math.sqrt(HEAD_DIM)


def back_first_kernel(
    chunk, da_ref, db_ref, on_a, on_b, of_a, of_b, statn, statf, qtn, qtf, ptfn, ptff, ptnf,
    vn, ktn, vf, ktf, dqf_ref, dqn_ref, dkn_ref, dvn_ref, dkf_ref, dvf_ref, key_acc, value_acc,
):
    i = pl.program_id(0)
    n = pl.num_programs(0) // 2

    @pl.when(i == 0)
    def _():
        for ref in (key_acc, value_acc, dkn_ref, dvn_ref):
            ref[...] = jnp.zeros_like(ref)

    first = (i % n) < n // 2
    do = jnp.where(first, da_ref[...], db_ref[...])

    @pl.when(i < n)
    def _():
        o = jnp.where(first, of_a[...], of_b[...])
        for h in range(2):
            qt = qtf[head_rows(h), :]
            cols = head_rows(h)
            near = back_weights(do[:, cols], o[:, cols], statf[0, h : h + 1, :])
            far = back_weights(do[:, cols], o[:, cols], statf[0, 2 + h : 3 + h, :])
            grad = back_half(chunk, h, near, qt, ptfn, vn, ktn, dkn_ref, dvn_ref)
            grad += back_half(chunk, h, far, qt, ptff, vf, ktf, key_acc, value_acc)
            dqf_ref[:, cols] = (grad * F32(SCORE_SCALE)).T.astype(BF16)

    @pl.when(i >= n)
    def _():
        o = jnp.where(first, on_a[...], on_b[...])
        for h in range(2):
            qt = qtn[head_rows(h), :]
            cols = head_rows(h)
            far = back_weights(do[:, cols], o[:, cols], statn[0, 2 + h : 3 + h, :])
            dqn_ref[cols, :] = back_half(chunk, h, far, qt, ptnf, vf, ktf, key_acc, value_acc)

    @pl.when(i == 2 * n - 1)
    def _():
        store_keys(key_acc, value_acc, dkf_ref, dvf_ref)


def back_first(da, db, on_a, on_b, of_a, of_b, statn, statf, qtn, qtf, ptfn, ptff, ptnf,
               vn, ktn, vf, ktf):
    rows = qtn.shape[1]
    seq = vn.shape[0]
    n = rows // ROWS
    h = n // 2
    near = lambda i: jnp.maximum(i - n, 0)
    far = lambda i: jnp.minimum(i, n - 1)
    own = lambda i: jnp.where(i < n, h + jnp.minimum(i, h - 1), jnp.minimum(i - n, h - 1))
    sib = lambda i: jnp.where(i < n, jnp.maximum(i, h), jnp.maximum(i - n - h, 0))
    row = lambda f: pl.BlockSpec((ROWS, 256), lambda i: (f(i), 0))
    col = lambda f: pl.BlockSpec((256, ROWS), lambda i: (0, f(i)))
    stat = lambda f: pl.BlockSpec((1, 8, ROWS), lambda i: (f(i), 0, 0))
    tile = lambda f: pl.BlockSpec((1, 2, seq, ROWS), lambda i: (f(i), 0, 0, 0))
    low = lambda f: lambda i: jnp.minimum(f(i), h - 1)
    high = lambda f: lambda i: jnp.maximum(f(i) - h, 0)
    part = jax.ShapeDtypeStruct((2, seq, HEAD_DIM), F32)
    flat = jax.ShapeDtypeStruct((rows, 256), BF16)
    pairs = 2 * rows * seq * 3
    return pl.pallas_call(
        partial(back_first_kernel, 512),
        out_shape=[flat, jax.ShapeDtypeStruct((256, rows), F32), part, part, flat, flat],
        grid=(2 * n,),
        in_specs=[
            row(own), row(sib), row(low(near)), row(high(near)), row(low(far)), row(high(far)),
            stat(near), stat(far), col(near), col(far), tile(far), tile(far), tile(near),
            once(vn.shape), once(ktn.shape), once(vf.shape), once(ktf.shape),
        ],
        out_specs=[
            row(far), col(near), once(part.shape), once(part.shape), once(flat.shape),
            once(flat.shape),
        ],
        scratch_shapes=[pltpu.VMEM(part.shape, F32), pltpu.VMEM(part.shape, F32)],
        compiler_params=params(),
        cost_estimate=cost(8 * pairs * HEAD_DIM, 2 * pairs),
        name="attend_back_far",
    )(da, db, on_a, on_b, of_a, of_b, statn, statf, qtn, qtf, ptfn, ptff, ptnf, vn, ktn, vf, ktf)


def back_second_kernel(
    chunk, da_ref, db_ref, on_a, on_b, statn, qtn, ptnn, vn, ktn, dqn_ref, dkn_ref, dvn_ref,
    dq_ref, dk_ref, dv_ref, key_acc, value_acc,
):
    i = pl.program_id(0)
    n = pl.num_programs(0)

    @pl.when(i == 0)
    def _():
        key_acc[...] = dkn_ref[...]
        value_acc[...] = dvn_ref[...]

    first = i < n // 2
    do = jnp.where(first, da_ref[...], db_ref[...])
    o = jnp.where(first, on_a[...], on_b[...])
    for h in range(2):
        qt = qtn[head_rows(h), :]
        cols = head_rows(h)
        near = back_weights(do[:, cols], o[:, cols], statn[0, h : h + 1, :])
        grad = back_half(chunk, h, near, qt, ptnn, vn, ktn, key_acc, value_acc)
        grad = grad + dqn_ref[cols, :]
        dq_ref[:, cols] = (grad * F32(SCORE_SCALE)).T.astype(BF16)

    @pl.when(i == n - 1)
    def _():
        store_keys(key_acc, value_acc, dk_ref, dv_ref)


def back_second(da, db, on_a, on_b, statn, qtn, ptnn, vn, ktn, dqn, dkn, dvn):
    rows = qtn.shape[1]
    seq = vn.shape[0]
    n = rows // ROWS
    h = n // 2
    row = lambda f: pl.BlockSpec((ROWS, 256), lambda i: (f(i), 0))
    col = pl.BlockSpec((256, ROWS), lambda i: (0, i))
    low = lambda i: jnp.minimum(i, h - 1)
    high = lambda i: jnp.maximum(i - h, 0)
    flat = jax.ShapeDtypeStruct((rows, 256), BF16)
    pairs = 2 * rows * seq
    return pl.pallas_call(
        partial(back_second_kernel, 512),
        out_shape=[flat, flat, flat],
        grid=(n,),
        in_specs=[
            row(low), row(high), row(low), row(high),
            pl.BlockSpec((1, 8, ROWS), lambda i: (i, 0, 0)), col,
            pl.BlockSpec((1, 2, seq, ROWS), lambda i: (i, 0, 0, 0)),
            once(vn.shape), once(ktn.shape), col, once(dkn.shape), once(dvn.shape),
        ],
        out_specs=[row(lambda i: i), once(flat.shape), once(flat.shape)],
        scratch_shapes=[pltpu.VMEM(dkn.shape, F32), pltpu.VMEM(dkn.shape, F32)],
        compiler_params=params(),
        cost_estimate=cost(8 * pairs * HEAD_DIM, 2 * pairs),
        name="attend_back_near",
    )(da, db, on_a, on_b, statn, qtn, ptnn, vn, ktn, dqn, dkn, dvn)


def mean(values):
    return jnp.mean(values, axis=-1, keepdims=True)


def norm(values):
    centered = values - mean(values)
    inverse = lax.rsqrt(mean(centered * centered) + EPS)
    return centered * inverse, inverse


def norm_back(incoming, normed, inverse, gain):
    scaled = incoming * gain
    return inverse * (scaled - mean(scaled) - normed * mean(scaled * normed))


def gelu_parts(v):
    bell = jnp.exp2(v * v * F32(-0.5 * LOG2E))
    t = 1.0 / (1.0 + F32(0.3275911 / math.sqrt(2.0)) * jnp.abs(v))
    series = t * (
        F32(0.5 * 0.254829592)
        + t
        * (
            F32(0.5 * -0.284496736)
            + t
            * (
                F32(0.5 * 1.421413741)
                + t * (F32(0.5 * -1.453152027) + t * F32(0.5 * 1.061405429))
            )
        )
    )
    tail = series * bell
    return bell * F32(1.0 / math.sqrt(2.0 * math.pi)), jnp.where(v >= 0, 1.0 - tail, tail)


def fold_rows(values):
    return jnp.sum(values.reshape(values.shape[0] // 8, 8, values.shape[1]), axis=0)


def rows_kernel(
    sizes, meta, xa_ref, xb_ref, oa_n, oa_f, ob_n, ob_f, cot_a, cot_b, p0, p1, p2, p3,
    u0, u1, u2, u3, vec_ref,
    outa_ref, outb_ref, resid_ref, da_ref, db_ref, mine_ref, theirs_ref, sums_ref,
    wo_ref, up_ref, down_ref, bias_ref, grad_acc, vec_acc, bias_acc,
):
    prompt_local, data_local = sizes
    i = pl.program_id(0)
    half = pl.num_programs(0) // 2
    rows = xa_ref.shape[0]
    quarter = u0.shape[1]

    @pl.when(i == 0)
    def _():
        for j, (pack, up_part) in enumerate(((p0, u0), (p1, u1), (p2, u2), (p3, u3))):
            wo_ref[j * HEAD_DIM : (j + 1) * HEAD_DIM, :] = pack[:HEAD_DIM, :]
            down_ref[j * quarter : (j + 1) * quarter, :] = pack[HEAD_DIM : HEAD_DIM + quarter, :]
            bias_ref[0:1, j * quarter : (j + 1) * quarter] = pack[
                HEAD_DIM + quarter : HEAD_DIM + quarter + 16, :quarter
            ].astype(F32)[0:1, :]
            up_ref[:, j * quarter : (j + 1) * quarter] = up_part[...]
        grad_acc[...] = jnp.zeros_like(grad_acc)
        vec_acc[...] = jnp.zeros_like(vec_acc)
        bias_acc[...] = jnp.zeros_like(bias_acc)

    here = i < half
    slot = jnp.where(here, meta[0], meta[0] ^ 2)
    index = (i % half) * rows + lax.broadcasted_iota(jnp.int32, (rows, 1), 0) - prompt_local
    live = jnp.logical_or(index < 0, slot * data_local + index < meta[2])

    out_bias, attn_gain, attn_shift = vec_ref[0:1, :], vec_ref[1:2, :], vec_ref[2:3, :]
    down_bias, mlp_gain, mlp_shift = vec_ref[3:4, :], vec_ref[4:5, :], vec_ref[5:6, :]
    x = jnp.where(here, xa_ref[...], xb_ref[...])
    attended = jnp.concatenate(
        [jnp.where(here, oa_n[...], oa_f[...]), jnp.where(here, ob_n[...], ob_f[...])], axis=1
    )
    normed_one, inverse_one = norm(x.astype(F32) + (mm(attended, wo_ref[...]) + out_bias))
    hidden = normed_one * attn_gain + attn_shift
    hidden_low = hidden.astype(BF16)
    pre = mm(hidden_low, up_ref[...]) + bias_ref[0:1, :]
    density, share = gelu_parts(pre)
    activated = (pre * share).astype(BF16)
    slope = share + pre * density
    mixed = hidden + (mm(activated, down_ref[...]) + down_bias)
    normed_two, inverse_two = norm(mixed)
    output = (normed_two * mlp_gain + mlp_shift).astype(BF16)

    @pl.when(here)
    def _():
        outa_ref[...] = output

    @pl.when(jnp.logical_not(here))
    def _():
        outb_ref[...] = output

    cotangent = jnp.where(live, jnp.where(here, cot_a[...], cot_b[...]).astype(F32), 0.0)
    mixed_grad = norm_back(cotangent, normed_two, inverse_two, mlp_gain)
    mixed_low = mixed_grad.astype(BF16)
    pre_grad = (mm(mixed_low, down_ref[...], NT) * slope).astype(BF16)
    hidden_grad = mixed_grad + mm(pre_grad, up_ref[...], NT)
    resid_grad = norm_back(hidden_grad, normed_one, inverse_one, attn_gain)
    resid_ref[...] = resid_grad
    resid_low = resid_grad.astype(BF16)
    attended_grad = mm(resid_low, wo_ref[...], NT).astype(BF16)
    da_ref[...] = attended_grad[:, :256]
    db_ref[...] = attended_grad[:, 256:]

    up_grad = mm(hidden_low, pre_grad, TN)
    down_grad = mm(mixed_low, activated, TN)
    out_grad = mm(resid_low, attended, TN)
    for j in range(4):
        cols = slice(j * quarter, (j + 1) * quarter)
        grad_acc[j, :, :quarter] += up_grad[:, cols]
        grad_acc[j, :, quarter : 2 * quarter] += down_grad[:, cols]
        grad_acc[j, :, 2 * quarter :] += out_grad[:, head_rows(j)]
    bias_acc[...] += fold_rows(pre_grad.astype(F32))
    for place, value in enumerate(
        (
            resid_grad,
            hidden_grad * normed_one,
            hidden_grad,
            mixed_grad,
            cotangent * normed_two,
            cotangent,
        )
    ):
        vec_acc[place] += fold_rows(value)

    @pl.when(i == pl.num_programs(0) - 1)
    def _():
        depth = grad_acc.shape[1]
        bias_grad = jnp.sum(bias_acc[...], axis=0, keepdims=True)
        for j in range(4):
            target = mine_ref if j < 2 else theirs_ref
            kind = target.dtype
            target[j % 2, :depth, :] = grad_acc[j].astype(kind)
            target[j % 2, depth:, :] = jnp.zeros((16, grad_acc.shape[2]), kind)
            target[j % 2, depth:, :quarter] = jnp.broadcast_to(
                bias_grad[:, j * quarter : (j + 1) * quarter], (16, quarter)
            ).astype(kind)
        for place in range(6):
            sums_ref[place : place + 1, :] = jnp.sum(vec_acc[place], axis=0, keepdims=True)
        sums_ref[6:8, :] = jnp.zeros((2, depth), F32)


def row_work(meta, xa, xb, oa, ob, cot, packs, ups, vec, sizes):
    rows, width = xa.shape
    step = 512
    n = rows // step
    quarter = ups[0].shape[1]
    hidden = 4 * quarter
    wide = 2 * quarter + HEAD_DIM
    near = lambda cols: pl.BlockSpec((step, cols), lambda i, meta: (jnp.minimum(i, n - 1), 0))
    far = lambda cols: pl.BlockSpec((step, cols), lambda i, meta: (jnp.maximum(i - n, 0), 0))
    row = lambda cols: pl.BlockSpec((step, cols), lambda i, meta: (i, 0))
    return pl.pallas_call(
        partial(rows_kernel, sizes),
        out_shape=[
            jax.ShapeDtypeStruct((rows, width), BF16),
            jax.ShapeDtypeStruct((rows, width), BF16),
            jax.ShapeDtypeStruct((2 * rows, width), F32),
            jax.ShapeDtypeStruct((2 * rows, 256), BF16),
            jax.ShapeDtypeStruct((2 * rows, 256), BF16),
            jax.ShapeDtypeStruct((2, width + 16, wide), F32),
            jax.ShapeDtypeStruct((2, width + 16, wide), BF16),
            jax.ShapeDtypeStruct((8, width), F32),
        ],
        grid_spec=pltpu.PrefetchScalarGridSpec(
            num_scalar_prefetch=1,
            grid=(2 * n,),
            in_specs=[near(width), far(width), near(256), far(256), near(256), far(256),
                      near(width), far(width)]
            + [once(item.shape) for item in packs + ups]
            + [once(vec.shape)],
            out_specs=[
                near(width),
                far(width),
                row(width),
                row(256),
                row(256),
                once((2, width + 16, wide)),
                once((2, width + 16, wide)),
                once((8, width)),
            ],
            scratch_shapes=[
                pltpu.VMEM((4 * HEAD_DIM, width), BF16),
                pltpu.VMEM((width, hidden), BF16),
                pltpu.VMEM((hidden, width), BF16),
                pltpu.VMEM((8, hidden), F32),
                pltpu.VMEM((4, width, wide), F32),
                pltpu.VMEM((6, 8, width), F32),
                pltpu.VMEM((8, hidden), F32),
            ],
        ),
        compiler_params=params(),
        cost_estimate=cost(
            3 * 2 * 2 * rows * width * (width + 2 * hidden), 24 * rows * width, 4 * rows * hidden
        ),
        name="row_work",
    )(meta, xa, xb, *oa, *ob, *cot, *packs, *ups, vec)


def input_grad_kernel(dq_ref, dk_ref, dv_ref, w_ref, resid_ref, own_ref, sib_ref):
    dz = jnp.concatenate([dq_ref[...], dk_ref[...], dv_ref[...]], axis=1)
    part = mm(dz, w_ref[...], NT)
    first = pl.program_id(0) < pl.num_programs(0) // 2

    @pl.when(first)
    def _():
        sib_ref[...] = part.astype(BF16)

    @pl.when(jnp.logical_not(first))
    def _():
        own_ref[...] = part + resid_ref[...]


def input_grad(dq, dk, dv, w, resid, offset):
    rows = dq.shape[0]
    width = w.shape[0]
    step = 512
    n = rows // step
    half = n // 2
    turned = pl.BlockSpec((step, 256), lambda i: ((i + half) % n, 0))
    return pl.pallas_call(
        input_grad_kernel,
        out_shape=[
            jax.ShapeDtypeStruct((rows // 2, width), F32),
            jax.ShapeDtypeStruct((rows // 2, width), BF16),
        ],
        grid=(n,),
        in_specs=[turned, turned, turned, once(w.shape),
                  pl.BlockSpec((step, width), lambda i: (jnp.maximum(i - half, 0) + offset * half, 0))],
        out_specs=[
            pl.BlockSpec((step, width), lambda i: (jnp.maximum(i - half, 0), 0)),
            pl.BlockSpec((step, width), lambda i: (jnp.minimum(i, half - 1), 0)),
        ],
        compiler_params=params(),
        cost_estimate=cost(2 * rows * width * 768, rows * width * 8),
        name="input_grad",
    )(dq, dk, dv, w, resid)


def weight_grad_kernel(before, xa_ref, xb_ref, dq_ref, dk_ref, dv_ref, *refs):
    i = pl.program_id(0)
    n = pl.num_programs(0)
    acc = refs[-1]

    @pl.when(i == 0)
    def _():
        acc[...] = refs[0][...] if before else jnp.zeros_like(acc)

    x = jnp.where(i < n // 2, xa_ref[...], xb_ref[...])
    dz = jnp.concatenate([dq_ref[...], dk_ref[...], dv_ref[...]], axis=1)
    acc[...] += mm(x, dz, TN)

    @pl.when(i == n - 1)
    def _():
        if before:
            own_ref, other_ref = refs[1:3]
            for which in range(3):
                lo = which * 256
                own_ref[which] = acc[:, lo : lo + HEAD_DIM]
                other_ref[which] = acc[:, lo + HEAD_DIM : lo + 256].astype(BF16)
        else:
            refs[0][...] = acc[...]


def weight_grad(xa, xb, dq, dk, dv, before):
    rows, width = xa.shape
    step = 512
    n = rows // step
    row = pl.BlockSpec((step, 256), lambda i: (i, 0))
    args = [xa, xb, dq, dk, dv]
    in_specs = [
        pl.BlockSpec((step, width), lambda i: (jnp.minimum(i, n - 1), 0)),
        pl.BlockSpec((step, width), lambda i: (jnp.maximum(i - n, 0), 0)),
        row,
        row,
        row,
    ]
    whole = (width, 768)
    heads = (3, width, HEAD_DIM)
    if before is not None:
        args.append(before)
        in_specs.append(once(whole))
        out_shape = [jax.ShapeDtypeStruct(heads, F32), jax.ShapeDtypeStruct(heads, BF16)]
        out_specs = [once(heads), once(heads)]
    else:
        out_shape = jax.ShapeDtypeStruct(whole, F32)
        out_specs = once(whole)
    return pl.pallas_call(
        partial(weight_grad_kernel, before is not None),
        out_shape=out_shape,
        grid=(2 * n,),
        in_specs=in_specs,
        out_specs=out_specs,
        scratch_shapes=[pltpu.VMEM(whole, F32)],
        compiler_params=params(),
        cost_estimate=cost(2 * 2 * rows * width * 768, rows * width * 8),
        name="weight_grad",
    )(*args)


def on_device(
    data_rows,
    prompt_rows,
    context_rows,
    test_rows,
    qkv_weight,
    out_bias,
    out_weight,
    attn_gain,
    attn_shift,
    up_weight,
    up_bias,
    down_weight,
    down_bias,
    mlp_gain,
    mlp_shift,
    data_cotangent,
    prompt_cotangent,
):
    data_local = data_rows.shape[1]
    prompt_local = prompt_rows.shape[0]
    width = prompt_rows.shape[1]
    quarter = up_weight.shape[1]
    sizes = (prompt_local, data_local)
    groups = lax.axis_size("ep")
    t = lax.axis_index("tp")
    mine = t >> 1
    other = 1 - mine

    def across(value):
        return lax.ppermute(value, "tp", [(i, i ^ 2) for i in range(4)])

    def beside(value):
        return lax.ppermute(value, "tp", [(i, i ^ 1) for i in range(4)])

    def pick(values, which):
        return lax.dynamic_index_in_dim(values, which, axis=0, keepdims=False)

    def stack(prompt_part, data_part):
        return jnp.concatenate([prompt_part, data_part], axis=0)

    w_far = across(qkv_weight)
    x_far = across(stack(prompt_rows, pick(data_rows, other)))
    x = stack(prompt_rows, pick(data_rows, mine))
    x_sib = beside(x)
    context = pick(context_rows, mine)
    live = context + pick(test_rows, mine)
    meta = jnp.stack([t, context, live]).astype(jnp.int32)

    qtn, kn, kxn, ktn, vn, vtn, w = project(meta, x, x_sib, qkv_weight, w_far, sizes, 0)
    ptnn, state, state_acc = attend(qtn, [(kn, kxn, vtn)], None, False)

    x_far, state = lax.optimization_barrier((x_far, state))
    x_far_sib = beside(x_far)
    qtf, kf, kxf, ktf, vf, vtf, _ = project(meta, x_far, x_far_sib, qkv_weight, w_far, sizes, 2)
    ptnf, on_a, on_b, statn = attend(qtn, [(kf, kxf, vtf)], (state, state_acc), True)
    ptfn, ptff, of_a, of_b, statf = attend(qtf, [(kn, kxn, vtn), (kf, kxf, vtf)], None, True)

    cot = stack(pick(prompt_cotangent, mine), pick(data_cotangent, mine))
    cot_far = across(stack(pick(prompt_cotangent, other), pick(data_cotangent, other)))
    bias_rows = jnp.zeros((16, width), BF16).at[0, :quarter].set(up_bias)
    pack = jnp.concatenate([out_weight, down_weight, bias_rows], axis=0)
    pack_far, up_far = across(pack), across(up_weight)
    packs = [pack, pack_far, beside(pack), beside(pack_far)]
    ups = [up_weight, up_far, beside(up_weight), beside(up_far)]
    vec = jnp.stack(
        [out_bias, attn_gain, attn_shift, down_bias, mlp_gain, mlp_shift, mlp_shift, mlp_shift]
    ).astype(F32)
    out, out_far, resid, da, db, grads_mine, grads_theirs, sums = row_work(
        meta, x, x_far, (on_a, of_a), (beside(on_b), beside(of_b)), (cot, cot_far), packs, ups,
        vec, sizes,
    )

    db = beside(db)
    pair = grads_mine + beside(grads_theirs).astype(F32)
    pair_far, da, db = lax.optimization_barrier((pair[1].astype(BF16), da, db))
    pair_far = across(pair_far)
    sums = lax.all_gather(sums, ("ep", "tp"))
    out_back = across(out_far)

    dqf, dqn, dkn, dvn, dkf, dvf = back_first(
        da, db, on_a, on_b, of_a, of_b, statn, statf, qtn, qtf, ptfn, ptff, ptnf, vn, ktn, vf, ktf
    )
    total = (pair[0] + pair_far.astype(F32)).astype(BF16)
    total, out_back, sums, dqf = lax.optimization_barrier((total, out_back, sums, dqf))
    far_own, far_sib = input_grad(dqf, dkf, dvf, w, resid, 1)
    far_sib = beside(far_sib)
    grad_far = weight_grad(x_far, x_far_sib, dqf, dkf, dvf, None)
    there = (far_own + far_sib.astype(F32)).astype(BF16)
    there, total, dqn = lax.optimization_barrier((there, total, dqn))
    there = across(there)
    total = lax.psum(total, "ep")

    dqn, dkn, dvn = back_second(da, db, on_a, on_b, statn, qtn, ptnn, vn, ktn, dqn, dkn, dvn)
    there, dqn = lax.optimization_barrier((there, dqn))
    qkv_own, qkv_other = weight_grad(x, x_sib, dqn, dkn, dvn, grad_far)
    qkv_sum = (qkv_own + across(qkv_other).astype(F32)).astype(BF16)
    near_own, near_sib = input_grad(dqn, dkn, dvn, w, resid, 0)
    near = near_own + beside(near_sib).astype(F32)

    def scatter(value):
        parts = value.reshape((groups, value.shape[0] // groups) + value.shape[1:])
        parts = lax.all_to_all(parts, "ep", 0, 0, tiled=True)
        return jnp.sum(parts.astype(F32), axis=0).astype(BF16)

    qkv_part = scatter(qkv_sum.reshape(3 * width, HEAD_DIM))
    qkv_part, total = lax.optimization_barrier((qkv_part, total))
    total = total.astype(F32)
    qkv_grad = lax.all_to_all(
        jnp.broadcast_to(qkv_part[None], (groups,) + qkv_part.shape), "ep", 0, 0, tiled=True
    )
    qkv_grad = qkv_grad.reshape(3, width, HEAD_DIM).astype(F32)
    prompt_sum = (near[:prompt_local] + there[:prompt_local].astype(F32)).astype(BF16)
    prompt_grad = lax.all_gather(scatter(prompt_sum), "ep", axis=0, tiled=True).astype(F32)

    which = lax.broadcasted_iota(jnp.int32, (2, 1, 1), 0)

    def by_episode(own, received):
        return jnp.where(which == mine, own[None], received[None])

    sums = jnp.sum(sums.reshape(-1, 8, width), axis=0)
    return (
        by_episode(out[prompt_local:], out_back[prompt_local:]),
        by_episode(out[:prompt_local], out_back[:prompt_local]),
        by_episode(near[prompt_local:].astype(BF16), there[prompt_local:]),
        prompt_grad,
        qkv_grad,
        sums[0],
        total[:width, 2 * quarter :].T,
        sums[1],
        sums[2],
        total[:width, :quarter],
        total[width, :quarter],
        total[:width, quarter : 2 * quarter].T,
        sums[3],
        sums[4],
        sums[5],
    )


def solution(mesh):
    return jax.shard_map(
        on_device,
        mesh=mesh,
        in_specs=(
            P("ep", "tp", None),
            P("tp", None),
            P("ep"),
            P("ep"),
            P(None, None, "tp"),
            P(),
            P("tp", None),
            P(),
            P(),
            P(None, "tp"),
            P("tp"),
            P("tp", None),
            P(),
            P(),
            P(),
            P("ep", "tp", None),
            P("ep", "tp", None),
        ),
        out_specs=(
            P("ep", "tp", None),
            P("ep", "tp", None),
            P("ep", "tp", None),
            P("tp", None),
            P(None, None, "tp"),
            P(),
            P("tp", None),
            P(),
            P(),
            P(None, "tp"),
            P("tp"),
            P("tp", None),
            P(),
            P(),
            P(),
        ),
        check_vma=False,
    )
```

```python
from functools import partial
import math

import jax
import jax.numpy as jnp
from jax import lax
from jax.experimental import pallas as pl
from jax.experimental.pallas import tpu as pltpu
from jax.sharding import PartitionSpec as P

HEAD_DIM = 128
ROWS = 512
SAMPLE = 256
EPS = 1e-05
MASKED = -1e30
LOG2E = math.log2(math.e)
LIMIT = 2.0**60
VMEM = 60 * 1024 * 1024
F32 = jnp.float32
BF16 = jnp.bfloat16
NN = (((1,), (0,)), ((), ()))
NT = (((1,), (1,)), ((), ()))
TN = (((0,), (0,)), ((), ()))


def mm(left, right, dims=NN):
    return lax.dot_general(left, right, dims, preferred_element_type=F32)


def params(**more):
    return pltpu.CompilerParams(vmem_limit_bytes=VMEM, **more)


def cost(flops, nbytes, trans=0):
    return pl.CostEstimate(
        flops=int(flops), bytes_accessed=int(nbytes), transcendentals=int(trans)
    )


def once(shape):
    return pl.BlockSpec(shape, lambda *_: (0,) * len(shape), pipeline_mode=pl.Buffered(1))


def extra_rows(values, count):
    width = values[0].shape[1]
    row = lax.broadcasted_iota(jnp.int32, (count, width), 0)
    out = jnp.zeros((count, width), F32)
    for index, value in enumerate(values):
        out = jnp.where(row == index, value, out)
    return out.astype(BF16)


def three_parts(row):
    high = row.astype(BF16).astype(F32)
    middle = (row - high).astype(BF16).astype(F32)
    return high, middle, row - high - middle


def clamp(i, low, high):
    return jnp.minimum(jnp.maximum(i, low), high)


def project_kernel(sizes, flip, meta, xa_ref, xb_ref, wa_ref, wb_ref, qt_ref, k_ref, kx_ref,
                   kt_ref, v_ref, vt_ref, w_ref, wt_ref):
    prompt_local, data_local = sizes
    i = pl.program_id(0)
    per_slot = pl.num_programs(0) // 2
    rows = xa_ref.shape[0]

    @pl.when(i == 0)
    def _():
        for which in range(3):
            for h, source in enumerate((wa_ref, wb_ref)):
                cols = slice(which * 256 + h * HEAD_DIM, which * 256 + (h + 1) * HEAD_DIM)
                w_ref[:, cols] = source[which]
                wt_ref[cols, :] = source[which].T

    x = jnp.where(i < per_slot, xa_ref[...], xb_ref[...])
    slot = jnp.where(i < per_slot, meta[0] ^ flip, meta[0] ^ flip ^ 1)
    row = lax.broadcasted_iota(jnp.int32, (rows, HEAD_DIM), 0)
    lane = lax.broadcasted_iota(jnp.int32, (rows, HEAD_DIM), 1)
    index = (i % per_slot) * rows + row - prompt_local
    attended = jnp.logical_or(index < 0, slot * data_local + index < meta[1])
    bias = jnp.where(attended, F32(0.0), F32(MASKED))
    ones = jnp.where(lane < 4, F32(1.0), F32(0.0))
    kx_ref[...] = jnp.where(lane == 0, bias, ones).astype(BF16)
    z = mm(x, w_ref[:, 256:]).astype(BF16)
    k_ref[...] = z[:, :256]
    v_ref[...] = z[:, 256:]
    zt = mm(wt_ref[...], x, NT)
    factor = F32(LOG2E / math.sqrt(HEAD_DIM))
    qt_ref[...] = (zt[:256] * factor).astype(BF16)
    kt_ref[...] = zt[256:512].astype(BF16)
    vt_ref[...] = zt[512:].astype(BF16)


def project(meta, xa, xb, wa, wb, sizes, flip):
    rows, width = xa.shape
    step = 512
    n = rows // step
    flat = jax.ShapeDtypeStruct((2 * rows, 256), BF16)
    tall = jax.ShapeDtypeStruct((256, 2 * rows), BF16)
    row = pl.BlockSpec((step, 256), lambda i, meta: (i, 0))
    col = pl.BlockSpec((256, step), lambda i, meta: (0, i))
    return pl.pallas_call(
        partial(project_kernel, sizes, flip),
        out_shape=[
            tall,
            flat,
            jax.ShapeDtypeStruct((2 * rows, HEAD_DIM), BF16),
            tall,
            flat,
            tall,
            jax.ShapeDtypeStruct((width, 768), BF16),
        ],
        grid_spec=pltpu.PrefetchScalarGridSpec(
            num_scalar_prefetch=1,
            grid=(2 * n,),
            in_specs=[
                pl.BlockSpec((step, width), lambda i, meta: (jnp.minimum(i, n - 1), 0)),
                pl.BlockSpec((step, width), lambda i, meta: (jnp.maximum(i - n, 0), 0)),
                once(wa.shape),
                once(wb.shape),
            ],
            out_specs=[
                col,
                row,
                pl.BlockSpec((step, HEAD_DIM), lambda i, meta: (i, 0)),
                col,
                row,
                col,
                once((width, 768)),
            ],
            scratch_shapes=[pltpu.VMEM((768, width), BF16)],
        ),
        compiler_params=params(),
        cost_estimate=cost(4 * 2 * rows * width * 768, 2 * rows * width * 8),
        name="project",
    )(meta, xa, xb, wa, wb)


def head_rows(h):
    return slice(h * HEAD_DIM, (h + 1) * HEAD_DIM)


def with_shift(qt, top):
    high, middle, low = three_parts(top)
    extra = extra_rows([jnp.ones_like(top), -high, -middle, -low], HEAD_DIM)
    return jnp.concatenate([qt, extra], axis=0)


def half_weights(chunk, h, qa, start, k_ref, kx_ref):
    here = pl.ds(start, chunk)
    keys = jnp.concatenate([k_ref[here, head_rows(h)], kx_ref[here, :]], axis=1)
    return mm(keys, qa)


def half_part(chunk, h, qa, start, k_ref, kx_ref, vt_ref, pt_ref):
    weight = jnp.exp2(half_weights(chunk, h, qa, start, k_ref, kx_ref))
    total = jnp.sum(weight.reshape(chunk // 8, 8, weight.shape[1]), axis=0)
    low = weight.astype(BF16)
    pt_ref[0, h, pl.ds(start, chunk), :] = low
    return total, mm(vt_ref[head_rows(h), pl.ds(start, chunk)], low)


def stale_shift(h, qt, k_ref):
    top = jnp.max(mm(k_ref[:SAMPLE, head_rows(h)], qt), axis=0, keepdims=True)
    return top, with_shift(qt, top)


def half_attend(chunk, h, shift, k_ref, kx_ref, vt_ref, pt_ref):
    top, qa = shift
    total = jnp.zeros((8, qa.shape[1]), F32)
    acc = jnp.zeros((HEAD_DIM, qa.shape[1]), F32)
    for start in range(0, k_ref.shape[0], chunk):
        more, product = half_part(chunk, h, qa, start, k_ref, kx_ref, vt_ref, pt_ref)
        total, acc = total + more, acc + product
    return top, jnp.sum(total, axis=0, keepdims=True), acc


def half_attend_exact(chunk, h, shift, k_ref, kx_ref, vt_ref, pt_ref):
    qt = shift[1][:HEAD_DIM]
    width = qt.shape[1]
    count = k_ref.shape[0] // chunk
    qa = with_shift(qt, jnp.zeros((1, width), F32))

    def find(j, top):
        found = half_weights(chunk, h, qa, pl.multiple_of(j * chunk, chunk), k_ref, kx_ref)
        return jnp.maximum(top, jnp.max(found, axis=0, keepdims=True))

    top = lax.fori_loop(0, count, find, jnp.full((1, width), MASKED, F32))
    qa = with_shift(qt, top)

    def add(j, state):
        start = pl.multiple_of(j * chunk, chunk)
        more, product = half_part(chunk, h, qa, start, k_ref, kx_ref, vt_ref, pt_ref)
        return state[0] + more, state[1] + product

    total, acc = lax.fori_loop(
        0, count, add, (jnp.zeros((8, width), F32), jnp.zeros((HEAD_DIM, width), F32))
    )
    return top, jnp.sum(total, axis=0, keepdims=True), acc


def merge(states):
    top = states[0][0]
    for state in states[1:]:
        top = jnp.maximum(top, state[0])
    scales = [jnp.exp2(state[0] - top) for state in states]
    total = sum(state[1] * scale for state, scale in zip(states, scales))
    factors = [scale / total for scale in scales]
    return factors, sum(state[2] * factor for state, factor in zip(states, factors))


def attend_kernel(chunk, halves, state_in, state_out, *refs):
    refs = list(refs)
    qt_ref = refs.pop(0)
    keys = [[refs.pop(0) for _ in range(3)] for _ in range(halves)]
    if state_in:
        old_ref, old_acc_ref = refs.pop(0), refs.pop(0)
    pts = [refs.pop(0) for _ in range(halves)]
    if state_out:
        new_ref, new_acc_ref = refs
    else:
        mine_ref, theirs_ref, stat_ref = refs
    i = pl.program_id(0)
    half_steps = pl.num_programs(0) // 2

    shifts = [
        [stale_shift(h, qt_ref[head_rows(h), :], key_refs[0]) for key_refs in keys]
        for h in range(2)
    ]

    def run(attend_half):
        worst = None
        for h in range(2):
            states = []
            if state_in:
                states.append(
                    (old_ref[0, h : h + 1, :], old_ref[0, 2 + h : 3 + h, :],
                     old_acc_ref[head_rows(h), :])
                )
            for shift, key_refs, pt_ref in zip(shifts[h], keys, pts):
                state = attend_half(chunk, h, shift, *key_refs, pt_ref)
                worst = state[1] if worst is None else jnp.maximum(worst, state[1])
                states.append(state)
            if state_out:
                new_ref[0, h : h + 1, :] = states[0][0]
                new_ref[0, 2 + h : 3 + h, :] = states[0][1]
                new_acc_ref[head_rows(h), :] = states[0][2]
            else:
                factors, result = merge(states)
                stat_ref[0, h : h + 1, :] = factors[0]
                stat_ref[0, 2 + h : 3 + h, :] = factors[1]
                low = result.T.astype(BF16)

                @pl.when(i < half_steps)
                def _():
                    mine_ref[:, head_rows(h)] = low

                @pl.when(i >= half_steps)
                def _():
                    theirs_ref[:, head_rows(h)] = low

        return worst

    worst = run(half_attend)

    @pl.when(jnp.logical_not(jnp.max(worst) <= LIMIT))
    def _():
        run(half_attend_exact)


def attend(qt, keys, state, last):
    rows = qt.shape[1]
    seq = keys[0][0].shape[0]
    n = rows // ROWS
    half = n // 2
    col = pl.BlockSpec((256, ROWS), lambda i: (0, i))
    stat = pl.BlockSpec((1, 8, ROWS), lambda i: (i, 0, 0))
    stat_shape = jax.ShapeDtypeStruct((n, 8, ROWS), F32)
    in_specs = [col]
    args = [qt]
    for key in keys:
        in_specs += [once(item.shape) for item in key]
        args += list(key)
    if state is not None:
        in_specs += [stat, col]
        args += list(state)
    out_specs = [pl.BlockSpec((1, 2, seq, ROWS), lambda i: (i, 0, 0, 0))] * len(keys)
    out_shape = [jax.ShapeDtypeStruct((n, 2, seq, ROWS), BF16)] * len(keys)
    if last:
        out_specs += [
            pl.BlockSpec((ROWS, 256), lambda i: (jnp.minimum(i, half - 1), 0)),
            pl.BlockSpec((ROWS, 256), lambda i: (jnp.maximum(i - half, 0), 0)),
            stat,
        ]
        out_shape += [jax.ShapeDtypeStruct((rows // 2, 256), BF16)] * 2 + [stat_shape]
    else:
        out_specs += [stat, col]
        out_shape += [stat_shape, jax.ShapeDtypeStruct((256, rows), F32)]
    pairs = 2 * rows * seq * len(keys)
    return pl.pallas_call(
        partial(attend_kernel, 512, len(keys), state is not None, not last),
        out_shape=out_shape,
        grid=(n,),
        in_specs=in_specs,
        out_specs=out_specs,
        compiler_params=params(),
        cost_estimate=cost(4 * pairs * HEAD_DIM * 2, 2 * pairs, pairs),
        name="attend",
    )(*args)


def back_weights(do, o, factors):
    dot_t = do.astype(F32).T
    delta = jnp.sum(dot_t * o.astype(F32).T, axis=0, keepdims=True)
    return [((dot_t * factor).astype(BF16), delta * factor) for factor in factors]


def back_half(chunk, h, grads, qt, pt_ref, v_ref, kt_ref, key_acc, value_acc):
    da, delta = grads
    query_grad = jnp.zeros((HEAD_DIM, qt.shape[1]), F32)
    for start in range(0, v_ref.shape[0], chunk):
        here = slice(start, start + chunk)
        prob = pt_ref[0, h, here, :]
        grad = mm(v_ref[here, head_rows(h)], da) - delta
        score = (prob.astype(F32) * grad).astype(BF16)
        value_acc[h, here, :] += mm(prob, da, NT)
        key_acc[h, here, :] += mm(score, qt, NT)
        query_grad = query_grad + mm(kt_ref[head_rows(h), here], score)
    return query_grad


def store_keys(key_acc, value_acc, dk_ref, dv_ref):
    for h in range(2):
        dk_ref[:, head_rows(h)] = (key_acc[h] * F32(1.0 / LOG2E)).astype(BF16)
        dv_ref[:, head_rows(h)] = value_acc[h].astype(BF16)


SCORE_SCALE = 1.0 / math.sqrt(HEAD_DIM)


def back_first_kernel(
    chunk, da_ref, db_ref, on_a, on_b, of_a, of_b, statn, statf, qtn, qtf, ptfn, ptff, ptnf,
    vn, ktn, vf, ktf, dqf_ref, dqn_ref, dkn_ref, dvn_ref, dkf_ref, dvf_ref, key_acc, value_acc,
):
    i = pl.program_id(0)
    n = pl.num_programs(0) // 2

    @pl.when(i == 0)
    def _():
        for ref in (key_acc, value_acc, dkn_ref, dvn_ref):
            ref[...] = jnp.zeros_like(ref)

    first = (i % n) < n // 2
    do = jnp.where(first, da_ref[...], db_ref[...])

    @pl.when(i < n)
    def _():
        o = jnp.where(first, of_a[...], of_b[...])
        grads = [
            back_weights(
                do[:, head_rows(h)],
                o[:, head_rows(h)],
                [statf[0, h : h + 1, :], statf[0, 2 + h : 3 + h, :]],
            )
            for h in range(2)
        ]
        for h in range(2):
            qt = qtf[head_rows(h), :]
            near, far = grads[h]
            grad = back_half(chunk, h, near, qt, ptfn, vn, ktn, dkn_ref, dvn_ref)
            grad += back_half(chunk, h, far, qt, ptff, vf, ktf, key_acc, value_acc)
            dqf_ref[:, head_rows(h)] = (grad * F32(SCORE_SCALE)).T.astype(BF16)

    @pl.when(i >= n)
    def _():
        o = jnp.where(first, on_a[...], on_b[...])
        grads = [
            back_weights(do[:, head_rows(h)], o[:, head_rows(h)], [statn[0, 2 + h : 3 + h, :]])
            for h in range(2)
        ]
        for h in range(2):
            qt = qtn[head_rows(h), :]
            dqn_ref[head_rows(h), :] = back_half(
                chunk, h, grads[h][0], qt, ptnf, vf, ktf, key_acc, value_acc
            )

    @pl.when(i == 2 * n - 1)
    def _():
        store_keys(key_acc, value_acc, dkf_ref, dvf_ref)


def back_first(da, db, on_a, on_b, of_a, of_b, statn, statf, qtn, qtf, ptfn, ptff, ptnf,
               vn, ktn, vf, ktf):
    rows = qtn.shape[1]
    seq = vn.shape[0]
    n = rows // ROWS
    h = n // 2
    near = lambda i: jnp.maximum(i - n, 0)
    far = lambda i: jnp.minimum(i, n - 1)
    own = lambda i: jnp.where(i < n, h + jnp.minimum(i, h - 1), jnp.minimum(i - n, h - 1))
    sib = lambda i: jnp.where(i < n, jnp.maximum(i, h), jnp.maximum(i - n - h, 0))
    row = lambda f: pl.BlockSpec((ROWS, 256), lambda i: (f(i), 0))
    col = lambda f: pl.BlockSpec((256, ROWS), lambda i: (0, f(i)))
    stat = lambda f: pl.BlockSpec((1, 8, ROWS), lambda i: (f(i), 0, 0))
    tile = lambda f: pl.BlockSpec((1, 2, seq, ROWS), lambda i: (f(i), 0, 0, 0))
    low = lambda f: lambda i: jnp.minimum(f(i), h - 1)
    high = lambda f: lambda i: jnp.maximum(f(i) - h, 0)
    part = jax.ShapeDtypeStruct((2, seq, HEAD_DIM), F32)
    flat = jax.ShapeDtypeStruct((rows, 256), BF16)
    pairs = 2 * rows * seq * 3
    return pl.pallas_call(
        partial(back_first_kernel, 512),
        out_shape=[flat, jax.ShapeDtypeStruct((256, rows), F32), part, part, flat, flat],
        grid=(2 * n,),
        in_specs=[
            row(own), row(sib), row(low(near)), row(high(near)), row(low(far)), row(high(far)),
            stat(near), stat(far), col(near), col(far), tile(far), tile(far), tile(near),
            once(vn.shape), once(ktn.shape), once(vf.shape), once(ktf.shape),
        ],
        out_specs=[
            row(far), col(near), once(part.shape), once(part.shape), once(flat.shape),
            once(flat.shape),
        ],
        scratch_shapes=[pltpu.VMEM(part.shape, F32), pltpu.VMEM(part.shape, F32)],
        compiler_params=params(),
        cost_estimate=cost(8 * pairs * HEAD_DIM, 2 * pairs),
        name="attend_back_far",
    )(da, db, on_a, on_b, of_a, of_b, statn, statf, qtn, qtf, ptfn, ptff, ptnf, vn, ktn, vf, ktf)


def back_second_kernel(
    chunk, da_ref, db_ref, on_a, on_b, statn, qtn, ptnn, vn, ktn, dqn_ref, dkn_ref, dvn_ref,
    dq_ref, dk_ref, dv_ref, key_acc, value_acc,
):
    i = pl.program_id(0)
    n = pl.num_programs(0)

    @pl.when(i == 0)
    def _():
        key_acc[...] = dkn_ref[...]
        value_acc[...] = dvn_ref[...]

    first = i < n // 2
    do = jnp.where(first, da_ref[...], db_ref[...])
    o = jnp.where(first, on_a[...], on_b[...])
    grads = [
        back_weights(do[:, head_rows(h)], o[:, head_rows(h)], [statn[0, h : h + 1, :]])
        for h in range(2)
    ]
    for h in range(2):
        qt = qtn[head_rows(h), :]
        grad = back_half(chunk, h, grads[h][0], qt, ptnn, vn, ktn, key_acc, value_acc)
        grad = grad + dqn_ref[head_rows(h), :]
        dq_ref[:, head_rows(h)] = (grad * F32(SCORE_SCALE)).T.astype(BF16)

    @pl.when(i == n - 1)
    def _():
        store_keys(key_acc, value_acc, dk_ref, dv_ref)


def back_second(da, db, on_a, on_b, statn, qtn, ptnn, vn, ktn, dqn, dkn, dvn):
    rows = qtn.shape[1]
    seq = vn.shape[0]
    n = rows // ROWS
    h = n // 2
    row = lambda f: pl.BlockSpec((ROWS, 256), lambda i: (f(i), 0))
    col = pl.BlockSpec((256, ROWS), lambda i: (0, i))
    low = lambda i: jnp.minimum(i, h - 1)
    high = lambda i: jnp.maximum(i - h, 0)
    flat = jax.ShapeDtypeStruct((rows, 256), BF16)
    pairs = 2 * rows * seq
    return pl.pallas_call(
        partial(back_second_kernel, 512),
        out_shape=[flat, flat, flat],
        grid=(n,),
        in_specs=[
            row(low), row(high), row(low), row(high),
            pl.BlockSpec((1, 8, ROWS), lambda i: (i, 0, 0)), col,
            pl.BlockSpec((1, 2, seq, ROWS), lambda i: (i, 0, 0, 0)),
            once(vn.shape), once(ktn.shape), col, once(dkn.shape), once(dvn.shape),
        ],
        out_specs=[row(lambda i: i), once(flat.shape), once(flat.shape)],
        scratch_shapes=[pltpu.VMEM(dkn.shape, F32), pltpu.VMEM(dkn.shape, F32)],
        compiler_params=params(),
        cost_estimate=cost(8 * pairs * HEAD_DIM, 2 * pairs),
        name="attend_back_near",
    )(da, db, on_a, on_b, statn, qtn, ptnn, vn, ktn, dqn, dkn, dvn)


def mean(values):
    return jnp.mean(values, axis=-1, keepdims=True)


def norm(values):
    centered = values - mean(values)
    inverse = lax.rsqrt(mean(centered * centered) + EPS)
    return centered * inverse, inverse


def norm_back(incoming, normed, inverse, gain):
    scaled = incoming * gain
    return inverse * (scaled - mean(scaled) - normed * mean(scaled * normed))


def gelu_parts(v):
    bell = jnp.exp2(v * v * F32(-0.5 * LOG2E))
    t = 1.0 / (1.0 + F32(0.3275911 / math.sqrt(2.0)) * jnp.abs(v))
    series = t * (
        F32(0.5 * 0.254829592)
        + t
        * (
            F32(0.5 * -0.284496736)
            + t
            * (
                F32(0.5 * 1.421413741)
                + t * (F32(0.5 * -1.453152027) + t * F32(0.5 * 1.061405429))
            )
        )
    )
    tail = series * bell
    return bell * F32(1.0 / math.sqrt(2.0 * math.pi)), jnp.where(v >= 0, 1.0 - tail, tail)


def fold_rows(values):
    return jnp.sum(values.reshape(values.shape[0] // 8, 8, values.shape[1]), axis=0)


def rows_kernel(
    sizes, meta, xa_ref, xb_ref, oa_n, oa_f, ob_n, ob_f, cot_a, cot_b, p0, p1, p2, p3,
    u0, u1, u2, u3, vec_ref,
    prompt_near, data_near, prompt_far, data_far, resid_ref, da_ref, db_ref, mine_ref,
    theirs_ref, sums_ref, wo_ref, up_ref, down_ref, bias_ref, grad_acc, vec_acc, bias_acc,
):
    prompt_local, data_local = sizes
    i = pl.program_id(0)
    here = i == 0
    rows = xa_ref.shape[0]
    quarter = u0.shape[1]
    part = rows // 2

    @pl.when(here)
    def _():
        for j, (pack, up_part) in enumerate(((p0, u0), (p1, u1), (p2, u2), (p3, u3))):
            cols = slice(j * quarter, (j + 1) * quarter)
            wo_ref[head_rows(j), :] = pack[:HEAD_DIM, :]
            down_ref[cols, :] = pack[HEAD_DIM : HEAD_DIM + quarter, :]
            bias_ref[0:1, cols] = pack[
                HEAD_DIM + quarter : HEAD_DIM + quarter + 16, :quarter
            ].astype(F32)[0:1, :]
            up_ref[:, cols] = up_part[...]
        grad_acc[...] = jnp.zeros_like(grad_acc)
        vec_acc[...] = jnp.zeros_like(vec_acc)
        bias_acc[...] = jnp.zeros_like(bias_acc)

    slot = jnp.where(here, meta[0], meta[0] ^ 2)
    out_bias, attn_gain, attn_shift = vec_ref[0:1, :], vec_ref[1:2, :], vec_ref[2:3, :]
    down_bias, mlp_gain, mlp_shift = vec_ref[3:4, :], vec_ref[4:5, :], vec_ref[5:6, :]
    subs = [slice(s * part, (s + 1) * part) for s in range(2)]
    state = [{}, {}]

    def choose(near_ref, far_ref, s):
        return jnp.where(here, near_ref[subs[s], :], far_ref[subs[s], :])

    def attention_branch(s):
        own = choose(oa_n, oa_f, s)
        sib = choose(ob_n, ob_f, s)
        attended = jnp.concatenate([own, sib], axis=1)
        x = choose(xa_ref, xb_ref, s).astype(F32)
        state[s].update(attended=attended, sum=x + (mm(attended, wo_ref[...]) + out_bias))

    def first_norm(s):
        normed, inverse = norm(state[s].pop("sum"))
        hidden = normed * attn_gain + attn_shift
        state[s].update(one=normed, inv_one=inverse, hidden=hidden, low=hidden.astype(BF16))

    def up_project(s):
        state[s].update(pre=mm(state[s]["low"], up_ref[...]) + bias_ref[0:1, :])

    def activate(s):
        pre = state[s].pop("pre")
        density, share = gelu_parts(pre)
        state[s].update(act=(pre * share).astype(BF16), slope=share + pre * density)

    def down_project(s):
        state[s].update(
            mixed=state[s].pop("hidden") + (mm(state[s]["act"], down_ref[...]) + down_bias)
        )

    def second_norm(s):
        normed, inverse = norm(state[s].pop("mixed"))
        output = (normed * mlp_gain + mlp_shift).astype(BF16)

        def store(prompt_ref, data_ref):
            split = max(0, min(part, prompt_local - s * part))
            if split:
                prompt_ref[s * part : s * part + split, :] = output[:split]
            if split < part:
                begin = s * part + split - prompt_local
                data_ref[begin : begin + part - split, :] = output[split:]

        @pl.when(here)
        def _():
            store(prompt_near, data_near)

        @pl.when(jnp.logical_not(here))
        def _():
            store(prompt_far, data_far)

        index = s * part + lax.broadcasted_iota(jnp.int32, (part, 1), 0) - prompt_local
        live = jnp.logical_or(index < 0, slot * data_local + index < meta[2])
        cotangent = jnp.where(live, choose(cot_a, cot_b, s).astype(F32), 0.0)
        mixed_grad = norm_back(cotangent, normed, inverse, mlp_gain)
        vec_acc[3] += fold_rows(mixed_grad)
        vec_acc[4] += fold_rows(cotangent * normed)
        vec_acc[5] += fold_rows(cotangent)
        state[s].update(mixed_grad=mixed_grad, mixed_low=mixed_grad.astype(BF16))

    def activate_back(s):
        act_grad = mm(state[s]["mixed_low"], down_ref[...], NT)
        pre_grad = (act_grad * state[s].pop("slope")).astype(BF16)
        bias_acc[...] += fold_rows(pre_grad.astype(F32))
        state[s].update(pre_grad=pre_grad)

    def up_back(s):
        state[s].update(
            hidden_grad=state[s].pop("mixed_grad") + mm(state[s]["pre_grad"], up_ref[...], NT)
        )

    def first_norm_back(s):
        hidden_grad, normed = state[s].pop("hidden_grad"), state[s].pop("one")
        resid = norm_back(hidden_grad, normed, state[s].pop("inv_one"), attn_gain)
        resid_ref[subs[s], :] = resid
        vec_acc[0] += fold_rows(resid)
        vec_acc[1] += fold_rows(hidden_grad * normed)
        vec_acc[2] += fold_rows(hidden_grad)
        state[s].update(resid=resid.astype(BF16))

    def attention_back(s):
        attended_grad = mm(state[s]["resid"], wo_ref[...], NT).astype(BF16)
        da_ref[subs[s], :] = attended_grad[:, :256]
        db_ref[subs[s], :] = attended_grad[:, 256:]

    def up_weight(s):
        grad = mm(state[s].pop("low"), state[s].pop("pre_grad"), TN)
        for j in range(4):
            grad_acc[j, :, :quarter] += grad[:, j * quarter : (j + 1) * quarter]

    def down_weight(s):
        grad = mm(state[s].pop("mixed_low"), state[s].pop("act"), TN)
        for j in range(4):
            grad_acc[j, :, quarter : 2 * quarter] += grad[:, j * quarter : (j + 1) * quarter]

    def out_weight(s):
        grad = mm(state[s].pop("resid"), state[s].pop("attended"), TN)
        for j in range(4):
            grad_acc[j, :, 2 * quarter :] += grad[:, head_rows(j)]

    for stage, s in (
        (attention_branch, 0), (attention_branch, 1), (first_norm, 0), (up_project, 0),
        (first_norm, 1), (activate, 0), (up_project, 1), (down_project, 0), (activate, 1),
        (second_norm, 0), (down_project, 1), (activate_back, 0), (second_norm, 1),
        (down_weight, 0), (up_back, 0), (activate_back, 1), (first_norm_back, 0),
        (up_back, 1), (up_weight, 0), (first_norm_back, 1), (attention_back, 0),
        (down_weight, 1), (out_weight, 0), (up_weight, 1), (attention_back, 1), (out_weight, 1),
    ):
        stage(s)

    @pl.when(i == pl.num_programs(0) - 1)
    def _():
        for j in range(4):
            target = mine_ref if j < 2 else theirs_ref
            target[j % 2] = grad_acc[j].astype(target.dtype)
        for place in range(6):
            sums_ref[place : place + 1, :] = jnp.sum(vec_acc[place], axis=0, keepdims=True)
        bias_grad = jnp.sum(bias_acc[...], axis=0, keepdims=True)
        per_row = bias_grad.shape[1] // 2 // quarter
        for g in range(4):
            found = jnp.zeros((1, quarter), F32)
            for j, flip in enumerate((0, 2, 1, 3)):
                piece = bias_grad[:, j * quarter : (j + 1) * quarter]
                found = jnp.where((meta[0] ^ flip) == g, piece, found)
            row, col = 6 + g // per_row, (g % per_row) * quarter
            sums_ref[row : row + 1, col : col + quarter] = found


def row_work(meta, xa, xb, oa, ob, cot, packs, ups, vec, sizes):
    rows, width = xa.shape
    prompt_local, data_local = sizes
    quarter = ups[0].shape[1]
    hidden = 4 * quarter
    wide = 2 * quarter + HEAD_DIM
    whole = lambda count, cols: once((count, cols))
    row = lambda cols: pl.BlockSpec((rows, cols), lambda i, meta: (i, 0))
    return pl.pallas_call(
        partial(rows_kernel, sizes),
        out_shape=[
            jax.ShapeDtypeStruct((prompt_local, width), BF16),
            jax.ShapeDtypeStruct((data_local, width), BF16),
            jax.ShapeDtypeStruct((prompt_local, width), BF16),
            jax.ShapeDtypeStruct((data_local, width), BF16),
            jax.ShapeDtypeStruct((2 * rows, width), F32),
            jax.ShapeDtypeStruct((2 * rows, 256), BF16),
            jax.ShapeDtypeStruct((2 * rows, 256), BF16),
            jax.ShapeDtypeStruct((2, width, wide), F32),
            jax.ShapeDtypeStruct((2, width, wide), BF16),
            jax.ShapeDtypeStruct((8, width), F32),
        ],
        grid_spec=pltpu.PrefetchScalarGridSpec(
            num_scalar_prefetch=1,
            grid=(2,),
            in_specs=[whole(rows, width)] * 2 + [whole(rows, 256)] * 4 + [whole(rows, width)] * 2
            + [once(item.shape) for item in packs + ups]
            + [once(vec.shape)],
            out_specs=[
                whole(prompt_local, width),
                whole(data_local, width),
                whole(prompt_local, width),
                whole(data_local, width),
                row(width),
                row(256),
                row(256),
                once((2, width, wide)),
                once((2, width, wide)),
                once((8, width)),
            ],
            scratch_shapes=[
                pltpu.VMEM((4 * HEAD_DIM, width), BF16),
                pltpu.VMEM((width, hidden), BF16),
                pltpu.VMEM((hidden, width), BF16),
                pltpu.VMEM((8, hidden), F32),
                pltpu.VMEM((4, width, wide), F32),
                pltpu.VMEM((6, 8, width), F32),
                pltpu.VMEM((8, hidden), F32),
            ],
        ),
        compiler_params=params(),
        cost_estimate=cost(
            3 * 2 * 2 * rows * width * (width + 2 * hidden), 24 * rows * width, 4 * rows * hidden
        ),
        name="row_work",
    )(meta, xa, xb, *oa, *ob, *cot, *packs, *ups, vec)


def project_back_kernel(
    prompt_local, steps, before, xa_ref, xb_ref, dq_ref, dk_ref, dv_ref, w_ref, resid_ref, *refs
):
    refs = list(refs)
    before_ref = refs.pop(0) if before else None
    prompt_ref, data_ref, sib_ref, grad_ref, acc = refs
    i = pl.program_id(0)
    n = pl.num_programs(0)
    step = xa_ref.shape[0]

    @pl.when(i == 0)
    def _():
        acc[...] = before_ref[...] if before else jnp.zeros_like(acc)

    dz = jnp.concatenate([dq_ref[...], dk_ref[...], dv_ref[...]], axis=1)
    part = mm(dz, w_ref[...], NT)
    acc[...] += mm(jnp.where(i < n // 2, xb_ref[...], xa_ref[...]), dz, TN)

    @pl.when(i < n // 2)
    def _():
        sib_ref[...] = part.astype(BF16)

    for j in range(steps):

        @pl.when(i == n // 2 + j)
        def _():
            total = part + resid_ref[...]
            split = max(0, min(step, prompt_local - j * step))
            if split:
                prompt_ref[j * step : j * step + split, :] = total[:split]
            if split < step:
                begin = j * step + split - prompt_local
                data_ref[begin : begin + step - split, :] = total[split:]

    @pl.when(i == n - 1)
    def _():
        if before:
            groups, _, _, depth, _ = grad_ref.shape
            for g in range(groups):
                for which in range(3):
                    for h in range(2):
                        cols = slice(which * 256 + h * HEAD_DIM, which * 256 + (h + 1) * HEAD_DIM)
                        grad_ref[g, h, which] = acc[g * depth : (g + 1) * depth, cols].astype(BF16)
        else:
            grad_ref[...] = acc[...]


def project_back(xa, xb, dq, dk, dv, w, resid, offset, prompt_local, before, groups):
    rows, width = xa.shape
    step = 512
    n = rows // step
    turned = pl.BlockSpec((step, 256), lambda i: ((i + n) % (2 * n), 0))
    low = lambda i: (jnp.minimum(i, n - 1), 0)
    high = lambda i: (jnp.maximum(i - n, 0), 0)
    whole = (width, 768)
    args = [xa, xb, dq, dk, dv, w, resid]
    in_specs = [
        pl.BlockSpec((step, width), high),
        pl.BlockSpec((step, width), low),
        turned,
        turned,
        turned,
        once(whole),
        pl.BlockSpec((step, width), lambda i: (jnp.maximum(i - n, 0) + offset * n, 0)),
    ]
    grad = whole
    if before is not None:
        args.append(before)
        in_specs.append(once(whole))
        grad = (groups, 2, 3, width // groups, HEAD_DIM)
    return pl.pallas_call(
        partial(project_back_kernel, prompt_local, n, before is not None),
        out_shape=[
            jax.ShapeDtypeStruct((prompt_local, width), F32),
            jax.ShapeDtypeStruct((rows - prompt_local, width), F32),
            jax.ShapeDtypeStruct((rows, width), BF16),
            jax.ShapeDtypeStruct(grad, F32 if before is None else BF16),
        ],
        grid=(2 * n,),
        in_specs=in_specs,
        out_specs=[
            once((prompt_local, width)),
            once((rows - prompt_local, width)),
            pl.BlockSpec((step, width), low),
            once(grad),
        ],
        scratch_shapes=[pltpu.VMEM(whole, F32)],
        compiler_params=params(),
        cost_estimate=cost(8 * rows * width * 768, rows * width * 16),
        name="project_back",
    )(*args)


def on_device(
    data_rows,
    prompt_rows,
    context_rows,
    test_rows,
    qkv_weight,
    out_bias,
    out_weight,
    attn_gain,
    attn_shift,
    up_weight,
    up_bias,
    down_weight,
    down_bias,
    mlp_gain,
    mlp_shift,
    data_cotangent,
    prompt_cotangent,
):
    data_local = data_rows.shape[1]
    prompt_local = prompt_rows.shape[0]
    width = prompt_rows.shape[1]
    quarter = up_weight.shape[1]
    sizes = (prompt_local, data_local)
    groups = lax.axis_size("ep")
    t = lax.axis_index("tp")
    mine = t >> 1
    other = 1 - mine

    def across(value):
        return lax.ppermute(value, "tp", [(i, i ^ 2) for i in range(4)])

    def beside(value):
        return lax.ppermute(value, "tp", [(i, i ^ 1) for i in range(4)])

    def pick(values, which):
        return lax.dynamic_index_in_dim(values, which, axis=0, keepdims=False)

    def stack(prompt_part, data_part):
        return jnp.concatenate([prompt_part, data_part], axis=0)

    w_far = across(qkv_weight)
    x_far = across(stack(prompt_rows, pick(data_rows, other)))
    x = stack(prompt_rows, pick(data_rows, mine))
    x_sib = beside(x)
    context = pick(context_rows, mine)
    live = context + pick(test_rows, mine)
    meta = jnp.stack([t, context, live]).astype(jnp.int32)

    qtn, kn, kxn, ktn, vn, vtn, w = project(meta, x, x_sib, qkv_weight, w_far, sizes, 0)
    ptnn, state, state_acc = attend(qtn, [(kn, kxn, vtn)], None, False)

    x_far, state = lax.optimization_barrier((x_far, state))
    x_far_sib = beside(x_far)
    qtf, kf, kxf, ktf, vf, vtf, _ = project(meta, x_far, x_far_sib, qkv_weight, w_far, sizes, 2)
    ptnf, on_a, on_b, statn = attend(qtn, [(kf, kxf, vtf)], (state, state_acc), True)
    ptfn, ptff, of_a, of_b, statf = attend(qtf, [(kn, kxn, vtn), (kf, kxf, vtf)], None, True)

    cot = stack(pick(prompt_cotangent, mine), pick(data_cotangent, mine))
    cot_far = across(stack(pick(prompt_cotangent, other), pick(data_cotangent, other)))
    bias_rows = jnp.pad(up_bias[None], ((0, 15), (0, width - quarter)))
    pack = jnp.concatenate([out_weight, down_weight, bias_rows], axis=0)
    pack_far, up_far = across(pack), across(up_weight)
    packs = [pack, pack_far, beside(pack), beside(pack_far)]
    ups = [up_weight, up_far, beside(up_weight), beside(up_far)]
    vec = jnp.stack(
        [out_bias, attn_gain, attn_shift, down_bias, mlp_gain, mlp_shift, mlp_shift, mlp_shift]
    ).astype(F32)
    (prompt_near, data_near, prompt_far, data_far, resid, da, db, grads_mine, grads_theirs,
     sums) = row_work(
        meta, x, x_far, (on_a, of_a), (beside(on_b), beside(of_b)), (cot, cot_far), packs, ups,
        vec, sizes,
    )

    def exchange(parts, axes):
        return lax.all_to_all(parts, axes, 0, 0, tiled=True)

    def scatter(parts):
        return jnp.sum(exchange(parts, "ep").astype(F32), axis=0)

    def gather(part, axes="ep", count=groups):
        return exchange(jnp.broadcast_to(part[None], (count,) + part.shape), axes)

    db = beside(db)
    pair = grads_mine + beside(grads_theirs).astype(F32)
    pair_far, da, db = lax.optimization_barrier((pair[1].astype(BF16), da, db))
    pair_far = across(pair_far)
    sums = gather(sums, ("ep", "tp"), 4 * groups)
    prompt_back, data_back = across(prompt_far), across(data_far)

    dqf, dqn, dkn, dvn, dkf, dvf = back_first(
        da, db, on_a, on_b, of_a, of_b, statn, statf, qtn, qtf, ptfn, ptff, ptnf, vn, ktn, vf, ktf
    )
    total = (pair[0] + pair_far.astype(F32)).astype(BF16)
    total, prompt_back, data_back, sums, dqf = lax.optimization_barrier(
        (total, prompt_back, data_back, sums, dqf)
    )
    total = scatter(total.reshape(groups, width // groups, total.shape[1])).astype(BF16)
    far_prompt, far_data, far_sib, grad_far = project_back(
        x_far, x_far_sib, dqf, dkf, dvf, w, resid, 1, prompt_local, None, groups
    )
    far_sib = beside(far_sib).astype(F32)
    far_prompt = (far_prompt + far_sib[:prompt_local]).astype(BF16)
    far_data = (far_data + far_sib[prompt_local:]).astype(BF16)
    far_prompt, far_data, total, dqn = lax.optimization_barrier(
        (far_prompt, far_data, total, dqn)
    )
    far_prompt, far_data, total = across(far_prompt), across(far_data), gather(total)

    dqn, dkn, dvn = back_second(da, db, on_a, on_b, statn, qtn, ptnn, vn, ktn, dqn, dkn, dvn)
    far_prompt, far_data, total, dqn = lax.optimization_barrier(
        (far_prompt, far_data, total, dqn)
    )
    near_prompt, near_data, near_sib, grad_parts = project_back(
        x, x_sib, dqn, dkn, dvn, w, resid, 0, prompt_local, grad_far, groups
    )
    qkv = scatter(grad_parts)
    near_sib = beside(near_sib).astype(F32)
    qkv = (qkv[0] + across(qkv[1].astype(BF16)).astype(F32)).astype(BF16)
    qkv = gather(qkv).transpose(1, 0, 2, 3).reshape(3, width, HEAD_DIM).astype(F32)

    near_prompt = near_prompt + near_sib[:prompt_local] + far_prompt.astype(F32)
    near_prompt = near_prompt.astype(BF16).reshape(groups, prompt_local // groups, width)
    prompt_grad = gather(scatter(near_prompt).astype(BF16))
    prompt_grad = prompt_grad.reshape(prompt_local, width).astype(F32)
    near_data = (near_data + near_sib[prompt_local:]).astype(BF16)

    which = lax.broadcasted_iota(jnp.int32, (2, 1, 1), 0)

    def by_episode(own, received):
        return jnp.where(which == mine, own[None], received[None])

    sums = jnp.sum(sums, axis=0)
    total = total.reshape(width, -1).astype(F32)
    bias_grad = lax.dynamic_slice_in_dim(sums[6:8].reshape(-1), t * quarter, quarter)
    return (
        by_episode(data_near, data_back),
        by_episode(prompt_near, prompt_back),
        by_episode(near_data, far_data),
        prompt_grad,
        qkv,
        sums[0],
        total[:, 2 * quarter :].T,
        sums[1],
        sums[2],
        total[:, :quarter],
        bias_grad,
        total[:, quarter : 2 * quarter].T,
        sums[3],
        sums[4],
        sums[5],
    )


def solution(mesh):
    return jax.shard_map(
        on_device,
        mesh=mesh,
        in_specs=(
            P("ep", "tp", None),
            P("tp", None),
            P("ep"),
            P("ep"),
            P(None, None, "tp"),
            P(),
            P("tp", None),
            P(),
            P(),
            P(None, "tp"),
            P("tp"),
            P("tp", None),
            P(),
            P(),
            P(),
            P("ep", "tp", None),
            P("ep", "tp", None),
        ),
        out_specs=(
            P("ep", "tp", None),
            P("ep", "tp", None),
            P("ep", "tp", None),
            P("tp", None),
            P(None, None, "tp"),
            P(),
            P("tp", None),
            P(),
            P(),
            P(None, "tp"),
            P("tp"),
            P("tp", None),
            P(),
            P(),
            P(),
        ),
        check_vma=False,
    )
```

```python
from functools import partial
import math

import jax
import jax.numpy as jnp
from jax import lax
from jax.experimental import pallas as pl
from jax.experimental.pallas import tpu as pltpu
from jax.sharding import PartitionSpec as P

HEAD_DIM = 128
ROWS = 512
SAMPLE = 256
EPS = 1e-05
MASKED = -1e30
LOG2E = math.log2(math.e)
LIMIT = 2.0**60
VMEM = 60 * 1024 * 1024
F32 = jnp.float32
BF16 = jnp.bfloat16
NN = (((1,), (0,)), ((), ()))
NT = (((1,), (1,)), ((), ()))
TN = (((0,), (0,)), ((), ()))


def mm(left, right, dims=NN):
    return lax.dot_general(left, right, dims, preferred_element_type=F32)


def params(**more):
    return pltpu.CompilerParams(vmem_limit_bytes=VMEM, **more)


def cost(flops, nbytes, trans=0):
    return pl.CostEstimate(
        flops=int(flops), bytes_accessed=int(nbytes), transcendentals=int(trans)
    )


def once(shape):
    return pl.BlockSpec(shape, lambda *_: (0,) * len(shape), pipeline_mode=pl.Buffered(1))


def extra_rows(values, count):
    width = values[0].shape[1]
    row = lax.broadcasted_iota(jnp.int32, (count, width), 0)
    out = jnp.zeros((count, width), F32)
    for index, value in enumerate(values):
        out = jnp.where(row == index, value, out)
    return out.astype(BF16)


def three_parts(row):
    high = row.astype(BF16).astype(F32)
    middle = (row - high).astype(BF16).astype(F32)
    return high, middle, row - high - middle


def clamp(i, low, high):
    return jnp.minimum(jnp.maximum(i, low), high)


def project_kernel(sizes, flip, meta, xa_ref, xb_ref, wa_ref, wb_ref, qt_ref, q_ref, k_ref,
                   kx_ref, kt_ref, v_ref, vt_ref, w_ref, wt_ref):
    prompt_local, data_local = sizes
    i = pl.program_id(0)
    per_slot = pl.num_programs(0) // 2
    rows = xa_ref.shape[0]

    @pl.when(i == 0)
    def _():
        for which in range(3):
            for h, source in enumerate((wa_ref, wb_ref)):
                cols = slice(which * 256 + h * HEAD_DIM, which * 256 + (h + 1) * HEAD_DIM)
                w_ref[:, cols] = source[which]
                wt_ref[cols, :] = source[which].T

    x = jnp.where(i < per_slot, xa_ref[...], xb_ref[...])
    slot = jnp.where(i < per_slot, meta[0] ^ flip, meta[0] ^ flip ^ 1)
    row = lax.broadcasted_iota(jnp.int32, (rows, HEAD_DIM), 0)
    lane = lax.broadcasted_iota(jnp.int32, (rows, HEAD_DIM), 1)
    index = (i % per_slot) * rows + row - prompt_local
    attended = jnp.logical_or(index < 0, slot * data_local + index < meta[1])
    bias = jnp.where(attended, F32(0.0), F32(MASKED))
    ones = jnp.where(lane < 4, F32(1.0), F32(0.0))
    kx_ref[...] = jnp.where(lane == 0, bias, ones).astype(BF16)
    factor = F32(LOG2E / math.sqrt(HEAD_DIM))
    z = mm(x, w_ref[...])
    q_ref[...] = (z[:, :256] * factor).astype(BF16)
    k_ref[...] = z[:, 256:512].astype(BF16)
    v_ref[...] = z[:, 512:].astype(BF16)
    zt = mm(wt_ref[...], x, NT)
    qt_ref[...] = (zt[:256] * factor).astype(BF16)
    kt_ref[...] = zt[256:512].astype(BF16)
    vt_ref[...] = zt[512:].astype(BF16)


def project(meta, xa, xb, wa, wb, sizes, flip):
    rows, width = xa.shape
    step = 512
    n = rows // step
    flat = jax.ShapeDtypeStruct((2 * rows, 256), BF16)
    tall = jax.ShapeDtypeStruct((256, 2 * rows), BF16)
    row = pl.BlockSpec((step, 256), lambda i, meta: (i, 0))
    col = pl.BlockSpec((256, step), lambda i, meta: (0, i))
    return pl.pallas_call(
        partial(project_kernel, sizes, flip),
        out_shape=[
            tall,
            flat,
            flat,
            jax.ShapeDtypeStruct((2 * rows, HEAD_DIM), BF16),
            tall,
            flat,
            tall,
            jax.ShapeDtypeStruct((width, 768), BF16),
        ],
        grid_spec=pltpu.PrefetchScalarGridSpec(
            num_scalar_prefetch=1,
            grid=(2 * n,),
            in_specs=[
                pl.BlockSpec((step, width), lambda i, meta: (jnp.minimum(i, n - 1), 0)),
                pl.BlockSpec((step, width), lambda i, meta: (jnp.maximum(i - n, 0), 0)),
                once(wa.shape),
                once(wb.shape),
            ],
            out_specs=[
                col,
                row,
                row,
                pl.BlockSpec((step, HEAD_DIM), lambda i, meta: (i, 0)),
                col,
                row,
                col,
                once((width, 768)),
            ],
            scratch_shapes=[pltpu.VMEM((768, width), BF16)],
        ),
        compiler_params=params(),
        cost_estimate=cost(4 * 2 * rows * width * 768, 2 * rows * width * 8),
        name="project",
    )(meta, xa, xb, wa, wb)


def head_rows(h):
    return slice(h * HEAD_DIM, (h + 1) * HEAD_DIM)


def with_shift(qt, top):
    high, middle, low = three_parts(top)
    extra = extra_rows([jnp.ones_like(top), -high, -middle, -low], HEAD_DIM)
    return jnp.concatenate([qt, extra], axis=0)


def half_scores(chunk, h, qa, start, k_ref, kx_ref):
    here = pl.ds(start, chunk)
    keys = jnp.concatenate([k_ref[here, head_rows(h)], kx_ref[here, :]], axis=1)
    return mm(keys, qa)


def half_part(h, start, scores, vt_ref, pt_ref):
    chunk = scores.shape[0]
    weight = jnp.exp2(scores)
    total = jnp.sum(weight.reshape(chunk // 8, 8, weight.shape[1]), axis=0)
    low = weight.astype(BF16)
    pt_ref[0, h, pl.ds(start, chunk), :] = low
    return total, mm(vt_ref[head_rows(h), pl.ds(start, chunk)], low)


def stale_shift(h, qt, k_ref):
    top = jnp.max(mm(k_ref[:SAMPLE, head_rows(h)], qt), axis=0, keepdims=True)
    return top, with_shift(qt, top)


def fast_states(chunk, shifts, keys, pts):
    tiles = [
        (h, j, start)
        for h in range(2)
        for j in range(len(keys))
        for start in range(0, keys[0][0].shape[0], chunk)
    ]

    def scores(tile):
        h, j, start = tile
        return half_scores(chunk, h, shifts[h][j][1], start, keys[j][0], keys[j][1])

    sums = {}
    ahead = scores(tiles[0])
    for place, (h, j, start) in enumerate(tiles):
        now = ahead
        if place + 1 < len(tiles):
            ahead = scores(tiles[place + 1])
        total, product = half_part(h, start, now, keys[j][2], pts[j])
        if (h, j) in sums:
            total, product = sums[h, j][0] + total, sums[h, j][1] + product
        sums[h, j] = total, product
    return [
        [
            (shifts[h][j][0], jnp.sum(sums[h, j][0], axis=0, keepdims=True), sums[h, j][1])
            for j in range(len(keys))
        ]
        for h in range(2)
    ]


def half_attend_exact(chunk, h, shift, k_ref, kx_ref, vt_ref, pt_ref):
    qt = shift[1][:HEAD_DIM]
    width = qt.shape[1]
    count = k_ref.shape[0] // chunk
    qa = with_shift(qt, jnp.zeros((1, width), F32))

    def find(j, top):
        found = half_scores(chunk, h, qa, pl.multiple_of(j * chunk, chunk), k_ref, kx_ref)
        return jnp.maximum(top, jnp.max(found, axis=0, keepdims=True))

    top = lax.fori_loop(0, count, find, jnp.full((1, width), MASKED, F32))
    qa = with_shift(qt, top)

    def add(j, state):
        start = pl.multiple_of(j * chunk, chunk)
        found = half_scores(chunk, h, qa, start, k_ref, kx_ref)
        more, product = half_part(h, start, found, vt_ref, pt_ref)
        return state[0] + more, state[1] + product

    total, acc = lax.fori_loop(
        0, count, add, (jnp.zeros((8, width), F32), jnp.zeros((HEAD_DIM, width), F32))
    )
    return top, jnp.sum(total, axis=0, keepdims=True), acc


def merge(states):
    top = states[0][0]
    for state in states[1:]:
        top = jnp.maximum(top, state[0])
    scales = [jnp.exp2(state[0] - top) for state in states]
    total = sum(state[1] * scale for state, scale in zip(states, scales))
    factors = [scale / total for scale in scales]
    return factors, sum(state[2] * factor for state, factor in zip(states, factors))


def attend_kernel(chunk, halves, state_in, state_out, *refs):
    refs = list(refs)
    qt_ref = refs.pop(0)
    keys = [[refs.pop(0) for _ in range(3)] for _ in range(halves)]
    if state_in:
        old_ref, old_acc_ref = refs.pop(0), refs.pop(0)
    pts = [refs.pop(0) for _ in range(halves)]
    if state_out:
        new_ref, new_acc_ref = refs
    else:
        mine_ref, theirs_ref, stat_ref = refs
    i = pl.program_id(0)
    half_steps = pl.num_programs(0) // 2

    shifts = [
        [stale_shift(h, qt_ref[head_rows(h), :], key_refs[0]) for key_refs in keys]
        for h in range(2)
    ]

    def finish(new_states):
        worst = None
        for h in range(2):
            states = []
            if state_in:
                states.append(
                    (old_ref[0, h : h + 1, :], old_ref[0, 2 + h : 3 + h, :],
                     old_acc_ref[head_rows(h), :])
                )
            for state in new_states[h]:
                worst = state[1] if worst is None else jnp.maximum(worst, state[1])
                states.append(state)
            if state_out:
                new_ref[0, h : h + 1, :] = states[0][0]
                new_ref[0, 2 + h : 3 + h, :] = states[0][1]
                new_acc_ref[head_rows(h), :] = states[0][2]
            else:
                factors, result = merge(states)
                stat_ref[0, h : h + 1, :] = factors[0]
                stat_ref[0, 2 + h : 3 + h, :] = factors[1]
                low = result.T.astype(BF16)

                @pl.when(i < half_steps)
                def _():
                    mine_ref[:, head_rows(h)] = low

                @pl.when(i >= half_steps)
                def _():
                    theirs_ref[:, head_rows(h)] = low

        return worst

    worst = finish(fast_states(chunk, shifts, keys, pts))

    @pl.when(jnp.logical_not(jnp.max(worst) <= LIMIT))
    def _():
        finish(
            [
                [
                    half_attend_exact(256, h, shifts[h][j], *keys[j], pts[j])
                    for j in range(halves)
                ]
                for h in range(2)
            ]
        )


def attend(qt, keys, state, last, chunk):
    rows = qt.shape[1]
    seq = keys[0][0].shape[0]
    n = rows // ROWS
    half = n // 2
    col = pl.BlockSpec((256, ROWS), lambda i: (0, i))
    stat = pl.BlockSpec((1, 8, ROWS), lambda i: (i, 0, 0))
    stat_shape = jax.ShapeDtypeStruct((n, 8, ROWS), F32)
    in_specs = [col]
    args = [qt]
    for key in keys:
        in_specs += [once(item.shape) for item in key]
        args += list(key)
    if state is not None:
        in_specs += [stat, col]
        args += list(state)
    out_specs = [pl.BlockSpec((1, 2, seq, ROWS), lambda i: (i, 0, 0, 0))] * len(keys)
    out_shape = [jax.ShapeDtypeStruct((n, 2, seq, ROWS), BF16)] * len(keys)
    if last:
        out_specs += [
            pl.BlockSpec((ROWS, 256), lambda i: (jnp.minimum(i, half - 1), 0)),
            pl.BlockSpec((ROWS, 256), lambda i: (jnp.maximum(i - half, 0), 0)),
            stat,
        ]
        out_shape += [jax.ShapeDtypeStruct((rows // 2, 256), BF16)] * 2 + [stat_shape]
    else:
        out_specs += [stat, col]
        out_shape += [stat_shape, jax.ShapeDtypeStruct((256, rows), F32)]
    pairs = 2 * rows * seq * len(keys)
    return pl.pallas_call(
        partial(attend_kernel, chunk, len(keys), state is not None, not last),
        out_shape=out_shape,
        grid=(n,),
        in_specs=in_specs,
        out_specs=out_specs,
        compiler_params=params(),
        cost_estimate=cost(4 * pairs * HEAD_DIM * 2, 2 * pairs, pairs),
        name="attend",
    )(*args)


def back_weights(do, o, factors):
    dot_t = do.astype(F32).T
    delta = jnp.sum(dot_t * o.astype(F32).T, axis=0, keepdims=True)
    found = []
    for factor in factors:
        scaled = dot_t * factor
        found.append((scaled.astype(BF16), scaled.T.astype(BF16), delta * factor))
    return found


def back_tiles(chunk, jobs):
    tiles = [
        (job, start) for job in range(len(jobs)) for start in range(0, jobs[0][4].shape[0], chunk)
    ]

    def ask(tile):
        job, start = tile
        h, grads, _, _, v_ref, _, _, _ = jobs[job]
        return mm(v_ref[start : start + chunk, head_rows(h)], grads[0])

    result = [None] * len(jobs)
    ahead = ask(tiles[0])
    for place, (job, start) in enumerate(tiles):
        grad = ahead
        if place + 1 < len(tiles):
            ahead = ask(tiles[place + 1])
        h, grads, q_rows, pt_ref, _, kt_ref, key_acc, value_acc = jobs[job]
        here = slice(start, start + chunk)
        prob = pt_ref[0, h, here, :]
        score = (prob.astype(F32) * (grad - grads[2])).astype(BF16)
        value_acc[h, here, :] += mm(prob, grads[1])
        key_acc[h, here, :] += mm(score, q_rows)
        part = mm(kt_ref[head_rows(h), here], score)
        result[job] = part if result[job] is None else result[job] + part
    return result


def store_keys(key_acc, value_acc, dk_ref, dv_ref):
    for h in range(2):
        dk_ref[:, head_rows(h)] = (key_acc[h] * F32(1.0 / LOG2E)).astype(BF16)
        dv_ref[:, head_rows(h)] = value_acc[h].astype(BF16)


SCORE_SCALE = 1.0 / math.sqrt(HEAD_DIM)


def back_first_kernel(
    chunk, da_ref, db_ref, on_a, on_b, of_a, of_b, statn, statf, qn, qf, ptfn, ptff, ptnf,
    vn, ktn, vf, ktf, dqf_ref, dqn_ref, dkn_ref, dvn_ref, dkf_ref, dvf_ref, key_acc, value_acc,
):
    i = pl.program_id(0)
    n = pl.num_programs(0) // 2

    @pl.when(i == 0)
    def _():
        for ref in (key_acc, value_acc, dkn_ref, dvn_ref):
            ref[...] = jnp.zeros_like(ref)

    first = (i % n) < n // 2
    do = jnp.where(first, da_ref[...], db_ref[...])

    @pl.when(i < n)
    def _():
        o = jnp.where(first, of_a[...], of_b[...])
        grads = [
            back_weights(
                do[:, head_rows(h)],
                o[:, head_rows(h)],
                [statf[0, h : h + 1, :], statf[0, 2 + h : 3 + h, :]],
            )
            for h in range(2)
        ]
        jobs = []
        for h in range(2):
            q_rows = qf[:, head_rows(h)]
            near, far = grads[h]
            jobs.append((h, near, q_rows, ptfn, vn, ktn, dkn_ref, dvn_ref))
            jobs.append((h, far, q_rows, ptff, vf, ktf, key_acc, value_acc))
        parts = back_tiles(chunk, jobs)
        for h in range(2):
            grad = (parts[2 * h] + parts[2 * h + 1]) * F32(SCORE_SCALE)
            dqf_ref[:, head_rows(h)] = grad.T.astype(BF16)

    @pl.when(i >= n)
    def _():
        o = jnp.where(first, on_a[...], on_b[...])
        grads = [
            back_weights(do[:, head_rows(h)], o[:, head_rows(h)], [statn[0, 2 + h : 3 + h, :]])
            for h in range(2)
        ]
        parts = back_tiles(
            chunk,
            [
                (h, grads[h][0], qn[:, head_rows(h)], ptnf, vf, ktf, key_acc, value_acc)
                for h in range(2)
            ],
        )
        for h in range(2):
            dqn_ref[head_rows(h), :] = parts[h]

    @pl.when(i == 2 * n - 1)
    def _():
        store_keys(key_acc, value_acc, dkf_ref, dvf_ref)


def back_first(da, db, on_a, on_b, of_a, of_b, statn, statf, qn, qf, ptfn, ptff, ptnf,
               vn, ktn, vf, ktf):
    rows = qn.shape[0]
    seq = vn.shape[0]
    n = rows // ROWS
    h = n // 2
    near = lambda i: jnp.maximum(i - n, 0)
    far = lambda i: jnp.minimum(i, n - 1)
    own = lambda i: jnp.where(i < n, h + jnp.minimum(i, h - 1), jnp.minimum(i - n, h - 1))
    sib = lambda i: jnp.where(i < n, jnp.maximum(i, h), jnp.maximum(i - n - h, 0))
    row = lambda f: pl.BlockSpec((ROWS, 256), lambda i: (f(i), 0))
    col = lambda f: pl.BlockSpec((256, ROWS), lambda i: (0, f(i)))
    stat = lambda f: pl.BlockSpec((1, 8, ROWS), lambda i: (f(i), 0, 0))
    tile = lambda f: pl.BlockSpec((1, 2, seq, ROWS), lambda i: (f(i), 0, 0, 0))
    low = lambda f: lambda i: jnp.minimum(f(i), h - 1)
    high = lambda f: lambda i: jnp.maximum(f(i) - h, 0)
    part = jax.ShapeDtypeStruct((2, seq, HEAD_DIM), F32)
    flat = jax.ShapeDtypeStruct((rows, 256), BF16)
    pairs = 2 * rows * seq * 3
    return pl.pallas_call(
        partial(back_first_kernel, 512),
        out_shape=[flat, jax.ShapeDtypeStruct((256, rows), F32), part, part, flat, flat],
        grid=(2 * n,),
        in_specs=[
            row(own), row(sib), row(low(near)), row(high(near)), row(low(far)), row(high(far)),
            stat(near), stat(far), row(near), row(far), tile(far), tile(far), tile(near),
            once(vn.shape), once(ktn.shape), once(vf.shape), once(ktf.shape),
        ],
        out_specs=[
            row(far), col(near), once(part.shape), once(part.shape), once(flat.shape),
            once(flat.shape),
        ],
        scratch_shapes=[pltpu.VMEM(part.shape, F32), pltpu.VMEM(part.shape, F32)],
        compiler_params=params(),
        cost_estimate=cost(8 * pairs * HEAD_DIM, 2 * pairs),
        name="attend_back_far",
    )(da, db, on_a, on_b, of_a, of_b, statn, statf, qn, qf, ptfn, ptff, ptnf, vn, ktn, vf, ktf)


def back_second_kernel(
    chunk, da_ref, db_ref, on_a, on_b, statn, qn, ptnn, vn, ktn, dqn_ref, dkn_ref, dvn_ref,
    dq_ref, dk_ref, dv_ref, key_acc, value_acc,
):
    i = pl.program_id(0)
    n = pl.num_programs(0)

    @pl.when(i == 0)
    def _():
        key_acc[...] = dkn_ref[...]
        value_acc[...] = dvn_ref[...]

    first = i < n // 2
    do = jnp.where(first, da_ref[...], db_ref[...])
    o = jnp.where(first, on_a[...], on_b[...])
    grads = [
        back_weights(do[:, head_rows(h)], o[:, head_rows(h)], [statn[0, h : h + 1, :]])
        for h in range(2)
    ]
    parts = back_tiles(
        chunk,
        [
            (h, grads[h][0], qn[:, head_rows(h)], ptnn, vn, ktn, key_acc, value_acc)
            for h in range(2)
        ],
    )
    for h in range(2):
        grad = (parts[h] + dqn_ref[head_rows(h), :]) * F32(SCORE_SCALE)
        dq_ref[:, head_rows(h)] = grad.T.astype(BF16)

    @pl.when(i == n - 1)
    def _():
        store_keys(key_acc, value_acc, dk_ref, dv_ref)


def back_second(da, db, on_a, on_b, statn, qn, ptnn, vn, ktn, dqn, dkn, dvn):
    rows = qn.shape[0]
    seq = vn.shape[0]
    n = rows // ROWS
    h = n // 2
    row = lambda f: pl.BlockSpec((ROWS, 256), lambda i: (f(i), 0))
    col = pl.BlockSpec((256, ROWS), lambda i: (0, i))
    low = lambda i: jnp.minimum(i, h - 1)
    high = lambda i: jnp.maximum(i - h, 0)
    flat = jax.ShapeDtypeStruct((rows, 256), BF16)
    pairs = 2 * rows * seq
    return pl.pallas_call(
        partial(back_second_kernel, 1024),
        out_shape=[flat, flat, flat],
        grid=(n,),
        in_specs=[
            row(low), row(high), row(low), row(high),
            pl.BlockSpec((1, 8, ROWS), lambda i: (i, 0, 0)), row(lambda i: i),
            pl.BlockSpec((1, 2, seq, ROWS), lambda i: (i, 0, 0, 0)),
            once(vn.shape), once(ktn.shape), col, once(dkn.shape), once(dvn.shape),
        ],
        out_specs=[row(lambda i: i), once(flat.shape), once(flat.shape)],
        scratch_shapes=[pltpu.VMEM(dkn.shape, F32), pltpu.VMEM(dkn.shape, F32)],
        compiler_params=params(),
        cost_estimate=cost(8 * pairs * HEAD_DIM, 2 * pairs),
        name="attend_back_near",
    )(da, db, on_a, on_b, statn, qn, ptnn, vn, ktn, dqn, dkn, dvn)


def mean(values):
    return jnp.mean(values, axis=-1, keepdims=True)


def norm(values):
    centered = values - mean(values)
    inverse = lax.rsqrt(mean(centered * centered) + EPS)
    return centered * inverse, inverse


def norm_back(incoming, normed, inverse, gain):
    scaled = incoming * gain
    return inverse * (scaled - mean(scaled) - normed * mean(scaled * normed))


def gelu_parts(v):
    bell = jnp.exp2(v * v * F32(-0.5 * LOG2E))
    t = 1.0 / (1.0 + F32(0.3275911 / math.sqrt(2.0)) * jnp.abs(v))
    series = t * (
        F32(0.5 * 0.254829592)
        + t
        * (
            F32(0.5 * -0.284496736)
            + t
            * (
                F32(0.5 * 1.421413741)
                + t * (F32(0.5 * -1.453152027) + t * F32(0.5 * 1.061405429))
            )
        )
    )
    tail = series * bell
    return bell * F32(1.0 / math.sqrt(2.0 * math.pi)), jnp.where(v >= 0, 1.0 - tail, tail)


def fold_rows(values):
    return jnp.sum(values.reshape(values.shape[0] // 8, 8, values.shape[1]), axis=0)


def rows_kernel(
    sizes, meta, xa_ref, xb_ref, oa_n, oa_f, ob_n, ob_f, cot_a, cot_b, p0, p1, p2, p3,
    u0, u1, u2, u3, vec_ref,
    prompt_near, data_near, prompt_far, data_far, resid_ref, da_ref, db_ref, send_ref,
    sums_ref, wo_ref, up_ref, down_ref, bias_ref, grad_acc, vec_acc, bias_acc,
):
    prompt_local, data_local = sizes
    i = pl.program_id(0)
    here = i == 0
    rows = xa_ref.shape[0]
    quarter = u0.shape[1]
    part = rows // 2

    @pl.when(here)
    def _():
        for j, (pack, up_part) in enumerate(((p0, u0), (p1, u1), (p2, u2), (p3, u3))):
            cols = slice(j * quarter, (j + 1) * quarter)
            wo_ref[head_rows(j), :] = pack[:HEAD_DIM, :]
            down_ref[cols, :] = pack[HEAD_DIM : HEAD_DIM + quarter, :]
            bias_ref[0:1, cols] = pack[
                HEAD_DIM + quarter : HEAD_DIM + quarter + 16, :quarter
            ].astype(F32)[0:1, :]
            up_ref[:, cols] = up_part[...]
        grad_acc[...] = jnp.zeros_like(grad_acc)
        vec_acc[...] = jnp.zeros_like(vec_acc)
        bias_acc[...] = jnp.zeros_like(bias_acc)

    slot = jnp.where(here, meta[0], meta[0] ^ 2)
    out_bias, attn_gain, attn_shift = vec_ref[0:1, :], vec_ref[1:2, :], vec_ref[2:3, :]
    down_bias, mlp_gain, mlp_shift = vec_ref[3:4, :], vec_ref[4:5, :], vec_ref[5:6, :]
    subs = [slice(s * part, (s + 1) * part) for s in range(2)]
    state = [{}, {}]

    def choose(near_ref, far_ref, s):
        return jnp.where(here, near_ref[subs[s], :], far_ref[subs[s], :])

    def attention_branch(s):
        own = choose(oa_n, oa_f, s)
        sib = choose(ob_n, ob_f, s)
        attended = jnp.concatenate([own, sib], axis=1)
        x = choose(xa_ref, xb_ref, s).astype(F32)
        state[s].update(attended=attended, sum=x + (mm(attended, wo_ref[...]) + out_bias))

    def first_norm(s):
        normed, inverse = norm(state[s].pop("sum"))
        hidden = normed * attn_gain + attn_shift
        state[s].update(one=normed, inv_one=inverse, hidden=hidden, low=hidden.astype(BF16))

    def up_project(s, j):
        cols = slice(j * quarter, (j + 1) * quarter)
        state[s]["pre", j] = mm(state[s]["low"], up_ref[:, cols]) + bias_ref[0:1, cols]

    def activate(s, j):
        pre = state[s].pop(("pre", j))
        density, share = gelu_parts(pre)
        state[s]["act", j] = (pre * share).astype(BF16)
        state[s]["slope", j] = share + pre * density
        if j == 3:
            state[s]["act"] = jnp.concatenate([state[s].pop(("act", k)) for k in range(4)], axis=1)

    def down_project(s):
        state[s].update(
            mixed=state[s].pop("hidden") + (mm(state[s]["act"], down_ref[...]) + down_bias)
        )

    def second_norm(s):
        normed, inverse = norm(state[s].pop("mixed"))
        output = (normed * mlp_gain + mlp_shift).astype(BF16)

        def store(prompt_ref, data_ref):
            split = max(0, min(part, prompt_local - s * part))
            if split:
                prompt_ref[s * part : s * part + split, :] = output[:split]
            if split < part:
                begin = s * part + split - prompt_local
                data_ref[begin : begin + part - split, :] = output[split:]

        @pl.when(here)
        def _():
            store(prompt_near, data_near)

        @pl.when(jnp.logical_not(here))
        def _():
            store(prompt_far, data_far)

        index = s * part + lax.broadcasted_iota(jnp.int32, (part, 1), 0) - prompt_local
        live = jnp.logical_or(index < 0, slot * data_local + index < meta[2])
        cotangent = jnp.where(live, choose(cot_a, cot_b, s).astype(F32), 0.0)
        mixed_grad = norm_back(cotangent, normed, inverse, mlp_gain)
        vec_acc[3] += fold_rows(mixed_grad)
        vec_acc[4] += fold_rows(cotangent * normed)
        vec_acc[5] += fold_rows(cotangent)
        state[s].update(mixed_grad=mixed_grad, mixed_low=mixed_grad.astype(BF16))

    def act_back(s, j):
        cols = slice(j * quarter, (j + 1) * quarter)
        state[s]["act_grad", j] = mm(state[s]["mixed_low"], down_ref[cols, :], NT)

    def pre_back(s, j):
        cols = slice(j * quarter, (j + 1) * quarter)
        pre_grad = (state[s].pop(("act_grad", j)) * state[s].pop(("slope", j))).astype(BF16)
        bias_acc[:, cols] += fold_rows(pre_grad.astype(F32))
        state[s]["pre_grad", j] = pre_grad
        if j == 3:
            state[s]["pre_grad"] = jnp.concatenate(
                [state[s].pop(("pre_grad", k)) for k in range(4)], axis=1
            )

    def up_back(s):
        state[s].update(
            hidden_grad=state[s].pop("mixed_grad") + mm(state[s]["pre_grad"], up_ref[...], NT)
        )

    def first_norm_back(s):
        hidden_grad, normed = state[s].pop("hidden_grad"), state[s].pop("one")
        resid = norm_back(hidden_grad, normed, state[s].pop("inv_one"), attn_gain)
        resid_ref[subs[s], :] = resid
        vec_acc[0] += fold_rows(resid)
        vec_acc[1] += fold_rows(hidden_grad * normed)
        vec_acc[2] += fold_rows(hidden_grad)
        state[s].update(resid=resid.astype(BF16))

    def attention_back(s):
        attended_grad = mm(state[s]["resid"], wo_ref[...], NT).astype(BF16)
        da_ref[subs[s], :] = attended_grad[:, :256]
        db_ref[subs[s], :] = attended_grad[:, 256:]

    def up_weight(s):
        grad = mm(state[s].pop("low"), state[s].pop("pre_grad"), TN)
        for j in range(4):
            grad_acc[j, :, :quarter] += grad[:, j * quarter : (j + 1) * quarter]

    def down_weight(s):
        grad = mm(state[s].pop("mixed_low"), state[s].pop("act"), TN)
        for j in range(4):
            grad_acc[j, :, quarter : 2 * quarter] += grad[:, j * quarter : (j + 1) * quarter]

    def out_weight(s):
        grad = mm(state[s].pop("resid"), state[s].pop("attended"), TN)
        for j in range(4):
            grad_acc[j, :, 2 * quarter :] += grad[:, head_rows(j)]

    def forward(s):
        return [(up_project, s, 0), (up_project, s, 1), (activate, s, 0), (up_project, s, 2),
                (activate, s, 1), (up_project, s, 3), (activate, s, 2), (activate, s, 3)]

    def backward(s):
        return [(act_back, s, 0), (act_back, s, 1), (pre_back, s, 0), (act_back, s, 2),
                (pre_back, s, 1), (act_back, s, 3), (pre_back, s, 2), (pre_back, s, 3)]

    for stage, *where in (
        [(attention_branch, 0), (attention_branch, 1), (first_norm, 0)]
        + forward(0)[:4]
        + [(first_norm, 1)]
        + forward(0)[4:]
        + [(down_project, 0)]
        + forward(1)[:4]
        + [(second_norm, 0)]
        + forward(1)[4:]
        + [(down_project, 1)]
        + backward(0)[:4]
        + [(second_norm, 1)]
        + backward(0)[4:]
        + [(up_back, 0), (down_weight, 0)]
        + backward(1)[:4]
        + [(first_norm_back, 0)]
        + backward(1)[4:]
        + [(up_back, 1), (up_weight, 0), (first_norm_back, 1), (attention_back, 0)]
        + [(down_weight, 1), (out_weight, 0), (up_weight, 1), (attention_back, 1), (out_weight, 1)]
    ):
        stage(*where)

    @pl.when(i == pl.num_programs(0) - 1)
    def _():
        for place in range(6):
            sums_ref[place : place + 1, :] = jnp.sum(vec_acc[place], axis=0, keepdims=True)
        bias_grad = jnp.sum(bias_acc[...], axis=0, keepdims=True)
        per_row = bias_grad.shape[1] // 2 // quarter
        for g in range(4):
            found = jnp.zeros((1, quarter), F32)
            for j, flip in enumerate((0, 2, 1, 3)):
                piece = bias_grad[:, j * quarter : (j + 1) * quarter]
                found = jnp.where((meta[0] ^ flip) == g, piece, found)
            row, col = 6 + g // per_row, (g % per_row) * quarter
            sums_ref[row : row + 1, col : col + quarter] = found
        depth = send_ref.shape[1] - 16
        groups = send_ref.shape[0] // 4
        width, wide = sums_ref.shape[1], send_ref.shape[2]
        per = sums_ref.shape[0] * width // groups
        for g in range(groups):
            row, col = g * per // width, g * per % width
            share = jnp.pad(sums_ref[row : row + 1, col : col + per], ((0, 0), (0, wide - per)))
            high, low, _ = three_parts(share)
            extra = extra_rows([high, low], 16)
            for j, flip in enumerate((0, 2, 1, 3)):
                target = g * 4 + (meta[0] ^ flip)
                send_ref[target, :depth] = grad_acc[j, g * depth : (g + 1) * depth].astype(BF16)
                send_ref[target, depth:] = extra


def row_work(meta, xa, xb, oa, ob, cot, packs, ups, vec, sizes, groups):
    rows, width = xa.shape
    prompt_local, data_local = sizes
    quarter = ups[0].shape[1]
    hidden = 4 * quarter
    wide = 2 * quarter + HEAD_DIM
    send = (4 * groups, width // groups + 16, wide)
    whole = lambda count, cols: once((count, cols))
    row = lambda cols: pl.BlockSpec((rows, cols), lambda i, meta: (i, 0))
    return pl.pallas_call(
        partial(rows_kernel, sizes),
        out_shape=[
            jax.ShapeDtypeStruct((prompt_local, width), BF16),
            jax.ShapeDtypeStruct((data_local, width), BF16),
            jax.ShapeDtypeStruct((prompt_local, width), BF16),
            jax.ShapeDtypeStruct((data_local, width), BF16),
            jax.ShapeDtypeStruct((2 * rows, width), F32),
            jax.ShapeDtypeStruct((2 * rows, 256), BF16),
            jax.ShapeDtypeStruct((2 * rows, 256), BF16),
            jax.ShapeDtypeStruct(send, BF16),
        ],
        grid_spec=pltpu.PrefetchScalarGridSpec(
            num_scalar_prefetch=1,
            grid=(2,),
            in_specs=[whole(rows, width)] * 2 + [whole(rows, 256)] * 4 + [whole(rows, width)] * 2
            + [once(item.shape) for item in packs + ups]
            + [once(vec.shape)],
            out_specs=[
                whole(prompt_local, width),
                whole(data_local, width),
                whole(prompt_local, width),
                whole(data_local, width),
                row(width),
                row(256),
                row(256),
                once(send),
            ],
            scratch_shapes=[
                pltpu.VMEM((8, width), F32),
                pltpu.VMEM((4 * HEAD_DIM, width), BF16),
                pltpu.VMEM((width, hidden), BF16),
                pltpu.VMEM((hidden, width), BF16),
                pltpu.VMEM((8, hidden), F32),
                pltpu.VMEM((4, width, wide), F32),
                pltpu.VMEM((6, 8, width), F32),
                pltpu.VMEM((8, hidden), F32),
            ],
        ),
        compiler_params=params(),
        cost_estimate=cost(
            3 * 2 * 2 * rows * width * (width + 2 * hidden), 24 * rows * width, 4 * rows * hidden
        ),
        name="row_work",
    )(meta, xa, xb, *oa, *ob, *cot, *packs, *ups, vec)


def project_back_kernel(
    prompt_local, steps, before, xa_ref, xb_ref, dq_ref, dk_ref, dv_ref, w_ref, resid_ref, *refs
):
    refs = list(refs)
    before_ref = refs.pop(0) if before else None
    prompt_ref, data_ref, sib_ref, *grad_refs, acc = refs
    i = pl.program_id(0)
    n = pl.num_programs(0)
    step = xa_ref.shape[0]

    @pl.when(i == 0)
    def _():
        acc[...] = before_ref[...] if before else jnp.zeros_like(acc)

    dz = jnp.concatenate([dq_ref[...], dk_ref[...], dv_ref[...]], axis=1)
    part = mm(dz, w_ref[...], NT)
    acc[...] += mm(jnp.where(i < n // 2, xb_ref[...], xa_ref[...]), dz, TN)

    @pl.when(i < n // 2)
    def _():
        sib_ref[...] = part.astype(BF16)

    for j in range(steps):

        @pl.when(i == n // 2 + j)
        def _():
            total = part + resid_ref[...]
            split = max(0, min(step, prompt_local - j * step))
            if split:
                prompt_ref[j * step : j * step + split, :] = total[:split]
            if split < step:
                begin = j * step + split - prompt_local
                data_ref[begin : begin + step - split, :] = total[split:]

    @pl.when(i == n - 1)
    def _():
        if before:
            groups, _, depth, _ = grad_refs[0].shape
            for g in range(groups):
                for which in range(3):
                    for h, ref in enumerate(grad_refs):
                        cols = slice(which * 256 + h * HEAD_DIM, which * 256 + (h + 1) * HEAD_DIM)
                        ref[g, which] = acc[g * depth : (g + 1) * depth, cols].astype(ref.dtype)
        else:
            grad_refs[0][...] = acc[...]


def project_back(xa, xb, dq, dk, dv, w, resid, offset, prompt_local, before, groups):
    rows, width = xa.shape
    step = 512
    n = rows // step
    turned = pl.BlockSpec((step, 256), lambda i: ((i + n) % (2 * n), 0))
    low = lambda i: (jnp.minimum(i, n - 1), 0)
    high = lambda i: (jnp.maximum(i - n, 0), 0)
    whole = (width, 768)
    args = [xa, xb, dq, dk, dv, w, resid]
    in_specs = [
        pl.BlockSpec((step, width), high),
        pl.BlockSpec((step, width), low),
        turned,
        turned,
        turned,
        once(whole),
        pl.BlockSpec((step, width), lambda i: (jnp.maximum(i - n, 0) + offset * n, 0)),
    ]
    grads = [jax.ShapeDtypeStruct(whole, F32)]
    if before is not None:
        args.append(before)
        in_specs.append(once(whole))
        pieces = (groups, 3, width // groups, HEAD_DIM)
        grads = [jax.ShapeDtypeStruct(pieces, F32), jax.ShapeDtypeStruct(pieces, BF16)]
    return pl.pallas_call(
        partial(project_back_kernel, prompt_local, n, before is not None),
        out_shape=[
            jax.ShapeDtypeStruct((prompt_local, width), F32),
            jax.ShapeDtypeStruct((rows - prompt_local, width), F32),
            jax.ShapeDtypeStruct((rows, width), BF16),
            *grads,
        ],
        grid=(2 * n,),
        in_specs=in_specs,
        out_specs=[
            once((prompt_local, width)),
            once((rows - prompt_local, width)),
            pl.BlockSpec((step, width), low),
            *[once(item.shape) for item in grads],
        ],
        scratch_shapes=[pltpu.VMEM(whole, F32)],
        compiler_params=params(),
        cost_estimate=cost(8 * rows * width * 768, rows * width * 16),
        name="project_back",
    )(*args)


def on_device(
    data_rows,
    prompt_rows,
    context_rows,
    test_rows,
    qkv_weight,
    out_bias,
    out_weight,
    attn_gain,
    attn_shift,
    up_weight,
    up_bias,
    down_weight,
    down_bias,
    mlp_gain,
    mlp_shift,
    data_cotangent,
    prompt_cotangent,
):
    data_local = data_rows.shape[1]
    prompt_local = prompt_rows.shape[0]
    width = prompt_rows.shape[1]
    quarter = up_weight.shape[1]
    sizes = (prompt_local, data_local)
    groups = lax.axis_size("ep")
    t = lax.axis_index("tp")
    mine = t >> 1
    other = 1 - mine

    def across(value):
        return lax.ppermute(value, "tp", [(i, i ^ 2) for i in range(4)])

    def beside(value):
        return lax.ppermute(value, "tp", [(i, i ^ 1) for i in range(4)])

    def pick(values, which):
        return lax.dynamic_index_in_dim(values, which, axis=0, keepdims=False)

    def stack(prompt_part, data_part):
        return jnp.concatenate([prompt_part, data_part], axis=0)

    w_far = across(qkv_weight)
    x_far = across(stack(prompt_rows, pick(data_rows, other)))
    x = stack(prompt_rows, pick(data_rows, mine))
    x_sib = beside(x)
    context = pick(context_rows, mine)
    live = context + pick(test_rows, mine)
    meta = jnp.stack([t, context, live]).astype(jnp.int32)

    qtn, qn, kn, kxn, ktn, vn, vtn, w = project(meta, x, x_sib, qkv_weight, w_far, sizes, 0)
    ptnn, state, state_acc = attend(qtn, [(kn, kxn, vtn)], None, False, 256)

    x_far, state = lax.optimization_barrier((x_far, state))
    x_far_sib = beside(x_far)
    qtf, qf, kf, kxf, ktf, vf, vtf, _ = project(meta, x_far, x_far_sib, qkv_weight, w_far, sizes, 2)
    ptnf, on_a, on_b, statn = attend(qtn, [(kf, kxf, vtf)], (state, state_acc), True, 1024)
    ptfn, ptff, of_a, of_b, statf = attend(
        qtf, [(kn, kxn, vtn), (kf, kxf, vtf)], None, True, 512
    )

    cot = stack(pick(prompt_cotangent, mine), pick(data_cotangent, mine))
    cot_far = across(stack(pick(prompt_cotangent, other), pick(data_cotangent, other)))
    bias_rows = jnp.pad(up_bias[None], ((0, 15), (0, width - quarter)))
    pack = jnp.concatenate([out_weight, down_weight, bias_rows], axis=0)
    pack_far, up_far = across(pack), across(up_weight)
    packs = [pack, pack_far, beside(pack), beside(pack_far)]
    ups = [up_weight, up_far, beside(up_weight), beside(up_far)]
    vec = jnp.stack(
        [out_bias, attn_gain, attn_shift, down_bias, mlp_gain, mlp_shift, mlp_shift, mlp_shift]
    ).astype(F32)
    (prompt_near, data_near, prompt_far, data_far, resid, da, db, send) = row_work(
        meta, x, x_far, (on_a, of_a), (beside(on_b), beside(of_b)), (cot, cot_far), packs, ups,
        vec, sizes, groups,
    )

    def exchange(parts, axes):
        return lax.all_to_all(parts, axes, 0, 0, tiled=True)

    def gather(part):
        return exchange(jnp.broadcast_to(part[None], (groups,) + part.shape), "ep")

    db = beside(db)
    send = exchange(send, ("ep", "tp"))
    prompt_back, data_back = across(prompt_far), across(data_far)

    dqf, dqn, dkn, dvn, dkf, dvf = back_first(
        da, db, on_a, on_b, of_a, of_b, statn, statf, qn, qf, ptfn, ptff, ptnf, vn, ktn, vf, ktf
    )
    send, prompt_back, data_back, dqf = lax.optimization_barrier(
        (send, prompt_back, data_back, dqf)
    )
    depth = width // groups
    total = jnp.sum(send.astype(F32), axis=0)
    part = total[depth : depth + 1] + total[depth + 1 : depth + 2]
    high = part.astype(BF16)
    low = (part - high.astype(F32)).astype(BF16)
    total = jnp.concatenate(
        [total[:depth].astype(BF16), high, low, jnp.zeros((14, total.shape[1]), BF16)], axis=0
    )
    total = gather(total)
    far_prompt, far_data, far_sib, grad_far = project_back(
        x_far, x_far_sib, dqf, dkf, dvf, w, resid, 1, prompt_local, None, groups
    )
    far_sib = beside(far_sib).astype(F32)
    far_prompt = (far_prompt + far_sib[:prompt_local]).astype(BF16)
    far_data = (far_data + far_sib[prompt_local:]).astype(BF16)
    far_prompt, far_data, dqn = lax.optimization_barrier((far_prompt, far_data, dqn))
    far_prompt, far_data = across(far_prompt), across(far_data)

    dqn, dkn, dvn = back_second(da, db, on_a, on_b, statn, qn, ptnn, vn, ktn, dqn, dkn, dvn)
    far_prompt, far_data, total, dqn = lax.optimization_barrier(
        (far_prompt, far_data, total, dqn)
    )
    near_prompt, near_data, near_sib, own_grad, other_grad = project_back(
        x, x_sib, dqn, dkn, dvn, w, resid, 0, prompt_local, grad_far, groups
    )
    near_sib = beside(near_sib).astype(F32)
    qkv = (own_grad + across(other_grad).astype(F32)).astype(BF16)
    qkv = qkv.reshape(groups, 3 * depth, HEAD_DIM)
    columns = width // HEAD_DIM
    prompt_depth = prompt_local // groups
    near_prompt = near_prompt + near_sib[:prompt_local] + far_prompt.astype(F32)
    near_prompt = near_prompt.astype(BF16).reshape(groups, prompt_depth, columns, HEAD_DIM)
    near_prompt = near_prompt.transpose(0, 2, 1, 3).reshape(groups, -1, HEAD_DIM)
    last = exchange(jnp.concatenate([qkv, near_prompt], axis=1), "ep")
    near_data = (near_data + near_sib[prompt_local:]).astype(BF16)
    last = gather(jnp.sum(last.astype(F32), axis=0).astype(BF16))
    qkv = last[:, : 3 * depth].reshape(groups, 3, depth, HEAD_DIM).transpose(1, 0, 2, 3)
    qkv = qkv.reshape(3, width, HEAD_DIM).astype(F32)
    prompt_grad = last[:, 3 * depth :].reshape(groups, columns, prompt_depth, HEAD_DIM)
    prompt_grad = prompt_grad.transpose(0, 2, 1, 3).reshape(prompt_local, width).astype(F32)

    which = lax.broadcasted_iota(jnp.int32, (2, 1, 1), 0)

    def by_episode(own, received):
        return jnp.where(which == mine, own[None], received[None])

    sums = total[:, depth : depth + 2, : 8 * width // groups].astype(F32)
    sums = (sums[:, 0] + sums[:, 1]).reshape(8, width)
    total = total[:, :depth].reshape(width, -1).astype(F32)
    bias_grad = lax.dynamic_slice_in_dim(sums[6:8].reshape(-1), t * quarter, quarter)
    return (
        by_episode(data_near, data_back),
        by_episode(prompt_near, prompt_back),
        by_episode(near_data, far_data),
        prompt_grad,
        qkv,
        sums[0],
        total[:, 2 * quarter :].T,
        sums[1],
        sums[2],
        total[:, :quarter],
        bias_grad,
        total[:, quarter : 2 * quarter].T,
        sums[3],
        sums[4],
        sums[5],
    )


def solution(mesh):
    return jax.shard_map(
        on_device,
        mesh=mesh,
        in_specs=(
            P("ep", "tp", None),
            P("tp", None),
            P("ep"),
            P("ep"),
            P(None, None, "tp"),
            P(),
            P("tp", None),
            P(),
            P(),
            P(None, "tp"),
            P("tp"),
            P("tp", None),
            P(),
            P(),
            P(),
            P("ep", "tp", None),
            P("ep", "tp", None),
        ),
        out_specs=(
            P("ep", "tp", None),
            P("ep", "tp", None),
            P("ep", "tp", None),
            P("tp", None),
            P(None, None, "tp"),
            P(),
            P("tp", None),
            P(),
            P(),
            P(None, "tp"),
            P("tp"),
            P("tp", None),
            P(),
            P(),
            P(),
        ),
        check_vma=False,
    )
```

```python
from functools import partial
import math

import jax
import jax.numpy as jnp
from jax import lax
from jax.experimental import pallas as pl
from jax.experimental.pallas import tpu as pltpu
from jax.sharding import PartitionSpec as P

HEAD_DIM = 128
ROWS = 512
BACK_ROWS = 256
SAMPLE = 256
EPS = 1e-05
MASKED = -1e30
LOG2E = math.log2(math.e)
LIMIT = 2.0**60
VMEM = 60 * 1024 * 1024
F32 = jnp.float32
BF16 = jnp.bfloat16
NN = (((1,), (0,)), ((), ()))
NT = (((1,), (1,)), ((), ()))
TN = (((0,), (0,)), ((), ()))


def mm(left, right, dims=NN):
    return lax.dot_general(left, right, dims, preferred_element_type=F32)


def params(**more):
    return pltpu.CompilerParams(vmem_limit_bytes=VMEM, **more)


def cost(flops, nbytes, trans=0):
    return pl.CostEstimate(
        flops=int(flops), bytes_accessed=int(nbytes), transcendentals=int(trans)
    )


def once(shape):
    return pl.BlockSpec(shape, lambda *_: (0,) * len(shape), pipeline_mode=pl.Buffered(1))


def extra_rows(values, count):
    width = values[0].shape[1]
    row = lax.broadcasted_iota(jnp.int32, (count, width), 0)
    out = jnp.zeros((count, width), F32)
    for index, value in enumerate(values):
        out = jnp.where(row == index, value, out)
    return out.astype(BF16)


def three_parts(row):
    high = row.astype(BF16).astype(F32)
    middle = (row - high).astype(BF16).astype(F32)
    return high, middle, row - high - middle


def clamp(i, low, high):
    return jnp.minimum(jnp.maximum(i, low), high)


def project_kernel(sizes, flip, meta, xa_ref, xb_ref, wa_ref, wb_ref, qt_ref, q_ref, k_ref,
                   kx_ref, kt_ref, v_ref, vt_ref, w_ref, wt_ref):
    prompt_local, data_local = sizes
    i = pl.program_id(0)
    per_slot = pl.num_programs(0) // 2
    rows = xa_ref.shape[0]

    @pl.when(i == 0)
    def _():
        for which in range(3):
            for h, source in enumerate((wa_ref, wb_ref)):
                cols = slice(which * 256 + h * HEAD_DIM, which * 256 + (h + 1) * HEAD_DIM)
                w_ref[:, cols] = source[which]
                wt_ref[cols, :] = source[which].T

    x = jnp.where(i < per_slot, xa_ref[...], xb_ref[...])
    slot = jnp.where(i < per_slot, meta[0] ^ flip, meta[0] ^ flip ^ 1)
    row = lax.broadcasted_iota(jnp.int32, (rows, HEAD_DIM), 0)
    lane = lax.broadcasted_iota(jnp.int32, (rows, HEAD_DIM), 1)
    index = (i % per_slot) * rows + row - prompt_local
    attended = jnp.logical_or(index < 0, slot * data_local + index < meta[1])
    bias = jnp.where(attended, F32(0.0), F32(MASKED))
    ones = jnp.where(lane < 4, F32(1.0), F32(0.0))
    kx_ref[...] = jnp.where(lane == 0, bias, ones).astype(BF16)
    factor = F32(LOG2E / math.sqrt(HEAD_DIM))
    z = mm(x, w_ref[...])
    q_ref[...] = (z[:, :256] * factor).astype(BF16)
    k_ref[...] = z[:, 256:512].astype(BF16)
    v_ref[...] = z[:, 512:].astype(BF16)
    zt = mm(wt_ref[...], x, NT)
    qt_ref[...] = (zt[:256] * factor).astype(BF16)
    kt_ref[...] = zt[256:512].astype(BF16)
    vt_ref[...] = zt[512:].astype(BF16)


def project(meta, xa, xb, wa, wb, sizes, flip):
    rows, width = xa.shape
    step = 512
    n = rows // step
    flat = jax.ShapeDtypeStruct((2 * rows, 256), BF16)
    tall = jax.ShapeDtypeStruct((256, 2 * rows), BF16)
    row = pl.BlockSpec((step, 256), lambda i, meta: (i, 0))
    col = pl.BlockSpec((256, step), lambda i, meta: (0, i))
    return pl.pallas_call(
        partial(project_kernel, sizes, flip),
        out_shape=[
            tall,
            flat,
            flat,
            jax.ShapeDtypeStruct((2 * rows, HEAD_DIM), BF16),
            tall,
            flat,
            tall,
            jax.ShapeDtypeStruct((width, 768), BF16),
        ],
        grid_spec=pltpu.PrefetchScalarGridSpec(
            num_scalar_prefetch=1,
            grid=(2 * n,),
            in_specs=[
                pl.BlockSpec((step, width), lambda i, meta: (jnp.minimum(i, n - 1), 0)),
                pl.BlockSpec((step, width), lambda i, meta: (jnp.maximum(i - n, 0), 0)),
                once(wa.shape),
                once(wb.shape),
            ],
            out_specs=[
                col,
                row,
                row,
                pl.BlockSpec((step, HEAD_DIM), lambda i, meta: (i, 0)),
                col,
                row,
                col,
                once((width, 768)),
            ],
            scratch_shapes=[pltpu.VMEM((768, width), BF16)],
        ),
        compiler_params=params(),
        cost_estimate=cost(4 * 2 * rows * width * 768, 2 * rows * width * 8),
        name="project",
    )(meta, xa, xb, wa, wb)


def head_rows(h):
    return slice(h * HEAD_DIM, (h + 1) * HEAD_DIM)


def with_shift(qt, top):
    high, middle, low = three_parts(top)
    extra = extra_rows([jnp.ones_like(top), -high, -middle, -low], HEAD_DIM)
    return jnp.concatenate([qt, extra], axis=0)


def half_scores(chunk, h, qa, start, k_ref, kx_ref):
    here = pl.ds(start, chunk)
    keys = jnp.concatenate([k_ref[here, head_rows(h)], kx_ref[here, :]], axis=1)
    return mm(keys, qa)


def half_part(h, start, scores, vt_ref, pt_ref):
    chunk = scores.shape[0]
    weight = jnp.exp2(scores)
    total = jnp.sum(weight.reshape(chunk // 8, 8, weight.shape[1]), axis=0)
    low = weight.astype(BF16)
    pt_ref[0, h, pl.ds(start, chunk), :] = low
    return total, mm(vt_ref[head_rows(h), pl.ds(start, chunk)], low)


def stale_shift(h, qt, k_ref):
    top = jnp.max(mm(k_ref[:SAMPLE, head_rows(h)], qt), axis=0, keepdims=True)
    return top, with_shift(qt, top)


def fast_states(chunk, shifts, keys, pts):
    tiles = [
        (h, j, start)
        for h in range(2)
        for j in range(len(keys))
        for start in range(0, keys[0][0].shape[0], chunk)
    ]

    def scores(tile):
        h, j, start = tile
        return half_scores(chunk, h, shifts[h][j][1], start, keys[j][0], keys[j][1])

    sums = {}
    ahead = scores(tiles[0])
    for place, (h, j, start) in enumerate(tiles):
        now = ahead
        if place + 1 < len(tiles):
            ahead = scores(tiles[place + 1])
        total, product = half_part(h, start, now, keys[j][2], pts[j])
        if (h, j) in sums:
            total, product = sums[h, j][0] + total, sums[h, j][1] + product
        sums[h, j] = total, product
    return [
        [
            (shifts[h][j][0], jnp.sum(sums[h, j][0], axis=0, keepdims=True), sums[h, j][1])
            for j in range(len(keys))
        ]
        for h in range(2)
    ]


def half_attend_exact(chunk, h, shift, k_ref, kx_ref, vt_ref, pt_ref):
    qt = shift[1][:HEAD_DIM]
    width = qt.shape[1]
    count = k_ref.shape[0] // chunk
    qa = with_shift(qt, jnp.zeros((1, width), F32))

    def find(j, top):
        found = half_scores(chunk, h, qa, pl.multiple_of(j * chunk, chunk), k_ref, kx_ref)
        return jnp.maximum(top, jnp.max(found, axis=0, keepdims=True))

    top = lax.fori_loop(0, count, find, jnp.full((1, width), MASKED, F32))
    qa = with_shift(qt, top)

    def add(j, state):
        start = pl.multiple_of(j * chunk, chunk)
        found = half_scores(chunk, h, qa, start, k_ref, kx_ref)
        more, product = half_part(h, start, found, vt_ref, pt_ref)
        return state[0] + more, state[1] + product

    total, acc = lax.fori_loop(
        0, count, add, (jnp.zeros((8, width), F32), jnp.zeros((HEAD_DIM, width), F32))
    )
    return top, jnp.sum(total, axis=0, keepdims=True), acc


def merge(states):
    top = states[0][0]
    for state in states[1:]:
        top = jnp.maximum(top, state[0])
    scales = [jnp.exp2(state[0] - top) for state in states]
    total = sum(state[1] * scale for state, scale in zip(states, scales))
    factors = [scale / total for scale in scales]
    return factors, sum(state[2] * factor for state, factor in zip(states, factors))


def redo(states, shifts, keys, pts):
    return [
        [half_attend_exact(256, h, shifts[h][j], *keys[j], pts[j]) for j in range(len(keys))]
        for h in range(2)
    ]


def run_halves(chunk, qt_ref, keys, pts, finish):
    shifts = [
        [stale_shift(h, qt_ref[head_rows(h), :], key_refs[0]) for key_refs in keys]
        for h in range(2)
    ]
    states = fast_states(chunk, shifts, keys, pts)
    worst = None
    for state in states[0] + states[1]:
        worst = state[1] if worst is None else jnp.maximum(worst, state[1])
    finish(states)

    @pl.when(jnp.logical_not(jnp.max(worst) <= LIMIT))
    def _():
        finish(redo(states, shifts, keys, pts))


def attend_first_kernel(chunk, qt_ref, k_ref, kx_ref, vt_ref, pt_ref, state_ref, acc_ref):
    def finish(states):
        for h in range(2):
            top, total, acc = states[h][0]
            state_ref[0, h : h + 1, :] = top
            state_ref[0, 2 + h : 3 + h, :] = total
            acc_ref[head_rows(h), :] = acc

    run_halves(chunk, qt_ref, [(k_ref, kx_ref, vt_ref)], [pt_ref], finish)


def attend_first(qt, key, chunk):
    rows = qt.shape[1]
    n = rows // ROWS
    col = pl.BlockSpec((256, ROWS), lambda i: (0, i))
    pairs = 2 * rows * rows
    return pl.pallas_call(
        partial(attend_first_kernel, chunk),
        out_shape=[
            jax.ShapeDtypeStruct((2 * n, 2, rows, ROWS), BF16),
            jax.ShapeDtypeStruct((n, 8, ROWS), F32),
            jax.ShapeDtypeStruct((256, rows), F32),
        ],
        grid=(n,),
        in_specs=[col] + [once(item.shape) for item in key],
        out_specs=[
            pl.BlockSpec((1, 2, rows, ROWS), lambda i: (i, 0, 0, 0)),
            pl.BlockSpec((1, 8, ROWS), lambda i: (i, 0, 0)),
            col,
        ],
        compiler_params=params(),
        cost_estimate=cost(4 * pairs * HEAD_DIM * 2, 2 * pairs, pairs),
        name="attend_near",
    )(qt, *key)


def attend_second_kernel(
    chunk, qtn_ref, qtf_ref, kn, kxn, vtn, kf, kxf, vtf, old_ref, old_acc_ref, _,
    ptn_ref, ptf_ref, mine_ref, sib_ref, stat_ref,
):
    i = pl.program_id(0)
    n = pl.num_programs(0) // 2
    near, far = (kn, kxn, vtn), (kf, kxf, vtf)

    def store(h, states):
        factors, result = merge(states)
        stat_ref[0, h : h + 1, :] = factors[0]
        stat_ref[0, 2 + h : 3 + h, :] = factors[1]
        low = result.T.astype(BF16)
        first = i % n < n // 2

        @pl.when(first)
        def _():
            mine_ref[:, head_rows(h)] = low

        @pl.when(jnp.logical_not(first))
        def _():
            sib_ref[:, head_rows(h)] = low

    @pl.when(i < n)
    def _():
        def finish(states):
            for h in range(2):
                old = (old_ref[0, h : h + 1, :], old_ref[0, 2 + h : 3 + h, :],
                       old_acc_ref[head_rows(h), :])
                store(h, [old, states[h][0]])

        run_halves(chunk, qtn_ref, [far], [ptf_ref], finish)

    @pl.when(i >= n)
    def _():
        def finish(states):
            for h in range(2):
                store(h, states[h])

        run_halves(chunk, qtf_ref, [near, far], [ptn_ref, ptf_ref], finish)


def mine_block(i, n):
    half = n // 2
    return (i // n) * half + jnp.minimum(i % n, half - 1)


def sib_block(i, n):
    half = n // 2
    return jnp.maximum((i // n) * half + i % n - half, jnp.maximum((i // n) * half - 1, 0))


def attend_second(qtn, qtf, near, far, pt, state, acc, chunk):
    rows = qtn.shape[1]
    n = rows // ROWS
    near_col = pl.BlockSpec((256, ROWS), lambda i: (0, jnp.minimum(i, n - 1)))
    pairs = 6 * rows * rows
    return pl.pallas_call(
        partial(attend_second_kernel, chunk),
        out_shape=[
            jax.ShapeDtypeStruct(pt.shape, BF16),
            jax.ShapeDtypeStruct(pt.shape, BF16),
            jax.ShapeDtypeStruct((rows, 256), BF16),
            jax.ShapeDtypeStruct((rows, 256), BF16),
            jax.ShapeDtypeStruct((2 * n, 8, ROWS), F32),
        ],
        grid=(2 * n,),
        in_specs=[near_col, pl.BlockSpec((256, ROWS), lambda i: (0, jnp.maximum(i - n, 0)))]
        + [once(item.shape) for item in near + far]
        + [
            pl.BlockSpec((1, 8, ROWS), lambda i: (jnp.minimum(i, n - 1), 0, 0)),
            near_col,
            pl.BlockSpec(memory_space=pl.ANY),
        ],
        out_specs=[
            pl.BlockSpec((1, 2, rows, ROWS), lambda i: (jnp.maximum(i, n), 0, 0, 0)),
            pl.BlockSpec((1, 2, rows, ROWS), lambda i: (i, 0, 0, 0)),
            pl.BlockSpec((ROWS, 256), lambda i: (mine_block(i, n), 0)),
            pl.BlockSpec((ROWS, 256), lambda i: (sib_block(i, n), 0)),
            pl.BlockSpec((1, 8, ROWS), lambda i: (i, 0, 0)),
        ],
        input_output_aliases={10: 0},
        compiler_params=params(),
        cost_estimate=cost(4 * pairs * HEAD_DIM * 2, 2 * pairs, pairs),
        name="attend_rest",
    )(qtn, qtf, *near, *far, state, acc, pt)


def back_weights(do, o, factors):
    dot_t = do.astype(F32).T
    delta = jnp.sum(dot_t * o.astype(F32).T, axis=0, keepdims=True)
    found = []
    for factor in factors:
        scaled = dot_t * factor
        high, middle, low = three_parts(delta * factor)
        extra = extra_rows([-high, -middle, -low], HEAD_DIM)
        found.append(
            (jnp.concatenate([scaled.astype(BF16), extra], axis=0), scaled.T.astype(BF16))
        )
    return found


def back_half(chunk, h, grads, q_rows, pt_ref, v_ref, kt_ref, key_acc, value_acc):
    ones = jnp.where(
        lax.broadcasted_iota(jnp.int32, (chunk, HEAD_DIM), 1) < 3, F32(1.0), F32(0.0)
    ).astype(BF16)
    result = jnp.zeros((HEAD_DIM, q_rows.shape[0]), F32)
    for start in range(0, v_ref.shape[0], chunk):
        here = slice(start, start + chunk)
        prob = pt_ref[0, h, here, :]
        values = jnp.concatenate([v_ref[here, head_rows(h)], ones], axis=1)
        score = (prob.astype(F32) * mm(values, grads[0])).astype(BF16)
        value_acc[h, here, :] += mm(prob, grads[1])
        key_acc[h, here, :] += mm(score, q_rows)
        result = result + mm(kt_ref[head_rows(h), here], score)
    return result


def attend_back_kernel(
    chunk, da_ref, db_ref, oa_ref, ob_ref, stat_ref, qn_ref, qf_ref, ptn_ref, ptf_ref,
    vn, ktn, vf, ktf, dq_ref, dk_ref, dv_ref, key_n, value_n, key_f, value_f,
):
    i = pl.program_id(0)
    n = pl.num_programs(0) // 2

    @pl.when(i == 0)
    def _():
        for ref in (key_n, value_n, key_f, value_f):
            ref[...] = jnp.zeros_like(ref)

    first = i % n < n // 2
    do = jnp.where(first, da_ref[...], db_ref[...])
    o = jnp.where(first, oa_ref[...], ob_ref[...])
    q = jnp.where(i < n, qn_ref[...], qf_ref[...])
    for h in range(2):
        cols = head_rows(h)
        near, far = back_weights(
            do[:, cols], o[:, cols], [stat_ref[0, h : h + 1, :], stat_ref[0, 2 + h : 3 + h, :]]
        )
        grad = back_half(chunk, h, near, q[:, cols], ptn_ref, vn, ktn, key_n, value_n)
        grad += back_half(chunk, h, far, q[:, cols], ptf_ref, vf, ktf, key_f, value_f)
        dq_ref[:, cols] = (grad * F32(1.0 / math.sqrt(HEAD_DIM))).T.astype(BF16)

    @pl.when(i == 2 * n - 1)
    def _():
        seq = vn.shape[0]
        for half, (keys, values) in enumerate(((key_n, value_n), (key_f, value_f))):
            rows = slice(half * seq, (half + 1) * seq)
            for h in range(2):
                dk_ref[rows, head_rows(h)] = (keys[h] * F32(1.0 / LOG2E)).astype(BF16)
                dv_ref[rows, head_rows(h)] = values[h].astype(BF16)


def attend_back(da, db, oa, ob, stat, qn, qf, ptn, ptf, vn, ktn, vf, ktf, chunk):
    rows = qn.shape[0]
    step = BACK_ROWS
    n = rows // step
    per = ROWS // step
    row = lambda f: pl.BlockSpec((step, 256), lambda i: (f(i), 0))
    tile = pl.BlockSpec((1, 2, rows, step), lambda i: (i // per, 0, 0, i % per))
    flat = jax.ShapeDtypeStruct((2 * rows, 256), BF16)
    acc = pltpu.VMEM((2, rows, HEAD_DIM), F32)
    pairs = 8 * rows * rows
    return pl.pallas_call(
        partial(attend_back_kernel, chunk),
        out_shape=[flat, flat, flat],
        grid=(2 * n,),
        in_specs=[
            row(lambda i: mine_block(i, n)),
            row(lambda i: sib_block(i, n)),
            row(lambda i: mine_block(i, n)),
            row(lambda i: sib_block(i, n)),
            pl.BlockSpec((1, 8, step), lambda i: (i // per, 0, i % per)),
            row(lambda i: jnp.minimum(i, n - 1)),
            row(lambda i: jnp.maximum(i - n, 0)),
            tile,
            tile,
        ]
        + [once(item.shape) for item in (vn, ktn, vf, ktf)],
        out_specs=[row(lambda i: i), once(flat.shape), once(flat.shape)],
        scratch_shapes=[acc, acc, acc, acc],
        compiler_params=params(),
        cost_estimate=cost(8 * pairs * HEAD_DIM, 2 * pairs),
        name="attend_back",
    )(da, db, oa, ob, stat, qn, qf, ptn, ptf, vn, ktn, vf, ktf)


def mean(values):
    return jnp.mean(values, axis=-1, keepdims=True)


def norm(values):
    centered = values - mean(values)
    inverse = lax.rsqrt(mean(centered * centered) + EPS)
    return centered * inverse, inverse


def norm_back(incoming, normed, inverse, gain):
    scaled = incoming * gain
    return inverse * (scaled - mean(scaled) - normed * mean(scaled * normed))


def gelu_parts(v):
    bell = jnp.exp2(v * v * F32(-0.5 * LOG2E))
    t = 1.0 / (1.0 + F32(0.3275911 / math.sqrt(2.0)) * jnp.abs(v))
    series = t * (
        F32(0.5 * 0.254829592)
        + t
        * (
            F32(0.5 * -0.284496736)
            + t
            * (
                F32(0.5 * 1.421413741)
                + t * (F32(0.5 * -1.453152027) + t * F32(0.5 * 1.061405429))
            )
        )
    )
    tail = series * bell
    return bell * F32(1.0 / math.sqrt(2.0 * math.pi)), jnp.where(v >= 0, 1.0 - tail, tail)


def fold_rows(values):
    return jnp.sum(values.reshape(values.shape[0] // 8, 8, values.shape[1]), axis=0)


def rows_kernel(
    sizes, meta, xa_ref, xb_ref, oa_ref, ob_ref, cot_a, cot_b, p0, p1, p2, p3,
    u0, u1, u2, u3, vec_ref,
    prompt_near, data_near, prompt_far, data_far, resid_ref, da_ref, db_ref, send_ref,
    sums_ref, wo_ref, up_ref, down_ref, bias_ref, grad_acc, vec_acc, bias_acc,
):
    prompt_local, data_local = sizes
    i = pl.program_id(0)
    half = pl.num_programs(0) // 2
    here = i < half
    rows = xa_ref.shape[0]
    quarter = u0.shape[1]

    @pl.when(i == 0)
    def _():
        for j, (pack, up_part) in enumerate(((p0, u0), (p1, u1), (p2, u2), (p3, u3))):
            cols = slice(j * quarter, (j + 1) * quarter)
            wo_ref[head_rows(j), :] = pack[:HEAD_DIM, :]
            down_ref[cols, :] = pack[HEAD_DIM : HEAD_DIM + quarter, :]
            bias_ref[0:1, cols] = pack[
                HEAD_DIM + quarter : HEAD_DIM + quarter + 16, :quarter
            ].astype(F32)[0:1, :]
            up_ref[:, cols] = up_part[...]
        grad_acc[...] = jnp.zeros_like(grad_acc)
        vec_acc[...] = jnp.zeros_like(vec_acc)
        bias_acc[...] = jnp.zeros_like(bias_acc)

    slot = jnp.where(here, meta[0], meta[0] ^ 2)
    index = (i % half) * rows + lax.broadcasted_iota(jnp.int32, (rows, 1), 0) - prompt_local
    live = jnp.logical_or(index < 0, slot * data_local + index < meta[2])

    out_bias, attn_gain, attn_shift = vec_ref[0:1, :], vec_ref[1:2, :], vec_ref[2:3, :]
    down_bias, mlp_gain, mlp_shift = vec_ref[3:4, :], vec_ref[4:5, :], vec_ref[5:6, :]
    x = jnp.where(here, xa_ref[...], xb_ref[...])
    attended = jnp.concatenate([oa_ref[...], ob_ref[...]], axis=1)
    normed_one, inverse_one = norm(x.astype(F32) + (mm(attended, wo_ref[...]) + out_bias))
    hidden = normed_one * attn_gain + attn_shift
    hidden_low = hidden.astype(BF16)
    pre = mm(hidden_low, up_ref[...]) + bias_ref[0:1, :]
    density, share = gelu_parts(pre)
    activated = (pre * share).astype(BF16)
    slope = share + pre * density
    mixed = hidden + (mm(activated, down_ref[...]) + down_bias)
    normed_two, inverse_two = norm(mixed)
    output = (normed_two * mlp_gain + mlp_shift).astype(BF16)
    for j in range(2):
        split = max(0, min(rows, prompt_local - j * rows))
        for place, (prompt_ref, data_ref) in enumerate(
            ((prompt_near, data_near), (prompt_far, data_far))
        ):

            @pl.when(i == place * half + j)
            def _():
                if split:
                    prompt_ref[j * rows : j * rows + split, :] = output[:split]
                if split < rows:
                    begin = j * rows + split - prompt_local
                    data_ref[begin : begin + rows - split, :] = output[split:]

    cotangent = jnp.where(live, jnp.where(here, cot_a[...], cot_b[...]).astype(F32), 0.0)
    mixed_grad = norm_back(cotangent, normed_two, inverse_two, mlp_gain)
    mixed_low = mixed_grad.astype(BF16)
    pre_grad = (mm(mixed_low, down_ref[...], NT) * slope).astype(BF16)
    hidden_grad = mixed_grad + mm(pre_grad, up_ref[...], NT)
    resid_grad = norm_back(hidden_grad, normed_one, inverse_one, attn_gain)
    resid_ref[...] = resid_grad
    resid_low = resid_grad.astype(BF16)
    attended_grad = mm(resid_low, wo_ref[...], NT).astype(BF16)
    da_ref[...] = attended_grad[:, :256]
    db_ref[...] = attended_grad[:, 256:]

    up_grad = mm(hidden_low, pre_grad, TN)
    down_grad = mm(mixed_low, activated, TN)
    out_grad = mm(resid_low, attended, TN)
    for j in range(4):
        cols = slice(j * quarter, (j + 1) * quarter)
        grad_acc[j, :, :quarter] += up_grad[:, cols]
        grad_acc[j, :, quarter : 2 * quarter] += down_grad[:, cols]
        grad_acc[j, :, 2 * quarter :] += out_grad[:, head_rows(j)]
    bias_acc[...] += fold_rows(pre_grad.astype(F32))
    for place, value in enumerate(
        (
            resid_grad,
            hidden_grad * normed_one,
            hidden_grad,
            mixed_grad,
            cotangent * normed_two,
            cotangent,
        )
    ):
        vec_acc[place] += fold_rows(value)

    @pl.when(i == pl.num_programs(0) - 1)
    def _():
        for place in range(6):
            sums_ref[place : place + 1, :] = jnp.sum(vec_acc[place], axis=0, keepdims=True)
        bias_grad = jnp.sum(bias_acc[...], axis=0, keepdims=True)
        per_row = bias_grad.shape[1] // 2 // quarter
        for g in range(4):
            found = jnp.zeros((1, quarter), F32)
            for j, flip in enumerate((0, 2, 1, 3)):
                piece = bias_grad[:, j * quarter : (j + 1) * quarter]
                found = jnp.where((meta[0] ^ flip) == g, piece, found)
            row, col = 6 + g // per_row, (g % per_row) * quarter
            sums_ref[row : row + 1, col : col + quarter] = found
        depth = send_ref.shape[1] - 16
        groups = send_ref.shape[0] // 4
        width, wide = sums_ref.shape[1], send_ref.shape[2]
        per = sums_ref.shape[0] * width // groups
        for g in range(groups):
            row, col = g * per // width, g * per % width
            part = jnp.pad(sums_ref[row : row + 1, col : col + per], ((0, 0), (0, wide - per)))
            high, low, _ = three_parts(part)
            extra = extra_rows([high, low], 16)
            for j, flip in enumerate((0, 2, 1, 3)):
                target = g * 4 + (meta[0] ^ flip)
                send_ref[target, :depth] = grad_acc[j, g * depth : (g + 1) * depth].astype(BF16)
                send_ref[target, depth:] = extra


def row_work(meta, xa, xb, oa, ob, cot, packs, ups, vec, sizes, groups):
    rows, width = xa.shape
    prompt_local, data_local = sizes
    step = 512
    n = rows // step
    quarter = ups[0].shape[1]
    hidden = 4 * quarter
    wide = 2 * quarter + HEAD_DIM
    send = (4 * groups, width // groups + 16, wide)
    near = pl.BlockSpec((step, width), lambda i, meta: (jnp.minimum(i, n - 1), 0))
    far = pl.BlockSpec((step, width), lambda i, meta: (jnp.maximum(i - n, 0), 0))
    row = lambda cols: pl.BlockSpec((step, cols), lambda i, meta: (i, 0))
    return pl.pallas_call(
        partial(rows_kernel, sizes),
        out_shape=[
            jax.ShapeDtypeStruct((prompt_local, width), BF16),
            jax.ShapeDtypeStruct((data_local, width), BF16),
            jax.ShapeDtypeStruct((prompt_local, width), BF16),
            jax.ShapeDtypeStruct((data_local, width), BF16),
            jax.ShapeDtypeStruct((2 * rows, width), F32),
            jax.ShapeDtypeStruct((2 * rows, 256), BF16),
            jax.ShapeDtypeStruct((2 * rows, 256), BF16),
            jax.ShapeDtypeStruct(send, BF16),
        ],
        grid_spec=pltpu.PrefetchScalarGridSpec(
            num_scalar_prefetch=1,
            grid=(2 * n,),
            in_specs=[near, far, row(256), row(256), near, far]
            + [once(item.shape) for item in packs + ups]
            + [once(vec.shape)],
            out_specs=[
                once((prompt_local, width)),
                once((data_local, width)),
                once((prompt_local, width)),
                once((data_local, width)),
                row(width),
                row(256),
                row(256),
                once(send),
            ],
            scratch_shapes=[
                pltpu.VMEM((8, width), F32),
                pltpu.VMEM((4 * HEAD_DIM, width), BF16),
                pltpu.VMEM((width, hidden), BF16),
                pltpu.VMEM((hidden, width), BF16),
                pltpu.VMEM((8, hidden), F32),
                pltpu.VMEM((4, width, wide), F32),
                pltpu.VMEM((6, 8, width), F32),
                pltpu.VMEM((8, hidden), F32),
            ],
        ),
        compiler_params=params(),
        cost_estimate=cost(
            3 * 2 * 2 * rows * width * (width + 2 * hidden), 24 * rows * width, 4 * rows * hidden
        ),
        name="row_work",
    )(meta, xa, xb, oa, ob, *cot, *packs, *ups, vec)


def choose_slot(i, per_slot, refs):
    found = refs[-1][...]
    for j in range(len(refs) - 2, -1, -1):
        found = jnp.where(i < (j + 1) * per_slot, refs[j][...], found)
    return found


def weight_grad_kernel(x0, x1, x2, x3, dq_ref, dk_ref, dv_ref, own_ref, other_ref, acc):
    i = pl.program_id(0)
    n = pl.num_programs(0)

    @pl.when(i == 0)
    def _():
        acc[...] = jnp.zeros_like(acc)

    dz = jnp.concatenate([dq_ref[...], dk_ref[...], dv_ref[...]], axis=1)
    acc[...] += mm(choose_slot(i, n // 4, [x0, x1, x2, x3]), dz, TN)

    @pl.when(i == n - 1)
    def _():
        groups, _, depth, _ = own_ref.shape
        for g in range(groups):
            for which in range(3):
                for h, ref in enumerate((own_ref, other_ref)):
                    cols = slice(which * 256 + h * HEAD_DIM, which * 256 + (h + 1) * HEAD_DIM)
                    ref[g, which] = acc[g * depth : (g + 1) * depth, cols].astype(ref.dtype)


def slot_specs(step, width, per_slot):
    def spec(j):
        return pl.BlockSpec((step, width), lambda i: (clamp(i - j * per_slot, 0, per_slot - 1), 0))

    return [spec(j) for j in range(4)]


def weight_grad(xs, dq, dk, dv, groups):
    rows, width = xs[0].shape
    step = 512
    row = pl.BlockSpec((step, 256), lambda i: (i, 0))
    pieces = (groups, 3, width // groups, HEAD_DIM)
    return pl.pallas_call(
        weight_grad_kernel,
        out_shape=[jax.ShapeDtypeStruct(pieces, F32), jax.ShapeDtypeStruct(pieces, BF16)],
        grid=(4 * rows // step,),
        in_specs=slot_specs(step, width, rows // step) + [row, row, row],
        out_specs=[once(pieces), once(pieces)],
        scratch_shapes=[pltpu.VMEM((width, 768), F32)],
        compiler_params=params(),
        cost_estimate=cost(2 * 4 * rows * width * 768, rows * width * 30),
        name="weight_grad",
    )(*xs, dq, dk, dv)


def input_grad_kernel(
    prompt_local, per_slot, dq_ref, dk_ref, dv_ref, w_ref, resid_ref, sib_ref, *own_refs
):
    i = pl.program_id(0)
    step = dq_ref.shape[0]
    half = pl.num_programs(0) // 2
    dz = jnp.concatenate([dq_ref[...], dk_ref[...], dv_ref[...]], axis=1)
    part = mm(dz, w_ref[...], NT)

    @pl.when(i < half)
    def _():
        sib_ref[...] = part.astype(BF16)

    for place in range(2):
        prompt_ref, data_ref = own_refs[2 * place : 2 * place + 2]
        for j in range(per_slot):
            split = max(0, min(step, prompt_local - j * step))

            @pl.when(i == half + (1 - place) * per_slot + j)
            def _():
                total = part + resid_ref[...]
                if split:
                    prompt_ref[j * step : j * step + split, :] = total[:split]
                if split < step:
                    begin = j * step + split - prompt_local
                    data_ref[begin : begin + step - split, :] = total[split:]


def input_grad(dq, dk, dv, w, resid, prompt_local):
    rows = dq.shape[0] // 4
    width = w.shape[0]
    step = 512
    n = rows // step

    def turn(i):
        slot = i // n
        return jnp.where(slot == 0, 3, jnp.where(slot == 1, 1, jnp.where(slot == 2, 2, 0))) * n + i % n

    def own(i):
        return jnp.where(i // n == 3, 0, n) + jnp.where(i // n < 2, 0, i % n)

    def sib(i):
        return jnp.where(i // n == 0, n + i % n, jnp.minimum(i - n, n - 1))

    turned = pl.BlockSpec((step, 256), lambda i: (turn(i), 0))
    data_local = rows - prompt_local
    own_shapes = [(prompt_local, width), (data_local, width)] * 2
    return pl.pallas_call(
        partial(input_grad_kernel, prompt_local, n),
        out_shape=[jax.ShapeDtypeStruct((2 * rows, width), BF16)]
        + [jax.ShapeDtypeStruct(shape, F32) for shape in own_shapes],
        grid=(4 * n,),
        in_specs=[turned, turned, turned, once(w.shape),
                  pl.BlockSpec((step, width), lambda i: (own(i), 0))],
        out_specs=[pl.BlockSpec((step, width), lambda i: (sib(i), 0))]
        + [once(shape) for shape in own_shapes],
        compiler_params=params(),
        cost_estimate=cost(2 * 4 * rows * width * 768, rows * width * 40),
        name="input_grad",
    )(dq, dk, dv, w, resid)


def on_device(
    data_rows,
    prompt_rows,
    context_rows,
    test_rows,
    qkv_weight,
    out_bias,
    out_weight,
    attn_gain,
    attn_shift,
    up_weight,
    up_bias,
    down_weight,
    down_bias,
    mlp_gain,
    mlp_shift,
    data_cotangent,
    prompt_cotangent,
):
    data_local = data_rows.shape[1]
    prompt_local = prompt_rows.shape[0]
    width = prompt_rows.shape[1]
    quarter = up_weight.shape[1]
    sizes = (prompt_local, data_local)
    groups = lax.axis_size("ep")
    t = lax.axis_index("tp")
    mine = t >> 1
    other = 1 - mine

    def across(value):
        return lax.ppermute(value, "tp", [(i, i ^ 2) for i in range(4)])

    def beside(value):
        return lax.ppermute(value, "tp", [(i, i ^ 1) for i in range(4)])

    def pick(values, which):
        return lax.dynamic_index_in_dim(values, which, axis=0, keepdims=False)

    def stack(prompt_part, data_part):
        return jnp.concatenate([prompt_part, data_part], axis=0)

    w_far = across(qkv_weight)
    x_far = across(stack(prompt_rows, pick(data_rows, other)))
    x = stack(prompt_rows, pick(data_rows, mine))
    x_sib = beside(x)
    context = pick(context_rows, mine)
    live = context + pick(test_rows, mine)
    meta = jnp.stack([t, context, live]).astype(jnp.int32)

    qtn, qn, kn, kxn, ktn, vn, vtn, w = project(meta, x, x_sib, qkv_weight, w_far, sizes, 0)
    ptn, state, state_acc = attend_first(qtn, (kn, kxn, vtn), 512)

    x_far, state = lax.optimization_barrier((x_far, state))
    x_far_sib = beside(x_far)
    qtf, qf, kf, kxf, ktf, vf, vtf, _ = project(meta, x_far, x_far_sib, qkv_weight, w_far, sizes, 2)
    ptn, ptf, oa, ob, stat = attend_second(
        qtn, qtf, (kn, kxn, vtn), (kf, kxf, vtf), ptn, state, state_acc, 512
    )

    cot = stack(pick(prompt_cotangent, mine), pick(data_cotangent, mine))
    cot_far = across(stack(pick(prompt_cotangent, other), pick(data_cotangent, other)))
    bias_rows = jnp.pad(up_bias[None], ((0, 15), (0, width - quarter)))
    pack = jnp.concatenate([out_weight, down_weight, bias_rows], axis=0)
    pack_far, up_far = across(pack), across(up_weight)
    packs = [pack, pack_far, beside(pack), beside(pack_far)]
    ups = [up_weight, up_far, beside(up_weight), beside(up_far)]
    vec = jnp.stack(
        [out_bias, attn_gain, attn_shift, down_bias, mlp_gain, mlp_shift, mlp_shift, mlp_shift]
    ).astype(F32)
    (prompt_near, data_near, prompt_far, data_far, resid, da, db, send) = row_work(
        meta, x, x_far, oa, beside(ob), (cot, cot_far), packs, ups, vec, sizes, groups
    )

    def exchange(parts, axes):
        return lax.all_to_all(parts, axes, 0, 0, tiled=True)

    def gather(part):
        return exchange(jnp.broadcast_to(part[None], (groups,) + part.shape), "ep")

    db = beside(db)
    send = exchange(send, ("ep", "tp"))
    prompt_back, data_back = across(prompt_far), across(data_far)

    dq, dk, dv = attend_back(
        da, db, oa, ob, stat, qn, qf, ptn, ptf, vn, ktn, vf, ktf, 512
    )
    send, prompt_back, data_back, dq = lax.optimization_barrier((send, prompt_back, data_back, dq))
    depth = width // groups
    total = jnp.sum(send.astype(F32), axis=0)
    part = total[depth : depth + 1] + total[depth + 1 : depth + 2]
    high = part.astype(BF16)
    low = (part - high.astype(F32)).astype(BF16)
    total = jnp.concatenate(
        [total[:depth].astype(BF16), high, low, jnp.zeros((14, total.shape[1]), BF16)], axis=0
    )

    own_grad, other_grad = weight_grad((x, x_sib, x_far, x_far_sib), dq, dk, dv, groups)
    other_grad = across(other_grad)
    sib, near_prompt, near_data, far_prompt, far_data = input_grad(
        dq, dk, dv, w, resid, prompt_local
    )
    slot_rows = prompt_local + data_local
    sib = beside(sib)
    qkv = (own_grad + other_grad.astype(F32)).astype(BF16).reshape(groups, 3 * depth, HEAD_DIM)
    qkv = exchange(qkv, "ep")
    sib = sib.astype(F32)
    far_prompt = across((far_prompt + sib[slot_rows : slot_rows + prompt_local]).astype(BF16))
    far_data = across((far_data + sib[slot_rows + prompt_local :]).astype(BF16))
    near_data = (near_data + sib[prompt_local:slot_rows]).astype(BF16)
    qkv = gather(jnp.sum(qkv.astype(F32), axis=0).astype(BF16))
    near_prompt = near_prompt + sib[:prompt_local] + far_prompt.astype(F32)
    near_prompt = near_prompt.astype(BF16).reshape(groups, prompt_local // groups, width)
    near_prompt = jnp.sum(exchange(near_prompt, "ep").astype(F32), axis=0).astype(BF16)
    prompt_grad = gather(near_prompt).reshape(prompt_local, width).astype(F32)
    total = gather(total)
    qkv = qkv.reshape(groups, 3, depth, HEAD_DIM).transpose(1, 0, 2, 3)
    qkv = qkv.reshape(3, width, HEAD_DIM).astype(F32)

    which = lax.broadcasted_iota(jnp.int32, (2, 1, 1), 0)

    def by_episode(own, received):
        return jnp.where(which == mine, own[None], received[None])

    sums = total[:, depth : depth + 2, : 8 * width // groups].astype(F32)
    sums = (sums[:, 0] + sums[:, 1]).reshape(8, width)
    total = total[:, :depth].reshape(width, -1).astype(F32)
    bias_grad = lax.dynamic_slice_in_dim(sums[6:8].reshape(-1), t * quarter, quarter)
    return (
        by_episode(data_near, data_back),
        by_episode(prompt_near, prompt_back),
        by_episode(near_data, far_data),
        prompt_grad,
        qkv,
        sums[0],
        total[:, 2 * quarter :].T,
        sums[1],
        sums[2],
        total[:, :quarter],
        bias_grad,
        total[:, quarter : 2 * quarter].T,
        sums[3],
        sums[4],
        sums[5],
    )


def solution(mesh):
    return jax.shard_map(
        on_device,
        mesh=mesh,
        in_specs=(
            P("ep", "tp", None),
            P("tp", None),
            P("ep"),
            P("ep"),
            P(None, None, "tp"),
            P(),
            P("tp", None),
            P(),
            P(),
            P(None, "tp"),
            P("tp"),
            P("tp", None),
            P(),
            P(),
            P(),
            P("ep", "tp", None),
            P("ep", "tp", None),
        ),
        out_specs=(
            P("ep", "tp", None),
            P("ep", "tp", None),
            P("ep", "tp", None),
            P("tp", None),
            P(None, None, "tp"),
            P(),
            P("tp", None),
            P(),
            P(),
            P(None, "tp"),
            P("tp"),
            P("tp", None),
            P(),
            P(),
            P(),
        ),
        check_vma=False,
    )
```

```python
from functools import partial
import math

import jax
import jax.numpy as jnp
from jax import lax
from jax.experimental import pallas as pl
from jax.experimental.pallas import tpu as pltpu
from jax.sharding import PartitionSpec as P

HEAD_DIM = 128
ROWS = 512
BACK_ROWS = 256
SAMPLE = 256
COST_SCALE = 10000
EPS = 1e-05
MASKED = -1e30
LOG2E = math.log2(math.e)
LIMIT = 2.0**60
VMEM = 60 * 1024 * 1024
F32 = jnp.float32
BF16 = jnp.bfloat16
NN = (((1,), (0,)), ((), ()))
NT = (((1,), (1,)), ((), ()))
TN = (((0,), (0,)), ((), ()))


def mm(left, right, dims=NN):
    return lax.dot_general(left, right, dims, preferred_element_type=F32)


def params(**more):
    return pltpu.CompilerParams(vmem_limit_bytes=VMEM, **more)


def cost(flops, nbytes, trans=0):
    scale = COST_SCALE
    return pl.CostEstimate(
        flops=int(flops) // scale, bytes_accessed=int(nbytes) // scale,
        transcendentals=int(trans) // scale,
    )


def once(shape):
    return pl.BlockSpec(shape, lambda *_: (0,) * len(shape), pipeline_mode=pl.Buffered(1))


def extra_rows(values, count):
    width = values[0].shape[1]
    row = lax.broadcasted_iota(jnp.int32, (count, width), 0)
    out = jnp.zeros((count, width), F32)
    for index, value in enumerate(values):
        out = jnp.where(row == index, value, out)
    return out.astype(BF16)


def three_parts(row):
    high = row.astype(BF16).astype(F32)
    middle = (row - high).astype(BF16).astype(F32)
    return high, middle, row - high - middle


def clamp(i, low, high):
    return jnp.minimum(jnp.maximum(i, low), high)


def project_kernel(sizes, flip, meta, xa_ref, xb_ref, wa_ref, wb_ref, qt_ref, q_ref, k_ref,
                   kx_ref, kt_ref, v_ref, vt_ref, w_ref, wt_ref):
    prompt_local, data_local = sizes
    i = pl.program_id(0)
    per_slot = pl.num_programs(0) // 2
    rows = xa_ref.shape[0]

    @pl.when(i == 0)
    def _():
        for which in range(3):
            for h, source in enumerate((wa_ref, wb_ref)):
                cols = slice(which * 256 + h * HEAD_DIM, which * 256 + (h + 1) * HEAD_DIM)
                w_ref[:, cols] = source[which]
                wt_ref[cols, :] = source[which].T

    x = jnp.where(i < per_slot, xa_ref[...], xb_ref[...])
    slot = jnp.where(i < per_slot, meta[0] ^ flip, meta[0] ^ flip ^ 1)
    row = lax.broadcasted_iota(jnp.int32, (rows, HEAD_DIM), 0)
    lane = lax.broadcasted_iota(jnp.int32, (rows, HEAD_DIM), 1)
    index = (i % per_slot) * rows + row - prompt_local
    attended = jnp.logical_or(index < 0, slot * data_local + index < meta[1])
    bias = jnp.where(attended, F32(0.0), F32(MASKED))
    ones = jnp.where(lane < 4, F32(1.0), F32(0.0))
    kx_ref[...] = jnp.where(lane == 0, bias, ones).astype(BF16)
    factor = F32(LOG2E / math.sqrt(HEAD_DIM))
    z = mm(x, w_ref[...])
    q_ref[...] = (z[:, :256] * factor).astype(BF16)
    k_ref[...] = z[:, 256:512].astype(BF16)
    v_ref[...] = z[:, 512:].astype(BF16)
    zt = mm(wt_ref[...], x, NT)
    qt_ref[...] = (zt[:256] * factor).astype(BF16)
    kt_ref[...] = zt[256:512].astype(BF16)
    vt_ref[...] = zt[512:].astype(BF16)


def project(meta, xa, xb, wa, wb, sizes, flip):
    rows, width = xa.shape
    step = 512
    n = rows // step
    flat = jax.ShapeDtypeStruct((2 * rows, 256), BF16)
    tall = jax.ShapeDtypeStruct((256, 2 * rows), BF16)
    row = pl.BlockSpec((step, 256), lambda i, meta: (i, 0))
    col = pl.BlockSpec((256, step), lambda i, meta: (0, i))
    return pl.pallas_call(
        partial(project_kernel, sizes, flip),
        out_shape=[
            tall,
            flat,
            flat,
            jax.ShapeDtypeStruct((2 * rows, HEAD_DIM), BF16),
            tall,
            flat,
            tall,
            jax.ShapeDtypeStruct((width, 768), BF16),
        ],
        grid_spec=pltpu.PrefetchScalarGridSpec(
            num_scalar_prefetch=1,
            grid=(2 * n,),
            in_specs=[
                pl.BlockSpec((step, width), lambda i, meta: (jnp.minimum(i, n - 1), 0)),
                pl.BlockSpec((step, width), lambda i, meta: (jnp.maximum(i - n, 0), 0)),
                once(wa.shape),
                once(wb.shape),
            ],
            out_specs=[
                col,
                row,
                row,
                pl.BlockSpec((step, HEAD_DIM), lambda i, meta: (i, 0)),
                col,
                row,
                col,
                once((width, 768)),
            ],
            scratch_shapes=[pltpu.VMEM((768, width), BF16)],
        ),
        compiler_params=params(),
        cost_estimate=cost(4 * 2 * rows * width * 768, 2 * rows * width * 8),
        name="project",
    )(meta, xa, xb, wa, wb)


def head_rows(h):
    return slice(h * HEAD_DIM, (h + 1) * HEAD_DIM)


def with_shift(qt, top):
    high, middle, low = three_parts(top)
    extra = extra_rows([jnp.ones_like(top), -high, -middle, -low], HEAD_DIM)
    return jnp.concatenate([qt, extra], axis=0)


def half_scores(chunk, h, qa, start, k_ref, kx_ref):
    here = pl.ds(start, chunk)
    keys = jnp.concatenate([k_ref[here, head_rows(h)], kx_ref[here, :]], axis=1)
    return mm(keys, qa)


def half_part(h, start, scores, vt_ref, pt_ref):
    chunk = scores.shape[0]
    weight = jnp.exp2(scores)
    total = jnp.sum(weight.reshape(chunk // 8, 8, weight.shape[1]), axis=0)
    low = weight.astype(BF16)
    pt_ref[0, h, pl.ds(start, chunk), :] = low
    return total, mm(vt_ref[head_rows(h), pl.ds(start, chunk)], low)


def stale_shift(h, qt, k_ref):
    top = jnp.max(mm(k_ref[:SAMPLE, head_rows(h)], qt), axis=0, keepdims=True)
    return top, with_shift(qt, top)


def fast_states(chunk, shifts, keys, pts):
    tiles = [
        (h, j, start)
        for h in range(2)
        for j in range(len(keys))
        for start in range(0, keys[0][0].shape[0], chunk)
    ]

    def scores(tile):
        h, j, start = tile
        return half_scores(chunk, h, shifts[h][j][1], start, keys[j][0], keys[j][1])

    sums = {}
    ahead = scores(tiles[0])
    for place, (h, j, start) in enumerate(tiles):
        now = ahead
        if place + 1 < len(tiles):
            ahead = scores(tiles[place + 1])
        total, product = half_part(h, start, now, keys[j][2], pts[j])
        if (h, j) in sums:
            total, product = sums[h, j][0] + total, sums[h, j][1] + product
        sums[h, j] = total, product
    return [
        [
            (shifts[h][j][0], jnp.sum(sums[h, j][0], axis=0, keepdims=True), sums[h, j][1])
            for j in range(len(keys))
        ]
        for h in range(2)
    ]


def half_attend_exact(chunk, h, shift, k_ref, kx_ref, vt_ref, pt_ref):
    qt = shift[1][:HEAD_DIM]
    width = qt.shape[1]
    count = k_ref.shape[0] // chunk
    qa = with_shift(qt, jnp.zeros((1, width), F32))

    def find(j, top):
        found = half_scores(chunk, h, qa, pl.multiple_of(j * chunk, chunk), k_ref, kx_ref)
        return jnp.maximum(top, jnp.max(found, axis=0, keepdims=True))

    top = lax.fori_loop(0, count, find, jnp.full((1, width), MASKED, F32))
    qa = with_shift(qt, top)

    def add(j, state):
        start = pl.multiple_of(j * chunk, chunk)
        found = half_scores(chunk, h, qa, start, k_ref, kx_ref)
        more, product = half_part(h, start, found, vt_ref, pt_ref)
        return state[0] + more, state[1] + product

    total, acc = lax.fori_loop(
        0, count, add, (jnp.zeros((8, width), F32), jnp.zeros((HEAD_DIM, width), F32))
    )
    return top, jnp.sum(total, axis=0, keepdims=True), acc


def merge(states):
    top = states[0][0]
    for state in states[1:]:
        top = jnp.maximum(top, state[0])
    scales = [jnp.exp2(state[0] - top) for state in states]
    total = sum(state[1] * scale for state, scale in zip(states, scales))
    factors = [scale / total for scale in scales]
    return factors, sum(state[2] * factor for state, factor in zip(states, factors))


def redo(states, shifts, keys, pts):
    return [
        [half_attend_exact(256, h, shifts[h][j], *keys[j], pts[j]) for j in range(len(keys))]
        for h in range(2)
    ]


def run_halves(chunk, qt_ref, keys, pts, finish):
    shifts = [
        [stale_shift(h, qt_ref[head_rows(h), :], key_refs[0]) for key_refs in keys]
        for h in range(2)
    ]
    states = fast_states(chunk, shifts, keys, pts)
    worst = None
    for state in states[0] + states[1]:
        worst = state[1] if worst is None else jnp.maximum(worst, state[1])
    finish(states)

    @pl.when(jnp.logical_not(jnp.max(worst) <= LIMIT))
    def _():
        finish(redo(states, shifts, keys, pts))


def attend_first_kernel(chunk, qt_ref, k_ref, kx_ref, vt_ref, pt_ref, state_ref, acc_ref):
    def finish(states):
        for h in range(2):
            top, total, acc = states[h][0]
            state_ref[0, h : h + 1, :] = top
            state_ref[0, 2 + h : 3 + h, :] = total
            acc_ref[head_rows(h), :] = acc

    run_halves(chunk, qt_ref, [(k_ref, kx_ref, vt_ref)], [pt_ref], finish)


def attend_first(qt, key, chunk):
    rows = qt.shape[1]
    n = rows // ROWS
    col = pl.BlockSpec((256, ROWS), lambda i: (0, i))
    pairs = 2 * rows * rows
    return pl.pallas_call(
        partial(attend_first_kernel, chunk),
        out_shape=[
            jax.ShapeDtypeStruct((2 * n, 2, rows, ROWS), BF16),
            jax.ShapeDtypeStruct((n, 8, ROWS), F32),
            jax.ShapeDtypeStruct((256, rows), F32),
        ],
        grid=(n,),
        in_specs=[col] + [once(item.shape) for item in key],
        out_specs=[
            pl.BlockSpec((1, 2, rows, ROWS), lambda i: (i, 0, 0, 0)),
            pl.BlockSpec((1, 8, ROWS), lambda i: (i, 0, 0)),
            col,
        ],
        compiler_params=params(),
        cost_estimate=cost(4 * pairs * HEAD_DIM * 2, 2 * pairs, pairs),
        name="attend_near",
    )(qt, *key)


def attend_second_kernel(
    chunk, qtn_ref, qtf_ref, kn, kxn, vtn, kf, kxf, vtf, old_ref, old_acc_ref, _,
    ptn_ref, ptf_ref, mine_ref, sib_ref, stat_ref,
):
    i = pl.program_id(0)
    n = pl.num_programs(0) // 2
    near, far = (kn, kxn, vtn), (kf, kxf, vtf)

    def store(h, states):
        factors, result = merge(states)
        stat_ref[0, h : h + 1, :] = factors[0]
        stat_ref[0, 2 + h : 3 + h, :] = factors[1]
        low = result.T.astype(BF16)
        first = i % n < n // 2

        @pl.when(first)
        def _():
            mine_ref[:, head_rows(h)] = low

        @pl.when(jnp.logical_not(first))
        def _():
            sib_ref[:, head_rows(h)] = low

    @pl.when(i < n)
    def _():
        def finish(states):
            for h in range(2):
                old = (old_ref[0, h : h + 1, :], old_ref[0, 2 + h : 3 + h, :],
                       old_acc_ref[head_rows(h), :])
                store(h, [old, states[h][0]])

        run_halves(chunk, qtn_ref, [far], [ptf_ref], finish)

    @pl.when(i >= n)
    def _():
        def finish(states):
            for h in range(2):
                store(h, states[h])

        run_halves(chunk, qtf_ref, [near, far], [ptn_ref, ptf_ref], finish)


def mine_block(i, n):
    half = n // 2
    return (i // n) * half + jnp.minimum(i % n, half - 1)


def sib_block(i, n):
    half = n // 2
    return jnp.maximum((i // n) * half + i % n - half, jnp.maximum((i // n) * half - 1, 0))


def attend_second(qtn, qtf, near, far, pt, state, acc, chunk):
    rows = qtn.shape[1]
    n = rows // ROWS
    near_col = pl.BlockSpec((256, ROWS), lambda i: (0, jnp.minimum(i, n - 1)))
    pairs = 6 * rows * rows
    return pl.pallas_call(
        partial(attend_second_kernel, chunk),
        out_shape=[
            jax.ShapeDtypeStruct(pt.shape, BF16),
            jax.ShapeDtypeStruct(pt.shape, BF16),
            jax.ShapeDtypeStruct((rows, 256), BF16),
            jax.ShapeDtypeStruct((rows, 256), BF16),
            jax.ShapeDtypeStruct((2 * n, 8, ROWS), F32),
        ],
        grid=(2 * n,),
        in_specs=[near_col, pl.BlockSpec((256, ROWS), lambda i: (0, jnp.maximum(i - n, 0)))]
        + [once(item.shape) for item in near + far]
        + [
            pl.BlockSpec((1, 8, ROWS), lambda i: (jnp.minimum(i, n - 1), 0, 0)),
            near_col,
            pl.BlockSpec(memory_space=pl.ANY),
        ],
        out_specs=[
            pl.BlockSpec((1, 2, rows, ROWS), lambda i: (jnp.maximum(i, n), 0, 0, 0)),
            pl.BlockSpec((1, 2, rows, ROWS), lambda i: (i, 0, 0, 0)),
            pl.BlockSpec((ROWS, 256), lambda i: (mine_block(i, n), 0)),
            pl.BlockSpec((ROWS, 256), lambda i: (sib_block(i, n), 0)),
            pl.BlockSpec((1, 8, ROWS), lambda i: (i, 0, 0)),
        ],
        input_output_aliases={10: 0},
        compiler_params=params(),
        cost_estimate=cost(4 * pairs * HEAD_DIM * 2, 2 * pairs, pairs),
        name="attend_rest",
    )(qtn, qtf, *near, *far, state, acc, pt)


def back_weights(do, o, factors):
    dot_t = do.astype(F32).T
    delta = jnp.sum(dot_t * o.astype(F32).T, axis=0, keepdims=True)
    found = []
    for factor in factors:
        scaled = dot_t * factor
        high, middle, low = three_parts(delta * factor)
        extra = extra_rows([-high, -middle, -low], HEAD_DIM)
        found.append(
            (jnp.concatenate([scaled.astype(BF16), extra], axis=0), scaled.T.astype(BF16))
        )
    return found


def back_half(chunk, grads, q_rows, cols, pt_ref, v_ref, kt_ref, key_acc, value_acc):
    ones = jnp.where(
        lax.broadcasted_iota(jnp.int32, (chunk, HEAD_DIM), 1) < 3, F32(1.0), F32(0.0)
    ).astype(BF16)
    result = jnp.zeros((HEAD_DIM, q_rows.shape[0]), F32)
    for start in range(0, v_ref.shape[0], chunk):
        here = slice(start, start + chunk)
        prob = pt_ref[0, 0, here, cols]
        values = jnp.concatenate([v_ref[here, :], ones], axis=1)
        score = (prob.astype(F32) * mm(values, grads[0])).astype(BF16)
        value_acc[here, :] += mm(prob, grads[1])
        key_acc[here, :] += mm(score, q_rows)
        result = result + mm(kt_ref[:, here], score)
    return result


def attend_back_kernel(
    chunk, h, da_ref, db_ref, oa_ref, ob_ref, stat_ref, qn_ref, qf_ref, ptn_ref, ptf_ref,
    vn, ktn, vf, ktf, dq_ref, dk_ref, dv_ref, key_n, value_n, key_f, value_f,
):
    i = pl.program_id(0)
    n = pl.num_programs(0) // 2

    @pl.when(i == 0)
    def _():
        for ref in (key_n, value_n, key_f, value_f):
            ref[...] = jnp.zeros_like(ref)

    first = i % n < n // 2
    do = jnp.where(first, da_ref[...], db_ref[...])
    o = jnp.where(first, oa_ref[...], ob_ref[...])
    q = jnp.where(i < n, qn_ref[...], qf_ref[...])
    for start in range(0, do.shape[0], BACK_ROWS):
        part = slice(start, start + BACK_ROWS)
        near, far = back_weights(
            do[part], o[part], [stat_ref[0, h : h + 1, part], stat_ref[0, 2 + h : 3 + h, part]]
        )
        grad = back_half(chunk, near, q[part], part, ptn_ref, vn, ktn, key_n, value_n)
        grad += back_half(chunk, far, q[part], part, ptf_ref, vf, ktf, key_f, value_f)
        dq_ref[part, :] = (grad * F32(1.0 / math.sqrt(HEAD_DIM))).T.astype(BF16)

    @pl.when(i == 2 * n - 1)
    def _():
        seq = vn.shape[0]
        for half, (keys, values) in enumerate(((key_n, value_n), (key_f, value_f))):
            rows = slice(half * seq, (half + 1) * seq)
            dk_ref[rows, :] = (keys[...] * F32(1.0 / LOG2E)).astype(BF16)
            dv_ref[rows, :] = values[...].astype(BF16)


def attend_back(h, da, db, oa, ob, stat, qn, qf, ptn, ptf, vn, ktn, vf, ktf, chunk):
    rows = qn.shape[0]
    step = ROWS
    n = rows // step
    row = lambda f: pl.BlockSpec((step, HEAD_DIM), lambda i: (f(i), h))
    tile = pl.BlockSpec((1, 1, rows, step), lambda i: (i, h, 0, 0))
    fixed = lambda shape, place: pl.BlockSpec(
        shape, lambda i: place, pipeline_mode=pl.Buffered(1)
    )
    flat = jax.ShapeDtypeStruct((2 * rows, HEAD_DIM), BF16)
    acc = pltpu.VMEM((rows, HEAD_DIM), F32)
    pairs = 4 * rows * rows
    return pl.pallas_call(
        partial(attend_back_kernel, chunk, h),
        out_shape=[flat, flat, flat],
        grid=(2 * n,),
        in_specs=[
            row(lambda i: mine_block(i, n)),
            row(lambda i: sib_block(i, n)),
            row(lambda i: mine_block(i, n)),
            row(lambda i: sib_block(i, n)),
            pl.BlockSpec((1, 8, step), lambda i: (i, 0, 0)),
            row(lambda i: jnp.minimum(i, n - 1)),
            row(lambda i: jnp.maximum(i - n, 0)),
            tile,
            tile,
        ]
        + [fixed((rows, HEAD_DIM), (0, h)), fixed((HEAD_DIM, rows), (h, 0))] * 2,
        out_specs=[
            pl.BlockSpec((step, HEAD_DIM), lambda i: (i, 0)), once(flat.shape), once(flat.shape)
        ],
        scratch_shapes=[acc, acc, acc, acc],
        compiler_params=params(),
        cost_estimate=cost(8 * pairs * HEAD_DIM, 2 * pairs),
        name="attend_back",
    )(da, db, oa, ob, stat, qn, qf, ptn, ptf, vn, ktn, vf, ktf)


def mean(values):
    return jnp.mean(values, axis=-1, keepdims=True)


def norm(values):
    centered = values - mean(values)
    inverse = lax.rsqrt(mean(centered * centered) + EPS)
    return centered * inverse, inverse


def norm_back(incoming, normed, inverse, gain):
    scaled = incoming * gain
    return inverse * (scaled - mean(scaled) - normed * mean(scaled * normed))


def gelu_parts(v):
    bell = jnp.exp2(v * v * F32(-0.5 * LOG2E))
    base = 1.0 + F32(0.3275911 / math.sqrt(2.0)) * jnp.abs(v)
    t = pl.reciprocal(base, approx=True)
    t = t * (2.0 - base * t)
    series = t * (
        F32(0.5 * 0.254829592)
        + t
        * (
            F32(0.5 * -0.284496736)
            + t
            * (
                F32(0.5 * 1.421413741)
                + t * (F32(0.5 * -1.453152027) + t * F32(0.5 * 1.061405429))
            )
        )
    )
    tail = series * bell
    return bell * F32(1.0 / math.sqrt(2.0 * math.pi)), jnp.where(v >= 0, 1.0 - tail, tail)


def fold_rows(values):
    return jnp.sum(values.reshape(values.shape[0] // 8, 8, values.shape[1]), axis=0)


def rows_kernel(
    sizes, meta, xa_ref, xb_ref, oa_ref, ob_ref, cot_a, cot_b, p0, p1, p2, p3,
    u0, u1, u2, u3, vec_ref,
    prompt_near, data_near, prompt_far, data_far, resid_ref, da_ref, db_ref, send_ref,
    sums_ref, wo_ref, up_ref, down_ref, wo_t, up_t, down_t, bias_ref, grad_acc, vec_acc, bias_acc,
):
    prompt_local, data_local = sizes
    i = pl.program_id(0)
    half = pl.num_programs(0) // 2
    here = i < half
    rows = xa_ref.shape[0]
    quarter = u0.shape[1]

    @pl.when(i == 0)
    def _():
        for j, (pack, up_part) in enumerate(((p0, u0), (p1, u1), (p2, u2), (p3, u3))):
            cols = slice(j * quarter, (j + 1) * quarter)
            wo_ref[head_rows(j), :] = pack[:HEAD_DIM, :]
            down_ref[cols, :] = pack[HEAD_DIM : HEAD_DIM + quarter, :]
            bias_ref[0:1, cols] = pack[
                HEAD_DIM + quarter : HEAD_DIM + quarter + 16, :quarter
            ].astype(F32)[0:1, :]
            up_ref[:, cols] = up_part[...]
            wo_t[:, head_rows(j)] = pack[:HEAD_DIM, :].T
            down_t[:, cols] = pack[HEAD_DIM : HEAD_DIM + quarter, :].T
            up_t[cols, :] = up_part[...].T
        grad_acc[...] = jnp.zeros_like(grad_acc)
        vec_acc[...] = jnp.zeros_like(vec_acc)
        bias_acc[...] = jnp.zeros_like(bias_acc)

    slot = jnp.where(here, meta[0], meta[0] ^ 2)
    index = (i % half) * rows + lax.broadcasted_iota(jnp.int32, (rows, 1), 0) - prompt_local
    live = jnp.logical_or(index < 0, slot * data_local + index < meta[2])

    out_bias, attn_gain, attn_shift = vec_ref[0:1, :], vec_ref[1:2, :], vec_ref[2:3, :]
    down_bias, mlp_gain, mlp_shift = vec_ref[3:4, :], vec_ref[4:5, :], vec_ref[5:6, :]
    x = jnp.where(here, xa_ref[...], xb_ref[...])
    attended = jnp.concatenate([oa_ref[...], ob_ref[...]], axis=1)
    normed_one, inverse_one = norm(x.astype(F32) + (mm(attended, wo_ref[...]) + out_bias))
    hidden = normed_one * attn_gain + attn_shift
    hidden_low = hidden.astype(BF16)
    pre = mm(hidden_low, up_ref[...]) + bias_ref[0:1, :]
    density, share = gelu_parts(pre)
    activated = (pre * share).astype(BF16)
    slope = share + pre * density
    mixed = hidden + (mm(activated, down_ref[...]) + down_bias)
    normed_two, inverse_two = norm(mixed)
    output = (normed_two * mlp_gain + mlp_shift).astype(BF16)
    for j in range(2):
        split = max(0, min(rows, prompt_local - j * rows))
        for place, (prompt_ref, data_ref) in enumerate(
            ((prompt_near, data_near), (prompt_far, data_far))
        ):

            @pl.when(i == place * half + j)
            def _():
                if split:
                    prompt_ref[j * rows : j * rows + split, :] = output[:split]
                if split < rows:
                    begin = j * rows + split - prompt_local
                    data_ref[begin : begin + rows - split, :] = output[split:]

    cotangent = jnp.where(live, jnp.where(here, cot_a[...], cot_b[...]).astype(F32), 0.0)
    mixed_grad = norm_back(cotangent, normed_two, inverse_two, mlp_gain)
    mixed_low = mixed_grad.astype(BF16)
    pre_grad = (mm(mixed_low, down_t[...]) * slope).astype(BF16)
    hidden_grad = mixed_grad + mm(pre_grad, up_t[...])
    resid_grad = norm_back(hidden_grad, normed_one, inverse_one, attn_gain)
    resid_ref[...] = resid_grad
    resid_low = resid_grad.astype(BF16)
    attended_grad = mm(resid_low, wo_t[...]).astype(BF16)
    da_ref[...] = attended_grad[:, :256]
    db_ref[...] = attended_grad[:, 256:]

    up_grad = mm(hidden_low, pre_grad, TN)
    down_grad = mm(mixed_low, activated, TN)
    out_grad = mm(resid_low, attended, TN)
    for j in range(4):
        cols = slice(j * quarter, (j + 1) * quarter)
        grad_acc[j, :, :quarter] += up_grad[:, cols]
        grad_acc[j, :, quarter : 2 * quarter] += down_grad[:, cols]
        grad_acc[j, :, 2 * quarter :] += out_grad[:, head_rows(j)]
    bias_acc[...] += fold_rows(pre_grad.astype(F32))
    for place, value in enumerate(
        (
            resid_grad,
            hidden_grad * normed_one,
            hidden_grad,
            mixed_grad,
            cotangent * normed_two,
            cotangent,
        )
    ):
        vec_acc[place] += fold_rows(value)

    @pl.when(i == pl.num_programs(0) - 1)
    def _():
        for place in range(6):
            sums_ref[place : place + 1, :] = jnp.sum(vec_acc[place], axis=0, keepdims=True)
        bias_grad = jnp.sum(bias_acc[...], axis=0, keepdims=True)
        per_row = bias_grad.shape[1] // 2 // quarter
        for g in range(4):
            found = jnp.zeros((1, quarter), F32)
            for j, flip in enumerate((0, 2, 1, 3)):
                piece = bias_grad[:, j * quarter : (j + 1) * quarter]
                found = jnp.where((meta[0] ^ flip) == g, piece, found)
            row, col = 6 + g // per_row, (g % per_row) * quarter
            sums_ref[row : row + 1, col : col + quarter] = found
        depth = send_ref.shape[1] - 16
        groups = send_ref.shape[0] // 4
        width, wide = sums_ref.shape[1], send_ref.shape[2]
        per = sums_ref.shape[0] * width // groups
        for g in range(groups):
            row, col = g * per // width, g * per % width
            part = jnp.pad(sums_ref[row : row + 1, col : col + per], ((0, 0), (0, wide - per)))
            high, low, _ = three_parts(part)
            extra = extra_rows([high, low], 16)
            for j, flip in enumerate((0, 2, 1, 3)):
                target = g * 4 + (meta[0] ^ flip)
                send_ref[target, :depth] = grad_acc[j, g * depth : (g + 1) * depth].astype(BF16)
                send_ref[target, depth:] = extra


def row_work(meta, xa, xb, oa, ob, cot, packs, ups, vec, sizes, groups):
    rows, width = xa.shape
    prompt_local, data_local = sizes
    step = 512
    n = rows // step
    quarter = ups[0].shape[1]
    hidden = 4 * quarter
    wide = 2 * quarter + HEAD_DIM
    send = (4 * groups, width // groups + 16, wide)
    near = pl.BlockSpec((step, width), lambda i, meta: (jnp.minimum(i, n - 1), 0))
    far = pl.BlockSpec((step, width), lambda i, meta: (jnp.maximum(i - n, 0), 0))
    row = lambda cols: pl.BlockSpec((step, cols), lambda i, meta: (i, 0))
    return pl.pallas_call(
        partial(rows_kernel, sizes),
        out_shape=[
            jax.ShapeDtypeStruct((prompt_local, width), BF16),
            jax.ShapeDtypeStruct((data_local, width), BF16),
            jax.ShapeDtypeStruct((prompt_local, width), BF16),
            jax.ShapeDtypeStruct((data_local, width), BF16),
            jax.ShapeDtypeStruct((2 * rows, width), F32),
            jax.ShapeDtypeStruct((2 * rows, 256), BF16),
            jax.ShapeDtypeStruct((2 * rows, 256), BF16),
            jax.ShapeDtypeStruct(send, BF16),
        ],
        grid_spec=pltpu.PrefetchScalarGridSpec(
            num_scalar_prefetch=1,
            grid=(2 * n,),
            in_specs=[near, far, row(256), row(256), near, far]
            + [once(item.shape) for item in packs + ups]
            + [once(vec.shape)],
            out_specs=[
                once((prompt_local, width)),
                once((data_local, width)),
                once((prompt_local, width)),
                once((data_local, width)),
                row(width),
                row(256),
                row(256),
                once(send),
            ],
            scratch_shapes=[
                pltpu.VMEM((8, width), F32),
                pltpu.VMEM((4 * HEAD_DIM, width), BF16),
                pltpu.VMEM((width, hidden), BF16),
                pltpu.VMEM((hidden, width), BF16),
                pltpu.VMEM((width, 4 * HEAD_DIM), BF16),
                pltpu.VMEM((hidden, width), BF16),
                pltpu.VMEM((width, hidden), BF16),
                pltpu.VMEM((8, hidden), F32),
                pltpu.VMEM((4, width, wide), F32),
                pltpu.VMEM((6, 8, width), F32),
                pltpu.VMEM((8, hidden), F32),
            ],
        ),
        compiler_params=params(),
        cost_estimate=cost(
            3 * 2 * 2 * rows * width * (width + 2 * hidden), 24 * rows * width, 4 * rows * hidden
        ),
        name="row_work",
    )(meta, xa, xb, oa, ob, *cot, *packs, *ups, vec)


def choose_slot(i, per_slot, refs):
    found = refs[-1][...]
    for j in range(len(refs) - 2, -1, -1):
        found = jnp.where(i < (j + 1) * per_slot, refs[j][...], found)
    return found


def weight_grad_kernel(x0, x1, x2, x3, dq_ref, dk_ref, dv_ref, grad_ref, acc):
    i = pl.program_id(0)
    n = pl.num_programs(0)

    @pl.when(i == 0)
    def _():
        acc[...] = jnp.zeros_like(acc)

    dz = jnp.concatenate([dq_ref[...], dk_ref[...], dv_ref[...]], axis=1)
    acc[...] += mm(choose_slot(i, n // 4, [x0, x1, x2, x3]), dz, TN)

    @pl.when(i == n - 1)
    def _():
        groups, _, depth, _ = grad_ref.shape
        for g in range(groups):
            for which in range(3):
                grad_ref[g, which] = acc[g * depth : (g + 1) * depth, head_rows(which)].astype(
                    grad_ref.dtype
                )


def slot_specs(step, width, per_slot):
    def spec(j):
        return pl.BlockSpec((step, width), lambda i: (clamp(i - j * per_slot, 0, per_slot - 1), 0))

    return [spec(j) for j in range(4)]


def weight_grad(xs, grads, groups, kind):
    rows, width = xs[0].shape
    step = 512
    row = pl.BlockSpec((step, HEAD_DIM), lambda i: (i, 0))
    pieces = (groups, 3, width // groups, HEAD_DIM)
    return pl.pallas_call(
        weight_grad_kernel,
        out_shape=jax.ShapeDtypeStruct(pieces, kind),
        grid=(4 * rows // step,),
        in_specs=slot_specs(step, width, rows // step) + [row, row, row],
        out_specs=once(pieces),
        scratch_shapes=[pltpu.VMEM((width, 3 * HEAD_DIM), F32)],
        compiler_params=params(),
        cost_estimate=cost(4 * rows * width * 768, rows * width * 30),
        name="weight_grad",
    )(*xs, *grads)


def input_grad_kernel(
    prompt_local, per_slot, q0, k0, v0, q1, k1, v1, w_ref, resid_ref, sib_ref, *own_refs
):
    i = pl.program_id(0)
    step = q0.shape[0]
    half = pl.num_programs(0) // 2
    dz = jnp.concatenate([ref[...] for ref in (q0, q1, k0, k1, v0, v1)], axis=1)
    part = mm(dz, w_ref[...], NT)

    @pl.when(i < half)
    def _():
        sib_ref[...] = part.astype(BF16)

    for place in range(2):
        prompt_ref, data_ref = own_refs[2 * place : 2 * place + 2]
        for j in range(per_slot):
            split = max(0, min(step, prompt_local - j * step))

            @pl.when(i == half + (1 - place) * per_slot + j)
            def _():
                total = part + resid_ref[...]
                if split:
                    prompt_ref[j * step : j * step + split, :] = total[:split]
                if split < step:
                    begin = j * step + split - prompt_local
                    data_ref[begin : begin + step - split, :] = total[split:]


def input_grad(own, other, w, resid, prompt_local):
    rows = own[0].shape[0] // 4
    width = w.shape[0]
    step = 512
    n = rows // step

    def turn(i):
        slot = i // n
        return jnp.where(slot == 0, 3, jnp.where(slot == 1, 1, jnp.where(slot == 2, 2, 0))) * n + i % n

    def own_place(i):
        return jnp.where(i // n == 3, 0, n) + jnp.where(i // n < 2, 0, i % n)

    def sib(i):
        return jnp.where(i // n == 0, n + i % n, jnp.minimum(i - n, n - 1))

    turned = pl.BlockSpec((step, HEAD_DIM), lambda i: (turn(i), 0))
    data_local = rows - prompt_local
    own_shapes = [(prompt_local, width), (data_local, width)] * 2
    return pl.pallas_call(
        partial(input_grad_kernel, prompt_local, n),
        out_shape=[jax.ShapeDtypeStruct((2 * rows, width), BF16)]
        + [jax.ShapeDtypeStruct(shape, F32) for shape in own_shapes],
        grid=(4 * n,),
        in_specs=[turned] * 6 + [once(w.shape),
                  pl.BlockSpec((step, width), lambda i: (own_place(i), 0))],
        out_specs=[pl.BlockSpec((step, width), lambda i: (sib(i), 0))]
        + [once(shape) for shape in own_shapes],
        compiler_params=params(),
        cost_estimate=cost(2 * 4 * rows * width * 768, rows * width * 40),
        name="input_grad",
    )(*own, *other, w, resid)


def on_device(
    data_rows,
    prompt_rows,
    context_rows,
    test_rows,
    qkv_weight,
    out_bias,
    out_weight,
    attn_gain,
    attn_shift,
    up_weight,
    up_bias,
    down_weight,
    down_bias,
    mlp_gain,
    mlp_shift,
    data_cotangent,
    prompt_cotangent,
):
    data_local = data_rows.shape[1]
    prompt_local = prompt_rows.shape[0]
    width = prompt_rows.shape[1]
    quarter = up_weight.shape[1]
    sizes = (prompt_local, data_local)
    groups = lax.axis_size("ep")
    t = lax.axis_index("tp")
    mine = t >> 1
    other = 1 - mine

    def across(value):
        return lax.ppermute(value, "tp", [(i, i ^ 2) for i in range(4)])

    def beside(value):
        return lax.ppermute(value, "tp", [(i, i ^ 1) for i in range(4)])

    def pick(values, which):
        return lax.dynamic_index_in_dim(values, which, axis=0, keepdims=False)

    def stack(prompt_part, data_part):
        return jnp.concatenate([prompt_part, data_part], axis=0)

    w_far = across(qkv_weight)
    x_far = across(stack(prompt_rows, pick(data_rows, other)))
    x = stack(prompt_rows, pick(data_rows, mine))
    x_sib = beside(x)
    context = pick(context_rows, mine)
    live = context + pick(test_rows, mine)
    meta = jnp.stack([t, context, live]).astype(jnp.int32)

    qtn, qn, kn, kxn, ktn, vn, vtn, w = project(meta, x, x_sib, qkv_weight, w_far, sizes, 0)
    ptn, state, state_acc = attend_first(qtn, (kn, kxn, vtn), 512)

    cot_far = stack(pick(prompt_cotangent, other), pick(data_cotangent, other))
    bias_rows = jnp.pad(up_bias[None], ((0, 15), (0, width - quarter)))
    pack = jnp.concatenate([out_weight, down_weight, bias_rows], axis=0)
    x_far, state, pack, up_weight = lax.optimization_barrier((x_far, state, pack, up_weight))
    pack_far, up_far = across(pack), across(up_weight)
    x_far_sib = beside(x_far)
    qtf, qf, kf, kxf, ktf, vf, vtf, _ = project(meta, x_far, x_far_sib, qkv_weight, w_far, sizes, 2)
    pack_far, up_far, cot_far, qtf = lax.optimization_barrier((pack_far, up_far, cot_far, qtf))
    cot_far = across(cot_far)
    ptn, ptf, oa, ob, stat = attend_second(
        qtn, qtf, (kn, kxn, vtn), (kf, kxf, vtf), ptn, state, state_acc, 512
    )

    cot = stack(pick(prompt_cotangent, mine), pick(data_cotangent, mine))
    packs = [pack, pack_far, beside(pack), beside(pack_far)]
    ups = [up_weight, up_far, beside(up_weight), beside(up_far)]
    vec = jnp.stack(
        [out_bias, attn_gain, attn_shift, down_bias, mlp_gain, mlp_shift, mlp_shift, mlp_shift]
    ).astype(F32)
    (prompt_near, data_near, prompt_far, data_far, resid, da, db, send) = row_work(
        meta, x, x_far, oa, beside(ob), (cot, cot_far), packs, ups, vec, sizes, groups
    )

    def exchange(parts, axes):
        return lax.all_to_all(parts, axes, 0, 0, tiled=True)

    def gather(part):
        return exchange(jnp.broadcast_to(part[None], (groups,) + part.shape), "ep")

    db = beside(db)
    send = exchange(send, ("ep", "tp"))
    prompt_back, data_back = across(prompt_far), across(data_far)

    depth = width // groups
    xs = (x, x_sib, x_far, x_far_sib)
    back = (oa, ob, stat, qn, qf, ptn, ptf, vn, ktn, vf, ktf, 512)
    other_head = attend_back(1, da, db, *back)
    send, prompt_back, data_back, *other_head = lax.optimization_barrier(
        (send, prompt_back, data_back, *other_head)
    )
    total = jnp.sum(send.astype(F32), axis=0)
    part = total[depth : depth + 1] + total[depth + 1 : depth + 2]
    high = part.astype(BF16)
    low = (part - high.astype(F32)).astype(BF16)
    total = jnp.concatenate(
        [total[:depth].astype(BF16), high, low, jnp.zeros((14, total.shape[1]), BF16)], axis=0
    )
    total = jnp.broadcast_to(total[None], (groups,) + total.shape)
    other_grad = weight_grad(xs, other_head, groups, BF16)
    total, other_grad, da, db = lax.optimization_barrier((total, other_grad, da, db))
    total, other_grad = exchange(total, "ep"), across(other_grad)
    own_head = attend_back(0, da, db, *back)
    total, other_grad, *own_head = lax.optimization_barrier((total, other_grad, *own_head))

    own_grad = weight_grad(xs, own_head, groups, F32)
    qkv = (own_grad + other_grad.astype(F32)).astype(BF16).reshape(groups, 3 * depth, HEAD_DIM)
    qkv, *own_head = lax.optimization_barrier((qkv, *own_head))
    qkv = exchange(qkv, "ep")
    sib, near_prompt, near_data, far_prompt, far_data = input_grad(
        own_head, other_head, w, resid, prompt_local
    )
    slot_rows = prompt_local + data_local
    sib = beside(sib)
    sib = sib.astype(F32)
    far_prompt = across((far_prompt + sib[slot_rows : slot_rows + prompt_local]).astype(BF16))
    far_data = across((far_data + sib[slot_rows + prompt_local :]).astype(BF16))
    near_data = (near_data + sib[prompt_local:slot_rows]).astype(BF16)
    qkv = gather(jnp.sum(qkv.astype(F32), axis=0).astype(BF16))
    near_prompt = near_prompt + sib[:prompt_local] + far_prompt.astype(F32)
    near_prompt = near_prompt.astype(BF16).reshape(groups, prompt_local // groups, width)
    near_prompt = jnp.sum(exchange(near_prompt, "ep").astype(F32), axis=0).astype(BF16)
    prompt_grad = gather(near_prompt).reshape(prompt_local, width).astype(F32)
    qkv = qkv.reshape(groups, 3, depth, HEAD_DIM).transpose(1, 0, 2, 3)
    qkv = qkv.reshape(3, width, HEAD_DIM).astype(F32)

    which = lax.broadcasted_iota(jnp.int32, (2, 1, 1), 0)

    def by_episode(own, received):
        return jnp.where(which == mine, own[None], received[None])

    sums = total[:, depth : depth + 2, : 8 * width // groups].astype(F32)
    sums = (sums[:, 0] + sums[:, 1]).reshape(8, width)
    total = total[:, :depth].reshape(width, -1).astype(F32)
    bias_grad = lax.dynamic_slice_in_dim(sums[6:8].reshape(-1), t * quarter, quarter)
    return (
        by_episode(data_near, data_back),
        by_episode(prompt_near, prompt_back),
        by_episode(near_data, far_data),
        prompt_grad,
        qkv,
        sums[0],
        total[:, 2 * quarter :].T,
        sums[1],
        sums[2],
        total[:, :quarter],
        bias_grad,
        total[:, quarter : 2 * quarter].T,
        sums[3],
        sums[4],
        sums[5],
    )


def solution(mesh):
    return jax.shard_map(
        on_device,
        mesh=mesh,
        in_specs=(
            P("ep", "tp", None),
            P("tp", None),
            P("ep"),
            P("ep"),
            P(None, None, "tp"),
            P(),
            P("tp", None),
            P(),
            P(),
            P(None, "tp"),
            P("tp"),
            P("tp", None),
            P(),
            P(),
            P(),
            P("ep", "tp", None),
            P("ep", "tp", None),
        ),
        out_specs=(
            P("ep", "tp", None),
            P("ep", "tp", None),
            P("ep", "tp", None),
            P("tp", None),
            P(None, None, "tp"),
            P(),
            P("tp", None),
            P(),
            P(),
            P(None, "tp"),
            P("tp"),
            P("tp", None),
            P(),
            P(),
            P(),
        ),
        check_vma=False,
    )
```

```python
from functools import partial
import math

import jax
import jax.numpy as jnp
from jax import lax
from jax.experimental import pallas as pl
from jax.experimental.pallas import tpu as pltpu
from jax.sharding import PartitionSpec as P

HEAD_DIM = 128
ROWS = 512
BACK_ROWS = 256
SAMPLE = 256
EPS = 1e-05
MASKED = -1e30
LOG2E = math.log2(math.e)
LIMIT = 2.0**60
VMEM = 60 * 1024 * 1024
F32 = jnp.float32
BF16 = jnp.bfloat16
NN = (((1,), (0,)), ((), ()))
NT = (((1,), (1,)), ((), ()))
TN = (((0,), (0,)), ((), ()))


def mm(left, right, dims=NN):
    return lax.dot_general(left, right, dims, preferred_element_type=F32)


def params(**more):
    return pltpu.CompilerParams(vmem_limit_bytes=VMEM, **more)


def cost(flops, nbytes, trans=0):
    return pl.CostEstimate(
        flops=int(flops), bytes_accessed=int(nbytes), transcendentals=int(trans)
    )


def once(shape):
    return pl.BlockSpec(shape, lambda *_: (0,) * len(shape), pipeline_mode=pl.Buffered(1))


def extra_rows(values, count):
    width = values[0].shape[1]
    row = lax.broadcasted_iota(jnp.int32, (count, width), 0)
    out = jnp.zeros((count, width), F32)
    for index, value in enumerate(values):
        out = jnp.where(row == index, value, out)
    return out.astype(BF16)


def three_parts(row):
    high = row.astype(BF16).astype(F32)
    middle = (row - high).astype(BF16).astype(F32)
    return high, middle, row - high - middle


def clamp(i, low, high):
    return jnp.minimum(jnp.maximum(i, low), high)


def project_kernel(sizes, flip, meta, xa_ref, xb_ref, wa_ref, wb_ref, qt_ref, q_ref, k_ref,
                   kx_ref, kt_ref, v_ref, vt_ref, w_ref, wt_ref):
    prompt_local, data_local = sizes
    i = pl.program_id(0)
    per_slot = pl.num_programs(0) // 2
    rows = xa_ref.shape[0]

    @pl.when(i == 0)
    def _():
        for which in range(3):
            for h, source in enumerate((wa_ref, wb_ref)):
                cols = slice(which * 256 + h * HEAD_DIM, which * 256 + (h + 1) * HEAD_DIM)
                w_ref[:, cols] = source[which]
                wt_ref[cols, :] = source[which].T

    x = jnp.where(i < per_slot, xa_ref[...], xb_ref[...])
    slot = jnp.where(i < per_slot, meta[0] ^ flip, meta[0] ^ flip ^ 1)
    row = lax.broadcasted_iota(jnp.int32, (rows, HEAD_DIM), 0)
    lane = lax.broadcasted_iota(jnp.int32, (rows, HEAD_DIM), 1)
    index = (i % per_slot) * rows + row - prompt_local
    attended = jnp.logical_or(index < 0, slot * data_local + index < meta[1])
    bias = jnp.where(attended, F32(0.0), F32(MASKED))
    ones = jnp.where(lane < 4, F32(1.0), F32(0.0))
    kx_ref[...] = jnp.where(lane == 0, bias, ones).astype(BF16)
    factor = F32(LOG2E / math.sqrt(HEAD_DIM))
    z = mm(x, w_ref[...])
    q_ref[...] = (z[:, :256] * factor).astype(BF16)
    k_ref[...] = z[:, 256:512].astype(BF16)
    v_ref[...] = z[:, 512:].astype(BF16)
    zt = mm(wt_ref[...], x, NT)
    qt_ref[...] = (zt[:256] * factor).astype(BF16)
    kt_ref[...] = zt[256:512].astype(BF16)
    vt_ref[...] = zt[512:].astype(BF16)


def project(meta, xa, xb, wa, wb, sizes, flip):
    rows, width = xa.shape
    step = 512
    n = rows // step
    flat = jax.ShapeDtypeStruct((2 * rows, 256), BF16)
    tall = jax.ShapeDtypeStruct((256, 2 * rows), BF16)
    row = pl.BlockSpec((step, 256), lambda i, meta: (i, 0))
    col = pl.BlockSpec((256, step), lambda i, meta: (0, i))
    return pl.pallas_call(
        partial(project_kernel, sizes, flip),
        out_shape=[
            tall,
            flat,
            flat,
            jax.ShapeDtypeStruct((2 * rows, HEAD_DIM), BF16),
            tall,
            flat,
            tall,
            jax.ShapeDtypeStruct((width, 768), BF16),
        ],
        grid_spec=pltpu.PrefetchScalarGridSpec(
            num_scalar_prefetch=1,
            grid=(2 * n,),
            in_specs=[
                pl.BlockSpec((step, width), lambda i, meta: (jnp.minimum(i, n - 1), 0)),
                pl.BlockSpec((step, width), lambda i, meta: (jnp.maximum(i - n, 0), 0)),
                once(wa.shape),
                once(wb.shape),
            ],
            out_specs=[
                col,
                row,
                row,
                pl.BlockSpec((step, HEAD_DIM), lambda i, meta: (i, 0)),
                col,
                row,
                col,
                once((width, 768)),
            ],
            scratch_shapes=[pltpu.VMEM((768, width), BF16)],
        ),
        compiler_params=params(),
        cost_estimate=cost(4 * 2 * rows * width * 768, 2 * rows * width * 8),
        name="project",
    )(meta, xa, xb, wa, wb)


def head_rows(h):
    return slice(h * HEAD_DIM, (h + 1) * HEAD_DIM)


def with_shift(qt, top):
    high, middle, low = three_parts(top)
    extra = extra_rows([jnp.ones_like(top), -high, -middle, -low], HEAD_DIM)
    return jnp.concatenate([qt, extra], axis=0)


def half_scores(chunk, h, qa, start, k_ref, kx_ref):
    here = pl.ds(start, chunk)
    keys = jnp.concatenate([k_ref[here, head_rows(h)], kx_ref[here, :]], axis=1)
    return mm(keys, qa)


def half_part(h, start, scores, vt_ref, pt_ref):
    chunk = scores.shape[0]
    weight = jnp.exp2(scores)
    total = jnp.sum(weight.reshape(chunk // 8, 8, weight.shape[1]), axis=0)
    low = weight.astype(BF16)
    pt_ref[0, h, pl.ds(start, chunk), :] = low
    return total, mm(vt_ref[head_rows(h), pl.ds(start, chunk)], low)


def stale_shift(h, qt, k_ref):
    top = jnp.max(mm(k_ref[:SAMPLE, head_rows(h)], qt), axis=0, keepdims=True)
    return top, with_shift(qt, top)


def fast_states(chunk, shifts, keys, pts):
    tiles = [
        (h, j, start)
        for h in range(2)
        for j in range(len(keys))
        for start in range(0, keys[0][0].shape[0], chunk)
    ]

    def scores(tile):
        h, j, start = tile
        return half_scores(chunk, h, shifts[h][j][1], start, keys[j][0], keys[j][1])

    sums = {}
    ahead = scores(tiles[0])
    for place, (h, j, start) in enumerate(tiles):
        now = ahead
        if place + 1 < len(tiles):
            ahead = scores(tiles[place + 1])
        total, product = half_part(h, start, now, keys[j][2], pts[j])
        if (h, j) in sums:
            total, product = sums[h, j][0] + total, sums[h, j][1] + product
        sums[h, j] = total, product
    return [
        [
            (shifts[h][j][0], jnp.sum(sums[h, j][0], axis=0, keepdims=True), sums[h, j][1])
            for j in range(len(keys))
        ]
        for h in range(2)
    ]


def half_attend_exact(chunk, h, shift, k_ref, kx_ref, vt_ref, pt_ref):
    qt = shift[1][:HEAD_DIM]
    width = qt.shape[1]
    count = k_ref.shape[0] // chunk
    qa = with_shift(qt, jnp.zeros((1, width), F32))

    def find(j, top):
        found = half_scores(chunk, h, qa, pl.multiple_of(j * chunk, chunk), k_ref, kx_ref)
        return jnp.maximum(top, jnp.max(found, axis=0, keepdims=True))

    top = lax.fori_loop(0, count, find, jnp.full((1, width), MASKED, F32))
    qa = with_shift(qt, top)

    def add(j, state):
        start = pl.multiple_of(j * chunk, chunk)
        found = half_scores(chunk, h, qa, start, k_ref, kx_ref)
        more, product = half_part(h, start, found, vt_ref, pt_ref)
        return state[0] + more, state[1] + product

    total, acc = lax.fori_loop(
        0, count, add, (jnp.zeros((8, width), F32), jnp.zeros((HEAD_DIM, width), F32))
    )
    return top, jnp.sum(total, axis=0, keepdims=True), acc


def merge(states):
    top = states[0][0]
    for state in states[1:]:
        top = jnp.maximum(top, state[0])
    scales = [jnp.exp2(state[0] - top) for state in states]
    total = sum(state[1] * scale for state, scale in zip(states, scales))
    factors = [scale / total for scale in scales]
    return factors, sum(state[2] * factor for state, factor in zip(states, factors))


def redo(states, shifts, keys, pts):
    return [
        [half_attend_exact(256, h, shifts[h][j], *keys[j], pts[j]) for j in range(len(keys))]
        for h in range(2)
    ]


def run_halves(chunk, qt_ref, keys, pts, finish):
    shifts = [
        [stale_shift(h, qt_ref[head_rows(h), :], key_refs[0]) for key_refs in keys]
        for h in range(2)
    ]
    states = fast_states(chunk, shifts, keys, pts)
    worst = None
    for state in states[0] + states[1]:
        worst = state[1] if worst is None else jnp.maximum(worst, state[1])
    finish(states)

    @pl.when(jnp.logical_not(jnp.max(worst) <= LIMIT))
    def _():
        finish(redo(states, shifts, keys, pts))


def attend_first_kernel(chunk, qt_ref, k_ref, kx_ref, vt_ref, pt_ref, state_ref, acc_ref):
    def finish(states):
        for h in range(2):
            top, total, acc = states[h][0]
            state_ref[0, h : h + 1, :] = top
            state_ref[0, 2 + h : 3 + h, :] = total
            acc_ref[head_rows(h), :] = acc

    run_halves(chunk, qt_ref, [(k_ref, kx_ref, vt_ref)], [pt_ref], finish)


def attend_first(qt, key, chunk):
    rows = qt.shape[1]
    n = rows // ROWS
    col = pl.BlockSpec((256, ROWS), lambda i: (0, i))
    pairs = 2 * rows * rows
    return pl.pallas_call(
        partial(attend_first_kernel, chunk),
        out_shape=[
            jax.ShapeDtypeStruct((2 * n, 2, rows, ROWS), BF16),
            jax.ShapeDtypeStruct((n, 8, ROWS), F32),
            jax.ShapeDtypeStruct((256, rows), F32),
        ],
        grid=(n,),
        in_specs=[col] + [once(item.shape) for item in key],
        out_specs=[
            pl.BlockSpec((1, 2, rows, ROWS), lambda i: (i, 0, 0, 0)),
            pl.BlockSpec((1, 8, ROWS), lambda i: (i, 0, 0)),
            col,
        ],
        compiler_params=params(),
        cost_estimate=cost(4 * pairs * HEAD_DIM * 2, 2 * pairs, pairs),
        name="attend_near",
    )(qt, *key)


def attend_second_kernel(
    chunk, qtn_ref, qtf_ref, kn, kxn, vtn, kf, kxf, vtf, old_ref, old_acc_ref, _,
    ptn_ref, ptf_ref, mine_ref, sib_ref, stat_ref,
):
    i = pl.program_id(0)
    n = pl.num_programs(0) // 2
    near, far = (kn, kxn, vtn), (kf, kxf, vtf)

    def store(h, states):
        factors, result = merge(states)
        stat_ref[0, h : h + 1, :] = factors[0]
        stat_ref[0, 2 + h : 3 + h, :] = factors[1]
        low = result.T.astype(BF16)
        first = i % n < n // 2

        @pl.when(first)
        def _():
            mine_ref[:, head_rows(h)] = low

        @pl.when(jnp.logical_not(first))
        def _():
            sib_ref[:, head_rows(h)] = low

    @pl.when(i < n)
    def _():
        def finish(states):
            for h in range(2):
                old = (old_ref[0, h : h + 1, :], old_ref[0, 2 + h : 3 + h, :],
                       old_acc_ref[head_rows(h), :])
                store(h, [old, states[h][0]])

        run_halves(chunk, qtn_ref, [far], [ptf_ref], finish)

    @pl.when(i >= n)
    def _():
        def finish(states):
            for h in range(2):
                store(h, states[h])

        run_halves(chunk, qtf_ref, [near, far], [ptn_ref, ptf_ref], finish)


def mine_block(i, n):
    half = n // 2
    return (i // n) * half + jnp.minimum(i % n, half - 1)


def sib_block(i, n):
    half = n // 2
    return jnp.maximum((i // n) * half + i % n - half, jnp.maximum((i // n) * half - 1, 0))


def attend_second(qtn, qtf, near, far, pt, state, acc, chunk):
    rows = qtn.shape[1]
    n = rows // ROWS
    near_col = pl.BlockSpec((256, ROWS), lambda i: (0, jnp.minimum(i, n - 1)))
    pairs = 6 * rows * rows
    return pl.pallas_call(
        partial(attend_second_kernel, chunk),
        out_shape=[
            jax.ShapeDtypeStruct(pt.shape, BF16),
            jax.ShapeDtypeStruct(pt.shape, BF16),
            jax.ShapeDtypeStruct((rows, 256), BF16),
            jax.ShapeDtypeStruct((rows, 256), BF16),
            jax.ShapeDtypeStruct((2 * n, 8, ROWS), F32),
        ],
        grid=(2 * n,),
        in_specs=[near_col, pl.BlockSpec((256, ROWS), lambda i: (0, jnp.maximum(i - n, 0)))]
        + [once(item.shape) for item in near + far]
        + [
            pl.BlockSpec((1, 8, ROWS), lambda i: (jnp.minimum(i, n - 1), 0, 0)),
            near_col,
            pl.BlockSpec(memory_space=pl.ANY),
        ],
        out_specs=[
            pl.BlockSpec((1, 2, rows, ROWS), lambda i: (jnp.maximum(i, n), 0, 0, 0)),
            pl.BlockSpec((1, 2, rows, ROWS), lambda i: (i, 0, 0, 0)),
            pl.BlockSpec((ROWS, 256), lambda i: (mine_block(i, n), 0)),
            pl.BlockSpec((ROWS, 256), lambda i: (sib_block(i, n), 0)),
            pl.BlockSpec((1, 8, ROWS), lambda i: (i, 0, 0)),
        ],
        input_output_aliases={10: 0},
        compiler_params=params(),
        cost_estimate=cost(4 * pairs * HEAD_DIM * 2, 2 * pairs, pairs),
        name="attend_rest",
    )(qtn, qtf, *near, *far, state, acc, pt)


def back_weights(do, o, factors):
    dot_t = do.astype(F32).T
    delta = jnp.sum(dot_t * o.astype(F32).T, axis=0, keepdims=True)
    found = []
    for factor in factors:
        scaled = dot_t * factor
        high, middle, low = three_parts(delta * factor)
        extra = extra_rows([-high, -middle, -low], HEAD_DIM)
        found.append(
            (jnp.concatenate([scaled.astype(BF16), extra], axis=0), scaled.T.astype(BF16))
        )
    return found


def back_half(chunk, h, grads, q_rows, pt_ref, v_ref, kt_ref, key_acc, value_acc):
    ones = jnp.where(
        lax.broadcasted_iota(jnp.int32, (chunk, HEAD_DIM), 1) < 3, F32(1.0), F32(0.0)
    ).astype(BF16)
    result = jnp.zeros((HEAD_DIM, q_rows.shape[0]), F32)
    for start in range(0, v_ref.shape[0], chunk):
        here = slice(start, start + chunk)
        prob = pt_ref[0, h, here, :]
        values = jnp.concatenate([v_ref[here, head_rows(h)], ones], axis=1)
        score = (prob.astype(F32) * mm(values, grads[0])).astype(BF16)
        value_acc[h, here, :] += mm(prob, grads[1])
        key_acc[h, here, :] += mm(score, q_rows)
        result = result + mm(kt_ref[head_rows(h), here], score)
    return result


def attend_back_kernel(
    chunk, da_ref, db_ref, oa_ref, ob_ref, stat_ref, qn_ref, qf_ref, ptn_ref, ptf_ref,
    vn, ktn, vf, ktf, dq_ref, dkv_ref, key_n, value_n, key_f, value_f,
):
    i = pl.program_id(0)
    n = pl.num_programs(0) // 2

    @pl.when(i == 0)
    def _():
        for ref in (key_n, value_n, key_f, value_f):
            ref[...] = jnp.zeros_like(ref)

    first = i % n < n // 2
    do = jnp.where(first, da_ref[...], db_ref[...])
    o = jnp.where(first, oa_ref[...], ob_ref[...])
    q = jnp.where(i < n, qn_ref[...], qf_ref[...])
    for h in range(2):
        cols = head_rows(h)
        near, far = back_weights(
            do[:, cols], o[:, cols], [stat_ref[0, h : h + 1, :], stat_ref[0, 2 + h : 3 + h, :]]
        )
        grad = back_half(chunk, h, near, q[:, cols], ptn_ref, vn, ktn, key_n, value_n)
        grad += back_half(chunk, h, far, q[:, cols], ptf_ref, vf, ktf, key_f, value_f)
        dq_ref[:, cols] = (grad * F32(1.0 / math.sqrt(HEAD_DIM))).T.astype(BF16)

    @pl.when(i == 2 * n - 1)
    def _():
        seq = vn.shape[0]
        for half, (keys, values) in enumerate(((key_n, value_n), (key_f, value_f))):
            for owner in range(2):
                source = slice(owner * seq // 2, (owner + 1) * seq // 2)
                begin = owner * seq + half * seq // 2
                rows = slice(begin, begin + seq // 2)
                for h in range(2):
                    dkv_ref[rows, head_rows(h)] = (keys[h, source] * F32(1.0 / LOG2E)).astype(BF16)
                    dkv_ref[rows, head_rows(2 + h)] = values[h, source].astype(BF16)


def attend_back(da, db, oa, ob, stat, qn, qf, ptn, ptf, vn, ktn, vf, ktf, chunk):
    rows = qn.shape[0]
    step = BACK_ROWS
    n = rows // step
    per = ROWS // step
    row = lambda f: pl.BlockSpec((step, 256), lambda i: (f(i), 0))
    tile = pl.BlockSpec((1, 2, rows, step), lambda i: (i // per, 0, 0, i % per))
    flat = jax.ShapeDtypeStruct((2 * rows, 256), BF16)
    wide = jax.ShapeDtypeStruct((2 * rows, 512), BF16)
    acc = pltpu.VMEM((2, rows, HEAD_DIM), F32)

    def own_first(i):
        return jnp.where(i % n < n // 2, 0, n // 2) + (i // n) * (n // 2) + i % n
    pairs = 8 * rows * rows
    return pl.pallas_call(
        partial(attend_back_kernel, chunk),
        out_shape=[flat, wide],
        grid=(2 * n,),
        in_specs=[
            row(lambda i: mine_block(i, n)),
            row(lambda i: sib_block(i, n)),
            row(lambda i: mine_block(i, n)),
            row(lambda i: sib_block(i, n)),
            pl.BlockSpec((1, 8, step), lambda i: (i // per, 0, i % per)),
            row(lambda i: jnp.minimum(i, n - 1)),
            row(lambda i: jnp.maximum(i - n, 0)),
            tile,
            tile,
        ]
        + [once(item.shape) for item in (vn, ktn, vf, ktf)],
        out_specs=[row(own_first), once(wide.shape)],
        scratch_shapes=[acc, acc, acc, acc],
        compiler_params=params(),
        cost_estimate=cost(8 * pairs * HEAD_DIM, 2 * pairs),
        name="attend_back",
    )(da, db, oa, ob, stat, qn, qf, ptn, ptf, vn, ktn, vf, ktf)


def mean(values):
    return jnp.mean(values, axis=-1, keepdims=True)


def norm(values):
    centered = values - mean(values)
    inverse = lax.rsqrt(mean(centered * centered) + EPS)
    return centered * inverse, inverse


def norm_back(incoming, normed, inverse, gain):
    scaled = incoming * gain
    return inverse * (scaled - mean(scaled) - normed * mean(scaled * normed))


def gelu_parts(v):
    bell = jnp.exp2(v * v * F32(-0.5 * LOG2E))
    base = 1.0 + F32(0.3275911 / math.sqrt(2.0)) * jnp.abs(v)
    t = pl.reciprocal(base, approx=True)
    t = t * (2.0 - base * t)
    series = t * (
        F32(0.5 * 0.254829592)
        + t
        * (
            F32(0.5 * -0.284496736)
            + t
            * (
                F32(0.5 * 1.421413741)
                + t * (F32(0.5 * -1.453152027) + t * F32(0.5 * 1.061405429))
            )
        )
    )
    tail = series * bell
    return bell * F32(1.0 / math.sqrt(2.0 * math.pi)), jnp.where(v >= 0, 1.0 - tail, tail)


def fold_rows(values):
    return jnp.sum(values.reshape(values.shape[0] // 8, 8, values.shape[1]), axis=0)


def rows_kernel(
    sizes, meta, xa_ref, xb_ref, oa_ref, ob_ref, cot_a, cot_b, p0, p1, p2, p3,
    u0, u1, u2, u3, vec_ref,
    prompt_near, data_near, prompt_far, data_far, resid_ref, da_ref, db_ref, send_ref,
    sums_ref, wo_ref, up_ref, down_ref, bias_ref, grad_acc, vec_acc, bias_acc,
):
    prompt_local, data_local = sizes
    i = pl.program_id(0)
    half = pl.num_programs(0) // 2
    here = i < half
    rows = xa_ref.shape[0]
    quarter = u0.shape[1]

    @pl.when(i == 0)
    def _():
        for j, (pack, up_part) in enumerate(((p0, u0), (p1, u1), (p2, u2), (p3, u3))):
            cols = slice(j * quarter, (j + 1) * quarter)
            wo_ref[head_rows(j), :] = pack[:HEAD_DIM, :]
            down_ref[cols, :] = pack[HEAD_DIM : HEAD_DIM + quarter, :]
            bias_ref[0:1, cols] = pack[
                HEAD_DIM + quarter : HEAD_DIM + quarter + 16, :quarter
            ].astype(F32)[0:1, :]
            up_ref[:, cols] = up_part[...]
        grad_acc[...] = jnp.zeros_like(grad_acc)
        vec_acc[...] = jnp.zeros_like(vec_acc)
        bias_acc[...] = jnp.zeros_like(bias_acc)

    slot = jnp.where(here, meta[0], meta[0] ^ 2)
    index = (i % half) * rows + lax.broadcasted_iota(jnp.int32, (rows, 1), 0) - prompt_local
    live = jnp.logical_or(index < 0, slot * data_local + index < meta[2])

    out_bias, attn_gain, attn_shift = vec_ref[0:1, :], vec_ref[1:2, :], vec_ref[2:3, :]
    down_bias, mlp_gain, mlp_shift = vec_ref[3:4, :], vec_ref[4:5, :], vec_ref[5:6, :]
    x = jnp.where(here, xa_ref[...], xb_ref[...])
    attended = jnp.concatenate([oa_ref[...], ob_ref[...]], axis=1)
    normed_one, inverse_one = norm(x.astype(F32) + (mm(attended, wo_ref[...]) + out_bias))
    hidden = normed_one * attn_gain + attn_shift
    hidden_low = hidden.astype(BF16)
    pre = mm(hidden_low, up_ref[...]) + bias_ref[0:1, :]
    density, share = gelu_parts(pre)
    activated = (pre * share).astype(BF16)
    slope = share + pre * density
    mixed = hidden + (mm(activated, down_ref[...]) + down_bias)
    normed_two, inverse_two = norm(mixed)
    output = (normed_two * mlp_gain + mlp_shift).astype(BF16)
    for j in range(2):
        split = max(0, min(rows, prompt_local - j * rows))
        for place, (prompt_ref, data_ref) in enumerate(
            ((prompt_near, data_near), (prompt_far, data_far))
        ):

            @pl.when(i == place * half + j)
            def _():
                if split:
                    prompt_ref[j * rows : j * rows + split, :] = output[:split]
                if split < rows:
                    begin = j * rows + split - prompt_local
                    data_ref[begin : begin + rows - split, :] = output[split:]

    cotangent = jnp.where(live, jnp.where(here, cot_a[...], cot_b[...]).astype(F32), 0.0)
    mixed_grad = norm_back(cotangent, normed_two, inverse_two, mlp_gain)
    mixed_low = mixed_grad.astype(BF16)
    pre_grad = (mm(mixed_low, down_ref[...], NT) * slope).astype(BF16)
    hidden_grad = mixed_grad + mm(pre_grad, up_ref[...], NT)
    resid_grad = norm_back(hidden_grad, normed_one, inverse_one, attn_gain)
    resid_ref[...] = resid_grad
    resid_low = resid_grad.astype(BF16)
    attended_grad = mm(resid_low, wo_ref[...], NT).astype(BF16)
    da_ref[...] = attended_grad[:, :256]
    db_ref[...] = attended_grad[:, 256:]

    up_grad = mm(hidden_low, pre_grad, TN)
    down_grad = mm(mixed_low, activated, TN)
    out_grad = mm(resid_low, attended, TN)
    for j in range(4):
        cols = slice(j * quarter, (j + 1) * quarter)
        grad_acc[j, :, :quarter] += up_grad[:, cols]
        grad_acc[j, :, quarter : 2 * quarter] += down_grad[:, cols]
        grad_acc[j, :, 2 * quarter :] += out_grad[:, head_rows(j)]
    bias_acc[...] += fold_rows(pre_grad.astype(F32))
    for place, value in enumerate(
        (
            resid_grad,
            hidden_grad * normed_one,
            hidden_grad,
            mixed_grad,
            cotangent * normed_two,
            cotangent,
        )
    ):
        vec_acc[place] += fold_rows(value)

    @pl.when(i == pl.num_programs(0) - 1)
    def _():
        for place in range(6):
            sums_ref[place : place + 1, :] = jnp.sum(vec_acc[place], axis=0, keepdims=True)
        bias_grad = jnp.sum(bias_acc[...], axis=0, keepdims=True)
        per_row = bias_grad.shape[1] // 2 // quarter
        for g in range(4):
            found = jnp.zeros((1, quarter), F32)
            for j, flip in enumerate((0, 2, 1, 3)):
                piece = bias_grad[:, j * quarter : (j + 1) * quarter]
                found = jnp.where((meta[0] ^ flip) == g, piece, found)
            row, col = 6 + g // per_row, (g % per_row) * quarter
            sums_ref[row : row + 1, col : col + quarter] = found
        depth = send_ref.shape[1] - 16
        groups = send_ref.shape[0] // 4
        width, wide = sums_ref.shape[1], send_ref.shape[2]
        per = sums_ref.shape[0] * width // groups
        for g in range(groups):
            row, col = g * per // width, g * per % width
            part = jnp.pad(sums_ref[row : row + 1, col : col + per], ((0, 0), (0, wide - per)))
            high, low, _ = three_parts(part)
            extra = extra_rows([high, low], 16)
            for j, flip in enumerate((0, 2, 1, 3)):
                target = g * 4 + (meta[0] ^ flip)
                send_ref[target, :depth] = grad_acc[j, g * depth : (g + 1) * depth].astype(BF16)
                send_ref[target, depth:] = extra


def row_work(meta, xa, xb, oa, ob, cot, packs, ups, vec, sizes, groups):
    rows, width = xa.shape
    prompt_local, data_local = sizes
    step = 512
    n = rows // step
    quarter = ups[0].shape[1]
    hidden = 4 * quarter
    wide = 2 * quarter + HEAD_DIM
    send = (4 * groups, width // groups + 16, wide)
    near = pl.BlockSpec((step, width), lambda i, meta: (jnp.minimum(i, n - 1), 0))
    far = pl.BlockSpec((step, width), lambda i, meta: (jnp.maximum(i - n, 0), 0))
    row = lambda cols: pl.BlockSpec((step, cols), lambda i, meta: (i, 0))
    return pl.pallas_call(
        partial(rows_kernel, sizes),
        out_shape=[
            jax.ShapeDtypeStruct((prompt_local, width), BF16),
            jax.ShapeDtypeStruct((data_local, width), BF16),
            jax.ShapeDtypeStruct((prompt_local, width), BF16),
            jax.ShapeDtypeStruct((data_local, width), BF16),
            jax.ShapeDtypeStruct((2 * rows, width), F32),
            jax.ShapeDtypeStruct((2 * rows, 256), BF16),
            jax.ShapeDtypeStruct((2 * rows, 256), BF16),
            jax.ShapeDtypeStruct(send, BF16),
        ],
        grid_spec=pltpu.PrefetchScalarGridSpec(
            num_scalar_prefetch=1,
            grid=(2 * n,),
            in_specs=[near, far, row(256), row(256), near, far]
            + [once(item.shape) for item in packs + ups]
            + [once(vec.shape)],
            out_specs=[
                once((prompt_local, width)),
                once((data_local, width)),
                once((prompt_local, width)),
                once((data_local, width)),
                row(width),
                row(256),
                row(256),
                once(send),
            ],
            scratch_shapes=[
                pltpu.VMEM((8, width), F32),
                pltpu.VMEM((4 * HEAD_DIM, width), BF16),
                pltpu.VMEM((width, hidden), BF16),
                pltpu.VMEM((hidden, width), BF16),
                pltpu.VMEM((8, hidden), F32),
                pltpu.VMEM((4, width, wide), F32),
                pltpu.VMEM((6, 8, width), F32),
                pltpu.VMEM((8, hidden), F32),
            ],
        ),
        compiler_params=params(),
        cost_estimate=cost(
            3 * 2 * 2 * rows * width * (width + 2 * hidden), 24 * rows * width, 4 * rows * hidden
        ),
        name="row_work",
    )(meta, xa, xb, oa, ob, *cot, *packs, *ups, vec)


def on_device(
    data_rows,
    prompt_rows,
    context_rows,
    test_rows,
    qkv_weight,
    out_bias,
    out_weight,
    attn_gain,
    attn_shift,
    up_weight,
    up_bias,
    down_weight,
    down_bias,
    mlp_gain,
    mlp_shift,
    data_cotangent,
    prompt_cotangent,
):
    data_local = data_rows.shape[1]
    prompt_local = prompt_rows.shape[0]
    width = prompt_rows.shape[1]
    quarter = up_weight.shape[1]
    sizes = (prompt_local, data_local)
    groups = lax.axis_size("ep")
    t = lax.axis_index("tp")
    mine = t >> 1
    other = 1 - mine

    def across(value):
        return lax.ppermute(value, "tp", [(i, i ^ 2) for i in range(4)])

    def beside(value):
        return lax.ppermute(value, "tp", [(i, i ^ 1) for i in range(4)])

    def pick(values, which):
        return lax.dynamic_index_in_dim(values, which, axis=0, keepdims=False)

    def stack(prompt_part, data_part):
        return jnp.concatenate([prompt_part, data_part], axis=0)

    w_far = across(qkv_weight)
    x_far = across(stack(prompt_rows, pick(data_rows, other)))
    x = stack(prompt_rows, pick(data_rows, mine))
    x_sib = beside(x)
    context = pick(context_rows, mine)
    live = context + pick(test_rows, mine)
    meta = jnp.stack([t, context, live]).astype(jnp.int32)

    qtn, qn, kn, kxn, ktn, vn, vtn, w = project(meta, x, x_sib, qkv_weight, w_far, sizes, 0)
    ptn, state, state_acc = attend_first(qtn, (kn, kxn, vtn), 512)

    bias_rows = jnp.pad(up_bias[None], ((0, 15), (0, width - quarter)))
    pack = jnp.concatenate([out_weight, down_weight, bias_rows], axis=0)
    x_far, state, pack, up_weight = lax.optimization_barrier((x_far, state, pack, up_weight))
    x_far_sib = beside(x_far)
    pack_far, up_far = across(pack), across(up_weight)
    cot_far = stack(pick(prompt_cotangent, other), pick(data_cotangent, other))
    x_far_sib, cot_far = lax.optimization_barrier((x_far_sib, cot_far))
    cot_far = across(cot_far)
    qtf, qf, kf, kxf, ktf, vf, vtf, _ = project(meta, x_far, x_far_sib, qkv_weight, w_far, sizes, 2)
    x_all = jnp.concatenate([x, x_far, x_sib, x_far_sib], axis=0)
    pack_far, up_far, x_all, qtf = lax.optimization_barrier((pack_far, up_far, x_all, qtf))
    ptn, ptf, oa, ob, stat = attend_second(
        qtn, qtf, (kn, kxn, vtn), (kf, kxf, vtf), ptn, state, state_acc, 512
    )

    cot = stack(pick(prompt_cotangent, mine), pick(data_cotangent, mine))
    packs = [pack, pack_far, beside(pack), beside(pack_far)]
    ups = [up_weight, up_far, beside(up_weight), beside(up_far)]
    vec = jnp.stack(
        [out_bias, attn_gain, attn_shift, down_bias, mlp_gain, mlp_shift, mlp_shift, mlp_shift]
    ).astype(F32)
    (prompt_near, data_near, prompt_far, data_far, resid, da, db, send) = row_work(
        meta, x, x_far, oa, beside(ob), (cot, cot_far), packs, ups, vec, sizes, groups
    )

    def dot(left, right, dims):
        return lax.dot_general(left, right, dims, preferred_element_type=F32)

    def exchange(parts, axes):
        return lax.all_to_all(parts, axes, 0, 0, tiled=True)

    def gather(part):
        return exchange(jnp.broadcast_to(part[None], (groups,) + part.shape), "ep")

    db = beside(db)
    send = exchange(send, ("ep", "tp"))
    prompt_back, data_back = across(prompt_far), across(data_far)

    dq, dkv = attend_back(
        da, db, oa, ob, stat, qn, qf, ptn, ptf, vn, ktn, vf, ktf, 512
    )
    send, prompt_back, data_back, dq = lax.optimization_barrier((send, prompt_back, data_back, dq))
    depth = width // groups
    total = jnp.sum(send.astype(F32), axis=0)
    part = total[depth : depth + 1] + total[depth + 1 : depth + 2]
    high = lax.optimization_barrier(part.astype(BF16))
    low = (part - high.astype(F32)).astype(BF16)
    total = jnp.concatenate(
        [total[:depth].astype(BF16), high, low, jnp.zeros((14, total.shape[1]), BF16)], axis=0
    )
    total = jnp.broadcast_to(total[None], (groups,) + total.shape)
    total, dq, dkv = lax.optimization_barrier((total, dq, dkv))
    total = exchange(total, "ep")

    slot_rows = prompt_local + data_local
    cut = 2 * slot_rows
    wq, wkv = w[:, :256], w[:, 256:]

    def rows_grad(part):
        return dot(dq[part], wq, NT) + dot(dkv[part], wkv, NT)

    sib = beside(rows_grad(slice(cut, None)).astype(BF16))
    own = rows_grad(slice(0, cut)) + resid
    grad_q, grad_kv = dot(x_all, dq, TN), dot(x_all, dkv, TN)

    def head_grad(h):
        return jnp.stack(
            [grad_q[:, head_rows(h)], grad_kv[:, head_rows(h)], grad_kv[:, head_rows(2 + h)]]
        )

    far_rows = own[slot_rows:] + sib[slot_rows:].astype(F32)
    far_prompt = across(far_rows[:prompt_local].astype(BF16))
    other_grad = head_grad(1).astype(BF16)
    far_prompt, other_grad = lax.optimization_barrier((far_prompt, other_grad))
    other_grad = across(other_grad)
    far_data = across(far_rows[prompt_local:].astype(BF16))
    near_rows = own[:slot_rows] + sib[:slot_rows].astype(F32)
    near_data = near_rows[prompt_local:].astype(BF16)

    near_prompt = near_rows[:prompt_local] + far_prompt.astype(F32)
    near_prompt = near_prompt.astype(BF16).reshape(groups, prompt_local // groups, width)
    qkv = (head_grad(0) + other_grad.astype(F32)).astype(BF16).reshape(groups, -1, HEAD_DIM)
    total, qkv = lax.optimization_barrier((total, qkv))
    qkv = exchange(qkv, "ep")
    qkv, near_prompt = lax.optimization_barrier((qkv, near_prompt))
    near_prompt = exchange(near_prompt, "ep")
    qkv = jnp.sum(qkv.astype(F32), axis=0).astype(BF16)
    near_prompt = jnp.sum(near_prompt.astype(F32), axis=0).astype(BF16)
    qkv_rows = qkv.shape[0]
    last = gather(jnp.concatenate([qkv, near_prompt.reshape(-1, HEAD_DIM)], axis=0))
    qkv = last[:, :qkv_rows].reshape(3, width, HEAD_DIM).astype(F32)
    prompt_grad = last[:, qkv_rows:].reshape(prompt_local, width).astype(F32)

    which = lax.broadcasted_iota(jnp.int32, (2, 1, 1), 0)

    def by_episode(own, received):
        return jnp.where(which == mine, own[None], received[None])

    sums = total[:, depth : depth + 2, : 8 * width // groups].astype(F32)
    sums = (sums[:, 0] + sums[:, 1]).reshape(8, width)
    total = total[:, :depth].reshape(width, -1).astype(F32)
    bias_grad = lax.dynamic_slice_in_dim(sums[6:8].reshape(-1), t * quarter, quarter)
    return (
        by_episode(data_near, data_back),
        by_episode(prompt_near, prompt_back),
        by_episode(near_data, far_data),
        prompt_grad,
        qkv,
        sums[0],
        total[:, 2 * quarter :].T,
        sums[1],
        sums[2],
        total[:, :quarter],
        bias_grad,
        total[:, quarter : 2 * quarter].T,
        sums[3],
        sums[4],
        sums[5],
    )


def solution(mesh):
    return jax.shard_map(
        on_device,
        mesh=mesh,
        in_specs=(
            P("ep", "tp", None),
            P("tp", None),
            P("ep"),
            P("ep"),
            P(None, None, "tp"),
            P(),
            P("tp", None),
            P(),
            P(),
            P(None, "tp"),
            P("tp"),
            P("tp", None),
            P(),
            P(),
            P(),
            P("ep", "tp", None),
            P("ep", "tp", None),
        ),
        out_specs=(
            P("ep", "tp", None),
            P("ep", "tp", None),
            P("ep", "tp", None),
            P("tp", None),
            P(None, None, "tp"),
            P(),
            P("tp", None),
            P(),
            P(),
            P(None, "tp"),
            P("tp"),
            P("tp", None),
            P(),
            P(),
            P(),
        ),
        check_vma=False,
    )
```

```python
from functools import partial
import math

import jax
import jax.numpy as jnp
from jax import lax
from jax.experimental import pallas as pl
from jax.experimental.pallas import tpu as pltpu
from jax.sharding import PartitionSpec as P

HEAD_DIM = 128
ROWS = 512
BACK_ROWS = 256
SAMPLE = 256
EPS = 1e-05
MASKED = -1e30
LOG2E = math.log2(math.e)
LIMIT = 2.0**60
VMEM = 60 * 1024 * 1024
F32 = jnp.float32
BF16 = jnp.bfloat16
NN = (((1,), (0,)), ((), ()))
NT = (((1,), (1,)), ((), ()))
TN = (((0,), (0,)), ((), ()))


def mm(left, right, dims=NN):
    return lax.dot_general(left, right, dims, preferred_element_type=F32)


def params(**more):
    return pltpu.CompilerParams(vmem_limit_bytes=VMEM, **more)


def cost(flops, nbytes, trans=0):
    return pl.CostEstimate(
        flops=int(flops), bytes_accessed=int(nbytes), transcendentals=int(trans)
    )


def once(shape):
    return pl.BlockSpec(shape, lambda *_: (0,) * len(shape), pipeline_mode=pl.Buffered(1))


def extra_rows(values, count):
    width = values[0].shape[1]
    row = lax.broadcasted_iota(jnp.int32, (count, width), 0)
    out = jnp.zeros((count, width), F32)
    for index, value in enumerate(values):
        out = jnp.where(row == index, value, out)
    return out.astype(BF16)


def three_parts(row):
    high = row.astype(BF16).astype(F32)
    middle = (row - high).astype(BF16).astype(F32)
    return high, middle, row - high - middle


def clamp(i, low, high):
    return jnp.minimum(jnp.maximum(i, low), high)


def project_kernel(sizes, flip, meta, xa_ref, xb_ref, wa_ref, wb_ref, qt_ref, q_ref, k_ref,
                   kx_ref, kt_ref, v_ref, vt_ref, w_ref, wt_ref):
    prompt_local, data_local = sizes
    i = pl.program_id(0)
    per_slot = pl.num_programs(0) // 2
    rows = xa_ref.shape[0]

    @pl.when(i == 0)
    def _():
        for which in range(3):
            for h, source in enumerate((wa_ref, wb_ref)):
                cols = slice(which * 256 + h * HEAD_DIM, which * 256 + (h + 1) * HEAD_DIM)
                w_ref[:, cols] = source[which]
                wt_ref[cols, :] = source[which].T

    x = jnp.where(i < per_slot, xa_ref[...], xb_ref[...])
    slot = jnp.where(i < per_slot, meta[0] ^ flip, meta[0] ^ flip ^ 1)
    row = lax.broadcasted_iota(jnp.int32, (rows, HEAD_DIM), 0)
    lane = lax.broadcasted_iota(jnp.int32, (rows, HEAD_DIM), 1)
    index = (i % per_slot) * rows + row - prompt_local
    attended = jnp.logical_or(index < 0, slot * data_local + index < meta[1])
    bias = jnp.where(attended, F32(0.0), F32(MASKED))
    ones = jnp.where(lane < 4, F32(1.0), F32(0.0))
    kx_ref[...] = jnp.where(lane == 0, bias, ones).astype(BF16)
    factor = F32(LOG2E / math.sqrt(HEAD_DIM))
    z = mm(x, w_ref[...])
    q_ref[...] = (z[:, :256] * factor).astype(BF16)
    k_ref[...] = z[:, 256:512].astype(BF16)
    v_ref[...] = z[:, 512:].astype(BF16)
    zt = mm(wt_ref[...], x, NT)
    qt_ref[...] = (zt[:256] * factor).astype(BF16)
    kt_ref[...] = zt[256:512].astype(BF16)
    vt_ref[...] = zt[512:].astype(BF16)


def project(meta, xa, xb, wa, wb, sizes, flip):
    rows, width = xa.shape
    step = 512
    n = rows // step
    flat = jax.ShapeDtypeStruct((2 * rows, 256), BF16)
    tall = jax.ShapeDtypeStruct((256, 2 * rows), BF16)
    row = pl.BlockSpec((step, 256), lambda i, meta: (i, 0))
    col = pl.BlockSpec((256, step), lambda i, meta: (0, i))
    return pl.pallas_call(
        partial(project_kernel, sizes, flip),
        out_shape=[
            tall,
            flat,
            flat,
            jax.ShapeDtypeStruct((2 * rows, HEAD_DIM), BF16),
            tall,
            flat,
            tall,
            jax.ShapeDtypeStruct((width, 768), BF16),
        ],
        grid_spec=pltpu.PrefetchScalarGridSpec(
            num_scalar_prefetch=1,
            grid=(2 * n,),
            in_specs=[
                pl.BlockSpec((step, width), lambda i, meta: (jnp.minimum(i, n - 1), 0)),
                pl.BlockSpec((step, width), lambda i, meta: (jnp.maximum(i - n, 0), 0)),
                once(wa.shape),
                once(wb.shape),
            ],
            out_specs=[
                col,
                row,
                row,
                pl.BlockSpec((step, HEAD_DIM), lambda i, meta: (i, 0)),
                col,
                row,
                col,
                once((width, 768)),
            ],
            scratch_shapes=[pltpu.VMEM((768, width), BF16)],
        ),
        compiler_params=params(),
        cost_estimate=cost(4 * 2 * rows * width * 768, 2 * rows * width * 8),
        name="project",
    )(meta, xa, xb, wa, wb)


def head_rows(h):
    return slice(h * HEAD_DIM, (h + 1) * HEAD_DIM)


def with_shift(qt, top):
    high, middle, low = three_parts(top)
    extra = extra_rows([jnp.ones_like(top), -high, -middle, -low], HEAD_DIM)
    return jnp.concatenate([qt, extra], axis=0)


def half_scores(chunk, h, qa, start, k_ref, kx_ref):
    here = pl.ds(start, chunk)
    keys = jnp.concatenate([k_ref[here, head_rows(h)], kx_ref[here, :]], axis=1)
    return mm(keys, qa)


def half_part(h, start, scores, vt_ref, pt_ref):
    chunk = scores.shape[0]
    weight = jnp.exp2(scores)
    total = jnp.sum(weight.reshape(chunk // 8, 8, weight.shape[1]), axis=0)
    low = weight.astype(BF16)
    pt_ref[0, h, pl.ds(start, chunk), :] = low
    return total, mm(vt_ref[head_rows(h), pl.ds(start, chunk)], low)


def stale_shift(h, qt, k_ref):
    top = jnp.max(mm(k_ref[:SAMPLE, head_rows(h)], qt), axis=0, keepdims=True)
    return top, with_shift(qt, top)


def fast_states(chunk, shifts, keys, pts):
    tiles = [
        (h, j, start)
        for h in range(2)
        for j in range(len(keys))
        for start in range(0, keys[0][0].shape[0], chunk)
    ]

    def scores(tile):
        h, j, start = tile
        return half_scores(chunk, h, shifts[h][j][1], start, keys[j][0], keys[j][1])

    sums = {}
    ahead = scores(tiles[0])
    for place, (h, j, start) in enumerate(tiles):
        now = ahead
        if place + 1 < len(tiles):
            ahead = scores(tiles[place + 1])
        total, product = half_part(h, start, now, keys[j][2], pts[j])
        if (h, j) in sums:
            total, product = sums[h, j][0] + total, sums[h, j][1] + product
        sums[h, j] = total, product
    return [
        [
            (shifts[h][j][0], jnp.sum(sums[h, j][0], axis=0, keepdims=True), sums[h, j][1])
            for j in range(len(keys))
        ]
        for h in range(2)
    ]


def half_attend_exact(chunk, h, shift, k_ref, kx_ref, vt_ref, pt_ref):
    qt = shift[1][:HEAD_DIM]
    width = qt.shape[1]
    count = k_ref.shape[0] // chunk
    qa = with_shift(qt, jnp.zeros((1, width), F32))

    def find(j, top):
        found = half_scores(chunk, h, qa, pl.multiple_of(j * chunk, chunk), k_ref, kx_ref)
        return jnp.maximum(top, jnp.max(found, axis=0, keepdims=True))

    top = lax.fori_loop(0, count, find, jnp.full((1, width), MASKED, F32))
    qa = with_shift(qt, top)

    def add(j, state):
        start = pl.multiple_of(j * chunk, chunk)
        found = half_scores(chunk, h, qa, start, k_ref, kx_ref)
        more, product = half_part(h, start, found, vt_ref, pt_ref)
        return state[0] + more, state[1] + product

    total, acc = lax.fori_loop(
        0, count, add, (jnp.zeros((8, width), F32), jnp.zeros((HEAD_DIM, width), F32))
    )
    return top, jnp.sum(total, axis=0, keepdims=True), acc


def merge(states):
    top = states[0][0]
    for state in states[1:]:
        top = jnp.maximum(top, state[0])
    scales = [jnp.exp2(state[0] - top) for state in states]
    total = sum(state[1] * scale for state, scale in zip(states, scales))
    factors = [scale / total for scale in scales]
    return factors, sum(state[2] * factor for state, factor in zip(states, factors))


def redo(states, shifts, keys, pts):
    return [
        [half_attend_exact(256, h, shifts[h][j], *keys[j], pts[j]) for j in range(len(keys))]
        for h in range(2)
    ]


def run_halves(chunk, qt_ref, keys, pts, finish):
    shifts = [
        [stale_shift(h, qt_ref[head_rows(h), :], key_refs[0]) for key_refs in keys]
        for h in range(2)
    ]
    states = fast_states(chunk, shifts, keys, pts)
    worst = None
    for state in states[0] + states[1]:
        worst = state[1] if worst is None else jnp.maximum(worst, state[1])
    finish(states)

    @pl.when(jnp.logical_not(jnp.max(worst) <= LIMIT))
    def _():
        finish(redo(states, shifts, keys, pts))


def attend_first_kernel(chunk, qt_ref, k_ref, kx_ref, vt_ref, pt_ref, state_ref, acc_ref):
    def finish(states):
        for h in range(2):
            top, total, acc = states[h][0]
            state_ref[0, h : h + 1, :] = top
            state_ref[0, 2 + h : 3 + h, :] = total
            acc_ref[head_rows(h), :] = acc

    run_halves(chunk, qt_ref, [(k_ref, kx_ref, vt_ref)], [pt_ref], finish)


def attend_first(qt, key, chunk):
    rows = qt.shape[1]
    n = rows // ROWS
    col = pl.BlockSpec((256, ROWS), lambda i: (0, i))
    pairs = 2 * rows * rows
    return pl.pallas_call(
        partial(attend_first_kernel, chunk),
        out_shape=[
            jax.ShapeDtypeStruct((2 * n, 2, rows, ROWS), BF16),
            jax.ShapeDtypeStruct((n, 8, ROWS), F32),
            jax.ShapeDtypeStruct((256, rows), F32),
        ],
        grid=(n,),
        in_specs=[col] + [once(item.shape) for item in key],
        out_specs=[
            pl.BlockSpec((1, 2, rows, ROWS), lambda i: (i, 0, 0, 0)),
            pl.BlockSpec((1, 8, ROWS), lambda i: (i, 0, 0)),
            col,
        ],
        compiler_params=params(),
        cost_estimate=cost(4 * pairs * HEAD_DIM * 2, 2 * pairs, pairs),
        name="attend_near",
    )(qt, *key)


def attend_second_kernel(
    chunk, qtn_ref, qtf_ref, kn, kxn, vtn, kf, kxf, vtf, old_ref, old_acc_ref, _,
    ptn_ref, ptf_ref, mine_ref, sib_ref, stat_ref,
):
    i = pl.program_id(0)
    n = pl.num_programs(0) // 2
    near, far = (kn, kxn, vtn), (kf, kxf, vtf)

    def store(h, states):
        factors, result = merge(states)
        stat_ref[0, h : h + 1, :] = factors[0]
        stat_ref[0, 2 + h : 3 + h, :] = factors[1]
        low = result.T.astype(BF16)
        first = i % n < n // 2

        @pl.when(first)
        def _():
            mine_ref[:, head_rows(h)] = low

        @pl.when(jnp.logical_not(first))
        def _():
            sib_ref[:, head_rows(h)] = low

    @pl.when(i < n)
    def _():
        def finish(states):
            for h in range(2):
                old = (old_ref[0, h : h + 1, :], old_ref[0, 2 + h : 3 + h, :],
                       old_acc_ref[head_rows(h), :])
                store(h, [old, states[h][0]])

        run_halves(chunk, qtn_ref, [far], [ptf_ref], finish)

    @pl.when(i >= n)
    def _():
        def finish(states):
            for h in range(2):
                store(h, states[h])

        run_halves(chunk, qtf_ref, [near, far], [ptn_ref, ptf_ref], finish)


def mine_block(i, n):
    half = n // 2
    return (i // n) * half + jnp.minimum(i % n, half - 1)


def sib_block(i, n):
    half = n // 2
    return jnp.maximum((i // n) * half + i % n - half, jnp.maximum((i // n) * half - 1, 0))


def attend_second(qtn, qtf, near, far, pt, state, acc, chunk):
    rows = qtn.shape[1]
    n = rows // ROWS
    near_col = pl.BlockSpec((256, ROWS), lambda i: (0, jnp.minimum(i, n - 1)))
    pairs = 6 * rows * rows
    return pl.pallas_call(
        partial(attend_second_kernel, chunk),
        out_shape=[
            jax.ShapeDtypeStruct(pt.shape, BF16),
            jax.ShapeDtypeStruct(pt.shape, BF16),
            jax.ShapeDtypeStruct((rows, 256), BF16),
            jax.ShapeDtypeStruct((rows, 256), BF16),
            jax.ShapeDtypeStruct((2 * n, 8, ROWS), F32),
        ],
        grid=(2 * n,),
        in_specs=[near_col, pl.BlockSpec((256, ROWS), lambda i: (0, jnp.maximum(i - n, 0)))]
        + [once(item.shape) for item in near + far]
        + [
            pl.BlockSpec((1, 8, ROWS), lambda i: (jnp.minimum(i, n - 1), 0, 0)),
            near_col,
            pl.BlockSpec(memory_space=pl.ANY),
        ],
        out_specs=[
            pl.BlockSpec((1, 2, rows, ROWS), lambda i: (jnp.maximum(i, n), 0, 0, 0)),
            pl.BlockSpec((1, 2, rows, ROWS), lambda i: (i, 0, 0, 0)),
            pl.BlockSpec((ROWS, 256), lambda i: (mine_block(i, n), 0)),
            pl.BlockSpec((ROWS, 256), lambda i: (sib_block(i, n), 0)),
            pl.BlockSpec((1, 8, ROWS), lambda i: (i, 0, 0)),
        ],
        input_output_aliases={10: 0},
        compiler_params=params(),
        cost_estimate=cost(4 * pairs * HEAD_DIM * 2, 2 * pairs, pairs),
        name="attend_rest",
    )(qtn, qtf, *near, *far, state, acc, pt)


def back_weights(do, o, factors):
    dot_t = do.astype(F32).T
    delta = jnp.sum(dot_t * o.astype(F32).T, axis=0, keepdims=True)
    found = []
    for factor in factors:
        scaled = dot_t * factor
        high, middle, low = three_parts(delta * factor)
        extra = extra_rows([-high, -middle, -low], HEAD_DIM)
        found.append(
            (jnp.concatenate([scaled.astype(BF16), extra], axis=0), scaled.T.astype(BF16))
        )
    return found


def back_half(chunk, h, grads, q_rows, pt_ref, v_ref, kt_ref, key_acc, value_acc):
    ones = jnp.where(
        lax.broadcasted_iota(jnp.int32, (chunk, HEAD_DIM), 1) < 3, F32(1.0), F32(0.0)
    ).astype(BF16)
    result = jnp.zeros((HEAD_DIM, q_rows.shape[0]), F32)
    for start in range(0, v_ref.shape[0], chunk):
        here = slice(start, start + chunk)
        prob = pt_ref[0, h, here, :]
        values = jnp.concatenate([v_ref[here, head_rows(h)], ones], axis=1)
        score = (prob.astype(F32) * mm(values, grads[0])).astype(BF16)
        value_acc[h, here, :] += mm(prob, grads[1])
        key_acc[h, here, :] += mm(score, q_rows)
        result = result + mm(kt_ref[head_rows(h), here], score)
    return result


def attend_back_kernel(
    chunk, da_ref, db_ref, oa_ref, ob_ref, stat_ref, qn_ref, qf_ref, ptn_ref, ptf_ref,
    vn, ktn, vf, ktf, dq_ref, dkv_ref, key_n, value_n, key_f, value_f,
):
    i = pl.program_id(0)
    n = pl.num_programs(0) // 2

    @pl.when(i == 0)
    def _():
        for ref in (key_n, value_n, key_f, value_f):
            ref[...] = jnp.zeros_like(ref)

    first = i % n < n // 2
    do = jnp.where(first, da_ref[...], db_ref[...])
    o = jnp.where(first, oa_ref[...], ob_ref[...])
    q = jnp.where(i < n, qn_ref[...], qf_ref[...])
    for h in range(2):
        cols = head_rows(h)
        near, far = back_weights(
            do[:, cols], o[:, cols], [stat_ref[0, h : h + 1, :], stat_ref[0, 2 + h : 3 + h, :]]
        )
        grad = back_half(chunk, h, near, q[:, cols], ptn_ref, vn, ktn, key_n, value_n)
        grad += back_half(chunk, h, far, q[:, cols], ptf_ref, vf, ktf, key_f, value_f)
        dq_ref[:, cols] = (grad * F32(1.0 / math.sqrt(HEAD_DIM))).T.astype(BF16)

    @pl.when(i == 2 * n - 1)
    def _():
        seq = vn.shape[0]
        for half, (keys, values) in enumerate(((key_n, value_n), (key_f, value_f))):
            for owner in range(2):
                source = slice(owner * seq // 2, (owner + 1) * seq // 2)
                begin = owner * seq + half * seq // 2
                rows = slice(begin, begin + seq // 2)
                for h in range(2):
                    dkv_ref[rows, head_rows(h)] = (keys[h, source] * F32(1.0 / LOG2E)).astype(BF16)
                    dkv_ref[rows, head_rows(2 + h)] = values[h, source].astype(BF16)


def attend_back(da, db, oa, ob, stat, qn, qf, ptn, ptf, vn, ktn, vf, ktf, chunk):
    rows = qn.shape[0]
    step = BACK_ROWS
    n = rows // step
    per = ROWS // step
    row = lambda f: pl.BlockSpec((step, 256), lambda i: (f(i), 0))
    tile = pl.BlockSpec((1, 2, rows, step), lambda i: (i // per, 0, 0, i % per))
    flat = jax.ShapeDtypeStruct((2 * rows, 256), BF16)
    wide = jax.ShapeDtypeStruct((2 * rows, 512), BF16)
    acc = pltpu.VMEM((2, rows, HEAD_DIM), F32)

    def own_first(i):
        return jnp.where(i % n < n // 2, 0, n // 2) + (i // n) * (n // 2) + i % n
    pairs = 8 * rows * rows
    return pl.pallas_call(
        partial(attend_back_kernel, chunk),
        out_shape=[flat, wide],
        grid=(2 * n,),
        in_specs=[
            row(lambda i: mine_block(i, n)),
            row(lambda i: sib_block(i, n)),
            row(lambda i: mine_block(i, n)),
            row(lambda i: sib_block(i, n)),
            pl.BlockSpec((1, 8, step), lambda i: (i // per, 0, i % per)),
            row(lambda i: jnp.minimum(i, n - 1)),
            row(lambda i: jnp.maximum(i - n, 0)),
            tile,
            tile,
        ]
        + [once(item.shape) for item in (vn, ktn, vf, ktf)],
        out_specs=[row(own_first), once(wide.shape)],
        scratch_shapes=[acc, acc, acc, acc],
        compiler_params=params(),
        cost_estimate=cost(8 * pairs * HEAD_DIM, 2 * pairs),
        name="attend_back",
    )(da, db, oa, ob, stat, qn, qf, ptn, ptf, vn, ktn, vf, ktf)


def mean(values):
    return jnp.mean(values, axis=-1, keepdims=True)


def norm(values):
    centered = values - mean(values)
    inverse = lax.rsqrt(mean(centered * centered) + EPS)
    return centered * inverse, inverse


def norm_back(incoming, normed, inverse, gain):
    scaled = incoming * gain
    return inverse * (scaled - mean(scaled) - normed * mean(scaled * normed))


def gelu_parts(v):
    bell = jnp.exp2(v * v * F32(-0.5 * LOG2E))
    base = 1.0 + F32(0.3275911 / math.sqrt(2.0)) * jnp.abs(v)
    t = pl.reciprocal(base, approx=True)
    t = t * (2.0 - base * t)
    series = t * (
        F32(0.5 * 0.254829592)
        + t
        * (
            F32(0.5 * -0.284496736)
            + t
            * (
                F32(0.5 * 1.421413741)
                + t * (F32(0.5 * -1.453152027) + t * F32(0.5 * 1.061405429))
            )
        )
    )
    tail = series * bell
    return bell * F32(1.0 / math.sqrt(2.0 * math.pi)), jnp.where(v >= 0, 1.0 - tail, tail)


def fold_rows(values):
    return jnp.sum(values.reshape(values.shape[0] // 8, 8, values.shape[1]), axis=0)


def rows_kernel(
    sizes, meta, xa_ref, xb_ref, oa_ref, ob_ref, cot_a, cot_b, p0, p1, p2, p3,
    u0, u1, u2, u3, vec_ref,
    prompt_near, data_near, prompt_far, data_far, resid_ref, da_ref, db_ref, send_ref,
    sums_ref, wo_ref, up_ref, down_ref, bias_ref, grad_acc, vec_acc, bias_acc,
):
    prompt_local, data_local = sizes
    i = pl.program_id(0)
    half = pl.num_programs(0) // 2
    here = i < half
    rows = xa_ref.shape[0]
    quarter = u0.shape[1]

    @pl.when(i == 0)
    def _():
        for j, (pack, up_part) in enumerate(((p0, u0), (p1, u1), (p2, u2), (p3, u3))):
            cols = slice(j * quarter, (j + 1) * quarter)
            wo_ref[head_rows(j), :] = pack[:HEAD_DIM, :]
            down_ref[cols, :] = pack[HEAD_DIM : HEAD_DIM + quarter, :]
            bias_ref[0:1, cols] = pack[
                HEAD_DIM + quarter : HEAD_DIM + quarter + 16, :quarter
            ].astype(F32)[0:1, :]
            up_ref[:, cols] = up_part[...]
        grad_acc[...] = jnp.zeros_like(grad_acc)
        vec_acc[...] = jnp.zeros_like(vec_acc)
        bias_acc[...] = jnp.zeros_like(bias_acc)

    slot = jnp.where(here, meta[0], meta[0] ^ 2)
    index = (i % half) * rows + lax.broadcasted_iota(jnp.int32, (rows, 1), 0) - prompt_local
    live = jnp.logical_or(index < 0, slot * data_local + index < meta[2])

    out_bias, attn_gain, attn_shift = vec_ref[0:1, :], vec_ref[1:2, :], vec_ref[2:3, :]
    down_bias, mlp_gain, mlp_shift = vec_ref[3:4, :], vec_ref[4:5, :], vec_ref[5:6, :]
    x = jnp.where(here, xa_ref[...], xb_ref[...])
    attended = jnp.concatenate([oa_ref[...], ob_ref[...]], axis=1)
    normed_one, inverse_one = norm(x.astype(F32) + (mm(attended, wo_ref[...]) + out_bias))
    hidden = normed_one * attn_gain + attn_shift
    hidden_low = hidden.astype(BF16)
    pre = mm(hidden_low, up_ref[...]) + bias_ref[0:1, :]
    density, share = gelu_parts(pre)
    activated = (pre * share).astype(BF16)
    slope = share + pre * density
    mixed = hidden + (mm(activated, down_ref[...]) + down_bias)
    normed_two, inverse_two = norm(mixed)
    output = (normed_two * mlp_gain + mlp_shift).astype(BF16)
    for j in range(2):
        split = max(0, min(rows, prompt_local - j * rows))
        for place, (prompt_ref, data_ref) in enumerate(
            ((prompt_near, data_near), (prompt_far, data_far))
        ):

            @pl.when(i == place * half + j)
            def _():
                if split:
                    prompt_ref[j * rows : j * rows + split, :] = output[:split]
                if split < rows:
                    begin = j * rows + split - prompt_local
                    data_ref[begin : begin + rows - split, :] = output[split:]

    cotangent = jnp.where(live, jnp.where(here, cot_a[...], cot_b[...]).astype(F32), 0.0)
    mixed_grad = norm_back(cotangent, normed_two, inverse_two, mlp_gain)
    mixed_low = mixed_grad.astype(BF16)
    pre_grad = (mm(mixed_low, down_ref[...], NT) * slope).astype(BF16)
    hidden_grad = mixed_grad + mm(pre_grad, up_ref[...], NT)
    resid_grad = norm_back(hidden_grad, normed_one, inverse_one, attn_gain)
    resid_ref[...] = resid_grad
    resid_low = resid_grad.astype(BF16)
    attended_grad = mm(resid_low, wo_ref[...], NT).astype(BF16)
    da_ref[...] = attended_grad[:, :256]
    db_ref[...] = attended_grad[:, 256:]

    up_grad = mm(hidden_low, pre_grad, TN)
    down_grad = mm(mixed_low, activated, TN)
    out_grad = mm(resid_low, attended, TN)
    for j in range(4):
        cols = slice(j * quarter, (j + 1) * quarter)
        grad_acc[j, :, :quarter] += up_grad[:, cols]
        grad_acc[j, :, quarter : 2 * quarter] += down_grad[:, cols]
        grad_acc[j, :, 2 * quarter :] += out_grad[:, head_rows(j)]
    bias_acc[...] += fold_rows(pre_grad.astype(F32))
    for place, value in enumerate(
        (
            resid_grad,
            hidden_grad * normed_one,
            hidden_grad,
            mixed_grad,
            cotangent * normed_two,
            cotangent,
        )
    ):
        vec_acc[place] += fold_rows(value)

    @pl.when(i == pl.num_programs(0) - 1)
    def _():
        for place in range(6):
            sums_ref[place : place + 1, :] = jnp.sum(vec_acc[place], axis=0, keepdims=True)
        bias_grad = jnp.sum(bias_acc[...], axis=0, keepdims=True)
        per_row = bias_grad.shape[1] // 2 // quarter
        for g in range(4):
            found = jnp.zeros((1, quarter), F32)
            for j, flip in enumerate((0, 2, 1, 3)):
                piece = bias_grad[:, j * quarter : (j + 1) * quarter]
                found = jnp.where((meta[0] ^ flip) == g, piece, found)
            row, col = 6 + g // per_row, (g % per_row) * quarter
            sums_ref[row : row + 1, col : col + quarter] = found
        depth = send_ref.shape[1] - 16
        groups = send_ref.shape[0] // 4
        width, wide = sums_ref.shape[1], send_ref.shape[2]
        per = sums_ref.shape[0] * width // groups
        for g in range(groups):
            row, col = g * per // width, g * per % width
            part = jnp.pad(sums_ref[row : row + 1, col : col + per], ((0, 0), (0, wide - per)))
            high, low, _ = three_parts(part)
            extra = extra_rows([high, low], 16)
            for j, flip in enumerate((0, 2, 1, 3)):
                target = g * 4 + (meta[0] ^ flip)
                send_ref[target, :depth] = grad_acc[j, g * depth : (g + 1) * depth].astype(BF16)
                send_ref[target, depth:] = extra


def row_work(meta, xa, xb, oa, ob, cot, packs, ups, vec, sizes, groups):
    rows, width = xa.shape
    prompt_local, data_local = sizes
    step = 512
    n = rows // step
    quarter = ups[0].shape[1]
    hidden = 4 * quarter
    wide = 2 * quarter + HEAD_DIM
    send = (4 * groups, width // groups + 16, wide)
    near = pl.BlockSpec((step, width), lambda i, meta: (jnp.minimum(i, n - 1), 0))
    far = pl.BlockSpec((step, width), lambda i, meta: (jnp.maximum(i - n, 0), 0))
    row = lambda cols: pl.BlockSpec((step, cols), lambda i, meta: (i, 0))
    return pl.pallas_call(
        partial(rows_kernel, sizes),
        out_shape=[
            jax.ShapeDtypeStruct((prompt_local, width), BF16),
            jax.ShapeDtypeStruct((data_local, width), BF16),
            jax.ShapeDtypeStruct((prompt_local, width), BF16),
            jax.ShapeDtypeStruct((data_local, width), BF16),
            jax.ShapeDtypeStruct((2 * rows, width), F32),
            jax.ShapeDtypeStruct((2 * rows, 256), BF16),
            jax.ShapeDtypeStruct((2 * rows, 256), BF16),
            jax.ShapeDtypeStruct(send, BF16),
        ],
        grid_spec=pltpu.PrefetchScalarGridSpec(
            num_scalar_prefetch=1,
            grid=(2 * n,),
            in_specs=[near, far, row(256), row(256), near, far]
            + [once(item.shape) for item in packs + ups]
            + [once(vec.shape)],
            out_specs=[
                once((prompt_local, width)),
                once((data_local, width)),
                once((prompt_local, width)),
                once((data_local, width)),
                row(width),
                row(256),
                row(256),
                once(send),
            ],
            scratch_shapes=[
                pltpu.VMEM((8, width), F32),
                pltpu.VMEM((4 * HEAD_DIM, width), BF16),
                pltpu.VMEM((width, hidden), BF16),
                pltpu.VMEM((hidden, width), BF16),
                pltpu.VMEM((8, hidden), F32),
                pltpu.VMEM((4, width, wide), F32),
                pltpu.VMEM((6, 8, width), F32),
                pltpu.VMEM((8, hidden), F32),
            ],
        ),
        compiler_params=params(),
        cost_estimate=cost(
            3 * 2 * 2 * rows * width * (width + 2 * hidden), 24 * rows * width, 4 * rows * hidden
        ),
        name="row_work",
    )(meta, xa, xb, oa, ob, *cot, *packs, *ups, vec)


def on_device(
    data_rows,
    prompt_rows,
    context_rows,
    test_rows,
    qkv_weight,
    out_bias,
    out_weight,
    attn_gain,
    attn_shift,
    up_weight,
    up_bias,
    down_weight,
    down_bias,
    mlp_gain,
    mlp_shift,
    data_cotangent,
    prompt_cotangent,
):
    data_local = data_rows.shape[1]
    prompt_local = prompt_rows.shape[0]
    width = prompt_rows.shape[1]
    quarter = up_weight.shape[1]
    sizes = (prompt_local, data_local)
    groups = lax.axis_size("ep")
    t = lax.axis_index("tp")
    mine = t >> 1
    other = 1 - mine

    def across(value):
        return lax.ppermute(value, "tp", [(i, i ^ 2) for i in range(4)])

    def beside(value):
        return lax.ppermute(value, "tp", [(i, i ^ 1) for i in range(4)])

    def pick(values, which):
        return lax.dynamic_index_in_dim(values, which, axis=0, keepdims=False)

    def stack(prompt_part, data_part):
        return jnp.concatenate([prompt_part, data_part], axis=0)

    w_far = across(qkv_weight)
    x_far = across(stack(prompt_rows, pick(data_rows, other)))
    x = stack(prompt_rows, pick(data_rows, mine))
    x_sib = beside(x)
    context = pick(context_rows, mine)
    live = context + pick(test_rows, mine)
    meta = jnp.stack([t, context, live]).astype(jnp.int32)

    qtn, qn, kn, kxn, ktn, vn, vtn, w = project(meta, x, x_sib, qkv_weight, w_far, sizes, 0)
    ptn, state, state_acc = attend_first(qtn, (kn, kxn, vtn), 512)

    bias_rows = jnp.pad(up_bias[None], ((0, 15), (0, width - quarter)))
    pack = jnp.concatenate([out_weight, down_weight, bias_rows], axis=0)
    x_far, state, pack, up_weight, x_late, x_sib_late = lax.optimization_barrier(
        (x_far, state, pack, up_weight, x, x_sib)
    )
    x_far_sib = beside(x_far)
    pack_far, up_far = across(pack), across(up_weight)
    cot_far = stack(pick(prompt_cotangent, other), pick(data_cotangent, other))
    x_far_sib, cot_far = lax.optimization_barrier((x_far_sib, cot_far))
    cot_far = across(cot_far)
    qtf, qf, kf, kxf, ktf, vf, vtf, _ = project(meta, x_far, x_far_sib, qkv_weight, w_far, sizes, 2)
    x_all = jnp.concatenate([x_late, x_far, x_sib_late, x_far_sib], axis=0)
    pack_far, up_far, x_all, qtf = lax.optimization_barrier((pack_far, up_far, x_all, qtf))
    ptn, ptf, oa, ob, stat = attend_second(
        qtn, qtf, (kn, kxn, vtn), (kf, kxf, vtf), ptn, state, state_acc, 512
    )

    ob_send, cot_far = lax.optimization_barrier((ob, cot_far))
    cot = stack(pick(prompt_cotangent, mine), pick(data_cotangent, mine))
    packs = [pack, pack_far, beside(pack), beside(pack_far)]
    ups = [up_weight, up_far, beside(up_weight), beside(up_far)]
    vec = jnp.stack(
        [out_bias, attn_gain, attn_shift, down_bias, mlp_gain, mlp_shift, mlp_shift, mlp_shift]
    ).astype(F32)
    (prompt_near, data_near, prompt_far, data_far, resid, da, db, send) = row_work(
        meta, x, x_far, oa, beside(ob_send), (cot, cot_far), packs, ups, vec, sizes, groups
    )

    def dot(left, right, dims):
        return lax.dot_general(left, right, dims, preferred_element_type=F32)

    def exchange(parts, axes):
        return lax.all_to_all(parts, axes, 0, 0, tiled=True)

    def gather(part):
        return exchange(jnp.broadcast_to(part[None], (groups,) + part.shape), "ep")

    db = beside(db)
    send = exchange(send, ("ep", "tp"))
    prompt_back, data_back = across(prompt_far), across(data_far)

    dq, dkv = attend_back(
        da, db, oa, ob, stat, qn, qf, ptn, ptf, vn, ktn, vf, ktf, 512
    )
    send, prompt_back, data_back, dq = lax.optimization_barrier((send, prompt_back, data_back, dq))
    depth = width // groups
    total = jnp.sum(send.astype(F32), axis=0)
    part = total[depth : depth + 1] + total[depth + 1 : depth + 2]
    high = lax.optimization_barrier(part.astype(BF16))
    low = (part - high.astype(F32)).astype(BF16)
    total = jnp.concatenate(
        [total[:depth].astype(BF16), high, low, jnp.zeros((14, total.shape[1]), BF16)], axis=0
    )
    total = jnp.broadcast_to(total[None], (groups,) + total.shape)
    total, dq, dkv = lax.optimization_barrier((total, dq, dkv))
    total = exchange(total, "ep")

    slot_rows = prompt_local + data_local
    cut = 2 * slot_rows
    wq, wkv = w[:, :256], w[:, 256:]

    def rows_grad(part):
        return dot(dq[part], wq, NT) + dot(dkv[part], wkv, NT)

    grad_q, grad_kv = dot(x_all, dq, TN), dot(x_all, dkv, TN)

    def head_grad(h):
        return jnp.stack(
            [grad_q[:, head_rows(h)], grad_kv[:, head_rows(h)], grad_kv[:, head_rows(2 + h)]]
        )

    other_grad, dq, dkv = lax.optimization_barrier((head_grad(1).astype(BF16), dq, dkv))
    other_grad = across(other_grad)
    sib = rows_grad(slice(cut, None)).astype(BF16)
    sib, dq, dkv = lax.optimization_barrier((sib, dq, dkv))
    sib = beside(sib)
    own = rows_grad(slice(0, cut)) + resid
    other_grad, own = lax.optimization_barrier((other_grad, own))
    far_rows = (own[slot_rows:] + sib[slot_rows:].astype(F32)).astype(BF16)
    far_prompt = across(far_rows[:prompt_local])
    far_data = across(far_rows[prompt_local:])
    near_rows = own[:slot_rows] + sib[:slot_rows].astype(F32)
    near_data = near_rows[prompt_local:].astype(BF16)

    columns = width // HEAD_DIM
    prompt = near_rows[:prompt_local] + far_prompt.astype(F32)
    prompt = prompt.astype(BF16).reshape(groups, prompt_local // groups, width)
    prompt = jnp.concatenate([prompt[:, :, head_rows(j)] for j in range(columns)], axis=1)
    qkv = (head_grad(0) + other_grad.astype(F32)).astype(BF16).reshape(groups, -1, HEAD_DIM)
    qkv_rows = qkv.shape[1]
    last = jnp.concatenate([qkv, prompt], axis=1)
    total, last = lax.optimization_barrier((total, last))
    last = gather(jnp.sum(exchange(last, "ep").astype(F32), axis=0).astype(BF16))
    qkv = last[:, :qkv_rows].reshape(3, width, HEAD_DIM).astype(F32)
    prompt = last[:, qkv_rows:].reshape(groups, columns, prompt_local // groups, HEAD_DIM)
    prompt_grad = jnp.concatenate([prompt[:, j] for j in range(columns)], axis=2)
    prompt_grad = prompt_grad.reshape(prompt_local, width).astype(F32)

    which = lax.broadcasted_iota(jnp.int32, (2, 1, 1), 0)

    def by_episode(own, received):
        return jnp.where(which == mine, own[None], received[None])

    sums = total[:, depth : depth + 2, : 8 * width // groups].astype(F32)
    sums = (sums[:, 0] + sums[:, 1]).reshape(8, width)
    total = total[:, :depth].reshape(width, -1).astype(F32)
    bias_grad = lax.dynamic_slice_in_dim(sums[6:8].reshape(-1), t * quarter, quarter)
    return (
        by_episode(data_near, data_back),
        by_episode(prompt_near, prompt_back),
        by_episode(near_data, far_data),
        prompt_grad,
        qkv,
        sums[0],
        total[:, 2 * quarter :].T,
        sums[1],
        sums[2],
        total[:, :quarter],
        bias_grad,
        total[:, quarter : 2 * quarter].T,
        sums[3],
        sums[4],
        sums[5],
    )


def solution(mesh):
    return jax.shard_map(
        on_device,
        mesh=mesh,
        in_specs=(
            P("ep", "tp", None),
            P("tp", None),
            P("ep"),
            P("ep"),
            P(None, None, "tp"),
            P(),
            P("tp", None),
            P(),
            P(),
            P(None, "tp"),
            P("tp"),
            P("tp", None),
            P(),
            P(),
            P(),
            P("ep", "tp", None),
            P("ep", "tp", None),
        ),
        out_specs=(
            P("ep", "tp", None),
            P("ep", "tp", None),
            P("ep", "tp", None),
            P("tp", None),
            P(None, None, "tp"),
            P(),
            P("tp", None),
            P(),
            P(),
            P(None, "tp"),
            P("tp"),
            P("tp", None),
            P(),
            P(),
            P(),
        ),
        check_vma=False,
    )
```

```python
from functools import partial
import math

import jax
import jax.numpy as jnp
from jax import lax
from jax.experimental import pallas as pl
from jax.experimental.pallas import tpu as pltpu
from jax.sharding import PartitionSpec as P

HEAD_DIM = 128
ROWS = 512
BACK_ROWS = 256
SAMPLE = 256
EPS = 1e-05
MASKED = -1e30
LOG2E = math.log2(math.e)
LIMIT = 2.0**60
VMEM = 60 * 1024 * 1024
F32 = jnp.float32
BF16 = jnp.bfloat16
NN = (((1,), (0,)), ((), ()))
NT = (((1,), (1,)), ((), ()))
TN = (((0,), (0,)), ((), ()))


def mm(left, right, dims=NN):
    return lax.dot_general(left, right, dims, preferred_element_type=F32)


def params(**more):
    return pltpu.CompilerParams(vmem_limit_bytes=VMEM, **more)


def cost(flops, nbytes, trans=0):
    return pl.CostEstimate(
        flops=int(flops), bytes_accessed=int(nbytes), transcendentals=int(trans)
    )


def once(shape):
    return pl.BlockSpec(shape, lambda *_: (0,) * len(shape), pipeline_mode=pl.Buffered(1))


def extra_rows(values, count):
    width = values[0].shape[1]
    row = lax.broadcasted_iota(jnp.int32, (count, width), 0)
    out = jnp.zeros((count, width), F32)
    for index, value in enumerate(values):
        out = jnp.where(row == index, value, out)
    return out.astype(BF16)


def three_parts(row):
    high = row.astype(BF16).astype(F32)
    middle = (row - high).astype(BF16).astype(F32)
    return high, middle, row - high - middle


def clamp(i, low, high):
    return jnp.minimum(jnp.maximum(i, low), high)


def project_kernel(sizes, flip, meta, xa_ref, xb_ref, wa_ref, wb_ref, *refs):
    refs = refs[1:] if flip else refs
    qt_ref, q_ref, k_ref, kx_ref, kt_ref, v_ref, vt_ref, w_ref, all_ref, wt_ref = refs
    prompt_local, data_local = sizes
    i = pl.program_id(0)
    per_slot = pl.num_programs(0) // 2
    rows = xa_ref.shape[0]

    @pl.when(i == 0)
    def _():
        for which in range(3):
            for h, source in enumerate((wa_ref, wb_ref)):
                cols = slice(which * 256 + h * HEAD_DIM, which * 256 + (h + 1) * HEAD_DIM)
                w_ref[:, cols] = source[which]
                wt_ref[cols, :] = source[which].T

    x = jnp.where(i < per_slot, xa_ref[...], xb_ref[...])
    all_ref[...] = x
    slot = jnp.where(i < per_slot, meta[0] ^ flip, meta[0] ^ flip ^ 1)
    row = lax.broadcasted_iota(jnp.int32, (rows, HEAD_DIM), 0)
    lane = lax.broadcasted_iota(jnp.int32, (rows, HEAD_DIM), 1)
    index = (i % per_slot) * rows + row - prompt_local
    attended = jnp.logical_or(index < 0, slot * data_local + index < meta[1])
    bias = jnp.where(attended, F32(0.0), F32(MASKED))
    ones = jnp.where(lane < 4, F32(1.0), F32(0.0))
    kx_ref[...] = jnp.where(lane == 0, bias, ones).astype(BF16)
    factor = F32(LOG2E / math.sqrt(HEAD_DIM))
    z = mm(x, w_ref[...])
    q_ref[...] = (z[:, :256] * factor).astype(BF16)
    k_ref[...] = z[:, 256:512].astype(BF16)
    v_ref[...] = z[:, 512:].astype(BF16)
    zt = mm(wt_ref[...], x, NT)
    qt_ref[...] = (zt[:256] * factor).astype(BF16)
    kt_ref[...] = zt[256:512].astype(BF16)
    vt_ref[...] = zt[512:].astype(BF16)


def project(meta, xa, xb, wa, wb, sizes, flip, joined=None):
    rows, width = xa.shape
    step = 512
    n = rows // step
    flat = jax.ShapeDtypeStruct((2 * rows, 256), BF16)
    tall = jax.ShapeDtypeStruct((256, 2 * rows), BF16)
    row = pl.BlockSpec((step, 256), lambda i, meta: (i, 0))
    col = pl.BlockSpec((256, step), lambda i, meta: (0, i))
    extra = [joined] if flip else []

    def own_first(i):
        return (i // n) * 2 * n + (n if flip else 0) + i % n

    return pl.pallas_call(
        partial(project_kernel, sizes, flip),
        out_shape=[
            tall,
            flat,
            flat,
            jax.ShapeDtypeStruct((2 * rows, HEAD_DIM), BF16),
            tall,
            flat,
            tall,
            jax.ShapeDtypeStruct((width, 768), BF16),
            jax.ShapeDtypeStruct((4 * rows, width), BF16),
        ],
        grid_spec=pltpu.PrefetchScalarGridSpec(
            num_scalar_prefetch=1,
            grid=(2 * n,),
            in_specs=[
                pl.BlockSpec((step, width), lambda i, meta: (jnp.minimum(i, n - 1), 0)),
                pl.BlockSpec((step, width), lambda i, meta: (jnp.maximum(i - n, 0), 0)),
                once(wa.shape),
                once(wb.shape),
            ]
            + [pl.BlockSpec(memory_space=pl.ANY)] * len(extra),
            out_specs=[
                col,
                row,
                row,
                pl.BlockSpec((step, HEAD_DIM), lambda i, meta: (i, 0)),
                col,
                row,
                col,
                once((width, 768)),
                pl.BlockSpec((step, width), lambda i, meta: (own_first(i), 0)),
            ],
            scratch_shapes=[pltpu.VMEM((768, width), BF16)],
        ),
        input_output_aliases={5: 8} if flip else {},
        compiler_params=params(),
        cost_estimate=cost(4 * 2 * rows * width * 768, 2 * rows * width * 8),
        name="project",
    )(meta, xa, xb, wa, wb, *extra)


def head_rows(h):
    return slice(h * HEAD_DIM, (h + 1) * HEAD_DIM)


def with_shift(qt, top):
    high, middle, low = three_parts(top)
    extra = extra_rows([jnp.ones_like(top), -high, -middle, -low], HEAD_DIM)
    return jnp.concatenate([qt, extra], axis=0)


def half_scores(chunk, h, qa, start, k_ref, kx_ref):
    here = pl.ds(start, chunk)
    keys = jnp.concatenate([k_ref[here, head_rows(h)], kx_ref[here, :]], axis=1)
    return mm(keys, qa)


def half_part(h, start, scores, vt_ref, pt_ref):
    chunk = scores.shape[0]
    weight = jnp.exp2(scores)
    total = jnp.sum(weight.reshape(chunk // 8, 8, weight.shape[1]), axis=0)
    low = weight.astype(BF16)
    pt_ref[0, h, pl.ds(start, chunk), :] = low
    return total, mm(vt_ref[head_rows(h), pl.ds(start, chunk)], low)


def stale_shift(h, qt, k_ref):
    top = jnp.max(mm(k_ref[:SAMPLE, head_rows(h)], qt), axis=0, keepdims=True)
    return top, with_shift(qt, top)


def fast_states(chunk, shifts, keys, pts):
    tiles = [
        (h, j, start)
        for h in range(2)
        for j in range(len(keys))
        for start in range(0, keys[0][0].shape[0], chunk)
    ]

    def scores(tile):
        h, j, start = tile
        return half_scores(chunk, h, shifts[h][j][1], start, keys[j][0], keys[j][1])

    sums = {}
    ahead = scores(tiles[0])
    for place, (h, j, start) in enumerate(tiles):
        now = ahead
        if place + 1 < len(tiles):
            ahead = scores(tiles[place + 1])
        total, product = half_part(h, start, now, keys[j][2], pts[j])
        if (h, j) in sums:
            total, product = sums[h, j][0] + total, sums[h, j][1] + product
        sums[h, j] = total, product
    return [
        [
            (shifts[h][j][0], jnp.sum(sums[h, j][0], axis=0, keepdims=True), sums[h, j][1])
            for j in range(len(keys))
        ]
        for h in range(2)
    ]


def half_attend_exact(chunk, h, shift, k_ref, kx_ref, vt_ref, pt_ref):
    qt = shift[1][:HEAD_DIM]
    width = qt.shape[1]
    count = k_ref.shape[0] // chunk
    qa = with_shift(qt, jnp.zeros((1, width), F32))

    def find(j, top):
        found = half_scores(chunk, h, qa, pl.multiple_of(j * chunk, chunk), k_ref, kx_ref)
        return jnp.maximum(top, jnp.max(found, axis=0, keepdims=True))

    top = lax.fori_loop(0, count, find, jnp.full((1, width), MASKED, F32))
    qa = with_shift(qt, top)

    def add(j, state):
        start = pl.multiple_of(j * chunk, chunk)
        found = half_scores(chunk, h, qa, start, k_ref, kx_ref)
        more, product = half_part(h, start, found, vt_ref, pt_ref)
        return state[0] + more, state[1] + product

    total, acc = lax.fori_loop(
        0, count, add, (jnp.zeros((8, width), F32), jnp.zeros((HEAD_DIM, width), F32))
    )
    return top, jnp.sum(total, axis=0, keepdims=True), acc


def merge(states):
    top = states[0][0]
    for state in states[1:]:
        top = jnp.maximum(top, state[0])
    scales = [jnp.exp2(state[0] - top) for state in states]
    total = sum(state[1] * scale for state, scale in zip(states, scales))
    factors = [scale / total for scale in scales]
    return factors, sum(state[2] * factor for state, factor in zip(states, factors))


def redo(states, shifts, keys, pts):
    return [
        [half_attend_exact(256, h, shifts[h][j], *keys[j], pts[j]) for j in range(len(keys))]
        for h in range(2)
    ]


def run_halves(chunk, qt_ref, keys, pts, finish):
    shifts = [
        [stale_shift(h, qt_ref[head_rows(h), :], key_refs[0]) for key_refs in keys]
        for h in range(2)
    ]
    states = fast_states(chunk, shifts, keys, pts)
    worst = None
    for state in states[0] + states[1]:
        worst = state[1] if worst is None else jnp.maximum(worst, state[1])
    finish(states)

    @pl.when(jnp.logical_not(jnp.max(worst) <= LIMIT))
    def _():
        finish(redo(states, shifts, keys, pts))


def attend_first_kernel(chunk, qt_ref, k_ref, kx_ref, vt_ref, pt_ref, state_ref, acc_ref):
    def finish(states):
        for h in range(2):
            top, total, acc = states[h][0]
            state_ref[0, h : h + 1, :] = top
            state_ref[0, 2 + h : 3 + h, :] = total
            acc_ref[head_rows(h), :] = acc

    run_halves(chunk, qt_ref, [(k_ref, kx_ref, vt_ref)], [pt_ref], finish)


def attend_first(qt, key, chunk):
    rows = qt.shape[1]
    n = rows // ROWS
    col = pl.BlockSpec((256, ROWS), lambda i: (0, i))
    pairs = 2 * rows * rows
    return pl.pallas_call(
        partial(attend_first_kernel, chunk),
        out_shape=[
            jax.ShapeDtypeStruct((2 * n, 2, rows, ROWS), BF16),
            jax.ShapeDtypeStruct((n, 8, ROWS), F32),
            jax.ShapeDtypeStruct((256, rows), F32),
        ],
        grid=(n,),
        in_specs=[col] + [once(item.shape) for item in key],
        out_specs=[
            pl.BlockSpec((1, 2, rows, ROWS), lambda i: (i, 0, 0, 0)),
            pl.BlockSpec((1, 8, ROWS), lambda i: (i, 0, 0)),
            col,
        ],
        compiler_params=params(),
        cost_estimate=cost(4 * pairs * HEAD_DIM * 2, 2 * pairs, pairs),
        name="attend_near",
    )(qt, *key)


def attend_second_kernel(
    chunk, qtn_ref, qtf_ref, kn, kxn, vtn, kf, kxf, vtf, old_ref, old_acc_ref, _,
    ptn_ref, ptf_ref, mine_ref, sib_ref, stat_ref,
):
    i = pl.program_id(0)
    n = pl.num_programs(0) // 2
    near, far = (kn, kxn, vtn), (kf, kxf, vtf)

    def store(h, states):
        factors, result = merge(states)
        stat_ref[0, h : h + 1, :] = factors[0]
        stat_ref[0, 2 + h : 3 + h, :] = factors[1]
        low = result.T.astype(BF16)
        first = i % n < n // 2

        @pl.when(first)
        def _():
            mine_ref[:, head_rows(h)] = low

        @pl.when(jnp.logical_not(first))
        def _():
            sib_ref[:, head_rows(h)] = low

    @pl.when(i < n)
    def _():
        def finish(states):
            for h in range(2):
                old = (old_ref[0, h : h + 1, :], old_ref[0, 2 + h : 3 + h, :],
                       old_acc_ref[head_rows(h), :])
                store(h, [old, states[h][0]])

        run_halves(chunk, qtn_ref, [far], [ptf_ref], finish)

    @pl.when(i >= n)
    def _():
        def finish(states):
            for h in range(2):
                store(h, states[h])

        run_halves(chunk, qtf_ref, [near, far], [ptn_ref, ptf_ref], finish)


def mine_block(i, n):
    half = n // 2
    return (i // n) * half + jnp.minimum(i % n, half - 1)


def sib_block(i, n):
    half = n // 2
    return jnp.maximum((i // n) * half + i % n - half, jnp.maximum((i // n) * half - 1, 0))


def attend_second(qtn, qtf, near, far, pt, state, acc, chunk):
    rows = qtn.shape[1]
    n = rows // ROWS
    near_col = pl.BlockSpec((256, ROWS), lambda i: (0, jnp.minimum(i, n - 1)))
    pairs = 6 * rows * rows
    return pl.pallas_call(
        partial(attend_second_kernel, chunk),
        out_shape=[
            jax.ShapeDtypeStruct(pt.shape, BF16),
            jax.ShapeDtypeStruct(pt.shape, BF16),
            jax.ShapeDtypeStruct((rows, 256), BF16),
            jax.ShapeDtypeStruct((rows, 256), BF16),
            jax.ShapeDtypeStruct((2 * n, 8, ROWS), F32),
        ],
        grid=(2 * n,),
        in_specs=[near_col, pl.BlockSpec((256, ROWS), lambda i: (0, jnp.maximum(i - n, 0)))]
        + [once(item.shape) for item in near + far]
        + [
            pl.BlockSpec((1, 8, ROWS), lambda i: (jnp.minimum(i, n - 1), 0, 0)),
            near_col,
            pl.BlockSpec(memory_space=pl.ANY),
        ],
        out_specs=[
            pl.BlockSpec((1, 2, rows, ROWS), lambda i: (jnp.maximum(i, n), 0, 0, 0)),
            pl.BlockSpec((1, 2, rows, ROWS), lambda i: (i, 0, 0, 0)),
            pl.BlockSpec((ROWS, 256), lambda i: (mine_block(i, n), 0)),
            pl.BlockSpec((ROWS, 256), lambda i: (sib_block(i, n), 0)),
            pl.BlockSpec((1, 8, ROWS), lambda i: (i, 0, 0)),
        ],
        input_output_aliases={10: 0},
        compiler_params=params(),
        cost_estimate=cost(4 * pairs * HEAD_DIM * 2, 2 * pairs, pairs),
        name="attend_rest",
    )(qtn, qtf, *near, *far, state, acc, pt)


def back_weights(do, o, factors):
    dot_t = do.astype(F32).T
    delta = jnp.sum(dot_t * o.astype(F32).T, axis=0, keepdims=True)
    found = []
    for factor in factors:
        scaled = dot_t * factor
        high, middle, low = three_parts(delta * factor)
        extra = extra_rows([-high, -middle, -low], HEAD_DIM)
        found.append(
            (jnp.concatenate([scaled.astype(BF16), extra], axis=0), scaled.T.astype(BF16))
        )
    return found


def back_half(chunk, h, grads, q_rows, pt_ref, v_ref, kt_ref, key_acc, value_acc):
    ones = jnp.where(
        lax.broadcasted_iota(jnp.int32, (chunk, HEAD_DIM), 1) < 3, F32(1.0), F32(0.0)
    ).astype(BF16)
    result = jnp.zeros((HEAD_DIM, q_rows.shape[0]), F32)
    for start in range(0, v_ref.shape[0], chunk):
        here = slice(start, start + chunk)
        prob = pt_ref[0, h, here, :]
        values = jnp.concatenate([v_ref[here, head_rows(h)], ones], axis=1)
        score = (prob.astype(F32) * mm(values, grads[0])).astype(BF16)
        value_acc[h, here, :] += mm(prob, grads[1])
        key_acc[h, here, :] += mm(score, q_rows)
        result = result + mm(kt_ref[head_rows(h), here], score)
    return result


def attend_back_kernel(
    chunk, da_ref, db_ref, oa_ref, ob_ref, stat_ref, qn_ref, qf_ref, ptn_ref, ptf_ref,
    vn, ktn, vf, ktf, dz_ref, key_n, value_n, key_f, value_f,
):
    i = pl.program_id(0)
    n = pl.num_programs(0) // 2

    @pl.when(i == 0)
    def _():
        for ref in (key_n, value_n, key_f, value_f):
            ref[...] = jnp.zeros_like(ref)

    first = i % n < n // 2
    do = jnp.where(first, da_ref[...], db_ref[...])
    o = jnp.where(first, oa_ref[...], ob_ref[...])
    q = jnp.where(i < n, qn_ref[...], qf_ref[...])
    place = jnp.where(first, 0, n // 2) + (i // n) * (n // 2) + i % n
    rows = pl.ds(pl.multiple_of(place * q.shape[0], q.shape[0]), q.shape[0])
    for h in range(2):
        cols = head_rows(h)
        near, far = back_weights(
            do[:, cols], o[:, cols], [stat_ref[0, h : h + 1, :], stat_ref[0, 2 + h : 3 + h, :]]
        )
        grad = back_half(chunk, h, near, q[:, cols], ptn_ref, vn, ktn, key_n, value_n)
        grad += back_half(chunk, h, far, q[:, cols], ptf_ref, vf, ktf, key_f, value_f)
        dz_ref[rows, cols] = (grad * F32(1.0 / math.sqrt(HEAD_DIM))).T.astype(BF16)

    @pl.when(i == 2 * n - 1)
    def _():
        seq = vn.shape[0]
        for half, (keys, values) in enumerate(((key_n, value_n), (key_f, value_f))):
            for owner in range(2):
                source = slice(owner * seq // 2, (owner + 1) * seq // 2)
                begin = owner * seq + half * seq // 2
                rows = slice(begin, begin + seq // 2)
                for h in range(2):
                    dz_ref[rows, head_rows(2 + h)] = (keys[h, source] * F32(1.0 / LOG2E)).astype(BF16)
                    dz_ref[rows, head_rows(4 + h)] = values[h, source].astype(BF16)


def attend_back(da, db, oa, ob, stat, qn, qf, ptn, ptf, vn, ktn, vf, ktf, chunk):
    rows = qn.shape[0]
    step = BACK_ROWS
    n = rows // step
    per = ROWS // step
    row = lambda f: pl.BlockSpec((step, 256), lambda i: (f(i), 0))
    tile = pl.BlockSpec((1, 2, rows, step), lambda i: (i // per, 0, 0, i % per))
    wide = jax.ShapeDtypeStruct((2 * rows, 768), BF16)
    acc = pltpu.VMEM((2, rows, HEAD_DIM), F32)
    pairs = 8 * rows * rows
    return pl.pallas_call(
        partial(attend_back_kernel, chunk),
        out_shape=wide,
        grid=(2 * n,),
        in_specs=[
            row(lambda i: mine_block(i, n)),
            row(lambda i: sib_block(i, n)),
            row(lambda i: mine_block(i, n)),
            row(lambda i: sib_block(i, n)),
            pl.BlockSpec((1, 8, step), lambda i: (i // per, 0, i % per)),
            row(lambda i: jnp.minimum(i, n - 1)),
            row(lambda i: jnp.maximum(i - n, 0)),
            tile,
            tile,
        ]
        + [once(item.shape) for item in (vn, ktn, vf, ktf)],
        out_specs=once(wide.shape),
        scratch_shapes=[acc, acc, acc, acc],
        compiler_params=params(),
        cost_estimate=cost(8 * pairs * HEAD_DIM, 2 * pairs),
        name="attend_back",
    )(da, db, oa, ob, stat, qn, qf, ptn, ptf, vn, ktn, vf, ktf)


def mean(values):
    return jnp.mean(values, axis=-1, keepdims=True)


def norm(values):
    centered = values - mean(values)
    inverse = lax.rsqrt(mean(centered * centered) + EPS)
    return centered * inverse, inverse


def norm_back(incoming, normed, inverse, gain):
    scaled = incoming * gain
    return inverse * (scaled - mean(scaled) - normed * mean(scaled * normed))


def gelu_parts(v):
    bell = jnp.exp2(v * v * F32(-0.5 * LOG2E))
    base = 1.0 + F32(0.3275911 / math.sqrt(2.0)) * jnp.abs(v)
    t = pl.reciprocal(base, approx=True)
    t = t * (2.0 - base * t)
    series = t * (
        F32(0.5 * 0.254829592)
        + t
        * (
            F32(0.5 * -0.284496736)
            + t
            * (
                F32(0.5 * 1.421413741)
                + t * (F32(0.5 * -1.453152027) + t * F32(0.5 * 1.061405429))
            )
        )
    )
    tail = series * bell
    return bell * F32(1.0 / math.sqrt(2.0 * math.pi)), jnp.where(v >= 0, 1.0 - tail, tail)


def fold_rows(values):
    return jnp.sum(values.reshape(values.shape[0] // 8, 8, values.shape[1]), axis=0)


def rows_kernel(
    sizes, meta, xa_ref, xb_ref, oa_ref, ob_ref, cot_a, cot_b, p0, p1, p2, p3,
    u0, u1, u2, u3, vec_ref,
    prompt_near, data_near, prompt_far, data_far, resid_ref, da_ref, db_ref, send_ref,
    sums_ref, wo_ref, up_ref, down_ref, bias_ref, grad_acc, vec_acc, bias_acc,
):
    prompt_local, data_local = sizes
    i = pl.program_id(0)
    half = pl.num_programs(0) // 2
    here = i < half
    rows = xa_ref.shape[0]
    quarter = u0.shape[1]

    @pl.when(i == 0)
    def _():
        for j, (pack, up_part) in enumerate(((p0, u0), (p1, u1), (p2, u2), (p3, u3))):
            cols = slice(j * quarter, (j + 1) * quarter)
            wo_ref[head_rows(j), :] = pack[:HEAD_DIM, :]
            down_ref[cols, :] = pack[HEAD_DIM : HEAD_DIM + quarter, :]
            bias_ref[0:1, cols] = pack[
                HEAD_DIM + quarter : HEAD_DIM + quarter + 16, :quarter
            ].astype(F32)[0:1, :]
            up_ref[:, cols] = up_part[...]
        grad_acc[...] = jnp.zeros_like(grad_acc)
        vec_acc[...] = jnp.zeros_like(vec_acc)
        bias_acc[...] = jnp.zeros_like(bias_acc)

    slot = jnp.where(here, meta[0], meta[0] ^ 2)
    index = (i % half) * rows + lax.broadcasted_iota(jnp.int32, (rows, 1), 0) - prompt_local
    live = jnp.logical_or(index < 0, slot * data_local + index < meta[2])

    out_bias, attn_gain, attn_shift = vec_ref[0:1, :], vec_ref[1:2, :], vec_ref[2:3, :]
    down_bias, mlp_gain, mlp_shift = vec_ref[3:4, :], vec_ref[4:5, :], vec_ref[5:6, :]
    x = jnp.where(here, xa_ref[...], xb_ref[...])
    attended = jnp.concatenate([oa_ref[...], ob_ref[...]], axis=1)
    normed_one, inverse_one = norm(x.astype(F32) + (mm(attended, wo_ref[...]) + out_bias))
    hidden = normed_one * attn_gain + attn_shift
    hidden_low = hidden.astype(BF16)
    pre = mm(hidden_low, up_ref[...]) + bias_ref[0:1, :]
    density, share = gelu_parts(pre)
    activated = (pre * share).astype(BF16)
    slope = share + pre * density
    mixed = hidden + (mm(activated, down_ref[...]) + down_bias)
    normed_two, inverse_two = norm(mixed)
    output = (normed_two * mlp_gain + mlp_shift).astype(BF16)
    for j in range(2):
        split = max(0, min(rows, prompt_local - j * rows))
        for place, (prompt_ref, data_ref) in enumerate(
            ((prompt_near, data_near), (prompt_far, data_far))
        ):

            @pl.when(i == place * half + j)
            def _():
                if split:
                    prompt_ref[j * rows : j * rows + split, :] = output[:split]
                if split < rows:
                    begin = j * rows + split - prompt_local
                    data_ref[begin : begin + rows - split, :] = output[split:]

    cotangent = jnp.where(live, jnp.where(here, cot_a[...], cot_b[...]).astype(F32), 0.0)
    mixed_grad = norm_back(cotangent, normed_two, inverse_two, mlp_gain)
    mixed_low = mixed_grad.astype(BF16)
    pre_grad = (mm(mixed_low, down_ref[...], NT) * slope).astype(BF16)
    hidden_grad = mixed_grad + mm(pre_grad, up_ref[...], NT)
    resid_grad = norm_back(hidden_grad, normed_one, inverse_one, attn_gain)
    resid_ref[...] = resid_grad
    resid_low = resid_grad.astype(BF16)
    attended_grad = mm(resid_low, wo_ref[...], NT).astype(BF16)
    da_ref[...] = attended_grad[:, :256]
    db_ref[...] = attended_grad[:, 256:]

    up_grad = mm(hidden_low, pre_grad, TN)
    down_grad = mm(mixed_low, activated, TN)
    out_grad = mm(resid_low, attended, TN)
    for j in range(4):
        cols = slice(j * quarter, (j + 1) * quarter)
        grad_acc[j, :, :quarter] += up_grad[:, cols]
        grad_acc[j, :, quarter : 2 * quarter] += down_grad[:, cols]
        grad_acc[j, :, 2 * quarter :] += out_grad[:, head_rows(j)]
    bias_acc[...] += fold_rows(pre_grad.astype(F32))
    for place, value in enumerate(
        (
            resid_grad,
            hidden_grad * normed_one,
            hidden_grad,
            mixed_grad,
            cotangent * normed_two,
            cotangent,
        )
    ):
        vec_acc[place] += fold_rows(value)

    @pl.when(i == pl.num_programs(0) - 1)
    def _():
        for place in range(6):
            sums_ref[place : place + 1, :] = jnp.sum(vec_acc[place], axis=0, keepdims=True)
        bias_grad = jnp.sum(bias_acc[...], axis=0, keepdims=True)
        per_row = bias_grad.shape[1] // 2 // quarter
        for g in range(4):
            found = jnp.zeros((1, quarter), F32)
            for j, flip in enumerate((0, 2, 1, 3)):
                piece = bias_grad[:, j * quarter : (j + 1) * quarter]
                found = jnp.where((meta[0] ^ flip) == g, piece, found)
            row, col = 6 + g // per_row, (g % per_row) * quarter
            sums_ref[row : row + 1, col : col + quarter] = found
        depth = send_ref.shape[1] - 16
        groups = send_ref.shape[0] // 4
        width, wide = sums_ref.shape[1], send_ref.shape[2]
        per = sums_ref.shape[0] * width // groups
        for g in range(groups):
            row, col = g * per // width, g * per % width
            part = jnp.pad(sums_ref[row : row + 1, col : col + per], ((0, 0), (0, wide - per)))
            high, low, _ = three_parts(part)
            extra = extra_rows([high, low], 16)
            for j, flip in enumerate((0, 2, 1, 3)):
                target = g * 4 + (meta[0] ^ flip)
                send_ref[target, :depth] = grad_acc[j, g * depth : (g + 1) * depth].astype(BF16)
                send_ref[target, depth:] = extra


def row_work(meta, xa, xb, oa, ob, cot, packs, ups, vec, sizes, groups):
    rows, width = xa.shape
    prompt_local, data_local = sizes
    step = 512
    n = rows // step
    quarter = ups[0].shape[1]
    hidden = 4 * quarter
    wide = 2 * quarter + HEAD_DIM
    send = (4 * groups, width // groups + 16, wide)
    near = pl.BlockSpec((step, width), lambda i, meta: (jnp.minimum(i, n - 1), 0))
    far = pl.BlockSpec((step, width), lambda i, meta: (jnp.maximum(i - n, 0), 0))
    row = lambda cols: pl.BlockSpec((step, cols), lambda i, meta: (i, 0))
    return pl.pallas_call(
        partial(rows_kernel, sizes),
        out_shape=[
            jax.ShapeDtypeStruct((prompt_local, width), BF16),
            jax.ShapeDtypeStruct((data_local, width), BF16),
            jax.ShapeDtypeStruct((prompt_local, width), BF16),
            jax.ShapeDtypeStruct((data_local, width), BF16),
            jax.ShapeDtypeStruct((2 * rows, width), F32),
            jax.ShapeDtypeStruct((2 * rows, 256), BF16),
            jax.ShapeDtypeStruct((2 * rows, 256), BF16),
            jax.ShapeDtypeStruct(send, BF16),
        ],
        grid_spec=pltpu.PrefetchScalarGridSpec(
            num_scalar_prefetch=1,
            grid=(2 * n,),
            in_specs=[near, far, row(256), row(256), near, far]
            + [once(item.shape) for item in packs + ups]
            + [once(vec.shape)],
            out_specs=[
                once((prompt_local, width)),
                once((data_local, width)),
                once((prompt_local, width)),
                once((data_local, width)),
                row(width),
                row(256),
                row(256),
                once(send),
            ],
            scratch_shapes=[
                pltpu.VMEM((8, width), F32),
                pltpu.VMEM((4 * HEAD_DIM, width), BF16),
                pltpu.VMEM((width, hidden), BF16),
                pltpu.VMEM((hidden, width), BF16),
                pltpu.VMEM((8, hidden), F32),
                pltpu.VMEM((4, width, wide), F32),
                pltpu.VMEM((6, 8, width), F32),
                pltpu.VMEM((8, hidden), F32),
            ],
        ),
        compiler_params=params(),
        cost_estimate=cost(
            3 * 2 * 2 * rows * width * (width + 2 * hidden), 24 * rows * width, 4 * rows * hidden
        ),
        name="row_work",
    )(meta, xa, xb, oa, ob, *cot, *packs, *ups, vec)


def on_device(
    data_rows,
    prompt_rows,
    context_rows,
    test_rows,
    qkv_weight,
    out_bias,
    out_weight,
    attn_gain,
    attn_shift,
    up_weight,
    up_bias,
    down_weight,
    down_bias,
    mlp_gain,
    mlp_shift,
    data_cotangent,
    prompt_cotangent,
):
    data_local = data_rows.shape[1]
    prompt_local = prompt_rows.shape[0]
    width = prompt_rows.shape[1]
    quarter = up_weight.shape[1]
    sizes = (prompt_local, data_local)
    groups = lax.axis_size("ep")
    t = lax.axis_index("tp")
    mine = t >> 1
    other = 1 - mine

    def across(value):
        return lax.ppermute(value, "tp", [(i, i ^ 2) for i in range(4)])

    def beside(value):
        return lax.ppermute(value, "tp", [(i, i ^ 1) for i in range(4)])

    def pick(values, which):
        return lax.dynamic_index_in_dim(values, which, axis=0, keepdims=False)

    def stack(prompt_part, data_part):
        return jnp.concatenate([prompt_part, data_part], axis=0)

    w_far = across(qkv_weight)
    x_far = across(stack(prompt_rows, pick(data_rows, other)))
    x = stack(prompt_rows, pick(data_rows, mine))
    x_sib = beside(x)
    context = pick(context_rows, mine)
    live = context + pick(test_rows, mine)
    meta = jnp.stack([t, context, live]).astype(jnp.int32)

    qtn, qn, kn, kxn, ktn, vn, vtn, w, x_all = project(
        meta, x, x_sib, qkv_weight, w_far, sizes, 0
    )
    ptn, state, state_acc = attend_first(qtn, (kn, kxn, vtn), 512)

    bias_rows = jnp.pad(up_bias[None], ((0, 15), (0, width - quarter)))
    pack = jnp.concatenate([out_weight, down_weight, bias_rows], axis=0)
    x_far, state, pack, up_weight = lax.optimization_barrier((x_far, state, pack, up_weight))
    x_far_sib = beside(x_far)
    pack_far, up_far = across(pack), across(up_weight)
    cot_far = stack(pick(prompt_cotangent, other), pick(data_cotangent, other))
    x_far_sib, cot_far = lax.optimization_barrier((x_far_sib, cot_far))
    cot_far = across(cot_far)
    qtf, qf, kf, kxf, ktf, vf, vtf, _, x_all = project(
        meta, x_far, x_far_sib, qkv_weight, w_far, sizes, 2, x_all
    )
    pack_far, up_far, qtf = lax.optimization_barrier((pack_far, up_far, qtf))
    packs = [pack, pack_far, beside(pack), beside(pack_far)]
    ups = [up_weight, up_far, beside(up_weight), beside(up_far)]
    cot = stack(pick(prompt_cotangent, mine), pick(data_cotangent, mine))
    vec = jnp.stack(
        [out_bias, attn_gain, attn_shift, down_bias, mlp_gain, mlp_shift, mlp_shift, mlp_shift]
    ).astype(F32)
    ptn, ptf, oa, ob, stat = attend_second(
        qtn, qtf, (kn, kxn, vtn), (kf, kxf, vtf), ptn, state, state_acc, 512
    )

    ob_send, cot_far, cot, vec, packs, ups = lax.optimization_barrier(
        (ob, cot_far, cot, vec, packs, ups)
    )
    (prompt_near, data_near, prompt_far, data_far, resid, da, db, send) = row_work(
        meta, x, x_far, oa, beside(ob_send), (cot, cot_far), packs, ups, vec, sizes, groups
    )

    def dot(left, right, dims):
        return lax.dot_general(left, right, dims, preferred_element_type=F32)

    def exchange(parts, axes):
        return lax.all_to_all(parts, axes, 0, 0, tiled=True)

    def gather(part):
        return exchange(jnp.broadcast_to(part[None], (groups,) + part.shape), "ep")

    db = beside(db)
    send = exchange(send, ("ep", "tp"))
    prompt_back, data_back = across(prompt_far), across(data_far)

    dz = attend_back(da, db, oa, ob, stat, qn, qf, ptn, ptf, vn, ktn, vf, ktf, 1024)
    send, prompt_back, data_back, dz = lax.optimization_barrier((send, prompt_back, data_back, dz))
    depth = width // groups
    total = jnp.sum(send.astype(F32), axis=0)
    part = total[depth : depth + 1] + total[depth + 1 : depth + 2]
    high = lax.optimization_barrier(part.astype(BF16))
    low = (part - high.astype(F32)).astype(BF16)
    total = jnp.concatenate(
        [total[:depth].astype(BF16), high, low, jnp.zeros((14, total.shape[1]), BF16)], axis=0
    )
    total = jnp.broadcast_to(total[None], (groups,) + total.shape)
    total, dz = lax.optimization_barrier((total, dz))
    total = exchange(total, "ep")

    slot_rows = prompt_local + data_local
    cut = 2 * slot_rows
    grad = dot(x_all, dz, TN)

    def head_grad(h):
        return jnp.stack([grad[:, head_rows(2 * which + h)] for which in range(3)])

    other_grad, dz = lax.optimization_barrier((head_grad(1).astype(BF16), dz))
    other_grad = across(other_grad)
    sib, dz = lax.optimization_barrier((dot(dz[cut:], w, NT).astype(BF16), dz))
    sib = beside(sib)
    own = dot(dz[:cut], w, NT) + resid
    other_grad, own = lax.optimization_barrier((other_grad, own))
    far_rows = (own[slot_rows:] + sib[slot_rows:].astype(F32)).astype(BF16)
    near_rows = own[:slot_rows] + sib[:slot_rows].astype(F32)
    near_data = near_rows[prompt_local:].astype(BF16)

    columns = width // HEAD_DIM
    qkv = (head_grad(0) + other_grad.astype(F32)).astype(BF16).reshape(groups, -1, HEAD_DIM)
    qkv_rows = qkv.shape[1]
    total, qkv, far_rows = lax.optimization_barrier((total, qkv, far_rows))
    far_prompt = across(far_rows[:prompt_local])
    far_data = across(far_rows[prompt_local:])
    qkv = jnp.sum(exchange(qkv, "ep").astype(F32), axis=0).astype(BF16)
    prompt = near_rows[:prompt_local] + far_prompt.astype(F32)
    prompt = prompt.astype(BF16).reshape(groups, prompt_local // groups, width)
    prompt = jnp.sum(exchange(prompt, "ep").astype(F32), axis=0).astype(BF16)
    prompt = jnp.concatenate([prompt[:, head_rows(j)] for j in range(columns)], axis=0)
    last = gather(jnp.concatenate([qkv, prompt], axis=0))
    qkv = last[:, :qkv_rows].reshape(3, width, HEAD_DIM).astype(F32)
    prompt = last[:, qkv_rows:].reshape(groups, columns, prompt_local // groups, HEAD_DIM)
    prompt_grad = jnp.concatenate([prompt[:, j] for j in range(columns)], axis=2)
    prompt_grad = prompt_grad.reshape(prompt_local, width).astype(F32)

    which = lax.broadcasted_iota(jnp.int32, (2, 1, 1), 0)

    def by_episode(own, received):
        return jnp.where(which == mine, own[None], received[None])

    sums = total[:, depth : depth + 2, : 8 * width // groups].astype(F32)
    sums = (sums[:, 0] + sums[:, 1]).reshape(8, width)
    total = total[:, :depth].reshape(width, -1).astype(F32)
    bias_grad = lax.dynamic_slice_in_dim(sums[6:8].reshape(-1), t * quarter, quarter)
    return (
        by_episode(data_near, data_back),
        by_episode(prompt_near, prompt_back),
        by_episode(near_data, far_data),
        prompt_grad,
        qkv,
        sums[0],
        total[:, 2 * quarter :].T,
        sums[1],
        sums[2],
        total[:, :quarter],
        bias_grad,
        total[:, quarter : 2 * quarter].T,
        sums[3],
        sums[4],
        sums[5],
    )


def solution(mesh):
    return jax.shard_map(
        on_device,
        mesh=mesh,
        in_specs=(
            P("ep", "tp", None),
            P("tp", None),
            P("ep"),
            P("ep"),
            P(None, None, "tp"),
            P(),
            P("tp", None),
            P(),
            P(),
            P(None, "tp"),
            P("tp"),
            P("tp", None),
            P(),
            P(),
            P(),
            P("ep", "tp", None),
            P("ep", "tp", None),
        ),
        out_specs=(
            P("ep", "tp", None),
            P("ep", "tp", None),
            P("ep", "tp", None),
            P("tp", None),
            P(None, None, "tp"),
            P(),
            P("tp", None),
            P(),
            P(),
            P(None, "tp"),
            P("tp"),
            P("tp", None),
            P(),
            P(),
            P(),
        ),
        check_vma=False,
    )
```

```python
from functools import partial
import math

import jax
import jax.numpy as jnp
from jax import lax
from jax.experimental import pallas as pl
from jax.experimental.pallas import tpu as pltpu
from jax.sharding import PartitionSpec as P

HEAD_DIM = 128
ROWS = 512
BACK_ROWS = 256
SAMPLE = 256
EPS = 1e-05
MASKED = -1e30
LOG2E = math.log2(math.e)
LIMIT = 2.0**60
VMEM = 60 * 1024 * 1024
F32 = jnp.float32
BF16 = jnp.bfloat16
NN = (((1,), (0,)), ((), ()))
NT = (((1,), (1,)), ((), ()))
TN = (((0,), (0,)), ((), ()))


def mm(left, right, dims=NN):
    return lax.dot_general(left, right, dims, preferred_element_type=F32)


def params(**more):
    return pltpu.CompilerParams(vmem_limit_bytes=VMEM, **more)


def cost(flops, nbytes, trans=0):
    return pl.CostEstimate(
        flops=int(flops), bytes_accessed=int(nbytes), transcendentals=int(trans)
    )


def once(shape):
    return pl.BlockSpec(shape, lambda *_: (0,) * len(shape), pipeline_mode=pl.Buffered(1))


def extra_rows(values, count):
    width = values[0].shape[1]
    row = lax.broadcasted_iota(jnp.int32, (count, width), 0)
    out = jnp.zeros((count, width), F32)
    for index, value in enumerate(values):
        out = jnp.where(row == index, value, out)
    return out.astype(BF16)


def three_parts(row):
    high = row.astype(BF16).astype(F32)
    middle = (row - high).astype(BF16).astype(F32)
    return high, middle, row - high - middle


def clamp(i, low, high):
    return jnp.minimum(jnp.maximum(i, low), high)


def project_kernel(sizes, flip, meta, xa_ref, xb_ref, wa_ref, wb_ref, qt_ref, q_ref, k_ref,
                   kx_ref, kt_ref, v_ref, vt_ref, w_ref, wt_ref):
    prompt_local, data_local = sizes
    i = pl.program_id(0)
    per_slot = pl.num_programs(0) // 2
    rows = xa_ref.shape[0]

    @pl.when(i == 0)
    def _():
        for which in range(3):
            for h, source in enumerate((wa_ref, wb_ref)):
                cols = slice(which * 256 + h * HEAD_DIM, which * 256 + (h + 1) * HEAD_DIM)
                w_ref[:, cols] = source[which]
                wt_ref[cols, :] = source[which].T

    x = jnp.where(i < per_slot, xa_ref[...], xb_ref[...])
    slot = jnp.where(i < per_slot, meta[0] ^ flip, meta[0] ^ flip ^ 1)
    row = lax.broadcasted_iota(jnp.int32, (rows, HEAD_DIM), 0)
    lane = lax.broadcasted_iota(jnp.int32, (rows, HEAD_DIM), 1)
    index = (i % per_slot) * rows + row - prompt_local
    attended = jnp.logical_or(index < 0, slot * data_local + index < meta[1])
    bias = jnp.where(attended, F32(0.0), F32(MASKED))
    ones = jnp.where(lane < 4, F32(1.0), F32(0.0))
    kx_ref[...] = jnp.where(lane == 0, bias, ones).astype(BF16)
    factor = F32(LOG2E / math.sqrt(HEAD_DIM))
    z = mm(x, w_ref[...])
    q_ref[...] = (z[:, :256] * factor).astype(BF16)
    k_ref[...] = z[:, 256:512].astype(BF16)
    v_ref[...] = z[:, 512:].astype(BF16)
    zt = mm(wt_ref[...], x, NT)
    qt_ref[...] = (zt[:256] * factor).astype(BF16)
    kt_ref[...] = zt[256:512].astype(BF16)
    vt_ref[...] = zt[512:].astype(BF16)


def project(meta, xa, xb, wa, wb, sizes, flip):
    rows, width = xa.shape
    step = 512
    n = rows // step
    flat = jax.ShapeDtypeStruct((2 * rows, 256), BF16)
    tall = jax.ShapeDtypeStruct((256, 2 * rows), BF16)
    row = pl.BlockSpec((step, 256), lambda i, meta: (i, 0))
    col = pl.BlockSpec((256, step), lambda i, meta: (0, i))
    return pl.pallas_call(
        partial(project_kernel, sizes, flip),
        out_shape=[
            tall,
            flat,
            flat,
            jax.ShapeDtypeStruct((2 * rows, HEAD_DIM), BF16),
            tall,
            flat,
            tall,
            jax.ShapeDtypeStruct((width, 768), BF16),
        ],
        grid_spec=pltpu.PrefetchScalarGridSpec(
            num_scalar_prefetch=1,
            grid=(2 * n,),
            in_specs=[
                pl.BlockSpec((step, width), lambda i, meta: (jnp.minimum(i, n - 1), 0)),
                pl.BlockSpec((step, width), lambda i, meta: (jnp.maximum(i - n, 0), 0)),
                once(wa.shape),
                once(wb.shape),
            ],
            out_specs=[
                col,
                row,
                row,
                pl.BlockSpec((step, HEAD_DIM), lambda i, meta: (i, 0)),
                col,
                row,
                col,
                once((width, 768)),
            ],
            scratch_shapes=[pltpu.VMEM((768, width), BF16)],
        ),
        compiler_params=params(),
        cost_estimate=cost(4 * 2 * rows * width * 768, 2 * rows * width * 8),
        name="project",
    )(meta, xa, xb, wa, wb)


def head_rows(h):
    return slice(h * HEAD_DIM, (h + 1) * HEAD_DIM)


def with_shift(qt, top):
    high, middle, low = three_parts(top)
    extra = extra_rows([jnp.ones_like(top), -high, -middle, -low], HEAD_DIM)
    return jnp.concatenate([qt, extra], axis=0)


def half_scores(chunk, h, qa, start, k_ref, kx_ref):
    here = pl.ds(start, chunk)
    keys = jnp.concatenate([k_ref[here, head_rows(h)], kx_ref[here, :]], axis=1)
    return mm(keys, qa)


def half_part(h, start, scores, vt_ref, pt_ref):
    chunk = scores.shape[0]
    weight = jnp.exp2(scores)
    total = jnp.sum(weight.reshape(chunk // 8, 8, weight.shape[1]), axis=0)
    low = weight.astype(BF16)
    pt_ref[0, h, pl.ds(start, chunk), :] = low
    return total, mm(vt_ref[head_rows(h), pl.ds(start, chunk)], low)


def stale_shift(h, qt, k_ref):
    top = jnp.max(mm(k_ref[:SAMPLE, head_rows(h)], qt), axis=0, keepdims=True)
    return top, with_shift(qt, top)


def fast_states(chunk, shifts, keys, pts):
    tiles = [
        (h, j, start)
        for h in range(2)
        for j in range(len(keys))
        for start in range(0, keys[0][0].shape[0], chunk)
    ]

    def scores(tile):
        h, j, start = tile
        return half_scores(chunk, h, shifts[h][j][1], start, keys[j][0], keys[j][1])

    sums = {}
    ahead = scores(tiles[0])
    for place, (h, j, start) in enumerate(tiles):
        now = ahead
        if place + 1 < len(tiles):
            ahead = scores(tiles[place + 1])
        total, product = half_part(h, start, now, keys[j][2], pts[j])
        if (h, j) in sums:
            total, product = sums[h, j][0] + total, sums[h, j][1] + product
        sums[h, j] = total, product
    return [
        [
            (shifts[h][j][0], jnp.sum(sums[h, j][0], axis=0, keepdims=True), sums[h, j][1])
            for j in range(len(keys))
        ]
        for h in range(2)
    ]


def half_attend_exact(chunk, h, shift, k_ref, kx_ref, vt_ref, pt_ref):
    qt = shift[1][:HEAD_DIM]
    width = qt.shape[1]
    count = k_ref.shape[0] // chunk
    qa = with_shift(qt, jnp.zeros((1, width), F32))

    def find(j, top):
        found = half_scores(chunk, h, qa, pl.multiple_of(j * chunk, chunk), k_ref, kx_ref)
        return jnp.maximum(top, jnp.max(found, axis=0, keepdims=True))

    top = lax.fori_loop(0, count, find, jnp.full((1, width), MASKED, F32))
    qa = with_shift(qt, top)

    def add(j, state):
        start = pl.multiple_of(j * chunk, chunk)
        found = half_scores(chunk, h, qa, start, k_ref, kx_ref)
        more, product = half_part(h, start, found, vt_ref, pt_ref)
        return state[0] + more, state[1] + product

    total, acc = lax.fori_loop(
        0, count, add, (jnp.zeros((8, width), F32), jnp.zeros((HEAD_DIM, width), F32))
    )
    return top, jnp.sum(total, axis=0, keepdims=True), acc


def merge(states):
    top = states[0][0]
    for state in states[1:]:
        top = jnp.maximum(top, state[0])
    scales = [jnp.exp2(state[0] - top) for state in states]
    total = sum(state[1] * scale for state, scale in zip(states, scales))
    factors = [scale / total for scale in scales]
    return factors, sum(state[2] * factor for state, factor in zip(states, factors))


def redo(states, shifts, keys, pts):
    return [
        [half_attend_exact(256, h, shifts[h][j], *keys[j], pts[j]) for j in range(len(keys))]
        for h in range(2)
    ]


def run_halves(chunk, qt_ref, keys, pts, finish):
    shifts = [
        [stale_shift(h, qt_ref[head_rows(h), :], key_refs[0]) for key_refs in keys]
        for h in range(2)
    ]
    states = fast_states(chunk, shifts, keys, pts)
    worst = None
    for state in states[0] + states[1]:
        worst = state[1] if worst is None else jnp.maximum(worst, state[1])
    finish(states)

    @pl.when(jnp.logical_not(jnp.max(worst) <= LIMIT))
    def _():
        finish(redo(states, shifts, keys, pts))


def attend_first_kernel(chunk, qt_ref, k_ref, kx_ref, vt_ref, pt_ref, state_ref, acc_ref):
    def finish(states):
        for h in range(2):
            top, total, acc = states[h][0]
            state_ref[0, h : h + 1, :] = top
            state_ref[0, 2 + h : 3 + h, :] = total
            acc_ref[head_rows(h), :] = acc

    run_halves(chunk, qt_ref, [(k_ref, kx_ref, vt_ref)], [pt_ref], finish)


def attend_first(qt, key, chunk):
    rows = qt.shape[1]
    n = rows // ROWS
    col = pl.BlockSpec((256, ROWS), lambda i: (0, i))
    pairs = 2 * rows * rows
    return pl.pallas_call(
        partial(attend_first_kernel, chunk),
        out_shape=[
            jax.ShapeDtypeStruct((2 * n, 2, rows, ROWS), BF16),
            jax.ShapeDtypeStruct((n, 8, ROWS), F32),
            jax.ShapeDtypeStruct((256, rows), F32),
        ],
        grid=(n,),
        in_specs=[col] + [once(item.shape) for item in key],
        out_specs=[
            pl.BlockSpec((1, 2, rows, ROWS), lambda i: (i, 0, 0, 0)),
            pl.BlockSpec((1, 8, ROWS), lambda i: (i, 0, 0)),
            col,
        ],
        compiler_params=params(),
        cost_estimate=cost(4 * pairs * HEAD_DIM * 2, 2 * pairs, pairs),
        name="attend_near",
    )(qt, *key)


def attend_second_kernel(
    chunk, qtn_ref, qtf_ref, kn, kxn, vtn, kf, kxf, vtf, old_ref, old_acc_ref, _,
    ptn_ref, ptf_ref, mine_ref, sib_ref, stat_ref,
):
    i = pl.program_id(0)
    n = pl.num_programs(0) // 2
    near, far = (kn, kxn, vtn), (kf, kxf, vtf)

    def store(h, states):
        factors, result = merge(states)
        stat_ref[0, h : h + 1, :] = factors[0]
        stat_ref[0, 2 + h : 3 + h, :] = factors[1]
        low = result.T.astype(BF16)
        first = i % n < n // 2

        @pl.when(first)
        def _():
            mine_ref[:, head_rows(h)] = low

        @pl.when(jnp.logical_not(first))
        def _():
            sib_ref[:, head_rows(h)] = low

    @pl.when(i < n)
    def _():
        def finish(states):
            for h in range(2):
                old = (old_ref[0, h : h + 1, :], old_ref[0, 2 + h : 3 + h, :],
                       old_acc_ref[head_rows(h), :])
                store(h, [old, states[h][0]])

        run_halves(chunk, qtn_ref, [far], [ptf_ref], finish)

    @pl.when(i >= n)
    def _():
        def finish(states):
            for h in range(2):
                store(h, states[h])

        run_halves(chunk, qtf_ref, [near, far], [ptn_ref, ptf_ref], finish)


def mine_block(i, n):
    half = n // 2
    return (i // n) * half + jnp.minimum(i % n, half - 1)


def sib_block(i, n):
    half = n // 2
    return jnp.maximum((i // n) * half + i % n - half, jnp.maximum((i // n) * half - 1, 0))


def attend_second(qtn, qtf, near, far, pt, state, acc, chunk):
    rows = qtn.shape[1]
    n = rows // ROWS
    near_col = pl.BlockSpec((256, ROWS), lambda i: (0, jnp.minimum(i, n - 1)))
    pairs = 6 * rows * rows
    return pl.pallas_call(
        partial(attend_second_kernel, chunk),
        out_shape=[
            jax.ShapeDtypeStruct(pt.shape, BF16),
            jax.ShapeDtypeStruct(pt.shape, BF16),
            jax.ShapeDtypeStruct((rows, 256), BF16),
            jax.ShapeDtypeStruct((rows, 256), BF16),
            jax.ShapeDtypeStruct((2 * n, 8, ROWS), F32),
        ],
        grid=(2 * n,),
        in_specs=[near_col, pl.BlockSpec((256, ROWS), lambda i: (0, jnp.maximum(i - n, 0)))]
        + [once(item.shape) for item in near + far]
        + [
            pl.BlockSpec((1, 8, ROWS), lambda i: (jnp.minimum(i, n - 1), 0, 0)),
            near_col,
            pl.BlockSpec(memory_space=pl.ANY),
        ],
        out_specs=[
            pl.BlockSpec((1, 2, rows, ROWS), lambda i: (jnp.maximum(i, n), 0, 0, 0)),
            pl.BlockSpec((1, 2, rows, ROWS), lambda i: (i, 0, 0, 0)),
            pl.BlockSpec((ROWS, 256), lambda i: (mine_block(i, n), 0)),
            pl.BlockSpec((ROWS, 256), lambda i: (sib_block(i, n), 0)),
            pl.BlockSpec((1, 8, ROWS), lambda i: (i, 0, 0)),
        ],
        input_output_aliases={10: 0},
        compiler_params=params(),
        cost_estimate=cost(4 * pairs * HEAD_DIM * 2, 2 * pairs, pairs),
        name="attend_rest",
    )(qtn, qtf, *near, *far, state, acc, pt)


def back_weights(do, o, factors):
    dot_t = do.astype(F32).T
    delta = jnp.sum(dot_t * o.astype(F32).T, axis=0, keepdims=True)
    found = []
    for factor in factors:
        scaled = dot_t * factor
        high, middle, low = three_parts(delta * factor)
        extra = extra_rows([-high, -middle, -low], HEAD_DIM)
        found.append(
            (jnp.concatenate([scaled.astype(BF16), extra], axis=0), scaled.T.astype(BF16))
        )
    return found


def back_half(chunk, h, grads, q_rows, pt_ref, v_ref, kt_ref, key_acc, value_acc):
    ones = jnp.where(
        lax.broadcasted_iota(jnp.int32, (chunk, HEAD_DIM), 1) < 3, F32(1.0), F32(0.0)
    ).astype(BF16)
    result = jnp.zeros((HEAD_DIM, q_rows.shape[0]), F32)
    for start in range(0, v_ref.shape[0], chunk):
        here = slice(start, start + chunk)
        prob = pt_ref[0, h, here, :]
        values = jnp.concatenate([v_ref[here, head_rows(h)], ones], axis=1)
        score = prob * mm(values, grads[0]).astype(BF16)
        value_acc[h, here, :] += mm(prob, grads[1])
        key_acc[h, here, :] += mm(score, q_rows)
        result = result + mm(kt_ref[head_rows(h), here], score)
    return result


def attend_back_kernel(
    chunk, da_ref, db_ref, oa_ref, ob_ref, stat_ref, qn_ref, qf_ref, ptn_ref, ptf_ref,
    vn, ktn, vf, ktf, dq_ref, dkv_ref, key_n, value_n, key_f, value_f,
):
    i = pl.program_id(0)
    n = pl.num_programs(0) // 2

    @pl.when(i == 0)
    def _():
        for ref in (key_n, value_n, key_f, value_f):
            ref[...] = jnp.zeros_like(ref)

    first = i % n < n // 2
    do = jnp.where(first, da_ref[...], db_ref[...])
    o = jnp.where(first, oa_ref[...], ob_ref[...])
    q = jnp.where(i < n, qn_ref[...], qf_ref[...])
    for h in range(2):
        cols = head_rows(h)
        near, far = back_weights(
            do[:, cols], o[:, cols], [stat_ref[0, h : h + 1, :], stat_ref[0, 2 + h : 3 + h, :]]
        )
        grad = back_half(chunk, h, near, q[:, cols], ptn_ref, vn, ktn, key_n, value_n)
        grad += back_half(chunk, h, far, q[:, cols], ptf_ref, vf, ktf, key_f, value_f)
        dq_ref[:, cols] = (grad * F32(1.0 / math.sqrt(HEAD_DIM))).T.astype(BF16)

    @pl.when(i == 2 * n - 1)
    def _():
        seq = vn.shape[0]
        for half, (keys, values) in enumerate(((key_n, value_n), (key_f, value_f))):
            for owner in range(2):
                source = slice(owner * seq // 2, (owner + 1) * seq // 2)
                begin = owner * seq + half * seq // 2
                rows = slice(begin, begin + seq // 2)
                for h in range(2):
                    dkv_ref[rows, head_rows(h)] = (keys[h, source] * F32(1.0 / LOG2E)).astype(BF16)
                    dkv_ref[rows, head_rows(2 + h)] = values[h, source].astype(BF16)


def attend_back(da, db, oa, ob, stat, qn, qf, ptn, ptf, vn, ktn, vf, ktf, chunk):
    rows = qn.shape[0]
    step = BACK_ROWS
    n = rows // step
    per = ROWS // step
    row = lambda f: pl.BlockSpec((step, 256), lambda i: (f(i), 0))
    tile = pl.BlockSpec((1, 2, rows, step), lambda i: (i // per, 0, 0, i % per))
    flat = jax.ShapeDtypeStruct((2 * rows, 256), BF16)
    wide = jax.ShapeDtypeStruct((2 * rows, 512), BF16)
    acc = pltpu.VMEM((2, rows, HEAD_DIM), F32)

    def own_first(i):
        return jnp.where(i % n < n // 2, 0, n // 2) + (i // n) * (n // 2) + i % n
    pairs = 8 * rows * rows
    return pl.pallas_call(
        partial(attend_back_kernel, chunk),
        out_shape=[flat, wide],
        grid=(2 * n,),
        in_specs=[
            row(lambda i: mine_block(i, n)),
            row(lambda i: sib_block(i, n)),
            row(lambda i: mine_block(i, n)),
            row(lambda i: sib_block(i, n)),
            pl.BlockSpec((1, 8, step), lambda i: (i // per, 0, i % per)),
            row(lambda i: jnp.minimum(i, n - 1)),
            row(lambda i: jnp.maximum(i - n, 0)),
            tile,
            tile,
        ]
        + [once(item.shape) for item in (vn, ktn, vf, ktf)],
        out_specs=[row(own_first), once(wide.shape)],
        scratch_shapes=[acc, acc, acc, acc],
        compiler_params=params(),
        cost_estimate=cost(8 * pairs * HEAD_DIM, 2 * pairs),
        name="attend_back",
    )(da, db, oa, ob, stat, qn, qf, ptn, ptf, vn, ktn, vf, ktf)


def mean(values):
    return jnp.mean(values, axis=-1, keepdims=True)


def norm(values):
    centered = values - mean(values)
    inverse = lax.rsqrt(mean(centered * centered) + EPS)
    return centered * inverse, inverse


def norm_back(incoming, normed, inverse, gain):
    scaled = incoming * gain
    return inverse * (scaled - mean(scaled) - normed * mean(scaled * normed))


def gelu_parts(v):
    bell = jnp.exp2(v * v * F32(-0.5 * LOG2E))
    base = 1.0 + F32(0.3275911 / math.sqrt(2.0)) * jnp.abs(v)
    t = pl.reciprocal(base, approx=True)
    t = t * (2.0 - base * t)
    series = t * (
        F32(0.5 * 0.254829592)
        + t
        * (
            F32(0.5 * -0.284496736)
            + t
            * (
                F32(0.5 * 1.421413741)
                + t * (F32(0.5 * -1.453152027) + t * F32(0.5 * 1.061405429))
            )
        )
    )
    tail = series * bell
    return bell * F32(1.0 / math.sqrt(2.0 * math.pi)), jnp.where(v >= 0, 1.0 - tail, tail)


def fold_rows(values):
    return jnp.sum(values.reshape(values.shape[0] // 8, 8, values.shape[1]), axis=0)


def rows_kernel(
    sizes, meta, xa_ref, xb_ref, oa_ref, ob_ref, cot_a, cot_b, p0, p1, p2, p3,
    u0, u1, u2, u3, vec_ref,
    prompt_near, data_near, prompt_far, data_far, resid_ref, da_ref, db_ref, send_ref,
    sums_ref, wo_ref, up_ref, down_ref, bias_ref, grad_acc, vec_acc, bias_acc,
):
    prompt_local, data_local = sizes
    i = pl.program_id(0)
    half = pl.num_programs(0) // 2
    here = i < half
    rows = xa_ref.shape[0]
    quarter = u0.shape[1]

    @pl.when(i == 0)
    def _():
        for j, (pack, up_part) in enumerate(((p0, u0), (p1, u1), (p2, u2), (p3, u3))):
            cols = slice(j * quarter, (j + 1) * quarter)
            wo_ref[head_rows(j), :] = pack[:HEAD_DIM, :]
            down_ref[cols, :] = pack[HEAD_DIM : HEAD_DIM + quarter, :]
            bias_ref[0:1, cols] = pack[
                HEAD_DIM + quarter : HEAD_DIM + quarter + 16, :quarter
            ].astype(F32)[0:1, :]
            up_ref[:, cols] = up_part[...]
        grad_acc[...] = jnp.zeros_like(grad_acc)
        vec_acc[...] = jnp.zeros_like(vec_acc)
        bias_acc[...] = jnp.zeros_like(bias_acc)

    slot = jnp.where(here, meta[0], meta[0] ^ 2)
    index = (i % half) * rows + lax.broadcasted_iota(jnp.int32, (rows, 1), 0) - prompt_local
    live = jnp.logical_or(index < 0, slot * data_local + index < meta[2])

    out_bias, attn_gain, attn_shift = vec_ref[0:1, :], vec_ref[1:2, :], vec_ref[2:3, :]
    down_bias, mlp_gain, mlp_shift = vec_ref[3:4, :], vec_ref[4:5, :], vec_ref[5:6, :]
    x = jnp.where(here, xa_ref[...], xb_ref[...])
    attended = jnp.concatenate([oa_ref[...], ob_ref[...]], axis=1)
    normed_one, inverse_one = norm(x.astype(F32) + (mm(attended, wo_ref[...]) + out_bias))
    hidden = normed_one * attn_gain + attn_shift
    hidden_low = hidden.astype(BF16)
    pre = mm(hidden_low, up_ref[...]) + bias_ref[0:1, :]
    density, share = gelu_parts(pre)
    activated = (pre * share).astype(BF16)
    slope = (share + pre * density).astype(BF16)
    mixed = hidden + (mm(activated, down_ref[...]) + down_bias)
    normed_two, inverse_two = norm(mixed)
    output = (normed_two * mlp_gain + mlp_shift).astype(BF16)
    cotangent = jnp.where(live, jnp.where(here, cot_a[...], cot_b[...]).astype(F32), 0.0)
    mixed_grad = norm_back(cotangent, normed_two, inverse_two, mlp_gain)
    mixed_low = mixed_grad.astype(BF16)
    pre_grad = mm(mixed_low, down_ref[...], NT).astype(BF16) * slope
    hidden_grad = mixed_grad + mm(pre_grad, up_ref[...], NT)
    resid_grad = norm_back(hidden_grad, normed_one, inverse_one, attn_gain)
    resid_ref[...] = resid_grad
    resid_low = resid_grad.astype(BF16)
    attended_grad = mm(resid_low, wo_ref[...], NT).astype(BF16)
    da_ref[...] = attended_grad[:, :256]
    db_ref[...] = attended_grad[:, 256:]

    up_grad = mm(hidden_low, pre_grad, TN)
    down_grad = mm(mixed_low, activated, TN)
    out_grad = mm(resid_low, attended, TN)
    for j in range(4):
        cols = slice(j * quarter, (j + 1) * quarter)
        grad_acc[j, :, :quarter] += up_grad[:, cols]
        grad_acc[j, :, quarter : 2 * quarter] += down_grad[:, cols]
        grad_acc[j, :, 2 * quarter :] += out_grad[:, head_rows(j)]
    bias_acc[...] += fold_rows(pre_grad.astype(F32))
    for place, value in enumerate(
        (
            resid_grad,
            hidden_grad * normed_one,
            hidden_grad,
            mixed_grad,
            cotangent * normed_two,
            cotangent,
        )
    ):
        vec_acc[place] += fold_rows(value)

    for j in range(2):
        split = max(0, min(rows, prompt_local - j * rows))
        for place, (prompt_ref, data_ref) in enumerate(
            ((prompt_near, data_near), (prompt_far, data_far))
        ):

            @pl.when(i == place * half + j)
            def _():
                if split:
                    prompt_ref[j * rows : j * rows + split, :] = output[:split]
                if split < rows:
                    begin = j * rows + split - prompt_local
                    data_ref[begin : begin + rows - split, :] = output[split:]

    @pl.when(i == pl.num_programs(0) - 1)
    def _():
        for place in range(6):
            sums_ref[place : place + 1, :] = jnp.sum(vec_acc[place], axis=0, keepdims=True)
        bias_grad = jnp.sum(bias_acc[...], axis=0, keepdims=True)
        per_row = bias_grad.shape[1] // 2 // quarter
        for g in range(4):
            found = jnp.zeros((1, quarter), F32)
            for j, flip in enumerate((0, 2, 1, 3)):
                piece = bias_grad[:, j * quarter : (j + 1) * quarter]
                found = jnp.where((meta[0] ^ flip) == g, piece, found)
            row, col = 6 + g // per_row, (g % per_row) * quarter
            sums_ref[row : row + 1, col : col + quarter] = found
        depth = send_ref.shape[1] - 16
        groups = send_ref.shape[0] // 4
        width, wide = sums_ref.shape[1], send_ref.shape[2]
        per = sums_ref.shape[0] * width // groups
        for g in range(groups):
            row, col = g * per // width, g * per % width
            part = jnp.pad(sums_ref[row : row + 1, col : col + per], ((0, 0), (0, wide - per)))
            high, low, _ = three_parts(part)
            extra = extra_rows([high, low], 16)
            for j, flip in enumerate((0, 2, 1, 3)):
                target = g * 4 + (meta[0] ^ flip)
                send_ref[target, :depth] = grad_acc[j, g * depth : (g + 1) * depth].astype(BF16)
                send_ref[target, depth:] = extra


def row_work(meta, xa, xb, oa, ob, cot, packs, ups, vec, sizes, groups):
    rows, width = xa.shape
    prompt_local, data_local = sizes
    step = 512
    n = rows // step
    quarter = ups[0].shape[1]
    hidden = 4 * quarter
    wide = 2 * quarter + HEAD_DIM
    send = (4 * groups, width // groups + 16, wide)
    near = pl.BlockSpec((step, width), lambda i, meta: (jnp.minimum(i, n - 1), 0))
    far = pl.BlockSpec((step, width), lambda i, meta: (jnp.maximum(i - n, 0), 0))
    row = lambda cols: pl.BlockSpec((step, cols), lambda i, meta: (i, 0))
    return pl.pallas_call(
        partial(rows_kernel, sizes),
        out_shape=[
            jax.ShapeDtypeStruct((prompt_local, width), BF16),
            jax.ShapeDtypeStruct((data_local, width), BF16),
            jax.ShapeDtypeStruct((prompt_local, width), BF16),
            jax.ShapeDtypeStruct((data_local, width), BF16),
            jax.ShapeDtypeStruct((2 * rows, width), F32),
            jax.ShapeDtypeStruct((2 * rows, 256), BF16),
            jax.ShapeDtypeStruct((2 * rows, 256), BF16),
            jax.ShapeDtypeStruct(send, BF16),
        ],
        grid_spec=pltpu.PrefetchScalarGridSpec(
            num_scalar_prefetch=1,
            grid=(2 * n,),
            in_specs=[near, far, row(256), row(256), near, far]
            + [once(item.shape) for item in packs + ups]
            + [once(vec.shape)],
            out_specs=[
                once((prompt_local, width)),
                once((data_local, width)),
                once((prompt_local, width)),
                once((data_local, width)),
                row(width),
                row(256),
                row(256),
                once(send),
            ],
            scratch_shapes=[
                pltpu.VMEM((8, width), F32),
                pltpu.VMEM((4 * HEAD_DIM, width), BF16),
                pltpu.VMEM((width, hidden), BF16),
                pltpu.VMEM((hidden, width), BF16),
                pltpu.VMEM((8, hidden), F32),
                pltpu.VMEM((4, width, wide), F32),
                pltpu.VMEM((6, 8, width), F32),
                pltpu.VMEM((8, hidden), F32),
            ],
        ),
        compiler_params=params(),
        cost_estimate=cost(
            3 * 2 * 2 * rows * width * (width + 2 * hidden), 24 * rows * width, 4 * rows * hidden
        ),
        name="row_work",
    )(meta, xa, xb, oa, ob, *cot, *packs, *ups, vec)


def on_device(
    data_rows,
    prompt_rows,
    context_rows,
    test_rows,
    qkv_weight,
    out_bias,
    out_weight,
    attn_gain,
    attn_shift,
    up_weight,
    up_bias,
    down_weight,
    down_bias,
    mlp_gain,
    mlp_shift,
    data_cotangent,
    prompt_cotangent,
):
    data_local = data_rows.shape[1]
    prompt_local = prompt_rows.shape[0]
    width = prompt_rows.shape[1]
    quarter = up_weight.shape[1]
    sizes = (prompt_local, data_local)
    groups = lax.axis_size("ep")
    t = lax.axis_index("tp")
    mine = t >> 1
    other = 1 - mine

    def across(value):
        return lax.ppermute(value, "tp", [(i, i ^ 2) for i in range(4)])

    def beside(value):
        return lax.ppermute(value, "tp", [(i, i ^ 1) for i in range(4)])

    def pick(values, which):
        return lax.dynamic_index_in_dim(values, which, axis=0, keepdims=False)

    def stack(prompt_part, data_part):
        return jnp.concatenate([prompt_part, data_part], axis=0)

    w_far = across(qkv_weight)
    x_far = across(stack(prompt_rows, pick(data_rows, other)))
    x = stack(prompt_rows, pick(data_rows, mine))
    x_sib = beside(x)
    context = pick(context_rows, mine)
    live = context + pick(test_rows, mine)
    meta = jnp.stack([t, context, live]).astype(jnp.int32)

    qtn, qn, kn, kxn, ktn, vn, vtn, w = project(meta, x, x_sib, qkv_weight, w_far, sizes, 0)
    ptn, state, state_acc = attend_first(qtn, (kn, kxn, vtn), 512)

    bias_rows = jnp.pad(up_bias[None], ((0, 15), (0, width - quarter)))
    pack = jnp.concatenate([out_weight, down_weight, bias_rows], axis=0)
    x_far, state, pack, up_weight, x_late, x_sib_late = lax.optimization_barrier(
        (x_far, state, pack, up_weight, x, x_sib)
    )
    x_far_sib = beside(x_far)
    pack_far, up_far = across(pack), across(up_weight)
    cot_far = stack(pick(prompt_cotangent, other), pick(data_cotangent, other))
    x_far_sib, cot_far = lax.optimization_barrier((x_far_sib, cot_far))
    cot_far = across(cot_far)
    qtf, qf, kf, kxf, ktf, vf, vtf, _ = project(meta, x_far, x_far_sib, qkv_weight, w_far, sizes, 2)
    x_all = jnp.concatenate([x_late, x_far, x_sib_late, x_far_sib], axis=0)
    pack_far, up_far, x_all, qtf = lax.optimization_barrier((pack_far, up_far, x_all, qtf))
    ptn, ptf, oa, ob, stat = attend_second(
        qtn, qtf, (kn, kxn, vtn), (kf, kxf, vtf), ptn, state, state_acc, 512
    )

    ob_send, cot_far = lax.optimization_barrier((ob, cot_far))
    cot = stack(pick(prompt_cotangent, mine), pick(data_cotangent, mine))
    packs = [pack, pack_far, beside(pack), beside(pack_far)]
    ups = [up_weight, up_far, beside(up_weight), beside(up_far)]
    vec = jnp.stack(
        [out_bias, attn_gain, attn_shift, down_bias, mlp_gain, mlp_shift, mlp_shift, mlp_shift]
    ).astype(F32)
    (prompt_near, data_near, prompt_far, data_far, resid, da, db, send) = row_work(
        meta, x, x_far, oa, beside(ob_send), (cot, cot_far), packs, ups, vec, sizes, groups
    )

    def dot(left, right, dims):
        return lax.dot_general(left, right, dims, preferred_element_type=F32)

    def exchange(parts, axes):
        return lax.all_to_all(parts, axes, 0, 0, tiled=True)

    def gather(part):
        return exchange(jnp.broadcast_to(part[None], (groups,) + part.shape), "ep")

    db = beside(db)
    send = exchange(send, ("ep", "tp"))
    prompt_back, data_back = across(prompt_far), across(data_far)

    dq, dkv = attend_back(
        da, db, oa, ob, stat, qn, qf, ptn, ptf, vn, ktn, vf, ktf, 512
    )
    send, prompt_back, data_back, dq = lax.optimization_barrier((send, prompt_back, data_back, dq))
    depth = width // groups
    total = jnp.sum(send.astype(F32), axis=0)
    part = total[depth : depth + 1] + total[depth + 1 : depth + 2]
    high = lax.optimization_barrier(part.astype(BF16))
    low = (part - high.astype(F32)).astype(BF16)
    total = jnp.concatenate(
        [total[:depth].astype(BF16), high, low, jnp.zeros((14, total.shape[1]), BF16)], axis=0
    )
    total = jnp.broadcast_to(total[None], (groups,) + total.shape)
    total, dq, dkv = lax.optimization_barrier((total, dq, dkv))
    total = exchange(total, "ep")

    slot_rows = prompt_local + data_local
    cut = 2 * slot_rows
    wq, wkv = w[:, :256], w[:, 256:]

    def rows_grad(part):
        return dot(dq[part], wq, NT) + dot(dkv[part], wkv, NT)

    grad_q, grad_kv = dot(x_all, dq, TN), dot(x_all, dkv, TN)

    def head_grad(h):
        return jnp.stack(
            [grad_q[:, head_rows(h)], grad_kv[:, head_rows(h)], grad_kv[:, head_rows(2 + h)]]
        )

    other_grad, dq, dkv = lax.optimization_barrier((head_grad(1).astype(BF16), dq, dkv))
    other_grad = across(other_grad)
    sib = rows_grad(slice(cut, None)).astype(BF16)
    sib, dq, dkv = lax.optimization_barrier((sib, dq, dkv))
    sib = beside(sib)
    own = rows_grad(slice(0, cut)) + resid
    total, other_grad, own = lax.optimization_barrier((total, other_grad, own))
    far_rows = (own[slot_rows:] + sib[slot_rows:].astype(F32)).astype(BF16)
    near_rows = own[:slot_rows] + sib[:slot_rows].astype(F32)
    near_data = near_rows[prompt_local:].astype(BF16)

    columns = width // HEAD_DIM
    qkv = (head_grad(0) + other_grad.astype(F32)).astype(BF16).reshape(groups, -1, HEAD_DIM)
    qkv_rows = qkv.shape[1]
    qkv, far_rows = lax.optimization_barrier((qkv, far_rows))
    far_prompt = across(far_rows[:prompt_local])
    far_data = across(far_rows[prompt_local:])
    qkv = jnp.sum(exchange(qkv, "ep").astype(F32), axis=0).astype(BF16)
    prompt = near_rows[:prompt_local] + far_prompt.astype(F32)
    prompt = prompt.astype(BF16).reshape(groups, prompt_local // groups, width)
    prompt = jnp.sum(exchange(prompt, "ep").astype(F32), axis=0).astype(BF16)
    prompt = jnp.concatenate([prompt[:, head_rows(j)] for j in range(columns)], axis=0)
    last = gather(jnp.concatenate([qkv, prompt], axis=0))
    qkv = last[:, :qkv_rows].reshape(3, width, HEAD_DIM).astype(F32)
    prompt = last[:, qkv_rows:].reshape(groups, columns, prompt_local // groups, HEAD_DIM)
    prompt_grad = jnp.concatenate([prompt[:, j] for j in range(columns)], axis=2)
    prompt_grad = prompt_grad.reshape(prompt_local, width).astype(F32)

    which = lax.broadcasted_iota(jnp.int32, (2, 1, 1), 0)

    def by_episode(own, received):
        return jnp.where(which == mine, own[None], received[None])

    sums = total[:, depth : depth + 2, : 8 * width // groups].astype(F32)
    sums = (sums[:, 0] + sums[:, 1]).reshape(8, width)
    total = total[:, :depth].reshape(width, -1).astype(F32)
    bias_grad = lax.dynamic_slice_in_dim(sums[6:8].reshape(-1), t * quarter, quarter)
    return (
        by_episode(data_near, data_back),
        by_episode(prompt_near, prompt_back),
        by_episode(near_data, far_data),
        prompt_grad,
        qkv,
        sums[0],
        total[:, 2 * quarter :].T,
        sums[1],
        sums[2],
        total[:, :quarter],
        bias_grad,
        total[:, quarter : 2 * quarter].T,
        sums[3],
        sums[4],
        sums[5],
    )


def solution(mesh):
    return jax.shard_map(
        on_device,
        mesh=mesh,
        in_specs=(
            P("ep", "tp", None),
            P("tp", None),
            P("ep"),
            P("ep"),
            P(None, None, "tp"),
            P(),
            P("tp", None),
            P(),
            P(),
            P(None, "tp"),
            P("tp"),
            P("tp", None),
            P(),
            P(),
            P(),
            P("ep", "tp", None),
            P("ep", "tp", None),
        ),
        out_specs=(
            P("ep", "tp", None),
            P("ep", "tp", None),
            P("ep", "tp", None),
            P("tp", None),
            P(None, None, "tp"),
            P(),
            P("tp", None),
            P(),
            P(),
            P(None, "tp"),
            P("tp"),
            P("tp", None),
            P(),
            P(),
            P(),
        ),
        check_vma=False,
    )
```

```python
from functools import partial
import math

import jax
import jax.numpy as jnp
from jax import lax
from jax.experimental import pallas as pl
from jax.experimental.pallas import tpu as pltpu
from jax.sharding import PartitionSpec as P

HEAD_DIM = 128
ROWS = 512
BACK_ROWS = 256
ROW_STEP = 1024
SAMPLE = 256
EPS = 1e-05
MASKED = -1e30
LOG2E = math.log2(math.e)
LIMIT = 2.0**60
VMEM = 60 * 1024 * 1024
F32 = jnp.float32
BF16 = jnp.bfloat16
NN = (((1,), (0,)), ((), ()))
NT = (((1,), (1,)), ((), ()))
TN = (((0,), (0,)), ((), ()))


def mm(left, right, dims=NN):
    return lax.dot_general(left, right, dims, preferred_element_type=F32)


def params(**more):
    return pltpu.CompilerParams(vmem_limit_bytes=VMEM, **more)


def cost(flops, nbytes, trans=0):
    return pl.CostEstimate(
        flops=int(flops), bytes_accessed=int(nbytes), transcendentals=int(trans)
    )


def once(shape):
    return pl.BlockSpec(shape, lambda *_: (0,) * len(shape), pipeline_mode=pl.Buffered(1))


def extra_rows(values, count):
    width = values[0].shape[1]
    row = lax.broadcasted_iota(jnp.int32, (count, width), 0)
    out = jnp.zeros((count, width), F32)
    for index, value in enumerate(values):
        out = jnp.where(row == index, value, out)
    return out.astype(BF16)


def three_parts(row):
    high = row.astype(BF16).astype(F32)
    middle = (row - high).astype(BF16).astype(F32)
    return high, middle, row - high - middle


def clamp(i, low, high):
    return jnp.minimum(jnp.maximum(i, low), high)


def project_kernel(sizes, flip, meta, xa_ref, xb_ref, wa_ref, wb_ref, *refs):
    refs = refs[1:] if flip else refs
    qt_ref, q_ref, k_ref, kx_ref, kt_ref, v_ref, vt_ref, w_ref, all_ref, wt_ref = refs
    prompt_local, data_local = sizes
    i = pl.program_id(0)
    per_slot = pl.num_programs(0) // 2
    rows = xa_ref.shape[0]

    @pl.when(i == 0)
    def _():
        for which in range(3):
            for h, source in enumerate((wa_ref, wb_ref)):
                cols = slice(which * 256 + h * HEAD_DIM, which * 256 + (h + 1) * HEAD_DIM)
                w_ref[:, cols] = source[which]
                wt_ref[cols, :] = source[which].T

    x = jnp.where(i < per_slot, xa_ref[...], xb_ref[...])
    all_ref[...] = x
    slot = jnp.where(i < per_slot, meta[0] ^ flip, meta[0] ^ flip ^ 1)
    row = lax.broadcasted_iota(jnp.int32, (rows, HEAD_DIM), 0)
    lane = lax.broadcasted_iota(jnp.int32, (rows, HEAD_DIM), 1)
    index = (i % per_slot) * rows + row - prompt_local
    attended = jnp.logical_or(index < 0, slot * data_local + index < meta[1])
    bias = jnp.where(attended, F32(0.0), F32(MASKED))
    ones = jnp.where(lane < 4, F32(1.0), F32(0.0))
    kx_ref[...] = jnp.where(lane == 0, bias, ones).astype(BF16)
    factor = F32(LOG2E / math.sqrt(HEAD_DIM))
    z = mm(x, w_ref[...])
    q_ref[...] = (z[:, :256] * factor).astype(BF16)
    k_ref[...] = z[:, 256:512].astype(BF16)
    v_ref[...] = z[:, 512:].astype(BF16)
    zt = mm(wt_ref[...], x, NT)
    qt_ref[...] = (zt[:256] * factor).astype(BF16)
    kt_ref[...] = zt[256:512].astype(BF16)
    vt_ref[...] = zt[512:].astype(BF16)


def project(meta, xa, xb, wa, wb, sizes, flip, joined=None):
    rows, width = xa.shape
    step = 512
    n = rows // step
    flat = jax.ShapeDtypeStruct((2 * rows, 256), BF16)
    tall = jax.ShapeDtypeStruct((256, 2 * rows), BF16)
    row = pl.BlockSpec((step, 256), lambda i, meta: (i, 0))
    col = pl.BlockSpec((256, step), lambda i, meta: (0, i))
    extra = [joined] if flip else []

    def own_first(i):
        return (i // n) * 2 * n + (n if flip else 0) + i % n

    return pl.pallas_call(
        partial(project_kernel, sizes, flip),
        out_shape=[
            tall,
            flat,
            flat,
            jax.ShapeDtypeStruct((2 * rows, HEAD_DIM), BF16),
            tall,
            flat,
            tall,
            jax.ShapeDtypeStruct((width, 768), BF16),
            jax.ShapeDtypeStruct((4 * rows, width), BF16),
        ],
        grid_spec=pltpu.PrefetchScalarGridSpec(
            num_scalar_prefetch=1,
            grid=(2 * n,),
            in_specs=[
                pl.BlockSpec((step, width), lambda i, meta: (jnp.minimum(i, n - 1), 0)),
                pl.BlockSpec((step, width), lambda i, meta: (jnp.maximum(i - n, 0), 0)),
                once(wa.shape),
                once(wb.shape),
            ]
            + [pl.BlockSpec(memory_space=pl.ANY)] * len(extra),
            out_specs=[
                col,
                row,
                row,
                pl.BlockSpec((step, HEAD_DIM), lambda i, meta: (i, 0)),
                col,
                row,
                col,
                once((width, 768)),
                pl.BlockSpec((step, width), lambda i, meta: (own_first(i), 0)),
            ],
            scratch_shapes=[pltpu.VMEM((768, width), BF16)],
        ),
        input_output_aliases={5: 8} if flip else {},
        compiler_params=params(),
        cost_estimate=cost(4 * 2 * rows * width * 768, 2 * rows * width * 8),
        name="project",
    )(meta, xa, xb, wa, wb, *extra)


def head_rows(h):
    return slice(h * HEAD_DIM, (h + 1) * HEAD_DIM)


def with_shift(qt, top):
    high, middle, low = three_parts(top)
    extra = extra_rows([jnp.ones_like(top), -high, -middle, -low], HEAD_DIM)
    return jnp.concatenate([qt, extra], axis=0)


def half_scores(chunk, h, qa, start, k_ref, kx_ref):
    here = pl.ds(start, chunk)
    keys = jnp.concatenate([k_ref[here, head_rows(h)], kx_ref[here, :]], axis=1)
    return mm(keys, qa)


def half_part(h, start, scores, vt_ref, pt_ref):
    chunk = scores.shape[0]
    weight = jnp.exp2(scores)
    total = jnp.sum(weight.reshape(chunk // 8, 8, weight.shape[1]), axis=0)
    low = weight.astype(BF16)
    pt_ref[0, h, pl.ds(start, chunk), :] = low
    return total, mm(vt_ref[head_rows(h), pl.ds(start, chunk)], low)


def stale_shift(h, qt, k_ref):
    top = jnp.max(mm(k_ref[:SAMPLE, head_rows(h)], qt), axis=0, keepdims=True)
    return top, with_shift(qt, top)


def fast_states(chunk, shifts, keys, pts):
    tiles = [
        (h, j, start)
        for h in range(2)
        for j in range(len(keys))
        for start in range(0, keys[0][0].shape[0], chunk)
    ]

    def scores(tile):
        h, j, start = tile
        return half_scores(chunk, h, shifts[h][j][1], start, keys[j][0], keys[j][1])

    sums = {}
    ahead = scores(tiles[0])
    for place, (h, j, start) in enumerate(tiles):
        now = ahead
        if place + 1 < len(tiles):
            ahead = scores(tiles[place + 1])
        total, product = half_part(h, start, now, keys[j][2], pts[j])
        if (h, j) in sums:
            total, product = sums[h, j][0] + total, sums[h, j][1] + product
        sums[h, j] = total, product
    return [
        [
            (shifts[h][j][0], jnp.sum(sums[h, j][0], axis=0, keepdims=True), sums[h, j][1])
            for j in range(len(keys))
        ]
        for h in range(2)
    ]


def half_attend_exact(chunk, h, shift, k_ref, kx_ref, vt_ref, pt_ref):
    qt = shift[1][:HEAD_DIM]
    width = qt.shape[1]
    count = k_ref.shape[0] // chunk
    qa = with_shift(qt, jnp.zeros((1, width), F32))

    def find(j, top):
        found = half_scores(chunk, h, qa, pl.multiple_of(j * chunk, chunk), k_ref, kx_ref)
        return jnp.maximum(top, jnp.max(found, axis=0, keepdims=True))

    top = lax.fori_loop(0, count, find, jnp.full((1, width), MASKED, F32))
    qa = with_shift(qt, top)

    def add(j, state):
        start = pl.multiple_of(j * chunk, chunk)
        found = half_scores(chunk, h, qa, start, k_ref, kx_ref)
        more, product = half_part(h, start, found, vt_ref, pt_ref)
        return state[0] + more, state[1] + product

    total, acc = lax.fori_loop(
        0, count, add, (jnp.zeros((8, width), F32), jnp.zeros((HEAD_DIM, width), F32))
    )
    return top, jnp.sum(total, axis=0, keepdims=True), acc


def merge(states):
    top = states[0][0]
    for state in states[1:]:
        top = jnp.maximum(top, state[0])
    scales = [jnp.exp2(state[0] - top) for state in states]
    total = sum(state[1] * scale for state, scale in zip(states, scales))
    factors = [scale / total for scale in scales]
    return factors, sum(state[2] * factor for state, factor in zip(states, factors))


def redo(states, shifts, keys, pts):
    return [
        [half_attend_exact(256, h, shifts[h][j], *keys[j], pts[j]) for j in range(len(keys))]
        for h in range(2)
    ]


def run_halves(chunk, qt_ref, keys, pts, finish):
    shifts = [
        [stale_shift(h, qt_ref[head_rows(h), :], key_refs[0]) for key_refs in keys]
        for h in range(2)
    ]
    states = fast_states(chunk, shifts, keys, pts)
    worst = None
    for state in states[0] + states[1]:
        worst = state[1] if worst is None else jnp.maximum(worst, state[1])
    finish(states)

    @pl.when(jnp.logical_not(jnp.max(worst) <= LIMIT))
    def _():
        finish(redo(states, shifts, keys, pts))


def attend_first_kernel(chunk, qt_ref, k_ref, kx_ref, vt_ref, pt_ref, state_ref, acc_ref):
    def finish(states):
        for h in range(2):
            top, total, acc = states[h][0]
            state_ref[0, h : h + 1, :] = top
            state_ref[0, 2 + h : 3 + h, :] = total
            acc_ref[head_rows(h), :] = acc

    run_halves(chunk, qt_ref, [(k_ref, kx_ref, vt_ref)], [pt_ref], finish)


def attend_first(qt, key, chunk):
    rows = qt.shape[1]
    n = rows // ROWS
    col = pl.BlockSpec((256, ROWS), lambda i: (0, i))
    pairs = 2 * rows * rows
    return pl.pallas_call(
        partial(attend_first_kernel, chunk),
        out_shape=[
            jax.ShapeDtypeStruct((2 * n, 2, rows, ROWS), BF16),
            jax.ShapeDtypeStruct((n, 8, ROWS), F32),
            jax.ShapeDtypeStruct((256, rows), F32),
        ],
        grid=(n,),
        in_specs=[col] + [once(item.shape) for item in key],
        out_specs=[
            pl.BlockSpec((1, 2, rows, ROWS), lambda i: (i, 0, 0, 0)),
            pl.BlockSpec((1, 8, ROWS), lambda i: (i, 0, 0)),
            col,
        ],
        compiler_params=params(),
        cost_estimate=cost(4 * pairs * HEAD_DIM * 2, 2 * pairs, pairs),
        name="attend_near",
    )(qt, *key)


def attend_last_kernel(chunk, halves, qt_ref, *refs):
    keys = [refs[3 * j : 3 * j + 3] for j in range(halves)]
    refs = refs[3 * halves :]
    old_ref, old_acc_ref = refs[:2] if halves == 1 else (None, None)
    refs = refs[2:]
    pts, (mine_ref, sib_ref, stat_ref) = refs[:halves], refs[halves:]
    i = pl.program_id(0)

    def finish(states):
        for h in range(2):
            parts = states[h]
            if halves == 1:
                old = (old_ref[0, h : h + 1, :], old_ref[0, 2 + h : 3 + h, :],
                       old_acc_ref[head_rows(h), :])
                parts = [old] + parts
            factors, result = merge(parts)
            stat_ref[0, h : h + 1, :] = factors[0]
            stat_ref[0, 2 + h : 3 + h, :] = factors[1]
            low = result.T.astype(BF16)
            first = i < pl.num_programs(0) // 2

            @pl.when(first)
            def _():
                mine_ref[:, head_rows(h)] = low

            @pl.when(jnp.logical_not(first))
            def _():
                sib_ref[:, head_rows(h)] = low

    run_halves(chunk, qt_ref, keys, pts, finish)


def mine_block(i, n):
    half = n // 2
    return (i // n) * half + jnp.minimum(i % n, half - 1)


def sib_block(i, n):
    half = n // 2
    return jnp.maximum((i // n) * half + i % n - half, jnp.maximum((i // n) * half - 1, 0))


def attend_last(qt, keys, given, chunk):
    rows = qt.shape[1]
    n = rows // ROWS
    half = n // 2
    first = len(keys) == 1
    col = pl.BlockSpec((256, ROWS), lambda i: (0, i))
    stat = pl.BlockSpec((1, 8, ROWS), lambda i: (i, 0, 0))
    tile = pl.BlockSpec((1, 2, rows, ROWS), lambda i: (i if first else i + n, 0, 0, 0))
    flat = [item for key in keys for item in key]
    pairs = 2 * rows * rows * len(keys)
    return pl.pallas_call(
        partial(attend_last_kernel, chunk, len(keys)),
        out_shape=[jax.ShapeDtypeStruct((2 * n, 2, rows, ROWS), BF16)] * len(keys)
        + [jax.ShapeDtypeStruct((rows // 2, 256), BF16)] * 2
        + [jax.ShapeDtypeStruct((n, 8, ROWS), F32)],
        grid=(n,),
        in_specs=[col]
        + [once(item.shape) for item in flat]
        + ([stat, col] if first else [pl.BlockSpec(memory_space=pl.ANY)] * 2),
        out_specs=[tile] * len(keys)
        + [
            pl.BlockSpec((ROWS, 256), lambda i: (jnp.minimum(i, half - 1), 0)),
            pl.BlockSpec((ROWS, 256), lambda i: (jnp.maximum(i - half, 0), 0)),
            stat,
        ],
        input_output_aliases={} if first else {7: 0, 8: 1},
        compiler_params=params(),
        cost_estimate=cost(4 * pairs * HEAD_DIM * 2, 2 * pairs, pairs),
        name="attend_last",
    )(qt, *flat, *given)


def back_weights(do, o, factors):
    dot_t = do.astype(F32).T
    delta = jnp.sum(dot_t * o.astype(F32).T, axis=0, keepdims=True)
    found = []
    for factor in factors:
        scaled = dot_t * factor
        high, middle, low = three_parts(delta * factor)
        extra = extra_rows([-high, -middle, -low], HEAD_DIM)
        found.append(
            (jnp.concatenate([scaled.astype(BF16), extra], axis=0), scaled.T.astype(BF16))
        )
    return found


def back_half(chunk, h, grads, q_rows, pt_ref, v_ref, kt_ref, key_acc, value_acc):
    ones = jnp.where(
        lax.broadcasted_iota(jnp.int32, (chunk, HEAD_DIM), 1) < 3, F32(1.0), F32(0.0)
    ).astype(BF16)
    result = jnp.zeros((HEAD_DIM, q_rows.shape[0]), F32)
    for start in range(0, v_ref.shape[0], chunk):
        here = slice(start, start + chunk)
        prob = pt_ref[0, h, here, :]
        values = jnp.concatenate([v_ref[here, head_rows(h)], ones], axis=1)
        score = (prob.astype(F32) * mm(values, grads[0])).astype(BF16)
        value_acc[h, here, :] += mm(prob, grads[1])
        key_acc[h, here, :] += mm(score, q_rows)
        result = result + mm(kt_ref[head_rows(h), here], score)
    return result


def attend_back_kernel(
    chunk, da_ref, db_ref, on_a, on_b, of_a, of_b, statn, statf, qn_ref, qf_ref, ptn_ref, ptf_ref,
    vn, ktn, vf, ktf, dq_ref, dkv_ref, key_n, value_n, key_f, value_f,
):
    i = pl.program_id(0)
    n = pl.num_programs(0) // 2

    @pl.when(i == 0)
    def _():
        for ref in (key_n, value_n, key_f, value_f):
            ref[...] = jnp.zeros_like(ref)

    first = i % n < n // 2
    do = jnp.where(first, da_ref[...], db_ref[...])
    near_rows = i < n
    o = jnp.where(
        near_rows,
        jnp.where(first, on_a[...], on_b[...]),
        jnp.where(first, of_a[...], of_b[...]),
    )
    stat = jnp.where(near_rows, statn[0], statf[0])
    q = jnp.where(i < n, qn_ref[...], qf_ref[...])
    for h in range(2):
        cols = head_rows(h)
        near, far = back_weights(
            do[:, cols], o[:, cols], [stat[h : h + 1, :], stat[2 + h : 3 + h, :]]
        )
        grad = back_half(chunk, h, near, q[:, cols], ptn_ref, vn, ktn, key_n, value_n)
        grad += back_half(chunk, h, far, q[:, cols], ptf_ref, vf, ktf, key_f, value_f)
        dq_ref[:, cols] = (grad * F32(1.0 / math.sqrt(HEAD_DIM))).T.astype(BF16)

    @pl.when(i == 2 * n - 1)
    def _():
        seq = vn.shape[0]
        for half, (keys, values) in enumerate(((key_n, value_n), (key_f, value_f))):
            for owner in range(2):
                source = slice(owner * seq // 2, (owner + 1) * seq // 2)
                begin = owner * seq + half * seq // 2
                rows = slice(begin, begin + seq // 2)
                for h in range(2):
                    dkv_ref[rows, head_rows(h)] = (keys[h, source] * F32(1.0 / LOG2E)).astype(BF16)
                    dkv_ref[rows, head_rows(2 + h)] = values[h, source].astype(BF16)


def attend_back(da, db, results, stats, qn, qf, ptn, ptf, vn, ktn, vf, ktf, chunk):
    rows = qn.shape[0]
    step = BACK_ROWS
    n = rows // step
    per = ROWS // step
    row = lambda f: pl.BlockSpec((step, 256), lambda i: (f(i), 0))
    half = n // 2
    factor = lambda f: pl.BlockSpec((1, 8, step), lambda i: (f(i) // per, 0, f(i) % per))
    tile = pl.BlockSpec((1, 2, rows, step), lambda i: (i // per, 0, 0, i % per))
    flat = jax.ShapeDtypeStruct((2 * rows, 256), BF16)
    wide = jax.ShapeDtypeStruct((2 * rows, 512), BF16)
    acc = pltpu.VMEM((2, rows, HEAD_DIM), F32)

    def own_first(i):
        return jnp.where(i % n < n // 2, 0, n // 2) + (i // n) * (n // 2) + i % n
    pairs = 8 * rows * rows
    return pl.pallas_call(
        partial(attend_back_kernel, chunk),
        out_shape=[flat, wide],
        grid=(2 * n,),
        in_specs=[
            row(lambda i: mine_block(i, n)),
            row(lambda i: sib_block(i, n)),
        ]
        + [row(lambda i, j=j: clamp(i - j * half, 0, half - 1)) for j in range(4)]
        + [
            factor(lambda i: jnp.minimum(i, n - 1)),
            factor(lambda i: jnp.maximum(i - n, 0)),
            row(lambda i: jnp.minimum(i, n - 1)),
            row(lambda i: jnp.maximum(i - n, 0)),
            tile,
            tile,
        ]
        + [once(item.shape) for item in (vn, ktn, vf, ktf)],
        out_specs=[row(own_first), once(wide.shape)],
        scratch_shapes=[acc, acc, acc, acc],
        compiler_params=params(),
        cost_estimate=cost(8 * pairs * HEAD_DIM, 2 * pairs),
        name="attend_back",
    )(da, db, *results, *stats, qn, qf, ptn, ptf, vn, ktn, vf, ktf)


def mean(values):
    return jnp.mean(values, axis=-1, keepdims=True)


def norm(values):
    centered = values - mean(values)
    inverse = lax.rsqrt(mean(centered * centered) + EPS)
    return centered * inverse, inverse


def norm_back(incoming, normed, inverse, gain):
    scaled = incoming * gain
    return inverse * (scaled - mean(scaled) - normed * mean(scaled * normed))


def gelu_parts(v):
    bell = jnp.exp2(v * v * F32(-0.5 * LOG2E))
    base = 1.0 + F32(0.3275911 / math.sqrt(2.0)) * jnp.abs(v)
    t = pl.reciprocal(base, approx=True)
    t = t * (2.0 - base * t)
    series = t * (
        F32(0.5 * 0.254829592)
        + t
        * (
            F32(0.5 * -0.284496736)
            + t
            * (
                F32(0.5 * 1.421413741)
                + t * (F32(0.5 * -1.453152027) + t * F32(0.5 * 1.061405429))
            )
        )
    )
    tail = series * bell
    return bell * F32(1.0 / math.sqrt(2.0 * math.pi)), jnp.where(v >= 0, 1.0 - tail, tail)


def fold_rows(values):
    return jnp.sum(values.reshape(values.shape[0] // 8, 8, values.shape[1]), axis=0)


def rows_kernel(
    sizes, meta, xa_ref, xb_ref, oa_n, oa_f, ob_n, ob_f, cot_a, cot_b, p0, p1, p2, p3,
    u0, u1, u2, u3, vec_ref,
    prompt_near, data_near, prompt_far, data_far, resid_ref, da_ref, db_ref, send_ref,
    sums_ref, wo_ref, up_ref, down_ref, bias_ref, grad_acc, vec_acc, bias_acc,
):
    prompt_local, data_local = sizes
    i = pl.program_id(0)
    half = pl.num_programs(0) // 2
    here = i < half
    rows = xa_ref.shape[0]
    quarter = u0.shape[1]

    @pl.when(i == 0)
    def _():
        for j, (pack, up_part) in enumerate(((p0, u0), (p1, u1), (p2, u2), (p3, u3))):
            cols = slice(j * quarter, (j + 1) * quarter)
            wo_ref[head_rows(j), :] = pack[:HEAD_DIM, :]
            down_ref[cols, :] = pack[HEAD_DIM : HEAD_DIM + quarter, :]
            bias_ref[0:1, cols] = pack[
                HEAD_DIM + quarter : HEAD_DIM + quarter + 16, :quarter
            ].astype(F32)[0:1, :]
            up_ref[:, cols] = up_part[...]
        grad_acc[...] = jnp.zeros_like(grad_acc)
        vec_acc[...] = jnp.zeros_like(vec_acc)
        bias_acc[...] = jnp.zeros_like(bias_acc)

    slot = jnp.where(here, meta[0], meta[0] ^ 2)
    index = (i % half) * rows + lax.broadcasted_iota(jnp.int32, (rows, 1), 0) - prompt_local
    live = jnp.logical_or(index < 0, slot * data_local + index < meta[2])

    out_bias, attn_gain, attn_shift = vec_ref[0:1, :], vec_ref[1:2, :], vec_ref[2:3, :]
    down_bias, mlp_gain, mlp_shift = vec_ref[3:4, :], vec_ref[4:5, :], vec_ref[5:6, :]
    x = jnp.where(here, xa_ref[...], xb_ref[...])
    attended = jnp.concatenate(
        [jnp.where(here, oa_n[...], oa_f[...]), jnp.where(here, ob_n[...], ob_f[...])], axis=1
    )
    normed_one, inverse_one = norm(x.astype(F32) + (mm(attended, wo_ref[...]) + out_bias))
    hidden = normed_one * attn_gain + attn_shift
    hidden_low = hidden.astype(BF16)
    pre = mm(hidden_low, up_ref[...]) + bias_ref[0:1, :]
    density, share = gelu_parts(pre)
    activated = (pre * share).astype(BF16)
    slope = share + pre * density
    mixed = hidden + (mm(activated, down_ref[...]) + down_bias)
    normed_two, inverse_two = norm(mixed)
    output = (normed_two * mlp_gain + mlp_shift).astype(BF16)
    cotangent = jnp.where(live, jnp.where(here, cot_a[...], cot_b[...]).astype(F32), 0.0)
    mixed_grad = norm_back(cotangent, normed_two, inverse_two, mlp_gain)
    mixed_low = mixed_grad.astype(BF16)
    pre_grad = (mm(mixed_low, down_ref[...], NT) * slope).astype(BF16)
    hidden_grad = mixed_grad + mm(pre_grad, up_ref[...], NT)
    resid_grad = norm_back(hidden_grad, normed_one, inverse_one, attn_gain)
    resid_ref[...] = resid_grad
    resid_low = resid_grad.astype(BF16)
    attended_grad = mm(resid_low, wo_ref[...], NT).astype(BF16)
    da_ref[...] = attended_grad[:, :256]
    db_ref[...] = attended_grad[:, 256:]

    up_grad = mm(hidden_low, pre_grad, TN)
    down_grad = mm(mixed_low, activated, TN)
    out_grad = mm(resid_low, attended, TN)
    for j in range(4):
        cols = slice(j * quarter, (j + 1) * quarter)
        grad_acc[j, :, :quarter] += up_grad[:, cols]
        grad_acc[j, :, quarter : 2 * quarter] += down_grad[:, cols]
        grad_acc[j, :, 2 * quarter :] += out_grad[:, head_rows(j)]
    bias_acc[...] += fold_rows(pre_grad.astype(F32))
    for place, value in enumerate(
        (
            resid_grad,
            hidden_grad * normed_one,
            hidden_grad,
            mixed_grad,
            cotangent * normed_two,
            cotangent,
        )
    ):
        vec_acc[place] += fold_rows(value)

    for j in range((prompt_local + data_local) // rows):
        split = max(0, min(rows, prompt_local - j * rows))
        for place, (prompt_ref, data_ref) in enumerate(
            ((prompt_near, data_near), (prompt_far, data_far))
        ):

            @pl.when(i == place * half + j)
            def _():
                if split:
                    prompt_ref[j * rows : j * rows + split, :] = output[:split]
                if split < rows:
                    begin = j * rows + split - prompt_local
                    data_ref[begin : begin + rows - split, :] = output[split:]

    @pl.when(i == pl.num_programs(0) - 1)
    def _():
        for place in range(6):
            sums_ref[place : place + 1, :] = jnp.sum(vec_acc[place], axis=0, keepdims=True)
        bias_grad = jnp.sum(bias_acc[...], axis=0, keepdims=True)
        per_row = bias_grad.shape[1] // 2 // quarter
        for g in range(4):
            found = jnp.zeros((1, quarter), F32)
            for j, flip in enumerate((0, 2, 1, 3)):
                piece = bias_grad[:, j * quarter : (j + 1) * quarter]
                found = jnp.where((meta[0] ^ flip) == g, piece, found)
            row, col = 6 + g // per_row, (g % per_row) * quarter
            sums_ref[row : row + 1, col : col + quarter] = found
        depth = send_ref.shape[1] - 16
        groups = send_ref.shape[0] // 4
        width, wide = sums_ref.shape[1], send_ref.shape[2]
        per = sums_ref.shape[0] * width // groups
        for g in range(groups):
            row, col = g * per // width, g * per % width
            part = jnp.pad(sums_ref[row : row + 1, col : col + per], ((0, 0), (0, wide - per)))
            high, low, _ = three_parts(part)
            extra = extra_rows([high, low], 16)
            for j, flip in enumerate((0, 2, 1, 3)):
                target = g * 4 + (meta[0] ^ flip)
                send_ref[target, :depth] = grad_acc[j, g * depth : (g + 1) * depth].astype(BF16)
                send_ref[target, depth:] = extra


def row_work(meta, xa, xb, oa, ob, cot, packs, ups, vec, sizes, groups):
    rows, width = xa.shape
    prompt_local, data_local = sizes
    step = ROW_STEP
    n = rows // step
    quarter = ups[0].shape[1]
    hidden = 4 * quarter
    wide = 2 * quarter + HEAD_DIM
    send = (4 * groups, width // groups + 16, wide)
    near = lambda cols: pl.BlockSpec((step, cols), lambda i, meta: (jnp.minimum(i, n - 1), 0))
    far = lambda cols: pl.BlockSpec((step, cols), lambda i, meta: (jnp.maximum(i - n, 0), 0))
    row = lambda cols: pl.BlockSpec((step, cols), lambda i, meta: (i, 0))
    return pl.pallas_call(
        partial(rows_kernel, sizes),
        out_shape=[
            jax.ShapeDtypeStruct((prompt_local, width), BF16),
            jax.ShapeDtypeStruct((data_local, width), BF16),
            jax.ShapeDtypeStruct((prompt_local, width), BF16),
            jax.ShapeDtypeStruct((data_local, width), BF16),
            jax.ShapeDtypeStruct((2 * rows, width), F32),
            jax.ShapeDtypeStruct((2 * rows, 256), BF16),
            jax.ShapeDtypeStruct((2 * rows, 256), BF16),
            jax.ShapeDtypeStruct(send, BF16),
        ],
        grid_spec=pltpu.PrefetchScalarGridSpec(
            num_scalar_prefetch=1,
            grid=(2 * n,),
            in_specs=[near(width), far(width), near(256), far(256), near(256), far(256),
                      near(width), far(width)]
            + [once(item.shape) for item in packs + ups]
            + [once(vec.shape)],
            out_specs=[
                once((prompt_local, width)),
                once((data_local, width)),
                once((prompt_local, width)),
                once((data_local, width)),
                row(width),
                row(256),
                row(256),
                once(send),
            ],
            scratch_shapes=[
                pltpu.VMEM((8, width), F32),
                pltpu.VMEM((4 * HEAD_DIM, width), BF16),
                pltpu.VMEM((width, hidden), BF16),
                pltpu.VMEM((hidden, width), BF16),
                pltpu.VMEM((8, hidden), F32),
                pltpu.VMEM((4, width, wide), F32),
                pltpu.VMEM((6, 8, width), F32),
                pltpu.VMEM((8, hidden), F32),
            ],
        ),
        compiler_params=params(),
        cost_estimate=cost(
            3 * 2 * 2 * rows * width * (width + 2 * hidden), 24 * rows * width, 4 * rows * hidden
        ),
        name="row_work",
    )(meta, xa, xb, *oa, *ob, *cot, *packs, *ups, vec)


def on_device(
    data_rows,
    prompt_rows,
    context_rows,
    test_rows,
    qkv_weight,
    out_bias,
    out_weight,
    attn_gain,
    attn_shift,
    up_weight,
    up_bias,
    down_weight,
    down_bias,
    mlp_gain,
    mlp_shift,
    data_cotangent,
    prompt_cotangent,
):
    data_local = data_rows.shape[1]
    prompt_local = prompt_rows.shape[0]
    width = prompt_rows.shape[1]
    quarter = up_weight.shape[1]
    sizes = (prompt_local, data_local)
    groups = lax.axis_size("ep")
    t = lax.axis_index("tp")
    mine = t >> 1
    other = 1 - mine

    def across(value):
        return lax.ppermute(value, "tp", [(i, i ^ 2) for i in range(4)])

    def beside(value):
        return lax.ppermute(value, "tp", [(i, i ^ 1) for i in range(4)])

    def pick(values, which):
        return lax.dynamic_index_in_dim(values, which, axis=0, keepdims=False)

    def stack(prompt_part, data_part):
        return jnp.concatenate([prompt_part, data_part], axis=0)

    w_far = across(qkv_weight)
    x_far = across(stack(prompt_rows, pick(data_rows, other)))
    x = stack(prompt_rows, pick(data_rows, mine))
    x_sib = beside(x)
    context = pick(context_rows, mine)
    live = context + pick(test_rows, mine)
    meta = jnp.stack([t, context, live]).astype(jnp.int32)

    qtn, qn, kn, kxn, ktn, vn, vtn, w, x_all = project(
        meta, x, x_sib, qkv_weight, w_far, sizes, 0
    )
    ptn, state, state_acc = attend_first(qtn, (kn, kxn, vtn), 512)

    bias_rows = jnp.pad(up_bias[None], ((0, 15), (0, width - quarter)))
    pack = jnp.concatenate([out_weight, down_weight, bias_rows], axis=0)
    x_far, state, pack, up_weight = lax.optimization_barrier((x_far, state, pack, up_weight))
    x_far_sib = beside(x_far)
    pack_far, up_far = across(pack), across(up_weight)
    cot_far = stack(pick(prompt_cotangent, other), pick(data_cotangent, other))
    x_far_sib, cot_far = lax.optimization_barrier((x_far_sib, cot_far))
    cot_far = across(cot_far)
    qtf, qf, kf, kxf, ktf, vf, vtf, _, x_all = project(
        meta, x_far, x_far_sib, qkv_weight, w_far, sizes, 2, x_all
    )
    ptf, on_a, on_b, statn = attend_last(qtn, [(kf, kxf, vtf)], (state, state_acc), 512)
    pack_far, up_far, qtf = lax.optimization_barrier((pack_far, up_far, qtf))
    packs = [pack, pack_far, beside(pack), beside(pack_far)]
    ups = [up_weight, up_far, beside(up_weight), beside(up_far)]
    on_b, qtf, statn = lax.optimization_barrier((on_b, qtf, statn))
    on_received = beside(on_b)
    ptn, ptf, of_a, of_b, statf = attend_last(
        qtf, [(kn, kxn, vtn), (kf, kxf, vtf)], (ptn, ptf), 512
    )
    of_send, on_received, cot_far, packs, ups = lax.optimization_barrier(
        (of_b, on_received, cot_far, packs, ups)
    )
    cot = stack(pick(prompt_cotangent, mine), pick(data_cotangent, mine))
    vec = jnp.stack(
        [out_bias, attn_gain, attn_shift, down_bias, mlp_gain, mlp_shift, mlp_shift, mlp_shift]
    ).astype(F32)
    (prompt_near, data_near, prompt_far, data_far, resid, da, db, send) = row_work(
        meta, x, x_far, (on_a, of_a), (on_received, beside(of_send)), (cot, cot_far), packs, ups, vec, sizes, groups
    )

    def dot(left, right, dims):
        return lax.dot_general(left, right, dims, preferred_element_type=F32)

    def exchange(parts, axes):
        return lax.all_to_all(parts, axes, 0, 0, tiled=True)

    def gather(part):
        return exchange(jnp.broadcast_to(part[None], (groups,) + part.shape), "ep")

    db = beside(db)
    send = exchange(send, ("ep", "tp"))
    prompt_back, data_back = across(prompt_far), across(data_far)

    dq, dkv = attend_back(
        da, db, (on_a, on_b, of_a, of_b), (statn, statf), qn, qf, ptn, ptf, vn, ktn, vf, ktf, 512
    )
    send, prompt_back, data_back, dq = lax.optimization_barrier((send, prompt_back, data_back, dq))
    depth = width // groups
    total = jnp.sum(send.astype(F32), axis=0)
    part = total[depth : depth + 1] + total[depth + 1 : depth + 2]
    high = lax.optimization_barrier(part.astype(BF16))
    low = (part - high.astype(F32)).astype(BF16)
    total = jnp.concatenate(
        [total[:depth].astype(BF16), high, low, jnp.zeros((14, total.shape[1]), BF16)], axis=0
    )
    total = jnp.broadcast_to(total[None], (groups,) + total.shape)
    total, dq, dkv = lax.optimization_barrier((total, dq, dkv))
    total = exchange(total, "ep")

    slot_rows = prompt_local + data_local
    cut = 2 * slot_rows
    wq, wkv = w[:, :256], w[:, 256:]

    def rows_grad(part):
        return dot(dq[part], wq, NT) + dot(dkv[part], wkv, NT)

    grad_q, grad_kv = dot(x_all, dq, TN), dot(x_all, dkv, TN)

    def head_grad(h):
        return jnp.stack(
            [grad_q[:, head_rows(h)], grad_kv[:, head_rows(h)], grad_kv[:, head_rows(2 + h)]]
        )

    other_grad, dq, dkv = lax.optimization_barrier((head_grad(1).astype(BF16), dq, dkv))
    other_grad = across(other_grad)
    sib = rows_grad(slice(cut, None)).astype(BF16)
    sib, dq, dkv = lax.optimization_barrier((sib, dq, dkv))
    sib = beside(sib)
    own = rows_grad(slice(0, cut)) + resid
    other_grad, own = lax.optimization_barrier((other_grad, own))
    far_rows = (own[slot_rows:] + sib[slot_rows:].astype(F32)).astype(BF16)
    far_prompt = across(far_rows[:prompt_local])
    far_data = across(far_rows[prompt_local:])
    near_rows = own[:slot_rows] + sib[:slot_rows].astype(F32)
    near_data = near_rows[prompt_local:].astype(BF16)

    columns = width // HEAD_DIM
    prompt = near_rows[:prompt_local] + far_prompt.astype(F32)
    prompt = prompt.astype(BF16).reshape(groups, prompt_local // groups, width)
    prompt = jnp.concatenate([prompt[:, :, head_rows(j)] for j in range(columns)], axis=1)
    qkv = (head_grad(0) + other_grad.astype(F32)).astype(BF16).reshape(groups, -1, HEAD_DIM)
    qkv_rows = qkv.shape[1]
    last = jnp.concatenate([qkv, prompt], axis=1)
    total, last = lax.optimization_barrier((total, last))
    last = gather(jnp.sum(exchange(last, "ep").astype(F32), axis=0).astype(BF16))
    qkv = last[:, :qkv_rows].reshape(3, width, HEAD_DIM).astype(F32)
    prompt = last[:, qkv_rows:].reshape(groups, columns, prompt_local // groups, HEAD_DIM)
    prompt_grad = jnp.concatenate([prompt[:, j] for j in range(columns)], axis=2)
    prompt_grad = prompt_grad.reshape(prompt_local, width).astype(F32)

    which = lax.broadcasted_iota(jnp.int32, (2, 1, 1), 0)

    def by_episode(own, received):
        return jnp.where(which == mine, own[None], received[None])

    sums = total[:, depth : depth + 2, : 8 * width // groups].astype(F32)
    sums = (sums[:, 0] + sums[:, 1]).reshape(8, width)
    total = total[:, :depth].reshape(width, -1).astype(F32)
    bias_grad = lax.dynamic_slice_in_dim(sums[6:8].reshape(-1), t * quarter, quarter)
    return (
        by_episode(data_near, data_back),
        by_episode(prompt_near, prompt_back),
        by_episode(near_data, far_data),
        prompt_grad,
        qkv,
        sums[0],
        total[:, 2 * quarter :].T,
        sums[1],
        sums[2],
        total[:, :quarter],
        bias_grad,
        total[:, quarter : 2 * quarter].T,
        sums[3],
        sums[4],
        sums[5],
    )


def solution(mesh):
    return jax.shard_map(
        on_device,
        mesh=mesh,
        in_specs=(
            P("ep", "tp", None),
            P("tp", None),
            P("ep"),
            P("ep"),
            P(None, None, "tp"),
            P(),
            P("tp", None),
            P(),
            P(),
            P(None, "tp"),
            P("tp"),
            P("tp", None),
            P(),
            P(),
            P(),
            P("ep", "tp", None),
            P("ep", "tp", None),
        ),
        out_specs=(
            P("ep", "tp", None),
            P("ep", "tp", None),
            P("ep", "tp", None),
            P("tp", None),
            P(None, None, "tp"),
            P(),
            P("tp", None),
            P(),
            P(),
            P(None, "tp"),
            P("tp"),
            P("tp", None),
            P(),
            P(),
            P(),
        ),
        check_vma=False,
    )
```

```python
from functools import partial
import math

import jax
import jax.numpy as jnp
from jax import lax
from jax.experimental import pallas as pl
from jax.experimental.pallas import tpu as pltpu
from jax.sharding import PartitionSpec as P

HEAD_DIM = 128
ROWS = 512
BACK_ROWS = 256
ROW_STEP = 1024
SAMPLE = 256
EPS = 1e-05
MASKED = -1e30
LOG2E = math.log2(math.e)
LIMIT = 2.0**60
VMEM = 60 * 1024 * 1024
F32 = jnp.float32
BF16 = jnp.bfloat16
NN = (((1,), (0,)), ((), ()))
NT = (((1,), (1,)), ((), ()))
TN = (((0,), (0,)), ((), ()))


def mm(left, right, dims=NN):
    return lax.dot_general(left, right, dims, preferred_element_type=F32)


def params(**more):
    return pltpu.CompilerParams(vmem_limit_bytes=VMEM, **more)


def cost(flops, nbytes, trans=0):
    return pl.CostEstimate(
        flops=int(flops), bytes_accessed=int(nbytes), transcendentals=int(trans)
    )


def once(shape):
    return pl.BlockSpec(shape, lambda *_: (0,) * len(shape), pipeline_mode=pl.Buffered(1))


def extra_rows(values, count):
    width = values[0].shape[1]
    row = lax.broadcasted_iota(jnp.int32, (count, width), 0)
    out = jnp.zeros((count, width), F32)
    for index, value in enumerate(values):
        out = jnp.where(row == index, value, out)
    return out.astype(BF16)


def three_parts(row):
    high = row.astype(BF16).astype(F32)
    middle = (row - high).astype(BF16).astype(F32)
    return high, middle, row - high - middle


def clamp(i, low, high):
    return jnp.minimum(jnp.maximum(i, low), high)


def project_kernel(sizes, flip, meta, xa_ref, xb_ref, wa_ref, wb_ref, qt_ref, q_ref, k_ref,
                   kx_ref, kt_ref, v_ref, vt_ref, w_ref, wt_ref):
    prompt_local, data_local = sizes
    i = pl.program_id(0)
    per_slot = pl.num_programs(0) // 2
    rows = xa_ref.shape[0]

    @pl.when(i == 0)
    def _():
        for which in range(3):
            for h, source in enumerate((wa_ref, wb_ref)):
                cols = slice(which * 256 + h * HEAD_DIM, which * 256 + (h + 1) * HEAD_DIM)
                w_ref[:, cols] = source[which]
                wt_ref[cols, :] = source[which].T

    x = jnp.where(i < per_slot, xa_ref[...], xb_ref[...])
    slot = jnp.where(i < per_slot, meta[0] ^ flip, meta[0] ^ flip ^ 1)
    row = lax.broadcasted_iota(jnp.int32, (rows, HEAD_DIM), 0)
    lane = lax.broadcasted_iota(jnp.int32, (rows, HEAD_DIM), 1)
    index = (i % per_slot) * rows + row - prompt_local
    attended = jnp.logical_or(index < 0, slot * data_local + index < meta[1])
    bias = jnp.where(attended, F32(0.0), F32(MASKED))
    ones = jnp.where(lane < 4, F32(1.0), F32(0.0))
    kx_ref[...] = jnp.where(lane == 0, bias, ones).astype(BF16)
    factor = F32(LOG2E / math.sqrt(HEAD_DIM))
    z = mm(x, w_ref[...])
    q_ref[...] = (z[:, :256] * factor).astype(BF16)
    k_ref[...] = z[:, 256:512].astype(BF16)
    v_ref[...] = z[:, 512:].astype(BF16)
    zt = mm(wt_ref[...], x, NT)
    qt_ref[...] = (zt[:256] * factor).astype(BF16)
    kt_ref[...] = zt[256:512].astype(BF16)
    vt_ref[...] = zt[512:].astype(BF16)


def project(meta, xa, xb, wa, wb, sizes, flip):
    rows, width = xa.shape
    step = 512
    n = rows // step
    flat = jax.ShapeDtypeStruct((2 * rows, 256), BF16)
    tall = jax.ShapeDtypeStruct((256, 2 * rows), BF16)
    row = pl.BlockSpec((step, 256), lambda i, meta: (i, 0))
    col = pl.BlockSpec((256, step), lambda i, meta: (0, i))
    return pl.pallas_call(
        partial(project_kernel, sizes, flip),
        out_shape=[
            tall,
            flat,
            flat,
            jax.ShapeDtypeStruct((2 * rows, HEAD_DIM), BF16),
            tall,
            flat,
            tall,
            jax.ShapeDtypeStruct((width, 768), BF16),
        ],
        grid_spec=pltpu.PrefetchScalarGridSpec(
            num_scalar_prefetch=1,
            grid=(2 * n,),
            in_specs=[
                pl.BlockSpec((step, width), lambda i, meta: (jnp.minimum(i, n - 1), 0)),
                pl.BlockSpec((step, width), lambda i, meta: (jnp.maximum(i - n, 0), 0)),
                once(wa.shape),
                once(wb.shape),
            ],
            out_specs=[
                col,
                row,
                row,
                pl.BlockSpec((step, HEAD_DIM), lambda i, meta: (i, 0)),
                col,
                row,
                col,
                once((width, 768)),
            ],
            scratch_shapes=[pltpu.VMEM((768, width), BF16)],
        ),
        compiler_params=params(),
        cost_estimate=cost(4 * 2 * rows * width * 768, 2 * rows * width * 8),
        name="project",
    )(meta, xa, xb, wa, wb)


def head_rows(h):
    return slice(h * HEAD_DIM, (h + 1) * HEAD_DIM)


def with_shift(qt, top):
    high, middle, low = three_parts(top)
    extra = extra_rows([jnp.ones_like(top), -high, -middle, -low], HEAD_DIM)
    return jnp.concatenate([qt, extra], axis=0)


def half_scores(chunk, h, qa, start, k_ref, kx_ref):
    here = pl.ds(start, chunk)
    keys = jnp.concatenate([k_ref[here, head_rows(h)], kx_ref[here, :]], axis=1)
    return mm(keys, qa)


def half_part(h, start, scores, vt_ref, pt_ref):
    chunk = scores.shape[0]
    weight = jnp.exp2(scores)
    total = jnp.sum(weight.reshape(chunk // 8, 8, weight.shape[1]), axis=0)
    low = weight.astype(BF16)
    pt_ref[0, h, pl.ds(start, chunk), :] = low
    return total, mm(vt_ref[head_rows(h), pl.ds(start, chunk)], low)


def stale_shift(h, qt, k_ref):
    top = jnp.max(mm(k_ref[:SAMPLE, head_rows(h)], qt), axis=0, keepdims=True)
    return top, with_shift(qt, top)


def fast_states(chunk, shifts, keys, pts):
    tiles = [
        (h, j, start)
        for h in range(2)
        for j in range(len(keys))
        for start in range(0, keys[0][0].shape[0], chunk)
    ]

    def scores(tile):
        h, j, start = tile
        return half_scores(chunk, h, shifts[h][j][1], start, keys[j][0], keys[j][1])

    sums = {}
    ahead = scores(tiles[0])
    for place, (h, j, start) in enumerate(tiles):
        now = ahead
        if place + 1 < len(tiles):
            ahead = scores(tiles[place + 1])
        total, product = half_part(h, start, now, keys[j][2], pts[j])
        if (h, j) in sums:
            total, product = sums[h, j][0] + total, sums[h, j][1] + product
        sums[h, j] = total, product
    return [
        [
            (shifts[h][j][0], jnp.sum(sums[h, j][0], axis=0, keepdims=True), sums[h, j][1])
            for j in range(len(keys))
        ]
        for h in range(2)
    ]


def half_attend_exact(chunk, h, shift, k_ref, kx_ref, vt_ref, pt_ref):
    qt = shift[1][:HEAD_DIM]
    width = qt.shape[1]
    count = k_ref.shape[0] // chunk
    qa = with_shift(qt, jnp.zeros((1, width), F32))

    def find(j, top):
        found = half_scores(chunk, h, qa, pl.multiple_of(j * chunk, chunk), k_ref, kx_ref)
        return jnp.maximum(top, jnp.max(found, axis=0, keepdims=True))

    top = lax.fori_loop(0, count, find, jnp.full((1, width), MASKED, F32))
    qa = with_shift(qt, top)

    def add(j, state):
        start = pl.multiple_of(j * chunk, chunk)
        found = half_scores(chunk, h, qa, start, k_ref, kx_ref)
        more, product = half_part(h, start, found, vt_ref, pt_ref)
        return state[0] + more, state[1] + product

    total, acc = lax.fori_loop(
        0, count, add, (jnp.zeros((8, width), F32), jnp.zeros((HEAD_DIM, width), F32))
    )
    return top, jnp.sum(total, axis=0, keepdims=True), acc


def merge(states):
    top = states[0][0]
    for state in states[1:]:
        top = jnp.maximum(top, state[0])
    scales = [jnp.exp2(state[0] - top) for state in states]
    total = sum(state[1] * scale for state, scale in zip(states, scales))
    factors = [scale / total for scale in scales]
    return factors, sum(state[2] * factor for state, factor in zip(states, factors))


def redo(states, shifts, keys, pts):
    return [
        [half_attend_exact(256, h, shifts[h][j], *keys[j], pts[j]) for j in range(len(keys))]
        for h in range(2)
    ]


def run_halves(chunk, qt_ref, keys, pts, finish):
    shifts = [
        [stale_shift(h, qt_ref[head_rows(h), :], key_refs[0]) for key_refs in keys]
        for h in range(2)
    ]
    states = fast_states(chunk, shifts, keys, pts)
    worst = None
    for state in states[0] + states[1]:
        worst = state[1] if worst is None else jnp.maximum(worst, state[1])
    finish(states)

    @pl.when(jnp.logical_not(jnp.max(worst) <= LIMIT))
    def _():
        finish(redo(states, shifts, keys, pts))


def attend_first_kernel(chunk, qt_ref, k_ref, kx_ref, vt_ref, pt_ref, state_ref, acc_ref):
    def finish(states):
        for h in range(2):
            top, total, acc = states[h][0]
            state_ref[0, h : h + 1, :] = top
            state_ref[0, 2 + h : 3 + h, :] = total
            acc_ref[head_rows(h), :] = acc

    run_halves(chunk, qt_ref, [(k_ref, kx_ref, vt_ref)], [pt_ref], finish)


def attend_first(qt, key, chunk):
    rows = qt.shape[1]
    n = rows // ROWS
    col = pl.BlockSpec((256, ROWS), lambda i: (0, i))
    pairs = 2 * rows * rows
    return pl.pallas_call(
        partial(attend_first_kernel, chunk),
        out_shape=[
            jax.ShapeDtypeStruct((2 * n, 2, rows, ROWS), BF16),
            jax.ShapeDtypeStruct((n, 8, ROWS), F32),
            jax.ShapeDtypeStruct((256, rows), F32),
        ],
        grid=(n,),
        in_specs=[col] + [once(item.shape) for item in key],
        out_specs=[
            pl.BlockSpec((1, 2, rows, ROWS), lambda i: (i, 0, 0, 0)),
            pl.BlockSpec((1, 8, ROWS), lambda i: (i, 0, 0)),
            col,
        ],
        compiler_params=params(),
        cost_estimate=cost(4 * pairs * HEAD_DIM * 2, 2 * pairs, pairs),
        name="attend_near",
    )(qt, *key)


def attend_second_kernel(
    chunk, qtn_ref, qtf_ref, kn, kxn, vtn, kf, kxf, vtf, old_ref, old_acc_ref, _,
    ptn_ref, ptf_ref, mine_ref, sib_ref, stat_ref,
):
    i = pl.program_id(0)
    n = pl.num_programs(0) // 2
    near, far = (kn, kxn, vtn), (kf, kxf, vtf)

    def store(h, states):
        factors, result = merge(states)
        stat_ref[0, h : h + 1, :] = factors[0]
        stat_ref[0, 2 + h : 3 + h, :] = factors[1]
        low = result.T.astype(BF16)
        first = i % n < n // 2

        @pl.when(first)
        def _():
            mine_ref[:, head_rows(h)] = low

        @pl.when(jnp.logical_not(first))
        def _():
            sib_ref[:, head_rows(h)] = low

    @pl.when(i < n)
    def _():
        def finish(states):
            for h in range(2):
                old = (old_ref[0, h : h + 1, :], old_ref[0, 2 + h : 3 + h, :],
                       old_acc_ref[head_rows(h), :])
                store(h, [old, states[h][0]])

        run_halves(chunk, qtn_ref, [far], [ptf_ref], finish)

    @pl.when(i >= n)
    def _():
        def finish(states):
            for h in range(2):
                store(h, states[h])

        run_halves(chunk, qtf_ref, [near, far], [ptn_ref, ptf_ref], finish)


def mine_block(i, n):
    half = n // 2
    return (i // n) * half + jnp.minimum(i % n, half - 1)


def sib_block(i, n):
    half = n // 2
    return jnp.maximum((i // n) * half + i % n - half, jnp.maximum((i // n) * half - 1, 0))


def attend_second(qtn, qtf, near, far, pt, state, acc, chunk):
    rows = qtn.shape[1]
    n = rows // ROWS
    near_col = pl.BlockSpec((256, ROWS), lambda i: (0, jnp.minimum(i, n - 1)))
    pairs = 6 * rows * rows
    return pl.pallas_call(
        partial(attend_second_kernel, chunk),
        out_shape=[
            jax.ShapeDtypeStruct(pt.shape, BF16),
            jax.ShapeDtypeStruct(pt.shape, BF16),
            jax.ShapeDtypeStruct((rows, 256), BF16),
            jax.ShapeDtypeStruct((rows, 256), BF16),
            jax.ShapeDtypeStruct((2 * n, 8, ROWS), F32),
        ],
        grid=(2 * n,),
        in_specs=[near_col, pl.BlockSpec((256, ROWS), lambda i: (0, jnp.maximum(i - n, 0)))]
        + [once(item.shape) for item in near + far]
        + [
            pl.BlockSpec((1, 8, ROWS), lambda i: (jnp.minimum(i, n - 1), 0, 0)),
            near_col,
            pl.BlockSpec(memory_space=pl.ANY),
        ],
        out_specs=[
            pl.BlockSpec((1, 2, rows, ROWS), lambda i: (jnp.maximum(i, n), 0, 0, 0)),
            pl.BlockSpec((1, 2, rows, ROWS), lambda i: (i, 0, 0, 0)),
            pl.BlockSpec((ROWS, 256), lambda i: (mine_block(i, n), 0)),
            pl.BlockSpec((ROWS, 256), lambda i: (sib_block(i, n), 0)),
            pl.BlockSpec((1, 8, ROWS), lambda i: (i, 0, 0)),
        ],
        input_output_aliases={10: 0},
        compiler_params=params(),
        cost_estimate=cost(4 * pairs * HEAD_DIM * 2, 2 * pairs, pairs),
        name="attend_rest",
    )(qtn, qtf, *near, *far, state, acc, pt)


def back_weights(do, o, factors):
    dot_t = do.astype(F32).T
    delta = jnp.sum(dot_t * o.astype(F32).T, axis=0, keepdims=True)
    found = []
    for factor in factors:
        scaled = dot_t * factor
        high, middle, low = three_parts(delta * factor)
        extra = extra_rows([-high, -middle, -low], HEAD_DIM)
        found.append(
            (jnp.concatenate([scaled.astype(BF16), extra], axis=0), scaled.T.astype(BF16))
        )
    return found


def back_half(chunk, h, grads, q_rows, pt_ref, v_ref, kt_ref, key_acc, value_acc):
    ones = jnp.where(
        lax.broadcasted_iota(jnp.int32, (chunk, HEAD_DIM), 1) < 3, F32(1.0), F32(0.0)
    ).astype(BF16)
    result = jnp.zeros((HEAD_DIM, q_rows.shape[0]), F32)
    for start in range(0, v_ref.shape[0], chunk):
        here = slice(start, start + chunk)
        prob = pt_ref[0, h, here, :]
        values = jnp.concatenate([v_ref[here, head_rows(h)], ones], axis=1)
        score = (prob.astype(F32) * mm(values, grads[0])).astype(BF16)
        value_acc[h, here, :] += mm(prob, grads[1])
        key_acc[h, here, :] += mm(score, q_rows)
        result = result + mm(kt_ref[head_rows(h), here], score)
    return result


def attend_back_kernel(
    chunk, da_ref, db_ref, oa_ref, ob_ref, stat_ref, qn_ref, qf_ref, ptn_ref, ptf_ref,
    vn, ktn, vf, ktf, dz_ref, key_n, value_n, key_f, value_f,
):
    i = pl.program_id(0)
    n = pl.num_programs(0) // 2

    @pl.when(i == 0)
    def _():
        for ref in (key_n, value_n, key_f, value_f):
            ref[...] = jnp.zeros_like(ref)

    first = i % n < n // 2
    do = jnp.where(first, da_ref[...], db_ref[...])
    o = jnp.where(first, oa_ref[...], ob_ref[...])
    q = jnp.where(i < n, qn_ref[...], qf_ref[...])
    place = jnp.where(first, 0, n // 2) + (i // n) * (n // 2) + i % n
    rows = pl.ds(pl.multiple_of(place * q.shape[0], q.shape[0]), q.shape[0])
    for h in range(2):
        cols = head_rows(h)
        near, far = back_weights(
            do[:, cols], o[:, cols], [stat_ref[0, h : h + 1, :], stat_ref[0, 2 + h : 3 + h, :]]
        )
        grad = back_half(chunk, h, near, q[:, cols], ptn_ref, vn, ktn, key_n, value_n)
        grad += back_half(chunk, h, far, q[:, cols], ptf_ref, vf, ktf, key_f, value_f)
        dz_ref[rows, cols] = (grad * F32(1.0 / math.sqrt(HEAD_DIM))).T.astype(BF16)

    @pl.when(i == 2 * n - 1)
    def _():
        seq = vn.shape[0]
        for half, (keys, values) in enumerate(((key_n, value_n), (key_f, value_f))):
            for owner in range(2):
                source = slice(owner * seq // 2, (owner + 1) * seq // 2)
                begin = owner * seq + half * seq // 2
                rows = slice(begin, begin + seq // 2)
                for h in range(2):
                    dz_ref[rows, head_rows(2 + h)] = (keys[h, source] * F32(1.0 / LOG2E)).astype(BF16)
                    dz_ref[rows, head_rows(4 + h)] = values[h, source].astype(BF16)


def attend_back(da, db, oa, ob, stat, qn, qf, ptn, ptf, vn, ktn, vf, ktf, chunk):
    rows = qn.shape[0]
    step = BACK_ROWS
    n = rows // step
    per = ROWS // step
    row = lambda f: pl.BlockSpec((step, 256), lambda i: (f(i), 0))
    tile = pl.BlockSpec((1, 2, rows, step), lambda i: (i // per, 0, 0, i % per))
    wide = jax.ShapeDtypeStruct((2 * rows, 768), BF16)
    acc = pltpu.VMEM((2, rows, HEAD_DIM), F32)
    pairs = 8 * rows * rows
    return pl.pallas_call(
        partial(attend_back_kernel, chunk),
        out_shape=wide,
        grid=(2 * n,),
        in_specs=[
            row(lambda i: mine_block(i, n)),
            row(lambda i: sib_block(i, n)),
            row(lambda i: mine_block(i, n)),
            row(lambda i: sib_block(i, n)),
            pl.BlockSpec((1, 8, step), lambda i: (i // per, 0, i % per)),
            row(lambda i: jnp.minimum(i, n - 1)),
            row(lambda i: jnp.maximum(i - n, 0)),
            tile,
            tile,
        ]
        + [once(item.shape) for item in (vn, ktn, vf, ktf)],
        out_specs=once(wide.shape),
        scratch_shapes=[acc, acc, acc, acc],
        compiler_params=params(),
        cost_estimate=cost(8 * pairs * HEAD_DIM, 2 * pairs),
        name="attend_back",
    )(da, db, oa, ob, stat, qn, qf, ptn, ptf, vn, ktn, vf, ktf)


def mean(values):
    return jnp.mean(values, axis=-1, keepdims=True)


def norm(values):
    centered = values - mean(values)
    inverse = lax.rsqrt(mean(centered * centered) + EPS)
    return centered * inverse, inverse


def norm_back(incoming, normed, inverse, gain):
    scaled = incoming * gain
    return inverse * (scaled - mean(scaled) - normed * mean(scaled * normed))


def gelu_parts(v):
    bell = jnp.exp2(v * v * F32(-0.5 * LOG2E))
    base = 1.0 + F32(0.3275911 / math.sqrt(2.0)) * jnp.abs(v)
    t = pl.reciprocal(base, approx=True)
    t = t * (2.0 - base * t)
    series = t * (
        F32(0.5 * 0.254829592)
        + t
        * (
            F32(0.5 * -0.284496736)
            + t
            * (
                F32(0.5 * 1.421413741)
                + t * (F32(0.5 * -1.453152027) + t * F32(0.5 * 1.061405429))
            )
        )
    )
    tail = series * bell
    return bell * F32(1.0 / math.sqrt(2.0 * math.pi)), jnp.where(v >= 0, 1.0 - tail, tail)


def fold_rows(values):
    return jnp.sum(values.reshape(values.shape[0] // 8, 8, values.shape[1]), axis=0)


def rows_kernel(
    sizes, meta, xa_ref, xb_ref, oa_ref, ob_ref, cot_a, cot_b, p0, p1, p2, p3,
    u0, u1, u2, u3, vec_ref,
    prompt_near, data_near, prompt_far, data_far, resid_ref, da_ref, db_ref, send_ref,
    sums_ref, wo_ref, up_ref, down_ref, bias_ref, grad_acc, vec_acc, bias_acc,
):
    prompt_local, data_local = sizes
    i = pl.program_id(0)
    half = pl.num_programs(0) // 2
    here = i < half
    rows = xa_ref.shape[0]
    quarter = u0.shape[1]

    @pl.when(i == 0)
    def _():
        for j, (pack, up_part) in enumerate(((p0, u0), (p1, u1), (p2, u2), (p3, u3))):
            cols = slice(j * quarter, (j + 1) * quarter)
            wo_ref[head_rows(j), :] = pack[:HEAD_DIM, :]
            down_ref[cols, :] = pack[HEAD_DIM : HEAD_DIM + quarter, :]
            bias_ref[0:1, cols] = pack[
                HEAD_DIM + quarter : HEAD_DIM + quarter + 16, :quarter
            ].astype(F32)[0:1, :]
            up_ref[:, cols] = up_part[...]
        grad_acc[...] = jnp.zeros_like(grad_acc)
        vec_acc[...] = jnp.zeros_like(vec_acc)
        bias_acc[...] = jnp.zeros_like(bias_acc)

    slot = jnp.where(here, meta[0], meta[0] ^ 2)
    index = (i % half) * rows + lax.broadcasted_iota(jnp.int32, (rows, 1), 0) - prompt_local
    live = jnp.logical_or(index < 0, slot * data_local + index < meta[2])

    out_bias, attn_gain, attn_shift = vec_ref[0:1, :], vec_ref[1:2, :], vec_ref[2:3, :]
    down_bias, mlp_gain, mlp_shift = vec_ref[3:4, :], vec_ref[4:5, :], vec_ref[5:6, :]
    x = jnp.where(here, xa_ref[...], xb_ref[...])
    attended = jnp.concatenate([oa_ref[...], ob_ref[...]], axis=1)
    normed_one, inverse_one = norm(x.astype(F32) + (mm(attended, wo_ref[...]) + out_bias))
    hidden = normed_one * attn_gain + attn_shift
    hidden_low = hidden.astype(BF16)
    pre = mm(hidden_low, up_ref[...]) + bias_ref[0:1, :]
    density, share = gelu_parts(pre)
    activated = (pre * share).astype(BF16)
    slope = share + pre * density
    mixed = hidden + (mm(activated, down_ref[...]) + down_bias)
    normed_two, inverse_two = norm(mixed)
    output = (normed_two * mlp_gain + mlp_shift).astype(BF16)
    cotangent = jnp.where(live, jnp.where(here, cot_a[...], cot_b[...]).astype(F32), 0.0)
    mixed_grad = norm_back(cotangent, normed_two, inverse_two, mlp_gain)
    mixed_low = mixed_grad.astype(BF16)
    pre_grad = (mm(mixed_low, down_ref[...], NT) * slope).astype(BF16)
    hidden_grad = mixed_grad + mm(pre_grad, up_ref[...], NT)
    resid_grad = norm_back(hidden_grad, normed_one, inverse_one, attn_gain)
    resid_ref[...] = resid_grad
    resid_low = resid_grad.astype(BF16)
    attended_grad = mm(resid_low, wo_ref[...], NT).astype(BF16)
    da_ref[...] = attended_grad[:, :256]
    db_ref[...] = attended_grad[:, 256:]

    up_grad = mm(hidden_low, pre_grad, TN)
    down_grad = mm(mixed_low, activated, TN)
    out_grad = mm(resid_low, attended, TN)
    for j in range(4):
        cols = slice(j * quarter, (j + 1) * quarter)
        grad_acc[j, :, :quarter] += up_grad[:, cols]
        grad_acc[j, :, quarter : 2 * quarter] += down_grad[:, cols]
        grad_acc[j, :, 2 * quarter :] += out_grad[:, head_rows(j)]
    bias_acc[...] += fold_rows(pre_grad.astype(F32))
    for place, value in enumerate(
        (
            resid_grad,
            hidden_grad * normed_one,
            hidden_grad,
            mixed_grad,
            cotangent * normed_two,
            cotangent,
        )
    ):
        vec_acc[place] += fold_rows(value)

    for j in range((prompt_local + data_local) // rows):
        split = max(0, min(rows, prompt_local - j * rows))
        for place, (prompt_ref, data_ref) in enumerate(
            ((prompt_near, data_near), (prompt_far, data_far))
        ):

            @pl.when(i == place * half + j)
            def _():
                if split:
                    prompt_ref[j * rows : j * rows + split, :] = output[:split]
                if split < rows:
                    begin = j * rows + split - prompt_local
                    data_ref[begin : begin + rows - split, :] = output[split:]

    @pl.when(i == pl.num_programs(0) - 1)
    def _():
        for place in range(6):
            sums_ref[place : place + 1, :] = jnp.sum(vec_acc[place], axis=0, keepdims=True)
        bias_grad = jnp.sum(bias_acc[...], axis=0, keepdims=True)
        per_row = bias_grad.shape[1] // 2 // quarter
        for g in range(4):
            found = jnp.zeros((1, quarter), F32)
            for j, flip in enumerate((0, 2, 1, 3)):
                piece = bias_grad[:, j * quarter : (j + 1) * quarter]
                found = jnp.where((meta[0] ^ flip) == g, piece, found)
            row, col = 6 + g // per_row, (g % per_row) * quarter
            sums_ref[row : row + 1, col : col + quarter] = found
        depth = send_ref.shape[1] - 16
        groups = send_ref.shape[0] // 4
        width, wide = sums_ref.shape[1], send_ref.shape[2]
        per = sums_ref.shape[0] * width // groups
        for g in range(groups):
            row, col = g * per // width, g * per % width
            part = jnp.pad(sums_ref[row : row + 1, col : col + per], ((0, 0), (0, wide - per)))
            high, low, _ = three_parts(part)
            extra = extra_rows([high, low], 16)
            for j, flip in enumerate((0, 2, 1, 3)):
                target = g * 4 + (meta[0] ^ flip)
                send_ref[target, :depth] = grad_acc[j, g * depth : (g + 1) * depth].astype(BF16)
                send_ref[target, depth:] = extra


def row_work(meta, xa, xb, oa, ob, cot, packs, ups, vec, sizes, groups):
    rows, width = xa.shape
    prompt_local, data_local = sizes
    step = ROW_STEP
    n = rows // step
    quarter = ups[0].shape[1]
    hidden = 4 * quarter
    wide = 2 * quarter + HEAD_DIM
    send = (4 * groups, width // groups + 16, wide)
    near = pl.BlockSpec((step, width), lambda i, meta: (jnp.minimum(i, n - 1), 0))
    far = pl.BlockSpec((step, width), lambda i, meta: (jnp.maximum(i - n, 0), 0))
    row = lambda cols: pl.BlockSpec((step, cols), lambda i, meta: (i, 0))
    return pl.pallas_call(
        partial(rows_kernel, sizes),
        out_shape=[
            jax.ShapeDtypeStruct((prompt_local, width), BF16),
            jax.ShapeDtypeStruct((data_local, width), BF16),
            jax.ShapeDtypeStruct((prompt_local, width), BF16),
            jax.ShapeDtypeStruct((data_local, width), BF16),
            jax.ShapeDtypeStruct((2 * rows, width), F32),
            jax.ShapeDtypeStruct((2 * rows, 256), BF16),
            jax.ShapeDtypeStruct((2 * rows, 256), BF16),
            jax.ShapeDtypeStruct(send, BF16),
        ],
        grid_spec=pltpu.PrefetchScalarGridSpec(
            num_scalar_prefetch=1,
            grid=(2 * n,),
            in_specs=[near, far, row(256), row(256), near, far]
            + [once(item.shape) for item in packs + ups]
            + [once(vec.shape)],
            out_specs=[
                once((prompt_local, width)),
                once((data_local, width)),
                once((prompt_local, width)),
                once((data_local, width)),
                row(width),
                row(256),
                row(256),
                once(send),
            ],
            scratch_shapes=[
                pltpu.VMEM((8, width), F32),
                pltpu.VMEM((4 * HEAD_DIM, width), BF16),
                pltpu.VMEM((width, hidden), BF16),
                pltpu.VMEM((hidden, width), BF16),
                pltpu.VMEM((8, hidden), F32),
                pltpu.VMEM((4, width, wide), F32),
                pltpu.VMEM((6, 8, width), F32),
                pltpu.VMEM((8, hidden), F32),
            ],
        ),
        compiler_params=params(),
        cost_estimate=cost(
            3 * 2 * 2 * rows * width * (width + 2 * hidden), 24 * rows * width, 4 * rows * hidden
        ),
        name="row_work",
    )(meta, xa, xb, oa, ob, *cot, *packs, *ups, vec)


def on_device(
    data_rows,
    prompt_rows,
    context_rows,
    test_rows,
    qkv_weight,
    out_bias,
    out_weight,
    attn_gain,
    attn_shift,
    up_weight,
    up_bias,
    down_weight,
    down_bias,
    mlp_gain,
    mlp_shift,
    data_cotangent,
    prompt_cotangent,
):
    data_local = data_rows.shape[1]
    prompt_local = prompt_rows.shape[0]
    width = prompt_rows.shape[1]
    quarter = up_weight.shape[1]
    sizes = (prompt_local, data_local)
    groups = lax.axis_size("ep")
    t = lax.axis_index("tp")
    mine = t >> 1
    other = 1 - mine

    def across(value):
        return lax.ppermute(value, "tp", [(i, i ^ 2) for i in range(4)])

    def beside(value):
        return lax.ppermute(value, "tp", [(i, i ^ 1) for i in range(4)])

    def pick(values, which):
        return lax.dynamic_index_in_dim(values, which, axis=0, keepdims=False)

    def stack(prompt_part, data_part):
        return jnp.concatenate([prompt_part, data_part], axis=0)

    w_far = across(qkv_weight)
    x_far = across(stack(prompt_rows, pick(data_rows, other)))
    x = stack(prompt_rows, pick(data_rows, mine))
    x_sib = beside(x)
    context = pick(context_rows, mine)
    live = context + pick(test_rows, mine)
    meta = jnp.stack([t, context, live]).astype(jnp.int32)

    qtn, qn, kn, kxn, ktn, vn, vtn, w = project(meta, x, x_sib, qkv_weight, w_far, sizes, 0)
    ptn, state, state_acc = attend_first(qtn, (kn, kxn, vtn), 512)

    bias_rows = jnp.pad(up_bias[None], ((0, 15), (0, width - quarter)))
    pack = jnp.concatenate([out_weight, down_weight, bias_rows], axis=0)
    x_far, state, pack, up_weight, x_late, x_sib_late = lax.optimization_barrier(
        (x_far, state, pack, up_weight, x, x_sib)
    )
    x_far_sib = beside(x_far)
    pack_far, up_far = across(pack), across(up_weight)
    cot_far = stack(pick(prompt_cotangent, other), pick(data_cotangent, other))
    x_far_sib, cot_far = lax.optimization_barrier((x_far_sib, cot_far))
    cot_far = across(cot_far)
    qtf, qf, kf, kxf, ktf, vf, vtf, _ = project(meta, x_far, x_far_sib, qkv_weight, w_far, sizes, 2)
    x_all = jnp.concatenate([x_late, x_far, x_sib_late, x_far_sib], axis=0)
    pack_far, up_far, x_all, qtf = lax.optimization_barrier((pack_far, up_far, x_all, qtf))
    ptn, ptf, oa, ob, stat = attend_second(
        qtn, qtf, (kn, kxn, vtn), (kf, kxf, vtf), ptn, state, state_acc, 512
    )

    ob_send, cot_far = lax.optimization_barrier((ob, cot_far))
    cot = stack(pick(prompt_cotangent, mine), pick(data_cotangent, mine))
    packs = [pack, pack_far, beside(pack), beside(pack_far)]
    ups = [up_weight, up_far, beside(up_weight), beside(up_far)]
    vec = jnp.stack(
        [out_bias, attn_gain, attn_shift, down_bias, mlp_gain, mlp_shift, mlp_shift, mlp_shift]
    ).astype(F32)
    (prompt_near, data_near, prompt_far, data_far, resid, da, db, send) = row_work(
        meta, x, x_far, oa, beside(ob_send), (cot, cot_far), packs, ups, vec, sizes, groups
    )

    def dot(left, right, dims):
        return lax.dot_general(left, right, dims, preferred_element_type=F32)

    def exchange(parts, axes):
        return lax.all_to_all(parts, axes, 0, 0, tiled=True)

    def gather(part):
        return exchange(jnp.broadcast_to(part[None], (groups,) + part.shape), "ep")

    db = beside(db)
    send = exchange(send, ("ep", "tp"))
    prompt_back, data_back = across(prompt_far), across(data_far)

    dz = attend_back(da, db, oa, ob, stat, qn, qf, ptn, ptf, vn, ktn, vf, ktf, 512)
    send, prompt_back, data_back, dz = lax.optimization_barrier((send, prompt_back, data_back, dz))
    depth = width // groups
    total = jnp.sum(send.astype(F32), axis=0)
    part = total[depth : depth + 1] + total[depth + 1 : depth + 2]
    high = lax.optimization_barrier(part.astype(BF16))
    low = (part - high.astype(F32)).astype(BF16)
    total = jnp.concatenate(
        [total[:depth].astype(BF16), high, low, jnp.zeros((14, total.shape[1]), BF16)], axis=0
    )
    total = jnp.broadcast_to(total[None], (groups,) + total.shape)
    total, dz = lax.optimization_barrier((total, dz))
    total = exchange(total, "ep")

    slot_rows = prompt_local + data_local
    first_rows = [slot * slot_rows for slot in range(4)]

    def prompt_dot(slot):
        return dot(dz[first_rows[slot] : first_rows[slot] + prompt_local], w, NT)

    def data_dot(slot):
        return dot(dz[first_rows[slot] + prompt_local : first_rows[slot] + slot_rows], w, NT)

    sib_prompt = jnp.concatenate([prompt_dot(2), prompt_dot(3)], axis=0).astype(BF16)
    sib_prompt, dz = lax.optimization_barrier((sib_prompt, dz))
    sib_prompt = beside(sib_prompt)
    own_prompt = [prompt_dot(0), prompt_dot(1)]
    own_prompt, dz = lax.optimization_barrier((own_prompt, dz))
    grad = dot(x_all, dz, TN)

    def head_grad(h):
        return jnp.stack([grad[:, head_rows(2 * which + h)] for which in range(3)])

    near_prompt, far_prompt = [
        own_prompt[j]
        + resid[j * slot_rows : j * slot_rows + prompt_local]
        + sib_prompt[j * prompt_local : (j + 1) * prompt_local].astype(F32)
        for j in range(2)
    ]
    far_prompt, other_grad, dz = lax.optimization_barrier(
        (far_prompt.astype(BF16), head_grad(1).astype(BF16), dz)
    )
    far_prompt, other_grad = across(far_prompt), across(other_grad)

    sib_data = jnp.concatenate([data_dot(2), data_dot(3)], axis=0).astype(BF16)
    sib_data, dz = lax.optimization_barrier((sib_data, dz))
    sib_data = beside(sib_data)
    own_data = [
        data_dot(j) + resid[j * slot_rows + prompt_local : (j + 1) * slot_rows] for j in range(2)
    ]
    total, own_data, far_prompt, other_grad = lax.optimization_barrier(
        (total, own_data, far_prompt, other_grad)
    )
    near_data, far_data = [
        (own_data[j] + sib_data[j * data_local : (j + 1) * data_local].astype(F32)).astype(BF16)
        for j in range(2)
    ]
    far_data = across(far_data)

    columns = width // HEAD_DIM
    prompt = (near_prompt + far_prompt.astype(F32)).astype(BF16)
    prompt = prompt.reshape(groups, prompt_local // groups, width)
    prompt = jnp.concatenate([prompt[:, :, head_rows(j)] for j in range(columns)], axis=1)
    qkv = (head_grad(0) + other_grad.astype(F32)).astype(BF16).reshape(groups, -1, HEAD_DIM)
    qkv_rows = qkv.shape[1]
    last = jnp.concatenate([qkv, prompt], axis=1)
    last = gather(jnp.sum(exchange(last, "ep").astype(F32), axis=0).astype(BF16))
    qkv = last[:, :qkv_rows].reshape(3, width, HEAD_DIM).astype(F32)
    prompt = last[:, qkv_rows:].reshape(groups, columns, prompt_local // groups, HEAD_DIM)
    prompt_grad = jnp.concatenate([prompt[:, j] for j in range(columns)], axis=2)
    prompt_grad = prompt_grad.reshape(prompt_local, width).astype(F32)

    which = lax.broadcasted_iota(jnp.int32, (2, 1, 1), 0)

    def by_episode(own, received):
        return jnp.where(which == mine, own[None], received[None])

    sums = total[:, depth : depth + 2, : 8 * width // groups].astype(F32)
    sums = (sums[:, 0] + sums[:, 1]).reshape(8, width)
    total = total[:, :depth].reshape(width, -1).astype(F32)
    bias_grad = lax.dynamic_slice_in_dim(sums[6:8].reshape(-1), t * quarter, quarter)
    return (
        by_episode(data_near, data_back),
        by_episode(prompt_near, prompt_back),
        by_episode(near_data, far_data),
        prompt_grad,
        qkv,
        sums[0],
        total[:, 2 * quarter :].T,
        sums[1],
        sums[2],
        total[:, :quarter],
        bias_grad,
        total[:, quarter : 2 * quarter].T,
        sums[3],
        sums[4],
        sums[5],
    )


def solution(mesh):
    return jax.shard_map(
        on_device,
        mesh=mesh,
        in_specs=(
            P("ep", "tp", None),
            P("tp", None),
            P("ep"),
            P("ep"),
            P(None, None, "tp"),
            P(),
            P("tp", None),
            P(),
            P(),
            P(None, "tp"),
            P("tp"),
            P("tp", None),
            P(),
            P(),
            P(),
            P("ep", "tp", None),
            P("ep", "tp", None),
        ),
        out_specs=(
            P("ep", "tp", None),
            P("ep", "tp", None),
            P("ep", "tp", None),
            P("tp", None),
            P(None, None, "tp"),
            P(),
            P("tp", None),
            P(),
            P(),
            P(None, "tp"),
            P("tp"),
            P("tp", None),
            P(),
            P(),
            P(),
        ),
        check_vma=False,
    )
```

```python
from functools import partial
import math

import jax
import jax.numpy as jnp
from jax import lax
from jax.experimental import pallas as pl
from jax.experimental.pallas import tpu as pltpu
from jax.sharding import PartitionSpec as P

HEAD_DIM = 128
ROWS = 512
BACK_ROWS = 256
ROW_STEP = 1024
SAMPLE = 256
EPS = 1e-05
MASKED = -1e30
LOG2E = math.log2(math.e)
LIMIT = 2.0**60
VMEM = 60 * 1024 * 1024
F32 = jnp.float32
BF16 = jnp.bfloat16
NN = (((1,), (0,)), ((), ()))
NT = (((1,), (1,)), ((), ()))
TN = (((0,), (0,)), ((), ()))


def mm(left, right, dims=NN):
    return lax.dot_general(left, right, dims, preferred_element_type=F32)


def params(**more):
    return pltpu.CompilerParams(vmem_limit_bytes=VMEM, **more)


def cost(flops, nbytes, trans=0):
    return pl.CostEstimate(
        flops=int(flops), bytes_accessed=int(nbytes), transcendentals=int(trans)
    )


def once(shape):
    return pl.BlockSpec(shape, lambda *_: (0,) * len(shape), pipeline_mode=pl.Buffered(1))


def extra_rows(values, count):
    width = values[0].shape[1]
    row = lax.broadcasted_iota(jnp.int32, (count, width), 0)
    out = jnp.zeros((count, width), F32)
    for index, value in enumerate(values):
        out = jnp.where(row == index, value, out)
    return out.astype(BF16)


def three_parts(row):
    high = row.astype(BF16).astype(F32)
    middle = (row - high).astype(BF16).astype(F32)
    return high, middle, row - high - middle


def clamp(i, low, high):
    return jnp.minimum(jnp.maximum(i, low), high)


def project_kernel(sizes, flip, meta, xa_ref, xb_ref, wa_ref, wb_ref, *refs):
    refs = refs[1:] if flip else refs
    qt_ref, q_ref, k_ref, kx_ref, kt_ref, v_ref, vt_ref, w_ref, all_ref, wt_ref = refs
    prompt_local, data_local = sizes
    i = pl.program_id(0)
    per_slot = pl.num_programs(0) // 2
    rows = xa_ref.shape[0]

    @pl.when(i == 0)
    def _():
        for which in range(3):
            for h, source in enumerate((wa_ref, wb_ref)):
                cols = slice(which * 256 + h * HEAD_DIM, which * 256 + (h + 1) * HEAD_DIM)
                w_ref[:, cols] = source[which]
                wt_ref[cols, :] = source[which].T

    x = jnp.where(i < per_slot, xa_ref[...], xb_ref[...])
    all_ref[...] = x
    slot = jnp.where(i < per_slot, meta[0] ^ flip, meta[0] ^ flip ^ 1)
    row = lax.broadcasted_iota(jnp.int32, (rows, HEAD_DIM), 0)
    lane = lax.broadcasted_iota(jnp.int32, (rows, HEAD_DIM), 1)
    index = (i % per_slot) * rows + row - prompt_local
    attended = jnp.logical_or(index < 0, slot * data_local + index < meta[1])
    bias = jnp.where(attended, F32(0.0), F32(MASKED))
    ones = jnp.where(lane < 4, F32(1.0), F32(0.0))
    kx_ref[...] = jnp.where(lane == 0, bias, ones).astype(BF16)
    factor = F32(LOG2E / math.sqrt(HEAD_DIM))
    z = mm(x, w_ref[...])
    q_ref[...] = (z[:, :256] * factor).astype(BF16)
    k_ref[...] = z[:, 256:512].astype(BF16)
    v_ref[...] = z[:, 512:].astype(BF16)
    zt = mm(wt_ref[...], x, NT)
    qt_ref[...] = (zt[:256] * factor).astype(BF16)
    kt_ref[...] = zt[256:512].astype(BF16)
    vt_ref[...] = zt[512:].astype(BF16)


def project(meta, xa, xb, wa, wb, sizes, flip, joined=None):
    rows, width = xa.shape
    step = 512
    n = rows // step
    flat = jax.ShapeDtypeStruct((2 * rows, 256), BF16)
    tall = jax.ShapeDtypeStruct((256, 2 * rows), BF16)
    row = pl.BlockSpec((step, 256), lambda i, meta: (i, 0))
    col = pl.BlockSpec((256, step), lambda i, meta: (0, i))
    extra = [joined] if flip else []

    def own_first(i):
        return (i // n) * 2 * n + (n if flip else 0) + i % n

    return pl.pallas_call(
        partial(project_kernel, sizes, flip),
        out_shape=[
            tall,
            flat,
            flat,
            jax.ShapeDtypeStruct((2 * rows, HEAD_DIM), BF16),
            tall,
            flat,
            tall,
            jax.ShapeDtypeStruct((width, 768), BF16),
            jax.ShapeDtypeStruct((4 * rows, width), BF16),
        ],
        grid_spec=pltpu.PrefetchScalarGridSpec(
            num_scalar_prefetch=1,
            grid=(2 * n,),
            in_specs=[
                pl.BlockSpec((step, width), lambda i, meta: (jnp.minimum(i, n - 1), 0)),
                pl.BlockSpec((step, width), lambda i, meta: (jnp.maximum(i - n, 0), 0)),
                once(wa.shape),
                once(wb.shape),
            ]
            + [pl.BlockSpec(memory_space=pl.ANY)] * len(extra),
            out_specs=[
                col,
                row,
                row,
                pl.BlockSpec((step, HEAD_DIM), lambda i, meta: (i, 0)),
                col,
                row,
                col,
                once((width, 768)),
                pl.BlockSpec((step, width), lambda i, meta: (own_first(i), 0)),
            ],
            scratch_shapes=[pltpu.VMEM((768, width), BF16)],
        ),
        input_output_aliases={5: 8} if flip else {},
        compiler_params=params(),
        cost_estimate=cost(1, 1) if flip else cost(8 * rows * width * 768, rows * width * 16),
        name="project",
    )(meta, xa, xb, wa, wb, *extra)


def head_rows(h):
    return slice(h * HEAD_DIM, (h + 1) * HEAD_DIM)


def with_shift(qt, top):
    high, middle, low = three_parts(top)
    extra = extra_rows([jnp.ones_like(top), -high, -middle, -low], HEAD_DIM)
    return jnp.concatenate([qt, extra], axis=0)


def half_scores(chunk, h, qa, start, k_ref, kx_ref):
    here = pl.ds(start, chunk)
    keys = jnp.concatenate([k_ref[here, head_rows(h)], kx_ref[here, :]], axis=1)
    return mm(keys, qa)


def half_part(h, start, scores, vt_ref, pt_ref):
    chunk = scores.shape[0]
    weight = jnp.exp2(scores)
    total = jnp.sum(weight.reshape(chunk // 8, 8, weight.shape[1]), axis=0)
    low = weight.astype(BF16)
    pt_ref[0, h, pl.ds(start, chunk), :] = low
    return total, mm(vt_ref[head_rows(h), pl.ds(start, chunk)], low)


def stale_shift(h, qt, k_ref):
    top = jnp.max(mm(k_ref[:SAMPLE, head_rows(h)], qt), axis=0, keepdims=True)
    return top, with_shift(qt, top)


def fast_states(chunk, shifts, keys, pts):
    tiles = [
        (h, j, start)
        for h in range(2)
        for j in range(len(keys))
        for start in range(0, keys[0][0].shape[0], chunk)
    ]

    def scores(tile):
        h, j, start = tile
        return half_scores(chunk, h, shifts[h][j][1], start, keys[j][0], keys[j][1])

    sums = {}
    ahead = scores(tiles[0])
    for place, (h, j, start) in enumerate(tiles):
        now = ahead
        if place + 1 < len(tiles):
            ahead = scores(tiles[place + 1])
        total, product = half_part(h, start, now, keys[j][2], pts[j])
        if (h, j) in sums:
            total, product = sums[h, j][0] + total, sums[h, j][1] + product
        sums[h, j] = total, product
    return [
        [
            (shifts[h][j][0], jnp.sum(sums[h, j][0], axis=0, keepdims=True), sums[h, j][1])
            for j in range(len(keys))
        ]
        for h in range(2)
    ]


def half_attend_exact(chunk, h, shift, k_ref, kx_ref, vt_ref, pt_ref):
    qt = shift[1][:HEAD_DIM]
    width = qt.shape[1]
    count = k_ref.shape[0] // chunk
    qa = with_shift(qt, jnp.zeros((1, width), F32))

    def find(j, top):
        found = half_scores(chunk, h, qa, pl.multiple_of(j * chunk, chunk), k_ref, kx_ref)
        return jnp.maximum(top, jnp.max(found, axis=0, keepdims=True))

    top = lax.fori_loop(0, count, find, jnp.full((1, width), MASKED, F32))
    qa = with_shift(qt, top)

    def add(j, state):
        start = pl.multiple_of(j * chunk, chunk)
        found = half_scores(chunk, h, qa, start, k_ref, kx_ref)
        more, product = half_part(h, start, found, vt_ref, pt_ref)
        return state[0] + more, state[1] + product

    total, acc = lax.fori_loop(
        0, count, add, (jnp.zeros((8, width), F32), jnp.zeros((HEAD_DIM, width), F32))
    )
    return top, jnp.sum(total, axis=0, keepdims=True), acc


def merge(states):
    top = states[0][0]
    for state in states[1:]:
        top = jnp.maximum(top, state[0])
    scales = [jnp.exp2(state[0] - top) for state in states]
    total = sum(state[1] * scale for state, scale in zip(states, scales))
    factors = [scale / total for scale in scales]
    return factors, sum(state[2] * factor for state, factor in zip(states, factors))


def redo(states, shifts, keys, pts):
    return [
        [half_attend_exact(256, h, shifts[h][j], *keys[j], pts[j]) for j in range(len(keys))]
        for h in range(2)
    ]


def run_halves(chunk, qt_ref, keys, pts, finish):
    shifts = [
        [stale_shift(h, qt_ref[head_rows(h), :], key_refs[0]) for key_refs in keys]
        for h in range(2)
    ]
    states = fast_states(chunk, shifts, keys, pts)
    worst = None
    for state in states[0] + states[1]:
        worst = state[1] if worst is None else jnp.maximum(worst, state[1])
    finish(states)

    @pl.when(jnp.logical_not(jnp.max(worst) <= LIMIT))
    def _():
        finish(redo(states, shifts, keys, pts))


def attend_first_kernel(chunk, qt_ref, k_ref, kx_ref, vt_ref, pt_ref, state_ref, acc_ref):
    def finish(states):
        for h in range(2):
            top, total, acc = states[h][0]
            state_ref[0, h : h + 1, :] = top
            state_ref[0, 2 + h : 3 + h, :] = total
            acc_ref[head_rows(h), :] = acc

    run_halves(chunk, qt_ref, [(k_ref, kx_ref, vt_ref)], [pt_ref], finish)


def attend_first(qt, key, chunk):
    rows = qt.shape[1]
    n = rows // ROWS
    col = pl.BlockSpec((256, ROWS), lambda i: (0, i))
    pairs = 2 * rows * rows
    return pl.pallas_call(
        partial(attend_first_kernel, chunk),
        out_shape=[
            jax.ShapeDtypeStruct((2 * n, 2, rows, ROWS), BF16),
            jax.ShapeDtypeStruct((n, 8, ROWS), F32),
            jax.ShapeDtypeStruct((256, rows), F32),
        ],
        grid=(n,),
        in_specs=[col] + [once(item.shape) for item in key],
        out_specs=[
            pl.BlockSpec((1, 2, rows, ROWS), lambda i: (i, 0, 0, 0)),
            pl.BlockSpec((1, 8, ROWS), lambda i: (i, 0, 0)),
            col,
        ],
        compiler_params=params(),
        cost_estimate=cost(4 * pairs * HEAD_DIM * 2, 2 * pairs, pairs),
        name="attend_near",
    )(qt, *key)


def attend_second_kernel(
    chunk, qtn_ref, qtf_ref, kn, kxn, vtn, kf, kxf, vtf, old_ref, old_acc_ref, _,
    ptn_ref, ptf_ref, mine_ref, sib_ref, stat_ref,
):
    i = pl.program_id(0)
    n = pl.num_programs(0) // 2
    near, far = (kn, kxn, vtn), (kf, kxf, vtf)

    def store(h, states):
        factors, result = merge(states)
        stat_ref[0, h : h + 1, :] = factors[0]
        stat_ref[0, 2 + h : 3 + h, :] = factors[1]
        low = result.T.astype(BF16)
        first = i % n < n // 2

        @pl.when(first)
        def _():
            mine_ref[:, head_rows(h)] = low

        @pl.when(jnp.logical_not(first))
        def _():
            sib_ref[:, head_rows(h)] = low

    @pl.when(i < n)
    def _():
        def finish(states):
            for h in range(2):
                old = (old_ref[0, h : h + 1, :], old_ref[0, 2 + h : 3 + h, :],
                       old_acc_ref[head_rows(h), :])
                store(h, [old, states[h][0]])

        run_halves(chunk, qtn_ref, [far], [ptf_ref], finish)

    @pl.when(i >= n)
    def _():
        def finish(states):
            for h in range(2):
                store(h, states[h])

        run_halves(chunk, qtf_ref, [near, far], [ptn_ref, ptf_ref], finish)


def mine_block(i, n):
    half = n // 2
    return (i // n) * half + jnp.minimum(i % n, half - 1)


def sib_block(i, n):
    half = n // 2
    return jnp.maximum((i // n) * half + i % n - half, jnp.maximum((i // n) * half - 1, 0))


def attend_second(qtn, qtf, near, far, pt, state, acc, chunk):
    rows = qtn.shape[1]
    n = rows // ROWS
    near_col = pl.BlockSpec((256, ROWS), lambda i: (0, jnp.minimum(i, n - 1)))
    pairs = 6 * rows * rows
    return pl.pallas_call(
        partial(attend_second_kernel, chunk),
        out_shape=[
            jax.ShapeDtypeStruct(pt.shape, BF16),
            jax.ShapeDtypeStruct(pt.shape, BF16),
            jax.ShapeDtypeStruct((rows, 256), BF16),
            jax.ShapeDtypeStruct((rows, 256), BF16),
            jax.ShapeDtypeStruct((2 * n, 8, ROWS), F32),
        ],
        grid=(2 * n,),
        in_specs=[near_col, pl.BlockSpec((256, ROWS), lambda i: (0, jnp.maximum(i - n, 0)))]
        + [once(item.shape) for item in near + far]
        + [
            pl.BlockSpec((1, 8, ROWS), lambda i: (jnp.minimum(i, n - 1), 0, 0)),
            near_col,
            pl.BlockSpec(memory_space=pl.ANY),
        ],
        out_specs=[
            pl.BlockSpec((1, 2, rows, ROWS), lambda i: (jnp.maximum(i, n), 0, 0, 0)),
            pl.BlockSpec((1, 2, rows, ROWS), lambda i: (i, 0, 0, 0)),
            pl.BlockSpec((ROWS, 256), lambda i: (mine_block(i, n), 0)),
            pl.BlockSpec((ROWS, 256), lambda i: (sib_block(i, n), 0)),
            pl.BlockSpec((1, 8, ROWS), lambda i: (i, 0, 0)),
        ],
        input_output_aliases={10: 0},
        compiler_params=params(),
        cost_estimate=cost(1, 1),
        name="attend_rest",
    )(qtn, qtf, *near, *far, state, acc, pt)


def back_weights(do, o, factors):
    dot_t = do.astype(F32).T
    delta = jnp.sum(dot_t * o.astype(F32).T, axis=0, keepdims=True)
    found = []
    for factor in factors:
        scaled = dot_t * factor
        high, middle, low = three_parts(delta * factor)
        extra = extra_rows([-high, -middle, -low], HEAD_DIM)
        found.append(
            (jnp.concatenate([scaled.astype(BF16), extra], axis=0), scaled.T.astype(BF16))
        )
    return found


def back_half(chunk, h, grads, q_rows, pt_ref, v_ref, kt_ref, key_acc, value_acc):
    ones = jnp.where(
        lax.broadcasted_iota(jnp.int32, (chunk, HEAD_DIM), 1) < 3, F32(1.0), F32(0.0)
    ).astype(BF16)
    result = jnp.zeros((HEAD_DIM, q_rows.shape[0]), F32)
    for start in range(0, v_ref.shape[0], chunk):
        here = slice(start, start + chunk)
        prob = pt_ref[0, h, here, :]
        values = jnp.concatenate([v_ref[here, head_rows(h)], ones], axis=1)
        score = (prob.astype(F32) * mm(values, grads[0])).astype(BF16)
        value_acc[h, here, :] += mm(prob, grads[1])
        key_acc[h, here, :] += mm(score, q_rows)
        result = result + mm(kt_ref[head_rows(h), here], score)
    return result


def attend_back_kernel(
    chunk, da_ref, db_ref, oa_ref, ob_ref, stat_ref, qn_ref, qf_ref, ptn_ref, ptf_ref,
    vn, ktn, vf, ktf, dq_ref, dkv_ref, key_n, value_n, key_f, value_f,
):
    i = pl.program_id(0)
    n = pl.num_programs(0) // 2

    @pl.when(i == 0)
    def _():
        for ref in (key_n, value_n, key_f, value_f):
            ref[...] = jnp.zeros_like(ref)

    first = i % n < n // 2
    do = jnp.where(first, da_ref[...], db_ref[...])
    o = jnp.where(first, oa_ref[...], ob_ref[...])
    q = jnp.where(i < n, qn_ref[...], qf_ref[...])
    for h in range(2):
        cols = head_rows(h)
        near, far = back_weights(
            do[:, cols], o[:, cols], [stat_ref[0, h : h + 1, :], stat_ref[0, 2 + h : 3 + h, :]]
        )
        grad = back_half(chunk, h, near, q[:, cols], ptn_ref, vn, ktn, key_n, value_n)
        grad += back_half(chunk, h, far, q[:, cols], ptf_ref, vf, ktf, key_f, value_f)
        dq_ref[:, cols] = (grad * F32(1.0 / math.sqrt(HEAD_DIM))).T.astype(BF16)

    @pl.when(i == 2 * n - 1)
    def _():
        seq = vn.shape[0]
        for half, (keys, values) in enumerate(((key_n, value_n), (key_f, value_f))):
            for owner in range(2):
                source = slice(owner * seq // 2, (owner + 1) * seq // 2)
                begin = owner * seq + half * seq // 2
                rows = slice(begin, begin + seq // 2)
                for h in range(2):
                    dkv_ref[rows, head_rows(h)] = (keys[h, source] * F32(1.0 / LOG2E)).astype(BF16)
                    dkv_ref[rows, head_rows(2 + h)] = values[h, source].astype(BF16)


def attend_back(da, db, oa, ob, stat, qn, qf, ptn, ptf, vn, ktn, vf, ktf, chunk):
    rows = qn.shape[0]
    step = BACK_ROWS
    n = rows // step
    per = ROWS // step
    row = lambda f: pl.BlockSpec((step, 256), lambda i: (f(i), 0))
    tile = pl.BlockSpec((1, 2, rows, step), lambda i: (i // per, 0, 0, i % per))
    flat = jax.ShapeDtypeStruct((2 * rows, 256), BF16)
    wide = jax.ShapeDtypeStruct((2 * rows, 512), BF16)
    acc = pltpu.VMEM((2, rows, HEAD_DIM), F32)

    def own_first(i):
        return jnp.where(i % n < n // 2, 0, n // 2) + (i // n) * (n // 2) + i % n
    pairs = 8 * rows * rows
    return pl.pallas_call(
        partial(attend_back_kernel, chunk),
        out_shape=[flat, wide],
        grid=(2 * n,),
        in_specs=[
            row(lambda i: mine_block(i, n)),
            row(lambda i: sib_block(i, n)),
            row(lambda i: mine_block(i, n)),
            row(lambda i: sib_block(i, n)),
            pl.BlockSpec((1, 8, step), lambda i: (i // per, 0, i % per)),
            row(lambda i: jnp.minimum(i, n - 1)),
            row(lambda i: jnp.maximum(i - n, 0)),
            tile,
            tile,
        ]
        + [once(item.shape) for item in (vn, ktn, vf, ktf)],
        out_specs=[row(own_first), once(wide.shape)],
        scratch_shapes=[acc, acc, acc, acc],
        compiler_params=params(),
        cost_estimate=cost(8 * pairs * HEAD_DIM, 2 * pairs),
        name="attend_back",
    )(da, db, oa, ob, stat, qn, qf, ptn, ptf, vn, ktn, vf, ktf)


def mean(values):
    return jnp.mean(values, axis=-1, keepdims=True)


def norm(values):
    centered = values - mean(values)
    inverse = lax.rsqrt(mean(centered * centered) + EPS)
    return centered * inverse, inverse


def norm_back(incoming, normed, inverse, gain):
    scaled = incoming * gain
    return inverse * (scaled - mean(scaled) - normed * mean(scaled * normed))


def gelu_parts(v):
    bell = jnp.exp2(v * v * F32(-0.5 * LOG2E))
    base = 1.0 + F32(0.3275911 / math.sqrt(2.0)) * jnp.abs(v)
    t = pl.reciprocal(base, approx=True)
    t = t * (2.0 - base * t)
    series = t * (
        F32(0.5 * 0.254829592)
        + t
        * (
            F32(0.5 * -0.284496736)
            + t
            * (
                F32(0.5 * 1.421413741)
                + t * (F32(0.5 * -1.453152027) + t * F32(0.5 * 1.061405429))
            )
        )
    )
    tail = series * bell
    return bell * F32(1.0 / math.sqrt(2.0 * math.pi)), jnp.where(v >= 0, 1.0 - tail, tail)


def fold_rows(values):
    return jnp.sum(values.reshape(values.shape[0] // 8, 8, values.shape[1]), axis=0)


def rows_kernel(
    sizes, meta, xa_ref, xb_ref, oa_ref, ob_ref, cot_a, cot_b, p0, p1, p2, p3,
    u0, u1, u2, u3, vec_ref,
    prompt_near, data_near, prompt_far, data_far, resid_ref, da_ref, db_ref, send_ref,
    sums_ref, wo_ref, up_ref, down_ref, bias_ref, grad_acc, vec_acc, bias_acc,
):
    prompt_local, data_local = sizes
    i = pl.program_id(0)
    half = pl.num_programs(0) // 2
    here = i < half
    rows = xa_ref.shape[0]
    quarter = u0.shape[1]

    @pl.when(i == 0)
    def _():
        for j, (pack, up_part) in enumerate(((p0, u0), (p1, u1), (p2, u2), (p3, u3))):
            cols = slice(j * quarter, (j + 1) * quarter)
            wo_ref[head_rows(j), :] = pack[:HEAD_DIM, :]
            down_ref[cols, :] = pack[HEAD_DIM : HEAD_DIM + quarter, :]
            bias_ref[0:1, cols] = pack[
                HEAD_DIM + quarter : HEAD_DIM + quarter + 16, :quarter
            ].astype(F32)[0:1, :]
            up_ref[:, cols] = up_part[...]
        grad_acc[...] = jnp.zeros_like(grad_acc)
        vec_acc[...] = jnp.zeros_like(vec_acc)
        bias_acc[...] = jnp.zeros_like(bias_acc)

    slot = jnp.where(here, meta[0], meta[0] ^ 2)
    index = (i % half) * rows + lax.broadcasted_iota(jnp.int32, (rows, 1), 0) - prompt_local
    live = jnp.logical_or(index < 0, slot * data_local + index < meta[2])

    out_bias, attn_gain, attn_shift = vec_ref[0:1, :], vec_ref[1:2, :], vec_ref[2:3, :]
    down_bias, mlp_gain, mlp_shift = vec_ref[3:4, :], vec_ref[4:5, :], vec_ref[5:6, :]
    x = jnp.where(here, xa_ref[...], xb_ref[...])
    attended = jnp.concatenate([oa_ref[...], ob_ref[...]], axis=1)
    normed_one, inverse_one = norm(x.astype(F32) + (mm(attended, wo_ref[...]) + out_bias))
    hidden = normed_one * attn_gain + attn_shift
    hidden_low = hidden.astype(BF16)
    pre = mm(hidden_low, up_ref[...]) + bias_ref[0:1, :]
    density, share = gelu_parts(pre)
    activated = (pre * share).astype(BF16)
    slope = share + pre * density
    mixed = hidden + (mm(activated, down_ref[...]) + down_bias)
    normed_two, inverse_two = norm(mixed)
    output = (normed_two * mlp_gain + mlp_shift).astype(BF16)
    cotangent = jnp.where(live, jnp.where(here, cot_a[...], cot_b[...]).astype(F32), 0.0)
    mixed_grad = norm_back(cotangent, normed_two, inverse_two, mlp_gain)
    mixed_low = mixed_grad.astype(BF16)
    pre_grad = (mm(mixed_low, down_ref[...], NT) * slope).astype(BF16)
    hidden_grad = mixed_grad + mm(pre_grad, up_ref[...], NT)
    resid_grad = norm_back(hidden_grad, normed_one, inverse_one, attn_gain)
    resid_ref[...] = resid_grad
    resid_low = resid_grad.astype(BF16)
    attended_grad = mm(resid_low, wo_ref[...], NT).astype(BF16)
    da_ref[...] = attended_grad[:, :256]
    db_ref[...] = attended_grad[:, 256:]

    up_grad = mm(hidden_low, pre_grad, TN)
    down_grad = mm(mixed_low, activated, TN)
    out_grad = mm(resid_low, attended, TN)
    for j in range(4):
        cols = slice(j * quarter, (j + 1) * quarter)
        grad_acc[j, :, :quarter] += up_grad[:, cols]
        grad_acc[j, :, quarter : 2 * quarter] += down_grad[:, cols]
        grad_acc[j, :, 2 * quarter :] += out_grad[:, head_rows(j)]
    bias_acc[...] += fold_rows(pre_grad.astype(F32))
    for place, value in enumerate(
        (
            resid_grad,
            hidden_grad * normed_one,
            hidden_grad,
            mixed_grad,
            cotangent * normed_two,
            cotangent,
        )
    ):
        vec_acc[place] += fold_rows(value)

    for j in range((prompt_local + data_local) // rows):
        split = max(0, min(rows, prompt_local - j * rows))
        for place, (prompt_ref, data_ref) in enumerate(
            ((prompt_near, data_near), (prompt_far, data_far))
        ):

            @pl.when(i == place * half + j)
            def _():
                if split:
                    prompt_ref[j * rows : j * rows + split, :] = output[:split]
                if split < rows:
                    begin = j * rows + split - prompt_local
                    data_ref[begin : begin + rows - split, :] = output[split:]

    @pl.when(i == pl.num_programs(0) - 1)
    def _():
        for place in range(6):
            sums_ref[place : place + 1, :] = jnp.sum(vec_acc[place], axis=0, keepdims=True)
        bias_grad = jnp.sum(bias_acc[...], axis=0, keepdims=True)
        per_row = bias_grad.shape[1] // 2 // quarter
        for g in range(4):
            found = jnp.zeros((1, quarter), F32)
            for j, flip in enumerate((0, 2, 1, 3)):
                piece = bias_grad[:, j * quarter : (j + 1) * quarter]
                found = jnp.where((meta[0] ^ flip) == g, piece, found)
            row, col = 6 + g // per_row, (g % per_row) * quarter
            sums_ref[row : row + 1, col : col + quarter] = found
        depth = send_ref.shape[1] - 16
        groups = send_ref.shape[0] // 4
        width, wide = sums_ref.shape[1], send_ref.shape[2]
        per = sums_ref.shape[0] * width // groups
        for g in range(groups):
            row, col = g * per // width, g * per % width
            part = jnp.pad(sums_ref[row : row + 1, col : col + per], ((0, 0), (0, wide - per)))
            high, low, _ = three_parts(part)
            extra = extra_rows([high, low], 16)
            for j, flip in enumerate((0, 2, 1, 3)):
                target = g * 4 + (meta[0] ^ flip)
                send_ref[target, :depth] = grad_acc[j, g * depth : (g + 1) * depth].astype(BF16)
                send_ref[target, depth:] = extra


def row_work(meta, xa, xb, oa, ob, cot, packs, ups, vec, sizes, groups):
    rows, width = xa.shape
    prompt_local, data_local = sizes
    step = ROW_STEP
    n = rows // step
    quarter = ups[0].shape[1]
    hidden = 4 * quarter
    wide = 2 * quarter + HEAD_DIM
    send = (4 * groups, width // groups + 16, wide)
    near = pl.BlockSpec((step, width), lambda i, meta: (jnp.minimum(i, n - 1), 0))
    far = pl.BlockSpec((step, width), lambda i, meta: (jnp.maximum(i - n, 0), 0))
    row = lambda cols: pl.BlockSpec((step, cols), lambda i, meta: (i, 0))
    return pl.pallas_call(
        partial(rows_kernel, sizes),
        out_shape=[
            jax.ShapeDtypeStruct((prompt_local, width), BF16),
            jax.ShapeDtypeStruct((data_local, width), BF16),
            jax.ShapeDtypeStruct((prompt_local, width), BF16),
            jax.ShapeDtypeStruct((data_local, width), BF16),
            jax.ShapeDtypeStruct((2 * rows, width), F32),
            jax.ShapeDtypeStruct((2 * rows, 256), BF16),
            jax.ShapeDtypeStruct((2 * rows, 256), BF16),
            jax.ShapeDtypeStruct(send, BF16),
        ],
        grid_spec=pltpu.PrefetchScalarGridSpec(
            num_scalar_prefetch=1,
            grid=(2 * n,),
            in_specs=[near, far, row(256), row(256), near, far]
            + [once(item.shape) for item in packs + ups]
            + [once(vec.shape)],
            out_specs=[
                once((prompt_local, width)),
                once((data_local, width)),
                once((prompt_local, width)),
                once((data_local, width)),
                row(width),
                row(256),
                row(256),
                once(send),
            ],
            scratch_shapes=[
                pltpu.VMEM((8, width), F32),
                pltpu.VMEM((4 * HEAD_DIM, width), BF16),
                pltpu.VMEM((width, hidden), BF16),
                pltpu.VMEM((hidden, width), BF16),
                pltpu.VMEM((8, hidden), F32),
                pltpu.VMEM((4, width, wide), F32),
                pltpu.VMEM((6, 8, width), F32),
                pltpu.VMEM((8, hidden), F32),
            ],
        ),
        compiler_params=params(),
        cost_estimate=cost(
            3 * 2 * 2 * rows * width * (width + 2 * hidden), 24 * rows * width, 4 * rows * hidden
        ),
        name="row_work",
    )(meta, xa, xb, oa, ob, *cot, *packs, *ups, vec)


def on_device(
    data_rows,
    prompt_rows,
    context_rows,
    test_rows,
    qkv_weight,
    out_bias,
    out_weight,
    attn_gain,
    attn_shift,
    up_weight,
    up_bias,
    down_weight,
    down_bias,
    mlp_gain,
    mlp_shift,
    data_cotangent,
    prompt_cotangent,
):
    data_local = data_rows.shape[1]
    prompt_local = prompt_rows.shape[0]
    width = prompt_rows.shape[1]
    quarter = up_weight.shape[1]
    sizes = (prompt_local, data_local)
    groups = lax.axis_size("ep")
    t = lax.axis_index("tp")
    mine = t >> 1
    other = 1 - mine

    def across(value):
        return lax.ppermute(value, "tp", [(i, i ^ 2) for i in range(4)])

    def beside(value):
        return lax.ppermute(value, "tp", [(i, i ^ 1) for i in range(4)])

    def pick(values, which):
        return lax.dynamic_index_in_dim(values, which, axis=0, keepdims=False)

    def stack(prompt_part, data_part):
        return jnp.concatenate([prompt_part, data_part], axis=0)

    w_far = across(qkv_weight)
    x_far = stack(prompt_rows, pick(data_rows, other))
    x = stack(prompt_rows, pick(data_rows, mine))
    x_far, x, prompt_cotangent, data_cotangent = lax.optimization_barrier(
        (x_far, x, prompt_cotangent, data_cotangent)
    )
    x_far = across(x_far)
    x_sib = beside(x)
    cot = stack(pick(prompt_cotangent, mine), pick(data_cotangent, mine))
    cot_far = stack(pick(prompt_cotangent, other), pick(data_cotangent, other))
    vec = jnp.stack(
        [out_bias, attn_gain, attn_shift, down_bias, mlp_gain, mlp_shift, mlp_shift, mlp_shift]
    ).astype(F32)
    context = pick(context_rows, mine)
    live = context + pick(test_rows, mine)
    meta = jnp.stack([t, context, live]).astype(jnp.int32)
    meta, cot, cot_far, vec = lax.optimization_barrier((meta, cot, cot_far, vec))

    qtn, qn, kn, kxn, ktn, vn, vtn, w, x_all = project(
        meta, x, x_sib, qkv_weight, w_far, sizes, 0
    )
    ptn, state, state_acc = attend_first(qtn, (kn, kxn, vtn), 512)

    bias_rows = jnp.pad(up_bias[None], ((0, 15), (0, width - quarter)))
    pack = jnp.concatenate([out_weight, down_weight, bias_rows], axis=0)
    x_far, state, pack, up_weight, cot_far = lax.optimization_barrier(
        (x_far, state, pack, up_weight, cot_far)
    )
    x_far_sib = beside(x_far)
    pack_far, up_far = across(pack), across(up_weight)
    cot_far = across(cot_far)
    qtf, qf, kf, kxf, ktf, vf, vtf, _, x_all = project(
        meta, x_far, x_far_sib, qkv_weight, w_far, sizes, 2, x_all
    )
    ptn, ptf, oa, ob, stat = attend_second(
        qtn, qtf, (kn, kxn, vtn), (kf, kxf, vtf), ptn, state, state_acc, 512
    )

    ob_send, cot_far, pack_far, up_far = lax.optimization_barrier((ob, cot_far, pack_far, up_far))
    packs = [pack, pack_far, beside(pack), beside(pack_far)]
    ups = [up_weight, up_far, beside(up_weight), beside(up_far)]
    (prompt_near, data_near, prompt_far, data_far, resid, da, db, send) = row_work(
        meta, x, x_far, oa, beside(ob_send), (cot, cot_far), packs, ups, vec, sizes, groups
    )

    def dot(left, right, dims):
        return lax.dot_general(left, right, dims, preferred_element_type=F32)

    def exchange(parts, axes):
        return lax.all_to_all(parts, axes, 0, 0, tiled=True)

    def gather(part):
        return exchange(jnp.broadcast_to(part[None], (groups,) + part.shape), "ep")

    db = beside(db)
    send = exchange(send, ("ep", "tp"))
    prompt_back, data_back = across(prompt_far), across(data_far)

    dq, dkv = attend_back(
        da, db, oa, ob, stat, qn, qf, ptn, ptf, vn, ktn, vf, ktf, 512
    )
    send, prompt_back, data_back, dq = lax.optimization_barrier((send, prompt_back, data_back, dq))
    depth = width // groups
    total = jnp.sum(send.astype(F32), axis=0)
    part = total[depth : depth + 1] + total[depth + 1 : depth + 2]
    high = lax.optimization_barrier(part.astype(BF16))
    low = (part - high.astype(F32)).astype(BF16)
    total = jnp.concatenate(
        [total[:depth].astype(BF16), high, low, jnp.zeros((14, total.shape[1]), BF16)], axis=0
    )
    total = jnp.broadcast_to(total[None], (groups,) + total.shape)
    total, dq, dkv = lax.optimization_barrier((total, dq, dkv))
    total = exchange(total, "ep")

    slot_rows = prompt_local + data_local
    cut = 2 * slot_rows
    wq, wkv = w[:, :256], w[:, 256:]

    def rows_grad(part):
        return dot(dq[part], wq, NT) + dot(dkv[part], wkv, NT)

    grad_q, grad_kv = dot(x_all, dq, TN), dot(x_all, dkv, TN)

    def head_grad(h):
        return jnp.stack(
            [grad_q[:, head_rows(h)], grad_kv[:, head_rows(h)], grad_kv[:, head_rows(2 + h)]]
        )

    other_grad, dq, dkv = lax.optimization_barrier((head_grad(1).astype(BF16), dq, dkv))
    other_grad = across(other_grad)
    sib = rows_grad(slice(cut, None)).astype(BF16)
    sib, dq, dkv = lax.optimization_barrier((sib, dq, dkv))
    sib = beside(sib)
    own = rows_grad(slice(0, cut)) + resid
    other_grad, own = lax.optimization_barrier((other_grad, own))
    far_rows = (own[slot_rows:] + sib[slot_rows:].astype(F32)).astype(BF16)
    far_prompt = across(far_rows[:prompt_local])
    far_data = across(far_rows[prompt_local:])
    near_rows = own[:slot_rows] + sib[:slot_rows].astype(F32)
    near_data = near_rows[prompt_local:].astype(BF16)

    columns = width // HEAD_DIM
    prompt = near_rows[:prompt_local] + far_prompt.astype(F32)
    prompt = prompt.astype(BF16).reshape(groups, prompt_local // groups, width)
    prompt = jnp.concatenate([prompt[:, :, head_rows(j)] for j in range(columns)], axis=1)
    qkv = (head_grad(0) + other_grad.astype(F32)).astype(BF16).reshape(groups, -1, HEAD_DIM)
    qkv_rows = qkv.shape[1]
    last = jnp.concatenate([qkv, prompt], axis=1)
    total, last = lax.optimization_barrier((total, last))
    last = gather(jnp.sum(exchange(last, "ep").astype(F32), axis=0).astype(BF16))
    qkv = last[:, :qkv_rows].reshape(3, width, HEAD_DIM).astype(F32)
    prompt = last[:, qkv_rows:].reshape(groups, columns, prompt_local // groups, HEAD_DIM)
    prompt_grad = jnp.concatenate([prompt[:, j] for j in range(columns)], axis=2)
    prompt_grad = prompt_grad.reshape(prompt_local, width).astype(F32)

    which = lax.broadcasted_iota(jnp.int32, (2, 1, 1), 0)

    def by_episode(own, received):
        return jnp.where(which == mine, own[None], received[None])

    sums = total[:, depth : depth + 2, : 8 * width // groups].astype(F32)
    sums = (sums[:, 0] + sums[:, 1]).reshape(8, width)
    total = total[:, :depth].reshape(width, -1).astype(F32)
    bias_grad = lax.dynamic_slice_in_dim(sums[6:8].reshape(-1), t * quarter, quarter)
    return (
        by_episode(data_near, data_back),
        by_episode(prompt_near, prompt_back),
        by_episode(near_data, far_data),
        prompt_grad,
        qkv,
        sums[0],
        total[:, 2 * quarter :].T,
        sums[1],
        sums[2],
        total[:, :quarter],
        bias_grad,
        total[:, quarter : 2 * quarter].T,
        sums[3],
        sums[4],
        sums[5],
    )


def solution(mesh):
    return jax.shard_map(
        on_device,
        mesh=mesh,
        in_specs=(
            P("ep", "tp", None),
            P("tp", None),
            P("ep"),
            P("ep"),
            P(None, None, "tp"),
            P(),
            P("tp", None),
            P(),
            P(),
            P(None, "tp"),
            P("tp"),
            P("tp", None),
            P(),
            P(),
            P(),
            P("ep", "tp", None),
            P("ep", "tp", None),
        ),
        out_specs=(
            P("ep", "tp", None),
            P("ep", "tp", None),
            P("ep", "tp", None),
            P("tp", None),
            P(None, None, "tp"),
            P(),
            P("tp", None),
            P(),
            P(),
            P(None, "tp"),
            P("tp"),
            P("tp", None),
            P(),
            P(),
            P(),
        ),
        check_vma=False,
    )
```

```python
from functools import partial
import math

import jax
import jax.numpy as jnp
from jax import lax
from jax.experimental import pallas as pl
from jax.experimental.pallas import tpu as pltpu
from jax.sharding import PartitionSpec as P

HEAD_DIM = 128
ROWS = 512
BACK_ROWS = 256
ROW_STEP = 1024
GATHER_ROWS = 104
SAMPLE = 256
EPS = 1e-05
MASKED = -1e30
LOG2E = math.log2(math.e)
LIMIT = 2.0**60
VMEM = 60 * 1024 * 1024
F32 = jnp.float32
BF16 = jnp.bfloat16
NN = (((1,), (0,)), ((), ()))
NT = (((1,), (1,)), ((), ()))
TN = (((0,), (0,)), ((), ()))


def mm(left, right, dims=NN):
    return lax.dot_general(left, right, dims, preferred_element_type=F32)


def params(**more):
    return pltpu.CompilerParams(vmem_limit_bytes=VMEM, **more)


def cost(flops, nbytes, trans=0):
    return pl.CostEstimate(
        flops=int(flops), bytes_accessed=int(nbytes), transcendentals=int(trans)
    )


def once(shape):
    return pl.BlockSpec(shape, lambda *_: (0,) * len(shape), pipeline_mode=pl.Buffered(1))


def extra_rows(values, count):
    width = values[0].shape[1]
    row = lax.broadcasted_iota(jnp.int32, (count, width), 0)
    out = jnp.zeros((count, width), F32)
    for index, value in enumerate(values):
        out = jnp.where(row == index, value, out)
    return out.astype(BF16)


def three_parts(row):
    high = row.astype(BF16).astype(F32)
    middle = (row - high).astype(BF16).astype(F32)
    return high, middle, row - high - middle


def clamp(i, low, high):
    return jnp.minimum(jnp.maximum(i, low), high)


def project_kernel(sizes, flip, meta, xa_ref, xb_ref, wa_ref, wb_ref, *refs):
    refs = refs[1:] if flip else refs
    qt_ref, q_ref, k_ref, kx_ref, kt_ref, v_ref, vt_ref, w_ref, all_ref, wt_ref = refs
    prompt_local, data_local = sizes
    i = pl.program_id(0)
    per_slot = pl.num_programs(0) // 2
    rows = xa_ref.shape[0]

    @pl.when(i == 0)
    def _():
        for which in range(3):
            for h, source in enumerate((wa_ref, wb_ref)):
                cols = slice(which * 256 + h * HEAD_DIM, which * 256 + (h + 1) * HEAD_DIM)
                w_ref[:, cols] = source[which]
                wt_ref[cols, :] = source[which].T

    x = jnp.where(i < per_slot, xa_ref[...], xb_ref[...])
    all_ref[...] = x
    slot = jnp.where(i < per_slot, meta[0] ^ flip, meta[0] ^ flip ^ 1)
    row = lax.broadcasted_iota(jnp.int32, (rows, HEAD_DIM), 0)
    lane = lax.broadcasted_iota(jnp.int32, (rows, HEAD_DIM), 1)
    index = (i % per_slot) * rows + row - prompt_local
    attended = jnp.logical_or(index < 0, slot * data_local + index < meta[1])
    bias = jnp.where(attended, F32(0.0), F32(MASKED))
    ones = jnp.where(lane < 4, F32(1.0), F32(0.0))
    kx_ref[...] = jnp.where(lane == 0, bias, ones).astype(BF16)
    factor = F32(LOG2E / math.sqrt(HEAD_DIM))
    z = mm(x, w_ref[...])
    q_ref[...] = (z[:, :256] * factor).astype(BF16)
    k_ref[...] = z[:, 256:512].astype(BF16)
    v_ref[...] = z[:, 512:].astype(BF16)
    zt = mm(wt_ref[...], x, NT)
    qt_ref[...] = (zt[:256] * factor).astype(BF16)
    kt_ref[...] = zt[256:512].astype(BF16)
    vt_ref[...] = zt[512:].astype(BF16)


def project(meta, xa, xb, wa, wb, sizes, flip, joined=None):
    rows, width = xa.shape
    step = 512
    n = rows // step
    flat = jax.ShapeDtypeStruct((2 * rows, 256), BF16)
    tall = jax.ShapeDtypeStruct((256, 2 * rows), BF16)
    row = pl.BlockSpec((step, 256), lambda i, meta: (i, 0))
    col = pl.BlockSpec((256, step), lambda i, meta: (0, i))
    extra = [joined] if flip else []

    def own_first(i):
        return (i // n) * 2 * n + (n if flip else 0) + i % n

    return pl.pallas_call(
        partial(project_kernel, sizes, flip),
        out_shape=[
            tall,
            flat,
            flat,
            jax.ShapeDtypeStruct((2 * rows, HEAD_DIM), BF16),
            tall,
            flat,
            tall,
            jax.ShapeDtypeStruct((width, 768), BF16),
            jax.ShapeDtypeStruct((4 * rows, width), BF16),
        ],
        grid_spec=pltpu.PrefetchScalarGridSpec(
            num_scalar_prefetch=1,
            grid=(2 * n,),
            in_specs=[
                pl.BlockSpec((step, width), lambda i, meta: (jnp.minimum(i, n - 1), 0)),
                pl.BlockSpec((step, width), lambda i, meta: (jnp.maximum(i - n, 0), 0)),
                once(wa.shape),
                once(wb.shape),
            ]
            + [pl.BlockSpec(memory_space=pl.ANY)] * len(extra),
            out_specs=[
                col,
                row,
                row,
                pl.BlockSpec((step, HEAD_DIM), lambda i, meta: (i, 0)),
                col,
                row,
                col,
                once((width, 768)),
                pl.BlockSpec((step, width), lambda i, meta: (own_first(i), 0)),
            ],
            scratch_shapes=[pltpu.VMEM((768, width), BF16)],
        ),
        input_output_aliases={5: 8} if flip else {},
        compiler_params=params(),
        cost_estimate=cost(1, 1) if flip else cost(8 * rows * width * 768, rows * width * 16),
        name="project",
    )(meta, xa, xb, wa, wb, *extra)


def head_rows(h):
    return slice(h * HEAD_DIM, (h + 1) * HEAD_DIM)


def with_shift(qt, top):
    high, middle, low = three_parts(top)
    extra = extra_rows([jnp.ones_like(top), -high, -middle, -low], HEAD_DIM)
    return jnp.concatenate([qt, extra], axis=0)


def half_scores(chunk, h, qa, start, k_ref, kx_ref):
    here = pl.ds(start, chunk)
    keys = jnp.concatenate([k_ref[here, head_rows(h)], kx_ref[here, :]], axis=1)
    return mm(keys, qa)


def half_part(h, start, scores, vt_ref, pt_ref):
    chunk = scores.shape[0]
    weight = jnp.exp2(scores)
    total = jnp.sum(weight.reshape(chunk // 8, 8, weight.shape[1]), axis=0)
    low = weight.astype(BF16)
    pt_ref[0, h, pl.ds(start, chunk), :] = low
    return total, mm(vt_ref[head_rows(h), pl.ds(start, chunk)], low)


def stale_shift(h, qt, k_ref):
    top = jnp.max(mm(k_ref[:SAMPLE, head_rows(h)], qt), axis=0, keepdims=True)
    return top, with_shift(qt, top)


def fast_states(chunk, shifts, keys, pts):
    tiles = [
        (h, j, start)
        for h in range(2)
        for j in range(len(keys))
        for start in range(0, keys[0][0].shape[0], chunk)
    ]

    def scores(tile):
        h, j, start = tile
        return half_scores(chunk, h, shifts[h][j][1], start, keys[j][0], keys[j][1])

    sums = {}
    ahead = scores(tiles[0])
    for place, (h, j, start) in enumerate(tiles):
        now = ahead
        if place + 1 < len(tiles):
            ahead = scores(tiles[place + 1])
        total, product = half_part(h, start, now, keys[j][2], pts[j])
        if (h, j) in sums:
            total, product = sums[h, j][0] + total, sums[h, j][1] + product
        sums[h, j] = total, product
    return [
        [
            (shifts[h][j][0], jnp.sum(sums[h, j][0], axis=0, keepdims=True), sums[h, j][1])
            for j in range(len(keys))
        ]
        for h in range(2)
    ]


def half_attend_exact(chunk, h, shift, k_ref, kx_ref, vt_ref, pt_ref):
    qt = shift[1][:HEAD_DIM]
    width = qt.shape[1]
    count = k_ref.shape[0] // chunk
    qa = with_shift(qt, jnp.zeros((1, width), F32))

    def find(j, top):
        found = half_scores(chunk, h, qa, pl.multiple_of(j * chunk, chunk), k_ref, kx_ref)
        return jnp.maximum(top, jnp.max(found, axis=0, keepdims=True))

    top = lax.fori_loop(0, count, find, jnp.full((1, width), MASKED, F32))
    qa = with_shift(qt, top)

    def add(j, state):
        start = pl.multiple_of(j * chunk, chunk)
        found = half_scores(chunk, h, qa, start, k_ref, kx_ref)
        more, product = half_part(h, start, found, vt_ref, pt_ref)
        return state[0] + more, state[1] + product

    total, acc = lax.fori_loop(
        0, count, add, (jnp.zeros((8, width), F32), jnp.zeros((HEAD_DIM, width), F32))
    )
    return top, jnp.sum(total, axis=0, keepdims=True), acc


def merge(states):
    top = states[0][0]
    for state in states[1:]:
        top = jnp.maximum(top, state[0])
    scales = [jnp.exp2(state[0] - top) for state in states]
    total = sum(state[1] * scale for state, scale in zip(states, scales))
    factors = [scale / total for scale in scales]
    return factors, sum(state[2] * factor for state, factor in zip(states, factors))


def redo(states, shifts, keys, pts):
    return [
        [half_attend_exact(256, h, shifts[h][j], *keys[j], pts[j]) for j in range(len(keys))]
        for h in range(2)
    ]


def run_halves(chunk, qt_ref, keys, pts, finish):
    shifts = [
        [stale_shift(h, qt_ref[head_rows(h), :], key_refs[0]) for key_refs in keys]
        for h in range(2)
    ]
    states = fast_states(chunk, shifts, keys, pts)
    worst = None
    for state in states[0] + states[1]:
        worst = state[1] if worst is None else jnp.maximum(worst, state[1])
    finish(states)

    @pl.when(jnp.logical_not(jnp.max(worst) <= LIMIT))
    def _():
        finish(redo(states, shifts, keys, pts))


def attend_first_kernel(chunk, qt_ref, k_ref, kx_ref, vt_ref, pt_ref, state_ref, acc_ref):
    def finish(states):
        for h in range(2):
            top, total, acc = states[h][0]
            state_ref[0, h : h + 1, :] = top
            state_ref[0, 2 + h : 3 + h, :] = total
            acc_ref[head_rows(h), :] = acc

    run_halves(chunk, qt_ref, [(k_ref, kx_ref, vt_ref)], [pt_ref], finish)


def attend_first(qt, key, chunk):
    rows = qt.shape[1]
    n = rows // ROWS
    col = pl.BlockSpec((256, ROWS), lambda i: (0, i))
    pairs = 2 * rows * rows
    return pl.pallas_call(
        partial(attend_first_kernel, chunk),
        out_shape=[
            jax.ShapeDtypeStruct((2 * n, 2, rows, ROWS), BF16),
            jax.ShapeDtypeStruct((n, 8, ROWS), F32),
            jax.ShapeDtypeStruct((256, rows), F32),
        ],
        grid=(n,),
        in_specs=[col] + [once(item.shape) for item in key],
        out_specs=[
            pl.BlockSpec((1, 2, rows, ROWS), lambda i: (i, 0, 0, 0)),
            pl.BlockSpec((1, 8, ROWS), lambda i: (i, 0, 0)),
            col,
        ],
        compiler_params=params(),
        cost_estimate=cost(4 * pairs * HEAD_DIM * 2, 2 * pairs, pairs),
        name="attend_near",
    )(qt, *key)


def attend_second_kernel(
    chunk, qtn_ref, qtf_ref, kn, kxn, vtn, kf, kxf, vtf, old_ref, old_acc_ref, _,
    ptn_ref, ptf_ref, mine_ref, sib_ref, stat_ref,
):
    i = pl.program_id(0)
    n = pl.num_programs(0) // 2
    near, far = (kn, kxn, vtn), (kf, kxf, vtf)

    def store(h, states):
        factors, result = merge(states)
        stat_ref[0, h : h + 1, :] = factors[0]
        stat_ref[0, 2 + h : 3 + h, :] = factors[1]
        low = result.T.astype(BF16)
        first = i % n < n // 2

        @pl.when(first)
        def _():
            mine_ref[:, head_rows(h)] = low

        @pl.when(jnp.logical_not(first))
        def _():
            sib_ref[:, head_rows(h)] = low

    @pl.when(i < n)
    def _():
        def finish(states):
            for h in range(2):
                old = (old_ref[0, h : h + 1, :], old_ref[0, 2 + h : 3 + h, :],
                       old_acc_ref[head_rows(h), :])
                store(h, [old, states[h][0]])

        run_halves(chunk, qtn_ref, [far], [ptf_ref], finish)

    @pl.when(i >= n)
    def _():
        def finish(states):
            for h in range(2):
                store(h, states[h])

        run_halves(chunk, qtf_ref, [near, far], [ptn_ref, ptf_ref], finish)


def mine_block(i, n):
    half = n // 2
    return (i // n) * half + jnp.minimum(i % n, half - 1)


def sib_block(i, n):
    half = n // 2
    return jnp.maximum((i // n) * half + i % n - half, jnp.maximum((i // n) * half - 1, 0))


def attend_second(qtn, qtf, near, far, pt, state, acc, chunk):
    rows = qtn.shape[1]
    n = rows // ROWS
    near_col = pl.BlockSpec((256, ROWS), lambda i: (0, jnp.minimum(i, n - 1)))
    pairs = 6 * rows * rows
    return pl.pallas_call(
        partial(attend_second_kernel, chunk),
        out_shape=[
            jax.ShapeDtypeStruct(pt.shape, BF16),
            jax.ShapeDtypeStruct(pt.shape, BF16),
            jax.ShapeDtypeStruct((rows, 256), BF16),
            jax.ShapeDtypeStruct((rows, 256), BF16),
            jax.ShapeDtypeStruct((2 * n, 8, ROWS), F32),
        ],
        grid=(2 * n,),
        in_specs=[near_col, pl.BlockSpec((256, ROWS), lambda i: (0, jnp.maximum(i - n, 0)))]
        + [once(item.shape) for item in near + far]
        + [
            pl.BlockSpec((1, 8, ROWS), lambda i: (jnp.minimum(i, n - 1), 0, 0)),
            near_col,
            pl.BlockSpec(memory_space=pl.ANY),
        ],
        out_specs=[
            pl.BlockSpec((1, 2, rows, ROWS), lambda i: (jnp.maximum(i, n), 0, 0, 0)),
            pl.BlockSpec((1, 2, rows, ROWS), lambda i: (i, 0, 0, 0)),
            pl.BlockSpec((ROWS, 256), lambda i: (mine_block(i, n), 0)),
            pl.BlockSpec((ROWS, 256), lambda i: (sib_block(i, n), 0)),
            pl.BlockSpec((1, 8, ROWS), lambda i: (i, 0, 0)),
        ],
        input_output_aliases={10: 0},
        compiler_params=params(),
        cost_estimate=cost(1, 1),
        name="attend_rest",
    )(qtn, qtf, *near, *far, state, acc, pt)


def back_weights(do, o, factors):
    dot_t = do.astype(F32).T
    delta = jnp.sum(dot_t * o.astype(F32).T, axis=0, keepdims=True)
    found = []
    for factor in factors:
        scaled = dot_t * factor
        high, middle, low = three_parts(delta * factor)
        extra = extra_rows([-high, -middle, -low], HEAD_DIM)
        found.append(
            (jnp.concatenate([scaled.astype(BF16), extra], axis=0), scaled.T.astype(BF16))
        )
    return found


def back_half(chunk, h, grads, q_rows, pt_ref, v_ref, kt_ref, key_acc, value_acc):
    ones = jnp.where(
        lax.broadcasted_iota(jnp.int32, (chunk, HEAD_DIM), 1) < 3, F32(1.0), F32(0.0)
    ).astype(BF16)
    result = jnp.zeros((HEAD_DIM, q_rows.shape[0]), F32)
    for start in range(0, v_ref.shape[0], chunk):
        here = slice(start, start + chunk)
        prob = pt_ref[0, h, here, :]
        values = jnp.concatenate([v_ref[here, head_rows(h)], ones], axis=1)
        score = (prob.astype(F32) * mm(values, grads[0])).astype(BF16)
        value_acc[h, here, :] += mm(prob, grads[1])
        key_acc[h, here, :] += mm(score, q_rows)
        result = result + mm(kt_ref[head_rows(h), here], score)
    return result


def attend_back_kernel(
    chunk, da_ref, db_ref, oa_ref, ob_ref, stat_ref, qn_ref, qf_ref, ptn_ref, ptf_ref,
    vn, ktn, vf, ktf, dq_ref, dkv_ref, key_n, value_n, key_f, value_f,
):
    i = pl.program_id(0)
    n = pl.num_programs(0) // 2

    @pl.when(i == 0)
    def _():
        for ref in (key_n, value_n, key_f, value_f):
            ref[...] = jnp.zeros_like(ref)

    first = i % n < n // 2
    do = jnp.where(first, da_ref[...], db_ref[...])
    o = jnp.where(first, oa_ref[...], ob_ref[...])
    q = jnp.where(i < n, qn_ref[...], qf_ref[...])
    for h in range(2):
        cols = head_rows(h)
        near, far = back_weights(
            do[:, cols], o[:, cols], [stat_ref[0, h : h + 1, :], stat_ref[0, 2 + h : 3 + h, :]]
        )
        grad = back_half(chunk, h, near, q[:, cols], ptn_ref, vn, ktn, key_n, value_n)
        grad += back_half(chunk, h, far, q[:, cols], ptf_ref, vf, ktf, key_f, value_f)
        dq_ref[:, cols] = (grad * F32(1.0 / math.sqrt(HEAD_DIM))).T.astype(BF16)

    @pl.when(i == 2 * n - 1)
    def _():
        seq = vn.shape[0]
        for half, (keys, values) in enumerate(((key_n, value_n), (key_f, value_f))):
            for owner in range(2):
                source = slice(owner * seq // 2, (owner + 1) * seq // 2)
                begin = owner * seq + half * seq // 2
                rows = slice(begin, begin + seq // 2)
                for h in range(2):
                    dkv_ref[rows, head_rows(h)] = (keys[h, source] * F32(1.0 / LOG2E)).astype(BF16)
                    dkv_ref[rows, head_rows(2 + h)] = values[h, source].astype(BF16)


def attend_back(da, db, oa, ob, stat, qn, qf, ptn, ptf, vn, ktn, vf, ktf, chunk):
    rows = qn.shape[0]
    step = BACK_ROWS
    n = rows // step
    per = ROWS // step
    row = lambda f: pl.BlockSpec((step, 256), lambda i: (f(i), 0))
    tile = pl.BlockSpec((1, 2, rows, step), lambda i: (i // per, 0, 0, i % per))
    flat = jax.ShapeDtypeStruct((2 * rows, 256), BF16)
    wide = jax.ShapeDtypeStruct((2 * rows, 512), BF16)
    acc = pltpu.VMEM((2, rows, HEAD_DIM), F32)

    def own_first(i):
        return jnp.where(i % n < n // 2, 0, n // 2) + (i // n) * (n // 2) + i % n
    pairs = 8 * rows * rows
    return pl.pallas_call(
        partial(attend_back_kernel, chunk),
        out_shape=[flat, wide],
        grid=(2 * n,),
        in_specs=[
            row(lambda i: mine_block(i, n)),
            row(lambda i: sib_block(i, n)),
            row(lambda i: mine_block(i, n)),
            row(lambda i: sib_block(i, n)),
            pl.BlockSpec((1, 8, step), lambda i: (i // per, 0, i % per)),
            row(lambda i: jnp.minimum(i, n - 1)),
            row(lambda i: jnp.maximum(i - n, 0)),
            tile,
            tile,
        ]
        + [once(item.shape) for item in (vn, ktn, vf, ktf)],
        out_specs=[row(own_first), once(wide.shape)],
        scratch_shapes=[acc, acc, acc, acc],
        compiler_params=params(),
        cost_estimate=cost(8 * pairs * HEAD_DIM, 2 * pairs),
        name="attend_back",
    )(da, db, oa, ob, stat, qn, qf, ptn, ptf, vn, ktn, vf, ktf)


def mean(values):
    return jnp.mean(values, axis=-1, keepdims=True)


def norm(values):
    centered = values - mean(values)
    inverse = lax.rsqrt(mean(centered * centered) + EPS)
    return centered * inverse, inverse


def norm_back(incoming, normed, inverse, gain):
    scaled = incoming * gain
    return inverse * (scaled - mean(scaled) - normed * mean(scaled * normed))


def gelu_parts(v):
    bell = jnp.exp2(v * v * F32(-0.5 * LOG2E))
    base = 1.0 + F32(0.3275911 / math.sqrt(2.0)) * jnp.abs(v)
    t = pl.reciprocal(base, approx=True)
    t = t * (2.0 - base * t)
    series = t * (
        F32(0.5 * 0.254829592)
        + t
        * (
            F32(0.5 * -0.284496736)
            + t
            * (
                F32(0.5 * 1.421413741)
                + t * (F32(0.5 * -1.453152027) + t * F32(0.5 * 1.061405429))
            )
        )
    )
    tail = series * bell
    return bell * F32(1.0 / math.sqrt(2.0 * math.pi)), jnp.where(v >= 0, 1.0 - tail, tail)


def fold_rows(values):
    return jnp.sum(values.reshape(values.shape[0] // 8, 8, values.shape[1]), axis=0)


def rows_kernel(
    sizes, meta, xa_ref, xb_ref, oa_ref, ob_ref, cot_a, cot_b, p0, p1, p2, p3,
    u0, u1, u2, u3, vec_ref,
    prompt_near, data_near, prompt_far, data_far, resid_ref, da_ref, db_ref, send_ref,
    sums_ref, wo_ref, up_ref, down_ref, bias_ref, grad_acc, vec_acc, bias_acc,
):
    prompt_local, data_local = sizes
    i = pl.program_id(0)
    half = pl.num_programs(0) // 2
    here = i < half
    rows = xa_ref.shape[0]
    quarter = u0.shape[1]

    @pl.when(i == 0)
    def _():
        for j, (pack, up_part) in enumerate(((p0, u0), (p1, u1), (p2, u2), (p3, u3))):
            cols = slice(j * quarter, (j + 1) * quarter)
            wo_ref[head_rows(j), :] = pack[:HEAD_DIM, :]
            down_ref[cols, :] = pack[HEAD_DIM : HEAD_DIM + quarter, :]
            bias_ref[0:1, cols] = pack[
                HEAD_DIM + quarter : HEAD_DIM + quarter + 16, :quarter
            ].astype(F32)[0:1, :]
            up_ref[:, cols] = up_part[...]
        grad_acc[...] = jnp.zeros_like(grad_acc)
        vec_acc[...] = jnp.zeros_like(vec_acc)
        bias_acc[...] = jnp.zeros_like(bias_acc)

    slot = jnp.where(here, meta[0], meta[0] ^ 2)
    index = (i % half) * rows + lax.broadcasted_iota(jnp.int32, (rows, 1), 0) - prompt_local
    live = jnp.logical_or(index < 0, slot * data_local + index < meta[2])

    out_bias, attn_gain, attn_shift = vec_ref[0:1, :], vec_ref[1:2, :], vec_ref[2:3, :]
    down_bias, mlp_gain, mlp_shift = vec_ref[3:4, :], vec_ref[4:5, :], vec_ref[5:6, :]
    x = jnp.where(here, xa_ref[...], xb_ref[...])
    attended = jnp.concatenate([oa_ref[...], ob_ref[...]], axis=1)
    normed_one, inverse_one = norm(x.astype(F32) + (mm(attended, wo_ref[...]) + out_bias))
    hidden = normed_one * attn_gain + attn_shift
    hidden_low = hidden.astype(BF16)
    pre = mm(hidden_low, up_ref[...]) + bias_ref[0:1, :]
    density, share = gelu_parts(pre)
    activated = (pre * share).astype(BF16)
    slope = share + pre * density
    mixed = hidden + (mm(activated, down_ref[...]) + down_bias)
    normed_two, inverse_two = norm(mixed)
    output = (normed_two * mlp_gain + mlp_shift).astype(BF16)
    cotangent = jnp.where(live, jnp.where(here, cot_a[...], cot_b[...]).astype(F32), 0.0)
    mixed_grad = norm_back(cotangent, normed_two, inverse_two, mlp_gain)
    mixed_low = mixed_grad.astype(BF16)
    pre_grad = (mm(mixed_low, down_ref[...], NT) * slope).astype(BF16)
    hidden_grad = mixed_grad + mm(pre_grad, up_ref[...], NT)
    resid_grad = norm_back(hidden_grad, normed_one, inverse_one, attn_gain)
    resid_ref[...] = resid_grad
    resid_low = resid_grad.astype(BF16)
    attended_grad = mm(resid_low, wo_ref[...], NT).astype(BF16)
    da_ref[...] = attended_grad[:, :256]
    db_ref[...] = attended_grad[:, 256:]

    up_grad = mm(hidden_low, pre_grad, TN)
    down_grad = mm(mixed_low, activated, TN)
    out_grad = mm(resid_low, attended, TN)
    for j in range(4):
        cols = slice(j * quarter, (j + 1) * quarter)
        grad_acc[j, :, :quarter] += up_grad[:, cols]
        grad_acc[j, :, quarter : 2 * quarter] += down_grad[:, cols]
        grad_acc[j, :, 2 * quarter :] += out_grad[:, head_rows(j)]
    bias_acc[...] += fold_rows(pre_grad.astype(F32))
    for place, value in enumerate(
        (
            resid_grad,
            hidden_grad * normed_one,
            hidden_grad,
            mixed_grad,
            cotangent * normed_two,
            cotangent,
        )
    ):
        vec_acc[place] += fold_rows(value)

    for j in range((prompt_local + data_local) // rows):
        split = max(0, min(rows, prompt_local - j * rows))
        for place, (prompt_ref, data_ref) in enumerate(
            ((prompt_near, data_near), (prompt_far, data_far))
        ):

            @pl.when(i == place * half + j)
            def _():
                if split:
                    prompt_ref[j * rows : j * rows + split, :] = output[:split]
                if split < rows:
                    begin = j * rows + split - prompt_local
                    data_ref[begin : begin + rows - split, :] = output[split:]

    @pl.when(i == pl.num_programs(0) - 1)
    def _():
        for place in range(6):
            sums_ref[place : place + 1, :] = jnp.sum(vec_acc[place], axis=0, keepdims=True)
        bias_grad = jnp.sum(bias_acc[...], axis=0, keepdims=True)
        per_row = bias_grad.shape[1] // 2 // quarter
        for g in range(4):
            found = jnp.zeros((1, quarter), F32)
            for j, flip in enumerate((0, 2, 1, 3)):
                piece = bias_grad[:, j * quarter : (j + 1) * quarter]
                found = jnp.where((meta[0] ^ flip) == g, piece, found)
            row, col = 6 + g // per_row, (g % per_row) * quarter
            sums_ref[row : row + 1, col : col + quarter] = found
        depth = send_ref.shape[1] - 16
        groups = send_ref.shape[0] // 4
        width, wide = sums_ref.shape[1], send_ref.shape[2]
        per = sums_ref.shape[0] * width // groups
        for g in range(groups):
            row, col = g * per // width, g * per % width
            part = jnp.pad(sums_ref[row : row + 1, col : col + per], ((0, 0), (0, wide - per)))
            high, low, _ = three_parts(part)
            extra = extra_rows([high, low], 16)
            for j, flip in enumerate((0, 2, 1, 3)):
                target = g * 4 + (meta[0] ^ flip)
                send_ref[target, :depth] = grad_acc[j, g * depth : (g + 1) * depth].astype(BF16)
                send_ref[target, depth:] = extra


def row_work(meta, xa, xb, oa, ob, cot, packs, ups, vec, sizes, groups):
    rows, width = xa.shape
    prompt_local, data_local = sizes
    step = ROW_STEP
    n = rows // step
    quarter = ups[0].shape[1]
    hidden = 4 * quarter
    wide = 2 * quarter + HEAD_DIM
    send = (4 * groups, width // groups + 16, wide)
    near = pl.BlockSpec((step, width), lambda i, meta: (jnp.minimum(i, n - 1), 0))
    far = pl.BlockSpec((step, width), lambda i, meta: (jnp.maximum(i - n, 0), 0))
    row = lambda cols: pl.BlockSpec((step, cols), lambda i, meta: (i, 0))
    return pl.pallas_call(
        partial(rows_kernel, sizes),
        out_shape=[
            jax.ShapeDtypeStruct((prompt_local, width), BF16),
            jax.ShapeDtypeStruct((data_local, width), BF16),
            jax.ShapeDtypeStruct((prompt_local, width), BF16),
            jax.ShapeDtypeStruct((data_local, width), BF16),
            jax.ShapeDtypeStruct((2 * rows, width), F32),
            jax.ShapeDtypeStruct((2 * rows, 256), BF16),
            jax.ShapeDtypeStruct((2 * rows, 256), BF16),
            jax.ShapeDtypeStruct(send, BF16),
        ],
        grid_spec=pltpu.PrefetchScalarGridSpec(
            num_scalar_prefetch=1,
            grid=(2 * n,),
            in_specs=[near, far, row(256), row(256), near, far]
            + [once(item.shape) for item in packs + ups]
            + [once(vec.shape)],
            out_specs=[
                once((prompt_local, width)),
                once((data_local, width)),
                once((prompt_local, width)),
                once((data_local, width)),
                row(width),
                row(256),
                row(256),
                once(send),
            ],
            scratch_shapes=[
                pltpu.VMEM((8, width), F32),
                pltpu.VMEM((4 * HEAD_DIM, width), BF16),
                pltpu.VMEM((width, hidden), BF16),
                pltpu.VMEM((hidden, width), BF16),
                pltpu.VMEM((8, hidden), F32),
                pltpu.VMEM((4, width, wide), F32),
                pltpu.VMEM((6, 8, width), F32),
                pltpu.VMEM((8, hidden), F32),
            ],
        ),
        compiler_params=params(),
        cost_estimate=cost(
            3 * 2 * 2 * rows * width * (width + 2 * hidden), 24 * rows * width, 4 * rows * hidden
        ),
        name="row_work",
    )(meta, xa, xb, oa, ob, *cot, *packs, *ups, vec)


def on_device(
    data_rows,
    prompt_rows,
    context_rows,
    test_rows,
    qkv_weight,
    out_bias,
    out_weight,
    attn_gain,
    attn_shift,
    up_weight,
    up_bias,
    down_weight,
    down_bias,
    mlp_gain,
    mlp_shift,
    data_cotangent,
    prompt_cotangent,
):
    data_local = data_rows.shape[1]
    prompt_local = prompt_rows.shape[0]
    width = prompt_rows.shape[1]
    quarter = up_weight.shape[1]
    sizes = (prompt_local, data_local)
    groups = lax.axis_size("ep")
    t = lax.axis_index("tp")
    mine = t >> 1
    other = 1 - mine

    def across(value):
        return lax.ppermute(value, "tp", [(i, i ^ 2) for i in range(4)])

    def beside(value):
        return lax.ppermute(value, "tp", [(i, i ^ 1) for i in range(4)])

    def pick(values, which):
        return lax.dynamic_index_in_dim(values, which, axis=0, keepdims=False)

    def stack(prompt_part, data_part):
        return jnp.concatenate([prompt_part, data_part], axis=0)

    w_far = across(qkv_weight)
    x_far = stack(prompt_rows, pick(data_rows, other))
    x = stack(prompt_rows, pick(data_rows, mine))
    x_far, x, prompt_cotangent, data_cotangent = lax.optimization_barrier(
        (x_far, x, prompt_cotangent, data_cotangent)
    )
    x_far = across(x_far)
    x_sib = beside(x)
    cot = stack(pick(prompt_cotangent, mine), pick(data_cotangent, mine))
    cot_far = stack(pick(prompt_cotangent, other), pick(data_cotangent, other))
    vec = jnp.stack(
        [out_bias, attn_gain, attn_shift, down_bias, mlp_gain, mlp_shift, mlp_shift, mlp_shift]
    ).astype(F32)
    context = pick(context_rows, mine)
    live = context + pick(test_rows, mine)
    meta = jnp.stack([t, context, live]).astype(jnp.int32)
    meta, cot, cot_far, vec = lax.optimization_barrier((meta, cot, cot_far, vec))

    qtn, qn, kn, kxn, ktn, vn, vtn, w, x_all = project(
        meta, x, x_sib, qkv_weight, w_far, sizes, 0
    )
    ptn, state, state_acc = attend_first(qtn, (kn, kxn, vtn), 512)

    bias_rows = jnp.pad(up_bias[None], ((0, 15), (0, width - quarter)))
    pack = jnp.concatenate([out_weight, down_weight, bias_rows], axis=0)
    x_far, state, pack, up_weight, cot_far = lax.optimization_barrier(
        (x_far, state, pack, up_weight, cot_far)
    )
    x_far_sib = beside(x_far)
    pack_far, up_far = across(pack), across(up_weight)
    cot_far = across(cot_far)
    pack_sib, up_sib = beside(pack), beside(up_weight)
    qtf, qf, kf, kxf, ktf, vf, vtf, _, x_all = project(
        meta, x_far, x_far_sib, qkv_weight, w_far, sizes, 2, x_all
    )
    ptn, ptf, oa, ob, stat = attend_second(
        qtn, qtf, (kn, kxn, vtn), (kf, kxf, vtf), ptn, state, state_acc, 512
    )

    ob_send, cot_far, pack_far, up_far, pack_sib, up_sib = lax.optimization_barrier(
        (ob, cot_far, pack_far, up_far, pack_sib, up_sib)
    )
    packs = [pack, pack_far, pack_sib, beside(pack_far)]
    ups = [up_weight, up_far, up_sib, beside(up_far)]
    (prompt_near, data_near, prompt_far, data_far, resid, da, db, send) = row_work(
        meta, x, x_far, oa, beside(ob_send), (cot, cot_far), packs, ups, vec, sizes, groups
    )

    def dot(left, right, dims):
        return lax.dot_general(left, right, dims, preferred_element_type=F32)

    def exchange(parts, axes):
        return lax.all_to_all(parts, axes, 0, 0, tiled=True)

    def gather(part):
        return exchange(jnp.broadcast_to(part[None], (groups,) + part.shape), "ep")

    db = beside(db)
    send = exchange(send, ("ep", "tp"))
    prompt_back, data_back = across(prompt_far), across(data_far)

    dq, dkv = attend_back(
        da, db, oa, ob, stat, qn, qf, ptn, ptf, vn, ktn, vf, ktf, 512
    )
    send, prompt_back, data_back, dq = lax.optimization_barrier((send, prompt_back, data_back, dq))
    depth = width // groups
    total = jnp.sum(send.astype(F32), axis=0)
    part = total[depth : depth + 1] + total[depth + 1 : depth + 2]
    total = jnp.concatenate([total[:depth], part], axis=0)
    total = jnp.pad(total, ((0, GATHER_ROWS - depth - 1), (0, 0)))
    total, dq, dkv = lax.optimization_barrier((total, dq, dkv))
    total = lax.all_gather(total, "ep", axis=0, tiled=False)

    slot_rows = prompt_local + data_local
    cut = 2 * slot_rows
    wq, wkv = w[:, :256], w[:, 256:]

    def rows_grad(part):
        return dot(dq[part], wq, NT) + dot(dkv[part], wkv, NT)

    grad_q, grad_kv = dot(x_all, dq, TN), dot(x_all, dkv, TN)

    def head_grad(h):
        return jnp.stack(
            [grad_q[:, head_rows(h)], grad_kv[:, head_rows(h)], grad_kv[:, head_rows(2 + h)]]
        )

    other_grad, dq, dkv = lax.optimization_barrier((head_grad(1).astype(BF16), dq, dkv))
    other_grad = across(other_grad)
    sib = rows_grad(slice(cut, None)).astype(BF16)
    sib, dq, dkv = lax.optimization_barrier((sib, dq, dkv))
    sib = beside(sib)
    own = rows_grad(slice(0, cut)) + resid
    other_grad, own = lax.optimization_barrier((other_grad, own))
    far_rows = (own[slot_rows:] + sib[slot_rows:].astype(F32)).astype(BF16)
    far_prompt = across(far_rows[:prompt_local])
    far_data = across(far_rows[prompt_local:])
    near_rows = own[:slot_rows] + sib[:slot_rows].astype(F32)
    near_data = near_rows[prompt_local:].astype(BF16)

    columns = width // HEAD_DIM
    prompt = near_rows[:prompt_local] + far_prompt.astype(F32)
    prompt = prompt.astype(BF16).reshape(groups, prompt_local // groups, width)
    prompt = jnp.concatenate([prompt[:, :, head_rows(j)] for j in range(columns)], axis=1)
    qkv = (head_grad(0) + other_grad.astype(F32)).astype(BF16).reshape(groups, -1, HEAD_DIM)
    qkv_rows = qkv.shape[1]
    last = jnp.concatenate([qkv, prompt], axis=1)
    last = jnp.sum(exchange(last, "ep").astype(F32), axis=0).astype(BF16)
    total, last = lax.optimization_barrier((total, last))
    last = gather(last)
    qkv = last[:, :qkv_rows].reshape(3, width, HEAD_DIM).astype(F32)
    prompt = last[:, qkv_rows:].reshape(groups, columns, prompt_local // groups, HEAD_DIM)
    prompt_grad = jnp.concatenate([prompt[:, j] for j in range(columns)], axis=2)
    prompt_grad = prompt_grad.reshape(prompt_local, width).astype(F32)

    which = lax.broadcasted_iota(jnp.int32, (2, 1, 1), 0)

    def by_episode(own, received):
        return jnp.where(which == mine, own[None], received[None])

    sums = total[:, depth, : 8 * width // groups].reshape(8, width)
    total = total[:, :depth].reshape(width, -1)
    bias_grad = lax.dynamic_slice_in_dim(sums[6:8].reshape(-1), t * quarter, quarter)
    return (
        by_episode(data_near, data_back),
        by_episode(prompt_near, prompt_back),
        by_episode(near_data, far_data),
        prompt_grad,
        qkv,
        sums[0],
        total[:, 2 * quarter :].T,
        sums[1],
        sums[2],
        total[:, :quarter],
        bias_grad,
        total[:, quarter : 2 * quarter].T,
        sums[3],
        sums[4],
        sums[5],
    )


def solution(mesh):
    return jax.shard_map(
        on_device,
        mesh=mesh,
        in_specs=(
            P("ep", "tp", None),
            P("tp", None),
            P("ep"),
            P("ep"),
            P(None, None, "tp"),
            P(),
            P("tp", None),
            P(),
            P(),
            P(None, "tp"),
            P("tp"),
            P("tp", None),
            P(),
            P(),
            P(),
            P("ep", "tp", None),
            P("ep", "tp", None),
        ),
        out_specs=(
            P("ep", "tp", None),
            P("ep", "tp", None),
            P("ep", "tp", None),
            P("tp", None),
            P(None, None, "tp"),
            P(),
            P("tp", None),
            P(),
            P(),
            P(None, "tp"),
            P("tp"),
            P("tp", None),
            P(),
            P(),
            P(),
        ),
        check_vma=False,
    )
```

```python
from functools import partial
import math

import jax
import jax.numpy as jnp
from jax import lax
from jax.experimental import pallas as pl
from jax.experimental.pallas import tpu as pltpu
from jax.sharding import PartitionSpec as P

HEAD_DIM = 128
ROWS = 512
BACK_ROWS = 256
ROW_STEP = 1024
SAMPLE = 128
EPS = 1e-05
MASKED = -1e30
LOG2E = math.log2(math.e)
LIMIT = 2.0**60
VMEM = 60 * 1024 * 1024
F32 = jnp.float32
BF16 = jnp.bfloat16
NN = (((1,), (0,)), ((), ()))
NT = (((1,), (1,)), ((), ()))
TN = (((0,), (0,)), ((), ()))


def mm(left, right, dims=NN):
    return lax.dot_general(left, right, dims, preferred_element_type=F32)


def params(**more):
    return pltpu.CompilerParams(vmem_limit_bytes=VMEM, **more)


def cost(flops, nbytes, trans=0):
    return pl.CostEstimate(
        flops=int(flops), bytes_accessed=int(nbytes), transcendentals=int(trans)
    )


def once(shape):
    return pl.BlockSpec(shape, lambda *_: (0,) * len(shape), pipeline_mode=pl.Buffered(1))


def extra_rows(values, count):
    width = values[0].shape[1]
    row = lax.broadcasted_iota(jnp.int32, (count, width), 0)
    out = jnp.zeros((count, width), F32)
    for index, value in enumerate(values):
        out = jnp.where(row == index, value, out)
    return out.astype(BF16)


def three_parts(row):
    high = row.astype(BF16).astype(F32)
    middle = (row - high).astype(BF16).astype(F32)
    return high, middle, row - high - middle


def clamp(i, low, high):
    return jnp.minimum(jnp.maximum(i, low), high)


def project_kernel(sizes, flip, meta, xa_ref, xb_ref, wa_ref, wb_ref, *refs):
    if flip:
        _, qt_ref, q_ref, k_ref, kx_ref, kt_ref, v_ref, vt_ref, all_ref = refs
        w_ref, wt_ref = wa_ref, wb_ref
    else:
        qt_ref, q_ref, k_ref, kx_ref, kt_ref, v_ref, vt_ref, all_ref, w_ref, wt_ref = refs
    prompt_local, data_local = sizes
    i = pl.program_id(0)
    per_slot = pl.num_programs(0) // 2
    rows = xa_ref.shape[0]

    if not flip:

        @pl.when(i == 0)
        def _():
            for which in range(3):
                for h, source in enumerate((wa_ref, wb_ref)):
                    cols = slice(which * 256 + h * HEAD_DIM, which * 256 + (h + 1) * HEAD_DIM)
                    w_ref[:, cols] = source[which]
                    wt_ref[cols, :] = source[which].T

    x = jnp.where(i < per_slot, xa_ref[...], xb_ref[...])
    all_ref[...] = x
    slot = jnp.where(i < per_slot, meta[0] ^ flip, meta[0] ^ flip ^ 1)
    row = lax.broadcasted_iota(jnp.int32, (rows, HEAD_DIM), 0)
    lane = lax.broadcasted_iota(jnp.int32, (rows, HEAD_DIM), 1)
    index = (i % per_slot) * rows + row - prompt_local
    attended = jnp.logical_or(index < 0, slot * data_local + index < meta[1])
    bias = jnp.where(attended, F32(0.0), F32(MASKED))
    ones = jnp.where(lane < 4, F32(1.0), F32(0.0))
    kx_ref[...] = jnp.where(lane == 0, bias, ones).astype(BF16)
    factor = F32(LOG2E / math.sqrt(HEAD_DIM))
    z = mm(x, w_ref[...])
    q_ref[...] = (z[:, :256] * factor).astype(BF16)
    k_ref[...] = z[:, 256:512].astype(BF16)
    v_ref[...] = z[:, 512:].astype(BF16)
    zt = mm(wt_ref[...], x, NT)
    qt_ref[...] = (zt[:256] * factor).astype(BF16)
    kt_ref[...] = zt[256:512].astype(BF16)
    vt_ref[...] = zt[512:].astype(BF16)


def project(meta, xa, xb, wa, wb, sizes, flip, joined=None):
    rows, width = xa.shape
    step = 512
    n = rows // step
    flat = jax.ShapeDtypeStruct((2 * rows, 256), BF16)
    tall = jax.ShapeDtypeStruct((256, 2 * rows), BF16)
    row = pl.BlockSpec((step, 256), lambda i, meta: (i, 0))
    col = pl.BlockSpec((256, step), lambda i, meta: (0, i))
    extra = [joined] if flip else []
    joint = [(width, 768), (768, width)]
    weights = [] if flip else [jax.ShapeDtypeStruct(shape, BF16) for shape in joint]

    def own_first(i):
        return (i // n) * 2 * n + (n if flip else 0) + i % n

    return pl.pallas_call(
        partial(project_kernel, sizes, flip),
        out_shape=[
            tall,
            flat,
            flat,
            jax.ShapeDtypeStruct((2 * rows, HEAD_DIM), BF16),
            tall,
            flat,
            tall,
            jax.ShapeDtypeStruct((4 * rows, width), BF16),
        ]
        + weights,
        grid_spec=pltpu.PrefetchScalarGridSpec(
            num_scalar_prefetch=1,
            grid=(2 * n,),
            in_specs=[
                pl.BlockSpec((step, width), lambda i, meta: (jnp.minimum(i, n - 1), 0)),
                pl.BlockSpec((step, width), lambda i, meta: (jnp.maximum(i - n, 0), 0)),
                once(wa.shape),
                once(wb.shape),
            ]
            + [pl.BlockSpec(memory_space=pl.ANY)] * len(extra),
            out_specs=[
                col,
                row,
                row,
                pl.BlockSpec((step, HEAD_DIM), lambda i, meta: (i, 0)),
                col,
                row,
                col,
                pl.BlockSpec((step, width), lambda i, meta: (own_first(i), 0)),
            ]
            + [once(item.shape) for item in weights],
        ),
        input_output_aliases={5: 7} if flip else {},
        compiler_params=params(),
        cost_estimate=cost(1, 1) if flip else cost(8 * rows * width * 768, rows * width * 16),
        name="project",
    )(meta, xa, xb, wa, wb, *extra)


def head_rows(h):
    return slice(h * HEAD_DIM, (h + 1) * HEAD_DIM)


def with_shift(qt, top):
    high, middle, low = three_parts(top)
    extra = extra_rows([jnp.ones_like(top), -high, -middle, -low], HEAD_DIM)
    return jnp.concatenate([qt, extra], axis=0)


def half_scores(chunk, h, qa, start, k_ref, kx_ref):
    here = pl.ds(start, chunk)
    keys = jnp.concatenate([k_ref[here, head_rows(h)], kx_ref[here, :]], axis=1)
    return mm(keys, qa)


def half_part(h, start, scores, vt_ref, pt_ref):
    chunk = scores.shape[0]
    weight = jnp.exp2(scores)
    total = jnp.sum(weight.reshape(chunk // 8, 8, weight.shape[1]), axis=0)
    low = weight.astype(BF16)
    pt_ref[0, h, pl.ds(start, chunk), :] = low
    return total, mm(vt_ref[head_rows(h), pl.ds(start, chunk)], low)


def stale_shift(h, qt, k_ref):
    top = jnp.max(mm(k_ref[:SAMPLE, head_rows(h)], qt), axis=0, keepdims=True)
    return top, with_shift(qt, top)


def fast_states(chunk, shifts, keys, pts):
    tiles = [
        (h, j, start)
        for h in range(2)
        for j in range(len(keys))
        for start in range(0, keys[0][0].shape[0], chunk)
    ]

    def scores(tile):
        h, j, start = tile
        return half_scores(chunk, h, shifts[h][j][1], start, keys[j][0], keys[j][1])

    sums = {}
    ahead = scores(tiles[0])
    for place, (h, j, start) in enumerate(tiles):
        now = ahead
        if place + 1 < len(tiles):
            ahead = scores(tiles[place + 1])
        total, product = half_part(h, start, now, keys[j][2], pts[j])
        if (h, j) in sums:
            total, product = sums[h, j][0] + total, sums[h, j][1] + product
        sums[h, j] = total, product
    return [
        [
            (shifts[h][j][0], jnp.sum(sums[h, j][0], axis=0, keepdims=True), sums[h, j][1])
            for j in range(len(keys))
        ]
        for h in range(2)
    ]


def half_attend_exact(chunk, h, shift, k_ref, kx_ref, vt_ref, pt_ref):
    qt = shift[1][:HEAD_DIM]
    width = qt.shape[1]
    count = k_ref.shape[0] // chunk
    qa = with_shift(qt, jnp.zeros((1, width), F32))

    def find(j, top):
        found = half_scores(chunk, h, qa, pl.multiple_of(j * chunk, chunk), k_ref, kx_ref)
        return jnp.maximum(top, jnp.max(found, axis=0, keepdims=True))

    top = lax.fori_loop(0, count, find, jnp.full((1, width), MASKED, F32))
    qa = with_shift(qt, top)

    def add(j, state):
        start = pl.multiple_of(j * chunk, chunk)
        found = half_scores(chunk, h, qa, start, k_ref, kx_ref)
        more, product = half_part(h, start, found, vt_ref, pt_ref)
        return state[0] + more, state[1] + product

    total, acc = lax.fori_loop(
        0, count, add, (jnp.zeros((8, width), F32), jnp.zeros((HEAD_DIM, width), F32))
    )
    return top, jnp.sum(total, axis=0, keepdims=True), acc


def merge(states):
    top = states[0][0]
    for state in states[1:]:
        top = jnp.maximum(top, state[0])
    scales = [jnp.exp2(state[0] - top) for state in states]
    total = sum(state[1] * scale for state, scale in zip(states, scales))
    factors = [scale / total for scale in scales]
    return factors, sum(state[2] * factor for state, factor in zip(states, factors))


def redo(states, shifts, keys, pts):
    return [
        [half_attend_exact(256, h, shifts[h][j], *keys[j], pts[j]) for j in range(len(keys))]
        for h in range(2)
    ]


def run_halves(chunk, qt_ref, keys, pts, finish):
    shifts = [
        [stale_shift(h, qt_ref[head_rows(h), :], key_refs[0]) for key_refs in keys]
        for h in range(2)
    ]
    states = fast_states(chunk, shifts, keys, pts)
    worst = None
    for state in states[0] + states[1]:
        worst = state[1] if worst is None else jnp.maximum(worst, state[1])
    finish(states)

    @pl.when(jnp.logical_not(jnp.max(worst) <= LIMIT))
    def _():
        finish(redo(states, shifts, keys, pts))


def attend_first_kernel(chunk, qt_ref, k_ref, kx_ref, vt_ref, pt_ref, state_ref, acc_ref):
    def finish(states):
        for h in range(2):
            top, total, acc = states[h][0]
            state_ref[0, h : h + 1, :] = top
            state_ref[0, 2 + h : 3 + h, :] = total
            acc_ref[head_rows(h), :] = acc

    run_halves(chunk, qt_ref, [(k_ref, kx_ref, vt_ref)], [pt_ref], finish)


def attend_first(qt, key, chunk):
    rows = qt.shape[1]
    n = rows // ROWS
    col = pl.BlockSpec((256, ROWS), lambda i: (0, i))
    pairs = 2 * rows * rows
    return pl.pallas_call(
        partial(attend_first_kernel, chunk),
        out_shape=[
            jax.ShapeDtypeStruct((2 * n, 2, rows, ROWS), BF16),
            jax.ShapeDtypeStruct((n, 8, ROWS), F32),
            jax.ShapeDtypeStruct((256, rows), F32),
        ],
        grid=(n,),
        in_specs=[col] + [once(item.shape) for item in key],
        out_specs=[
            pl.BlockSpec((1, 2, rows, ROWS), lambda i: (i, 0, 0, 0)),
            pl.BlockSpec((1, 8, ROWS), lambda i: (i, 0, 0)),
            col,
        ],
        compiler_params=params(),
        cost_estimate=cost(4 * pairs * HEAD_DIM * 2, 2 * pairs, pairs),
        name="attend_near",
    )(qt, *key)


def attend_second_kernel(
    chunk, qtn_ref, qtf_ref, kn, kxn, vtn, kf, kxf, vtf, old_ref, old_acc_ref, _,
    ptn_ref, ptf_ref, mine_ref, sib_ref, stat_ref,
):
    i = pl.program_id(0)
    n = pl.num_programs(0) // 2
    near, far = (kn, kxn, vtn), (kf, kxf, vtf)

    def store(h, states):
        factors, result = merge(states)
        stat_ref[0, h : h + 1, :] = factors[0]
        stat_ref[0, 2 + h : 3 + h, :] = factors[1]
        low = result.T.astype(BF16)
        first = i % n < n // 2

        @pl.when(first)
        def _():
            mine_ref[:, head_rows(h)] = low

        @pl.when(jnp.logical_not(first))
        def _():
            sib_ref[:, head_rows(h)] = low

    @pl.when(i < n)
    def _():
        def finish(states):
            for h in range(2):
                old = (old_ref[0, h : h + 1, :], old_ref[0, 2 + h : 3 + h, :],
                       old_acc_ref[head_rows(h), :])
                store(h, [old, states[h][0]])

        run_halves(chunk, qtn_ref, [far], [ptf_ref], finish)

    @pl.when(i >= n)
    def _():
        def finish(states):
            for h in range(2):
                store(h, states[h])

        run_halves(chunk, qtf_ref, [near, far], [ptn_ref, ptf_ref], finish)


def mine_block(i, n):
    half = n // 2
    return (i // n) * half + jnp.minimum(i % n, half - 1)


def sib_block(i, n):
    half = n // 2
    return jnp.maximum((i // n) * half + i % n - half, jnp.maximum((i // n) * half - 1, 0))


def attend_second(qtn, qtf, near, far, pt, state, acc, chunk):
    rows = qtn.shape[1]
    n = rows // ROWS
    near_col = pl.BlockSpec((256, ROWS), lambda i: (0, jnp.minimum(i, n - 1)))
    pairs = 6 * rows * rows
    return pl.pallas_call(
        partial(attend_second_kernel, chunk),
        out_shape=[
            jax.ShapeDtypeStruct(pt.shape, BF16),
            jax.ShapeDtypeStruct(pt.shape, BF16),
            jax.ShapeDtypeStruct((rows, 256), BF16),
            jax.ShapeDtypeStruct((rows, 256), BF16),
            jax.ShapeDtypeStruct((2 * n, 8, ROWS), F32),
        ],
        grid=(2 * n,),
        in_specs=[near_col, pl.BlockSpec((256, ROWS), lambda i: (0, jnp.maximum(i - n, 0)))]
        + [once(item.shape) for item in near + far]
        + [
            pl.BlockSpec((1, 8, ROWS), lambda i: (jnp.minimum(i, n - 1), 0, 0)),
            near_col,
            pl.BlockSpec(memory_space=pl.ANY),
        ],
        out_specs=[
            pl.BlockSpec((1, 2, rows, ROWS), lambda i: (jnp.maximum(i, n), 0, 0, 0)),
            pl.BlockSpec((1, 2, rows, ROWS), lambda i: (i, 0, 0, 0)),
            pl.BlockSpec((ROWS, 256), lambda i: (mine_block(i, n), 0)),
            pl.BlockSpec((ROWS, 256), lambda i: (sib_block(i, n), 0)),
            pl.BlockSpec((1, 8, ROWS), lambda i: (i, 0, 0)),
        ],
        input_output_aliases={10: 0},
        compiler_params=params(),
        cost_estimate=cost(1, 1),
        name="attend_rest",
    )(qtn, qtf, *near, *far, state, acc, pt)


def back_weights(do, o, factors):
    dot_t = do.astype(F32).T
    delta = jnp.sum(dot_t * o.astype(F32).T, axis=0, keepdims=True)
    found = []
    for factor in factors:
        scaled = dot_t * factor
        high, middle, low = three_parts(delta * factor)
        extra = extra_rows([-high, -middle, -low], HEAD_DIM)
        found.append(
            (jnp.concatenate([scaled.astype(BF16), extra], axis=0), scaled.T.astype(BF16))
        )
    return found


def back_half(chunk, h, grads, q_rows, pt_ref, v_ref, kt_ref, key_acc, value_acc):
    ones = jnp.where(
        lax.broadcasted_iota(jnp.int32, (chunk, HEAD_DIM), 1) < 3, F32(1.0), F32(0.0)
    ).astype(BF16)
    result = jnp.zeros((HEAD_DIM, q_rows.shape[0]), F32)
    for start in range(0, v_ref.shape[0], chunk):
        here = slice(start, start + chunk)
        prob = pt_ref[0, h, here, :]
        values = jnp.concatenate([v_ref[here, head_rows(h)], ones], axis=1)
        score = (prob.astype(F32) * mm(values, grads[0])).astype(BF16)
        value_acc[h, here, :] += mm(prob, grads[1])
        key_acc[h, here, :] += mm(score, q_rows)
        result = result + mm(kt_ref[head_rows(h), here], score)
    return result


def attend_back_kernel(
    chunk, da_ref, db_ref, oa_ref, ob_ref, stat_ref, qn_ref, qf_ref, ptn_ref, ptf_ref,
    vn, ktn, vf, ktf, dq_ref, dkv_ref, key_n, value_n, key_f, value_f,
):
    i = pl.program_id(0)
    n = pl.num_programs(0) // 2

    @pl.when(i == 0)
    def _():
        for ref in (key_n, value_n, key_f, value_f):
            ref[...] = jnp.zeros_like(ref)

    first = i % n < n // 2
    do = jnp.where(first, da_ref[...], db_ref[...])
    o = jnp.where(first, oa_ref[...], ob_ref[...])
    q = jnp.where(i < n, qn_ref[...], qf_ref[...])
    for h in range(2):
        cols = head_rows(h)
        near, far = back_weights(
            do[:, cols], o[:, cols], [stat_ref[0, h : h + 1, :], stat_ref[0, 2 + h : 3 + h, :]]
        )
        grad = back_half(chunk, h, near, q[:, cols], ptn_ref, vn, ktn, key_n, value_n)
        grad += back_half(chunk, h, far, q[:, cols], ptf_ref, vf, ktf, key_f, value_f)
        dq_ref[:, cols] = (grad * F32(1.0 / math.sqrt(HEAD_DIM))).T.astype(BF16)

    @pl.when(i == 2 * n - 1)
    def _():
        seq = vn.shape[0]
        for half, (keys, values) in enumerate(((key_n, value_n), (key_f, value_f))):
            for owner in range(2):
                source = slice(owner * seq // 2, (owner + 1) * seq // 2)
                begin = owner * seq + half * seq // 2
                rows = slice(begin, begin + seq // 2)
                for h in range(2):
                    dkv_ref[rows, head_rows(h)] = (keys[h, source] * F32(1.0 / LOG2E)).astype(BF16)
                    dkv_ref[rows, head_rows(2 + h)] = values[h, source].astype(BF16)


def attend_back(da, db, oa, ob, stat, qn, qf, ptn, ptf, vn, ktn, vf, ktf, chunk):
    rows = qn.shape[0]
    step = BACK_ROWS
    n = rows // step
    per = ROWS // step
    row = lambda f: pl.BlockSpec((step, 256), lambda i: (f(i), 0))
    tile = pl.BlockSpec((1, 2, rows, step), lambda i: (i // per, 0, 0, i % per))
    flat = jax.ShapeDtypeStruct((2 * rows, 256), BF16)
    wide = jax.ShapeDtypeStruct((2 * rows, 512), BF16)
    acc = pltpu.VMEM((2, rows, HEAD_DIM), F32)

    def own_first(i):
        return jnp.where(i % n < n // 2, 0, n // 2) + (i // n) * (n // 2) + i % n
    pairs = 8 * rows * rows
    return pl.pallas_call(
        partial(attend_back_kernel, chunk),
        out_shape=[flat, wide],
        grid=(2 * n,),
        in_specs=[
            row(lambda i: mine_block(i, n)),
            row(lambda i: sib_block(i, n)),
            row(lambda i: mine_block(i, n)),
            row(lambda i: sib_block(i, n)),
            pl.BlockSpec((1, 8, step), lambda i: (i // per, 0, i % per)),
            row(lambda i: jnp.minimum(i, n - 1)),
            row(lambda i: jnp.maximum(i - n, 0)),
            tile,
            tile,
        ]
        + [once(item.shape) for item in (vn, ktn, vf, ktf)],
        out_specs=[row(own_first), once(wide.shape)],
        scratch_shapes=[acc, acc, acc, acc],
        compiler_params=params(),
        cost_estimate=cost(8 * pairs * HEAD_DIM, 2 * pairs),
        name="attend_back",
    )(da, db, oa, ob, stat, qn, qf, ptn, ptf, vn, ktn, vf, ktf)


def mean(values):
    return jnp.mean(values, axis=-1, keepdims=True)


def norm(values):
    centered = values - mean(values)
    inverse = lax.rsqrt(mean(centered * centered) + EPS)
    return centered * inverse, inverse


def norm_back(incoming, normed, inverse, gain):
    scaled = incoming * gain
    return inverse * (scaled - mean(scaled) - normed * mean(scaled * normed))


def gelu_parts(v):
    bell = jnp.exp2(v * v * F32(-0.5 * LOG2E))
    base = 1.0 + F32(0.3275911 / math.sqrt(2.0)) * jnp.abs(v)
    t = pl.reciprocal(base, approx=True)
    t = t * (2.0 - base * t)
    series = t * (
        F32(0.5 * 0.254829592)
        + t
        * (
            F32(0.5 * -0.284496736)
            + t
            * (
                F32(0.5 * 1.421413741)
                + t * (F32(0.5 * -1.453152027) + t * F32(0.5 * 1.061405429))
            )
        )
    )
    tail = series * bell
    return bell * F32(1.0 / math.sqrt(2.0 * math.pi)), jnp.where(v >= 0, 1.0 - tail, tail)


def fold_rows(values):
    return jnp.sum(values.reshape(values.shape[0] // 8, 8, values.shape[1]), axis=0)


def rows_kernel(
    sizes, meta, xa_ref, xb_ref, oa_ref, ob_ref, cot_a, cot_b, p0, p1, p2, p3,
    u0, u1, u2, u3, vec_ref,
    prompt_near, data_near, prompt_far, data_far, resid_ref, da_ref, db_ref, send_ref,
    sums_ref, wo_ref, up_ref, down_ref, bias_ref, grad_acc, vec_acc, bias_acc,
):
    prompt_local, data_local = sizes
    i = pl.program_id(0)
    half = pl.num_programs(0) // 2
    here = i < half
    rows = xa_ref.shape[0]
    quarter = u0.shape[1]

    @pl.when(i == 0)
    def _():
        for j, (pack, up_part) in enumerate(((p0, u0), (p1, u1), (p2, u2), (p3, u3))):
            cols = slice(j * quarter, (j + 1) * quarter)
            wo_ref[head_rows(j), :] = pack[:HEAD_DIM, :]
            down_ref[cols, :] = pack[HEAD_DIM : HEAD_DIM + quarter, :]
            bias_ref[0:1, cols] = pack[
                HEAD_DIM + quarter : HEAD_DIM + quarter + 16, :quarter
            ].astype(F32)[0:1, :]
            up_ref[:, cols] = up_part[...]
        grad_acc[...] = jnp.zeros_like(grad_acc)
        vec_acc[...] = jnp.zeros_like(vec_acc)
        bias_acc[...] = jnp.zeros_like(bias_acc)

    slot = jnp.where(here, meta[0], meta[0] ^ 2)
    index = (i % half) * rows + lax.broadcasted_iota(jnp.int32, (rows, 1), 0) - prompt_local
    live = jnp.logical_or(index < 0, slot * data_local + index < meta[2])

    out_bias, attn_gain, attn_shift = vec_ref[0:1, :], vec_ref[1:2, :], vec_ref[2:3, :]
    down_bias, mlp_gain, mlp_shift = vec_ref[3:4, :], vec_ref[4:5, :], vec_ref[5:6, :]
    x = jnp.where(here, xa_ref[...], xb_ref[...])
    attended = jnp.concatenate([oa_ref[...], ob_ref[...]], axis=1)
    normed_one, inverse_one = norm(x.astype(F32) + (mm(attended, wo_ref[...]) + out_bias))
    hidden = normed_one * attn_gain + attn_shift
    hidden_low = hidden.astype(BF16)
    pre = mm(hidden_low, up_ref[...]) + bias_ref[0:1, :]
    density, share = gelu_parts(pre)
    activated = (pre * share).astype(BF16)
    slope = share + pre * density
    mixed = hidden + (mm(activated, down_ref[...]) + down_bias)
    normed_two, inverse_two = norm(mixed)
    output = (normed_two * mlp_gain + mlp_shift).astype(BF16)
    cotangent = jnp.where(live, jnp.where(here, cot_a[...], cot_b[...]).astype(F32), 0.0)
    mixed_grad = norm_back(cotangent, normed_two, inverse_two, mlp_gain)
    mixed_low = mixed_grad.astype(BF16)
    pre_grad = (mm(mixed_low, down_ref[...], NT) * slope).astype(BF16)
    hidden_grad = mixed_grad + mm(pre_grad, up_ref[...], NT)
    resid_grad = norm_back(hidden_grad, normed_one, inverse_one, attn_gain)
    resid_ref[...] = resid_grad
    resid_low = resid_grad.astype(BF16)
    attended_grad = mm(resid_low, wo_ref[...], NT).astype(BF16)
    da_ref[...] = attended_grad[:, :256]
    db_ref[...] = attended_grad[:, 256:]

    up_grad = mm(hidden_low, pre_grad, TN)
    down_grad = mm(mixed_low, activated, TN)
    out_grad = mm(resid_low, attended, TN)
    for j in range(4):
        cols = slice(j * quarter, (j + 1) * quarter)
        grad_acc[j, :, :quarter] += up_grad[:, cols]
        grad_acc[j, :, quarter : 2 * quarter] += down_grad[:, cols]
        grad_acc[j, :, 2 * quarter :] += out_grad[:, head_rows(j)]
    bias_acc[...] += fold_rows(pre_grad.astype(F32))
    for place, value in enumerate(
        (
            resid_grad,
            hidden_grad * normed_one,
            hidden_grad,
            mixed_grad,
            cotangent * normed_two,
            cotangent,
        )
    ):
        vec_acc[place] += fold_rows(value)

    for j in range((prompt_local + data_local) // rows):
        split = max(0, min(rows, prompt_local - j * rows))
        for place, (prompt_ref, data_ref) in enumerate(
            ((prompt_near, data_near), (prompt_far, data_far))
        ):

            @pl.when(i == place * half + j)
            def _():
                if split:
                    prompt_ref[j * rows : j * rows + split, :] = output[:split]
                if split < rows:
                    begin = j * rows + split - prompt_local
                    data_ref[begin : begin + rows - split, :] = output[split:]

    @pl.when(i == pl.num_programs(0) - 1)
    def _():
        for place in range(6):
            sums_ref[place : place + 1, :] = jnp.sum(vec_acc[place], axis=0, keepdims=True)
        bias_grad = jnp.sum(bias_acc[...], axis=0, keepdims=True)
        per_row = bias_grad.shape[1] // 2 // quarter
        for g in range(4):
            found = jnp.zeros((1, quarter), F32)
            for j, flip in enumerate((0, 2, 1, 3)):
                piece = bias_grad[:, j * quarter : (j + 1) * quarter]
                found = jnp.where((meta[0] ^ flip) == g, piece, found)
            row, col = 6 + g // per_row, (g % per_row) * quarter
            sums_ref[row : row + 1, col : col + quarter] = found
        depth = send_ref.shape[1] - 16
        groups = send_ref.shape[0] // 4
        width, wide = sums_ref.shape[1], send_ref.shape[2]
        per = sums_ref.shape[0] * width // groups
        for g in range(groups):
            row, col = g * per // width, g * per % width
            part = jnp.pad(sums_ref[row : row + 1, col : col + per], ((0, 0), (0, wide - per)))
            high, low, _ = three_parts(part)
            extra = extra_rows([high, low], 16)
            for j, flip in enumerate((0, 2, 1, 3)):
                target = g * 4 + (meta[0] ^ flip)
                send_ref[target, :depth] = grad_acc[j, g * depth : (g + 1) * depth].astype(BF16)
                send_ref[target, depth:] = extra


def row_work(meta, xa, xb, oa, ob, cot, packs, ups, vec, sizes, groups):
    rows, width = xa.shape
    prompt_local, data_local = sizes
    step = ROW_STEP
    n = rows // step
    quarter = ups[0].shape[1]
    hidden = 4 * quarter
    wide = 2 * quarter + HEAD_DIM
    send = (4 * groups, width // groups + 16, wide)
    near = pl.BlockSpec((step, width), lambda i, meta: (jnp.minimum(i, n - 1), 0))
    far = pl.BlockSpec((step, width), lambda i, meta: (jnp.maximum(i - n, 0), 0))
    row = lambda cols: pl.BlockSpec((step, cols), lambda i, meta: (i, 0))
    return pl.pallas_call(
        partial(rows_kernel, sizes),
        out_shape=[
            jax.ShapeDtypeStruct((prompt_local, width), BF16),
            jax.ShapeDtypeStruct((data_local, width), BF16),
            jax.ShapeDtypeStruct((prompt_local, width), BF16),
            jax.ShapeDtypeStruct((data_local, width), BF16),
            jax.ShapeDtypeStruct((2 * rows, width), F32),
            jax.ShapeDtypeStruct((2 * rows, 256), BF16),
            jax.ShapeDtypeStruct((2 * rows, 256), BF16),
            jax.ShapeDtypeStruct(send, BF16),
        ],
        grid_spec=pltpu.PrefetchScalarGridSpec(
            num_scalar_prefetch=1,
            grid=(2 * n,),
            in_specs=[near, far, row(256), row(256), near, far]
            + [once(item.shape) for item in packs + ups]
            + [once(vec.shape)],
            out_specs=[
                once((prompt_local, width)),
                once((data_local, width)),
                once((prompt_local, width)),
                once((data_local, width)),
                row(width),
                row(256),
                row(256),
                once(send),
            ],
            scratch_shapes=[
                pltpu.VMEM((8, width), F32),
                pltpu.VMEM((4 * HEAD_DIM, width), BF16),
                pltpu.VMEM((width, hidden), BF16),
                pltpu.VMEM((hidden, width), BF16),
                pltpu.VMEM((8, hidden), F32),
                pltpu.VMEM((4, width, wide), F32),
                pltpu.VMEM((6, 8, width), F32),
                pltpu.VMEM((8, hidden), F32),
            ],
        ),
        compiler_params=params(),
        cost_estimate=cost(
            3 * 2 * 2 * rows * width * (width + 2 * hidden), 24 * rows * width, 4 * rows * hidden
        ),
        name="row_work",
    )(meta, xa, xb, oa, ob, *cot, *packs, *ups, vec)


def on_device(
    data_rows,
    prompt_rows,
    context_rows,
    test_rows,
    qkv_weight,
    out_bias,
    out_weight,
    attn_gain,
    attn_shift,
    up_weight,
    up_bias,
    down_weight,
    down_bias,
    mlp_gain,
    mlp_shift,
    data_cotangent,
    prompt_cotangent,
):
    data_local = data_rows.shape[1]
    prompt_local = prompt_rows.shape[0]
    width = prompt_rows.shape[1]
    quarter = up_weight.shape[1]
    sizes = (prompt_local, data_local)
    groups = lax.axis_size("ep")
    t = lax.axis_index("tp")
    mine = t >> 1
    other = 1 - mine

    def across(value):
        return lax.ppermute(value, "tp", [(i, i ^ 2) for i in range(4)])

    def beside(value):
        return lax.ppermute(value, "tp", [(i, i ^ 1) for i in range(4)])

    def pick(values, which):
        return lax.dynamic_index_in_dim(values, which, axis=0, keepdims=False)

    def stack(prompt_part, data_part):
        return jnp.concatenate([prompt_part, data_part], axis=0)

    w_far = across(qkv_weight)
    x_far = stack(prompt_rows, pick(data_rows, other))
    x = stack(prompt_rows, pick(data_rows, mine))
    x_far, x, prompt_cotangent, data_cotangent = lax.optimization_barrier(
        (x_far, x, prompt_cotangent, data_cotangent)
    )
    x_far = across(x_far)
    x_sib = beside(x)
    cot = stack(pick(prompt_cotangent, mine), pick(data_cotangent, mine))
    cot_far = stack(pick(prompt_cotangent, other), pick(data_cotangent, other))
    vec = jnp.stack(
        [out_bias, attn_gain, attn_shift, down_bias, mlp_gain, mlp_shift, mlp_shift, mlp_shift]
    ).astype(F32)
    context = pick(context_rows, mine)
    live = context + pick(test_rows, mine)
    meta = jnp.stack([t, context, live]).astype(jnp.int32)
    meta, cot, cot_far, vec = lax.optimization_barrier((meta, cot, cot_far, vec))

    qtn, qn, kn, kxn, ktn, vn, vtn, x_all, w, w_t = project(
        meta, x, x_sib, qkv_weight, w_far, sizes, 0
    )
    ptn, state, state_acc = attend_first(qtn, (kn, kxn, vtn), 512)

    bias_rows = jnp.pad(up_bias[None], ((0, 15), (0, width - quarter)))
    pack = jnp.concatenate([out_weight, down_weight, bias_rows], axis=0)
    x_far, state, pack, up_weight, cot_far = lax.optimization_barrier(
        (x_far, state, pack, up_weight, cot_far)
    )
    x_far_sib = beside(x_far)
    pack_far, up_far = across(pack), across(up_weight)
    cot_far = across(cot_far)
    pack_sib, up_sib = beside(pack), beside(up_weight)
    qtf, qf, kf, kxf, ktf, vf, vtf, x_all = project(
        meta, x_far, x_far_sib, w, w_t, sizes, 2, x_all
    )
    ptn, ptf, oa, ob, stat = attend_second(
        qtn, qtf, (kn, kxn, vtn), (kf, kxf, vtf), ptn, state, state_acc, 512
    )

    ob_send, cot_far, pack_far, up_far, pack_sib, up_sib = lax.optimization_barrier(
        (ob, cot_far, pack_far, up_far, pack_sib, up_sib)
    )
    packs = [pack, pack_far, pack_sib, beside(pack_far)]
    ups = [up_weight, up_far, up_sib, beside(up_far)]
    (prompt_near, data_near, prompt_far, data_far, resid, da, db, send) = row_work(
        meta, x, x_far, oa, beside(ob_send), (cot, cot_far), packs, ups, vec, sizes, groups
    )

    def dot(left, right, dims):
        return lax.dot_general(left, right, dims, preferred_element_type=F32)

    def exchange(parts, axes):
        return lax.all_to_all(parts, axes, 0, 0, tiled=True)

    def gather(part):
        return exchange(jnp.broadcast_to(part[None], (groups,) + part.shape), "ep")

    db = beside(db)
    send = exchange(send, ("ep", "tp"))
    prompt_back, data_back = across(prompt_far), across(data_far)

    dq, dkv = attend_back(
        da, db, oa, ob, stat, qn, qf, ptn, ptf, vn, ktn, vf, ktf, 512
    )
    send, prompt_back, data_back, dq = lax.optimization_barrier((send, prompt_back, data_back, dq))
    depth = width // groups
    total = jnp.sum(send.astype(F32), axis=0)
    part = total[depth : depth + 1] + total[depth + 1 : depth + 2]
    high = lax.optimization_barrier(part.astype(BF16))
    low = (part - high.astype(F32)).astype(BF16)
    total = jnp.concatenate(
        [total[:depth].astype(BF16), high, low, jnp.zeros((6, total.shape[1]), BF16)], axis=0
    )
    total = jnp.broadcast_to(total[None], (groups,) + total.shape)
    total, dq, dkv = lax.optimization_barrier((total, dq, dkv))
    total = exchange(total, "ep")

    slot_rows = prompt_local + data_local
    cut = 2 * slot_rows
    wq, wkv = w[:, :256], w[:, 256:]

    def rows_grad(part):
        return dot(dq[part], wq, NT) + dot(dkv[part], wkv, NT)

    grad_q, grad_kv = dot(x_all, dq, TN), dot(x_all, dkv, TN)

    def head_grad(h):
        return jnp.stack(
            [grad_q[:, head_rows(h)], grad_kv[:, head_rows(h)], grad_kv[:, head_rows(2 + h)]]
        )

    other_grad, dq, dkv = lax.optimization_barrier((head_grad(1).astype(BF16), dq, dkv))
    other_grad = across(other_grad)
    sib = rows_grad(slice(cut, None)).astype(BF16)
    sib, dq, dkv = lax.optimization_barrier((sib, dq, dkv))
    sib = beside(sib)
    own = rows_grad(slice(0, cut)) + resid
    other_grad, own = lax.optimization_barrier((other_grad, own))
    far_rows = (own[slot_rows:] + sib[slot_rows:].astype(F32)).astype(BF16)
    far_prompt = across(far_rows[:prompt_local])
    far_data = across(far_rows[prompt_local:])
    near_rows = own[:slot_rows] + sib[:slot_rows].astype(F32)
    near_data = near_rows[prompt_local:].astype(BF16)

    columns = width // HEAD_DIM
    prompt = near_rows[:prompt_local] + far_prompt.astype(F32)
    prompt = prompt.astype(BF16).reshape(groups, prompt_local // groups, width)
    prompt = jnp.concatenate([prompt[:, :, head_rows(j)] for j in range(columns)], axis=1)
    qkv = (head_grad(0) + other_grad.astype(F32)).astype(BF16).reshape(groups, -1, HEAD_DIM)
    qkv_rows = qkv.shape[1]
    last = jnp.concatenate([qkv, prompt], axis=1)
    total, last = lax.optimization_barrier((total, last))
    last = gather(jnp.sum(exchange(last, "ep").astype(F32), axis=0).astype(BF16))
    qkv = last[:, :qkv_rows].reshape(3, width, HEAD_DIM).astype(F32)
    prompt = last[:, qkv_rows:].reshape(groups, columns, prompt_local // groups, HEAD_DIM)
    prompt_grad = jnp.concatenate([prompt[:, j] for j in range(columns)], axis=2)
    prompt_grad = prompt_grad.reshape(prompt_local, width).astype(F32)

    which = lax.broadcasted_iota(jnp.int32, (2, 1, 1), 0)

    def by_episode(own, received):
        return jnp.where(which == mine, own[None], received[None])

    sums = total[:, depth : depth + 2, : 8 * width // groups].astype(F32)
    sums = (sums[:, 0] + sums[:, 1]).reshape(8, width)
    total = total[:, :depth].reshape(width, -1).astype(F32)
    bias_grad = lax.dynamic_slice_in_dim(sums[6:8].reshape(-1), t * quarter, quarter)
    return (
        by_episode(data_near, data_back),
        by_episode(prompt_near, prompt_back),
        by_episode(near_data, far_data),
        prompt_grad,
        qkv,
        sums[0],
        total[:, 2 * quarter :].T,
        sums[1],
        sums[2],
        total[:, :quarter],
        bias_grad,
        total[:, quarter : 2 * quarter].T,
        sums[3],
        sums[4],
        sums[5],
    )


def solution(mesh):
    return jax.shard_map(
        on_device,
        mesh=mesh,
        in_specs=(
            P("ep", "tp", None),
            P("tp", None),
            P("ep"),
            P("ep"),
            P(None, None, "tp"),
            P(),
            P("tp", None),
            P(),
            P(),
            P(None, "tp"),
            P("tp"),
            P("tp", None),
            P(),
            P(),
            P(),
            P("ep", "tp", None),
            P("ep", "tp", None),
        ),
        out_specs=(
            P("ep", "tp", None),
            P("ep", "tp", None),
            P("ep", "tp", None),
            P("tp", None),
            P(None, None, "tp"),
            P(),
            P("tp", None),
            P(),
            P(),
            P(None, "tp"),
            P("tp"),
            P("tp", None),
            P(),
            P(),
            P(),
        ),
        check_vma=False,
    )
```

```python
from functools import partial
import math

import jax
import jax.numpy as jnp
from jax import lax
from jax.experimental import pallas as pl
from jax.experimental.pallas import tpu as pltpu
from jax.sharding import PartitionSpec as P

HEAD_DIM = 128
ROWS = 512
BACK_ROWS = 256
ROW_STEP = 1024
SAMPLE = 128
EPS = 1e-05
MASKED = -1e30
LOG2E = math.log2(math.e)
LIMIT = 2.0**60
VMEM = 60 * 1024 * 1024
F32 = jnp.float32
BF16 = jnp.bfloat16
NN = (((1,), (0,)), ((), ()))
NT = (((1,), (1,)), ((), ()))
TN = (((0,), (0,)), ((), ()))


def mm(left, right, dims=NN):
    return lax.dot_general(left, right, dims, preferred_element_type=F32)


def params(**more):
    return pltpu.CompilerParams(vmem_limit_bytes=VMEM, **more)


def cost(flops, nbytes, trans=0):
    return pl.CostEstimate(
        flops=int(flops), bytes_accessed=int(nbytes), transcendentals=int(trans)
    )


def once(shape):
    return pl.BlockSpec(shape, lambda *_: (0,) * len(shape), pipeline_mode=pl.Buffered(1))


def extra_rows(values, count):
    width = values[0].shape[1]
    row = lax.broadcasted_iota(jnp.int32, (count, width), 0)
    out = jnp.zeros((count, width), F32)
    for index, value in enumerate(values):
        out = jnp.where(row == index, value, out)
    return out.astype(BF16)


def three_parts(row):
    high = row.astype(BF16).astype(F32)
    middle = (row - high).astype(BF16).astype(F32)
    return high, middle, row - high - middle


def clamp(i, low, high):
    return jnp.minimum(jnp.maximum(i, low), high)


def project_kernel(sizes, flip, meta, xa_ref, xb_ref, wa_ref, wb_ref, *refs):
    if flip:
        _, qt_ref, q_ref, k_ref, kx_ref, kt_ref, v_ref, vt_ref, all_ref = refs
        w_ref, wt_ref = wa_ref, wb_ref
    else:
        qt_ref, q_ref, k_ref, kx_ref, kt_ref, v_ref, vt_ref, all_ref, w_ref, wt_ref = refs
    prompt_local, data_local = sizes
    i = pl.program_id(0)
    per_slot = pl.num_programs(0) // 2
    rows = xa_ref.shape[0]

    if not flip:

        @pl.when(i == 0)
        def _():
            for which in range(3):
                for h, source in enumerate((wa_ref, wb_ref)):
                    cols = slice(which * 256 + h * HEAD_DIM, which * 256 + (h + 1) * HEAD_DIM)
                    w_ref[:, cols] = source[which]
                    wt_ref[cols, :] = source[which].T

    x = jnp.where(i < per_slot, xa_ref[...], xb_ref[...])
    all_ref[...] = x
    slot = jnp.where(i < per_slot, meta[0] ^ flip, meta[0] ^ flip ^ 1)
    row = lax.broadcasted_iota(jnp.int32, (rows, HEAD_DIM), 0)
    lane = lax.broadcasted_iota(jnp.int32, (rows, HEAD_DIM), 1)
    index = (i % per_slot) * rows + row - prompt_local
    attended = jnp.logical_or(index < 0, slot * data_local + index < meta[1])
    bias = jnp.where(attended, F32(0.0), F32(MASKED))
    ones = jnp.where(lane < 4, F32(1.0), F32(0.0))
    kx_ref[...] = jnp.where(lane == 0, bias, ones).astype(BF16)
    factor = F32(LOG2E / math.sqrt(HEAD_DIM))
    z = mm(x, w_ref[...])
    q_ref[...] = (z[:, :256] * factor).astype(BF16)
    k_ref[...] = z[:, 256:512].astype(BF16)
    v_ref[...] = z[:, 512:].astype(BF16)
    zt = mm(wt_ref[...], x, NT)
    qt_ref[...] = (zt[:256] * factor).astype(BF16)
    kt_ref[...] = zt[256:512].astype(BF16)
    vt_ref[...] = zt[512:].astype(BF16)


def project(meta, xa, xb, wa, wb, sizes, flip, joined=None):
    rows, width = xa.shape
    step = 512
    n = rows // step
    flat = jax.ShapeDtypeStruct((2 * rows, 256), BF16)
    tall = jax.ShapeDtypeStruct((256, 2 * rows), BF16)
    row = pl.BlockSpec((step, 256), lambda i, meta: (i, 0))
    col = pl.BlockSpec((256, step), lambda i, meta: (0, i))
    extra = [joined] if flip else []
    joint = [(width, 768), (768, width)]
    weights = [] if flip else [jax.ShapeDtypeStruct(shape, BF16) for shape in joint]

    def own_first(i):
        return (i // n) * 2 * n + (n if flip else 0) + i % n

    return pl.pallas_call(
        partial(project_kernel, sizes, flip),
        out_shape=[
            tall,
            flat,
            flat,
            jax.ShapeDtypeStruct((2 * rows, HEAD_DIM), BF16),
            tall,
            flat,
            tall,
            jax.ShapeDtypeStruct((4 * rows, width), BF16),
        ]
        + weights,
        grid_spec=pltpu.PrefetchScalarGridSpec(
            num_scalar_prefetch=1,
            grid=(2 * n,),
            in_specs=[
                pl.BlockSpec((step, width), lambda i, meta: (jnp.minimum(i, n - 1), 0)),
                pl.BlockSpec((step, width), lambda i, meta: (jnp.maximum(i - n, 0), 0)),
                once(wa.shape),
                once(wb.shape),
            ]
            + [pl.BlockSpec(memory_space=pl.ANY)] * len(extra),
            out_specs=[
                col,
                row,
                row,
                pl.BlockSpec((step, HEAD_DIM), lambda i, meta: (i, 0)),
                col,
                row,
                col,
                pl.BlockSpec((step, width), lambda i, meta: (own_first(i), 0)),
            ]
            + [once(item.shape) for item in weights],
        ),
        input_output_aliases={5: 7} if flip else {},
        compiler_params=params(),
        cost_estimate=cost(1, 1) if flip else cost(8 * rows * width * 768, rows * width * 16),
        name="project",
    )(meta, xa, xb, wa, wb, *extra)


def head_rows(h):
    return slice(h * HEAD_DIM, (h + 1) * HEAD_DIM)


def with_shift(qt, top):
    high, middle, low = three_parts(top)
    extra = extra_rows([jnp.ones_like(top), -high, -middle, -low], HEAD_DIM)
    return jnp.concatenate([qt, extra], axis=0)


def half_scores(chunk, h, qa, start, k_ref, kx_ref):
    here = pl.ds(start, chunk)
    keys = jnp.concatenate([k_ref[here, head_rows(h)], kx_ref[here, :]], axis=1)
    return mm(keys, qa)


def half_part(h, start, scores, vt_ref, pt_ref):
    chunk = scores.shape[0]
    weight = jnp.exp2(scores)
    total = jnp.sum(weight.reshape(chunk // 8, 8, weight.shape[1]), axis=0)
    low = weight.astype(BF16)
    pt_ref[0, h, pl.ds(start, chunk), :] = low
    return total, mm(vt_ref[head_rows(h), pl.ds(start, chunk)], low)


def stale_shift(h, qt, k_ref):
    top = jnp.max(mm(k_ref[:SAMPLE, head_rows(h)], qt), axis=0, keepdims=True)
    return top, with_shift(qt, top)


def fast_states(chunk, shifts, keys, pts):
    tiles = [
        (h, j, start)
        for h in range(2)
        for j in range(len(keys))
        for start in range(0, keys[0][0].shape[0], chunk)
    ]

    def scores(tile):
        h, j, start = tile
        return half_scores(chunk, h, shifts[h][j][1], start, keys[j][0], keys[j][1])

    sums = {}
    ahead = scores(tiles[0])
    for place, (h, j, start) in enumerate(tiles):
        now = ahead
        if place + 1 < len(tiles):
            ahead = scores(tiles[place + 1])
        total, product = half_part(h, start, now, keys[j][2], pts[j])
        if (h, j) in sums:
            total, product = sums[h, j][0] + total, sums[h, j][1] + product
        sums[h, j] = total, product
    return [
        [
            (shifts[h][j][0], jnp.sum(sums[h, j][0], axis=0, keepdims=True), sums[h, j][1])
            for j in range(len(keys))
        ]
        for h in range(2)
    ]


def half_attend_exact(chunk, h, shift, k_ref, kx_ref, vt_ref, pt_ref):
    qt = shift[1][:HEAD_DIM]
    width = qt.shape[1]
    count = k_ref.shape[0] // chunk
    qa = with_shift(qt, jnp.zeros((1, width), F32))

    def find(j, top):
        found = half_scores(chunk, h, qa, pl.multiple_of(j * chunk, chunk), k_ref, kx_ref)
        return jnp.maximum(top, jnp.max(found, axis=0, keepdims=True))

    top = lax.fori_loop(0, count, find, jnp.full((1, width), MASKED, F32))
    qa = with_shift(qt, top)

    def add(j, state):
        start = pl.multiple_of(j * chunk, chunk)
        found = half_scores(chunk, h, qa, start, k_ref, kx_ref)
        more, product = half_part(h, start, found, vt_ref, pt_ref)
        return state[0] + more, state[1] + product

    total, acc = lax.fori_loop(
        0, count, add, (jnp.zeros((8, width), F32), jnp.zeros((HEAD_DIM, width), F32))
    )
    return top, jnp.sum(total, axis=0, keepdims=True), acc


def merge(states):
    top = states[0][0]
    for state in states[1:]:
        top = jnp.maximum(top, state[0])
    scales = [jnp.exp2(state[0] - top) for state in states]
    total = sum(state[1] * scale for state, scale in zip(states, scales))
    factors = [scale / total for scale in scales]
    return factors, sum(state[2] * factor for state, factor in zip(states, factors))


def redo(states, shifts, keys, pts):
    return [
        [half_attend_exact(256, h, shifts[h][j], *keys[j], pts[j]) for j in range(len(keys))]
        for h in range(2)
    ]


def run_halves(chunk, qt_ref, keys, pts, finish):
    shifts = [
        [stale_shift(h, qt_ref[head_rows(h), :], key_refs[0]) for key_refs in keys]
        for h in range(2)
    ]
    states = fast_states(chunk, shifts, keys, pts)
    worst = None
    for state in states[0] + states[1]:
        worst = state[1] if worst is None else jnp.maximum(worst, state[1])
    finish(states)

    @pl.when(jnp.logical_not(jnp.max(worst) <= LIMIT))
    def _():
        finish(redo(states, shifts, keys, pts))


def attend_first_kernel(chunk, qt_ref, k_ref, kx_ref, vt_ref, pt_ref, state_ref, acc_ref):
    def finish(states):
        for h in range(2):
            top, total, acc = states[h][0]
            state_ref[0, h : h + 1, :] = top
            state_ref[0, 2 + h : 3 + h, :] = total
            acc_ref[head_rows(h), :] = acc

    run_halves(chunk, qt_ref, [(k_ref, kx_ref, vt_ref)], [pt_ref], finish)


def attend_first(qt, key, chunk):
    rows = qt.shape[1]
    n = rows // ROWS
    col = pl.BlockSpec((256, ROWS), lambda i: (0, i))
    pairs = 2 * rows * rows
    return pl.pallas_call(
        partial(attend_first_kernel, chunk),
        out_shape=[
            jax.ShapeDtypeStruct((2 * n, 2, rows, ROWS), BF16),
            jax.ShapeDtypeStruct((n, 8, ROWS), F32),
            jax.ShapeDtypeStruct((256, rows), F32),
        ],
        grid=(n,),
        in_specs=[col] + [once(item.shape) for item in key],
        out_specs=[
            pl.BlockSpec((1, 2, rows, ROWS), lambda i: (i, 0, 0, 0)),
            pl.BlockSpec((1, 8, ROWS), lambda i: (i, 0, 0)),
            col,
        ],
        compiler_params=params(),
        cost_estimate=cost(4 * pairs * HEAD_DIM * 2, 2 * pairs, pairs),
        name="attend_near",
    )(qt, *key)


def attend_second_kernel(
    chunk, qtn_ref, qtf_ref, kn, kxn, vtn, kf, kxf, vtf, old_ref, old_acc_ref, _,
    ptn_ref, ptf_ref, mine_ref, sib_ref, stat_ref,
):
    i = pl.program_id(0)
    n = pl.num_programs(0) // 2
    near, far = (kn, kxn, vtn), (kf, kxf, vtf)

    def store(h, states):
        factors, result = merge(states)
        stat_ref[0, h : h + 1, :] = factors[0]
        stat_ref[0, 2 + h : 3 + h, :] = factors[1]
        low = result.T.astype(BF16)
        first = i % n < n // 2

        @pl.when(first)
        def _():
            mine_ref[:, head_rows(h)] = low

        @pl.when(jnp.logical_not(first))
        def _():
            sib_ref[:, head_rows(h)] = low

    @pl.when(i < n)
    def _():
        def finish(states):
            for h in range(2):
                old = (old_ref[0, h : h + 1, :], old_ref[0, 2 + h : 3 + h, :],
                       old_acc_ref[head_rows(h), :])
                store(h, [old, states[h][0]])

        run_halves(chunk, qtn_ref, [far], [ptf_ref], finish)

    @pl.when(i >= n)
    def _():
        def finish(states):
            for h in range(2):
                store(h, states[h])

        run_halves(chunk, qtf_ref, [near, far], [ptn_ref, ptf_ref], finish)


def mine_block(i, n):
    half = n // 2
    return (i // n) * half + jnp.minimum(i % n, half - 1)


def sib_block(i, n):
    half = n // 2
    return jnp.maximum((i // n) * half + i % n - half, jnp.maximum((i // n) * half - 1, 0))


def attend_second(qtn, qtf, near, far, pt, state, acc, chunk):
    rows = qtn.shape[1]
    n = rows // ROWS
    near_col = pl.BlockSpec((256, ROWS), lambda i: (0, jnp.minimum(i, n - 1)))
    pairs = 6 * rows * rows
    return pl.pallas_call(
        partial(attend_second_kernel, chunk),
        out_shape=[
            jax.ShapeDtypeStruct(pt.shape, BF16),
            jax.ShapeDtypeStruct(pt.shape, BF16),
            jax.ShapeDtypeStruct((rows, 256), BF16),
            jax.ShapeDtypeStruct((rows, 256), BF16),
            jax.ShapeDtypeStruct((2 * n, 8, ROWS), F32),
        ],
        grid=(2 * n,),
        in_specs=[near_col, pl.BlockSpec((256, ROWS), lambda i: (0, jnp.maximum(i - n, 0)))]
        + [once(item.shape) for item in near + far]
        + [
            pl.BlockSpec((1, 8, ROWS), lambda i: (jnp.minimum(i, n - 1), 0, 0)),
            near_col,
            pl.BlockSpec(memory_space=pl.ANY),
        ],
        out_specs=[
            pl.BlockSpec((1, 2, rows, ROWS), lambda i: (jnp.maximum(i, n), 0, 0, 0)),
            pl.BlockSpec((1, 2, rows, ROWS), lambda i: (i, 0, 0, 0)),
            pl.BlockSpec((ROWS, 256), lambda i: (mine_block(i, n), 0)),
            pl.BlockSpec((ROWS, 256), lambda i: (sib_block(i, n), 0)),
            pl.BlockSpec((1, 8, ROWS), lambda i: (i, 0, 0)),
        ],
        input_output_aliases={10: 0},
        compiler_params=params(),
        cost_estimate=cost(1, 1),
        name="attend_rest",
    )(qtn, qtf, *near, *far, state, acc, pt)


def back_weights(do, o, factors):
    dot_t = do.astype(F32).T
    delta = jnp.sum(dot_t * o.astype(F32).T, axis=0, keepdims=True)
    found = []
    for factor in factors:
        scaled = dot_t * factor
        high, middle, low = three_parts(delta * factor)
        extra = extra_rows([-high, -middle, -low], HEAD_DIM)
        found.append(
            (jnp.concatenate([scaled.astype(BF16), extra], axis=0), scaled.T.astype(BF16))
        )
    return found


def back_half(chunk, h, grads, q_rows, pt_ref, v_ref, kt_ref, key_acc, value_acc):
    ones = jnp.where(
        lax.broadcasted_iota(jnp.int32, (chunk, HEAD_DIM), 1) < 3, F32(1.0), F32(0.0)
    ).astype(BF16)
    result = jnp.zeros((HEAD_DIM, q_rows.shape[0]), F32)
    for start in range(0, v_ref.shape[0], chunk):
        here = slice(start, start + chunk)
        prob = pt_ref[0, h, here, :]
        values = jnp.concatenate([v_ref[here, head_rows(h)], ones], axis=1)
        score = (prob.astype(F32) * mm(values, grads[0])).astype(BF16)
        value_acc[h, here, :] += mm(prob, grads[1])
        key_acc[h, here, :] += mm(score, q_rows)
        result = result + mm(kt_ref[head_rows(h), here], score)
    return result


def attend_back_kernel(
    chunk, da_ref, db_ref, oa_ref, ob_ref, stat_ref, qn_ref, qf_ref, ptn_ref, ptf_ref,
    vn, ktn, vf, ktf, dq_ref, dkv_ref, key_n, value_n, key_f, value_f,
):
    i = pl.program_id(0)
    n = pl.num_programs(0) // 2

    @pl.when(i == 0)
    def _():
        for ref in (key_n, value_n, key_f, value_f):
            ref[...] = jnp.zeros_like(ref)

    first = i % n < n // 2
    do = jnp.where(first, da_ref[...], db_ref[...])
    o = jnp.where(first, oa_ref[...], ob_ref[...])
    q = jnp.where(i < n, qn_ref[...], qf_ref[...])
    for h in range(2):
        cols = head_rows(h)
        near, far = back_weights(
            do[:, cols], o[:, cols], [stat_ref[0, h : h + 1, :], stat_ref[0, 2 + h : 3 + h, :]]
        )
        grad = back_half(chunk, h, near, q[:, cols], ptn_ref, vn, ktn, key_n, value_n)
        grad += back_half(chunk, h, far, q[:, cols], ptf_ref, vf, ktf, key_f, value_f)
        dq_ref[:, cols] = (grad * F32(1.0 / math.sqrt(HEAD_DIM))).T.astype(BF16)

    @pl.when(i == 2 * n - 1)
    def _():
        seq = vn.shape[0]
        for half, (keys, values) in enumerate(((key_n, value_n), (key_f, value_f))):
            for owner in range(2):
                source = slice(owner * seq // 2, (owner + 1) * seq // 2)
                begin = owner * seq + half * seq // 2
                rows = slice(begin, begin + seq // 2)
                for h in range(2):
                    dkv_ref[rows, head_rows(h)] = (keys[h, source] * F32(1.0 / LOG2E)).astype(BF16)
                    dkv_ref[rows, head_rows(2 + h)] = values[h, source].astype(BF16)


def attend_back(da, db, oa, ob, stat, qn, qf, ptn, ptf, vn, ktn, vf, ktf, chunk):
    rows = qn.shape[0]
    step = BACK_ROWS
    n = rows // step
    per = ROWS // step
    row = lambda f: pl.BlockSpec((step, 256), lambda i: (f(i), 0))
    tile = pl.BlockSpec((1, 2, rows, step), lambda i: (i // per, 0, 0, i % per))
    flat = jax.ShapeDtypeStruct((2 * rows, 256), BF16)
    wide = jax.ShapeDtypeStruct((2 * rows, 512), BF16)
    acc = pltpu.VMEM((2, rows, HEAD_DIM), F32)

    def own_first(i):
        return jnp.where(i % n < n // 2, 0, n // 2) + (i // n) * (n // 2) + i % n
    pairs = 8 * rows * rows
    return pl.pallas_call(
        partial(attend_back_kernel, chunk),
        out_shape=[flat, wide],
        grid=(2 * n,),
        in_specs=[
            row(lambda i: mine_block(i, n)),
            row(lambda i: sib_block(i, n)),
            row(lambda i: mine_block(i, n)),
            row(lambda i: sib_block(i, n)),
            pl.BlockSpec((1, 8, step), lambda i: (i // per, 0, i % per)),
            row(lambda i: jnp.minimum(i, n - 1)),
            row(lambda i: jnp.maximum(i - n, 0)),
            tile,
            tile,
        ]
        + [once(item.shape) for item in (vn, ktn, vf, ktf)],
        out_specs=[row(own_first), once(wide.shape)],
        scratch_shapes=[acc, acc, acc, acc],
        compiler_params=params(),
        cost_estimate=cost(8 * pairs * HEAD_DIM, 2 * pairs),
        name="attend_back",
    )(da, db, oa, ob, stat, qn, qf, ptn, ptf, vn, ktn, vf, ktf)


def mean(values):
    return jnp.mean(values, axis=-1, keepdims=True)


def norm(values):
    centered = values - mean(values)
    inverse = lax.rsqrt(mean(centered * centered) + EPS)
    return centered * inverse, inverse


def norm_back(incoming, normed, inverse, gain):
    scaled = incoming * gain
    return inverse * (scaled - mean(scaled) - normed * mean(scaled * normed))


def gelu_parts(v):
    bell = jnp.exp2(v * v * F32(-0.5 * LOG2E))
    base = 1.0 + F32(0.3275911 / math.sqrt(2.0)) * jnp.abs(v)
    t = pl.reciprocal(base, approx=True)
    t = t * (2.0 - base * t)
    series = t * (
        F32(0.5 * 0.254829592)
        + t
        * (
            F32(0.5 * -0.284496736)
            + t
            * (
                F32(0.5 * 1.421413741)
                + t * (F32(0.5 * -1.453152027) + t * F32(0.5 * 1.061405429))
            )
        )
    )
    tail = series * bell
    return bell * F32(1.0 / math.sqrt(2.0 * math.pi)), jnp.where(v >= 0, 1.0 - tail, tail)


def fold_rows(values):
    return jnp.sum(values.reshape(values.shape[0] // 8, 8, values.shape[1]), axis=0)


def rows_kernel(
    sizes, meta, xa_ref, xb_ref, oa_ref, ob_ref, cot_a, cot_b, p0, p1, p2, p3,
    u0, u1, u2, u3, vec_ref,
    prompt_near, data_near, prompt_far, data_far, resid_ref, da_ref, db_ref, send_ref,
    sums_ref, wo_ref, up_ref, down_ref, bias_ref, grad_acc, vec_acc, bias_acc,
):
    prompt_local, data_local = sizes
    i = pl.program_id(0)
    half = pl.num_programs(0) // 2
    here = i < half
    rows = xa_ref.shape[0]
    quarter = u0.shape[1]

    @pl.when(i == 0)
    def _():
        for j, (pack, up_part) in enumerate(((p0, u0), (p1, u1), (p2, u2), (p3, u3))):
            cols = slice(j * quarter, (j + 1) * quarter)
            wo_ref[head_rows(j), :] = pack[:HEAD_DIM, :]
            down_ref[cols, :] = pack[HEAD_DIM : HEAD_DIM + quarter, :]
            bias_ref[0:1, cols] = pack[
                HEAD_DIM + quarter : HEAD_DIM + quarter + 16, :quarter
            ].astype(F32)[0:1, :]
            up_ref[:, cols] = up_part[...]
        grad_acc[...] = jnp.zeros_like(grad_acc)
        vec_acc[...] = jnp.zeros_like(vec_acc)
        bias_acc[...] = jnp.zeros_like(bias_acc)

    slot = jnp.where(here, meta[0], meta[0] ^ 2)
    index = (i % half) * rows + lax.broadcasted_iota(jnp.int32, (rows, 1), 0) - prompt_local
    live = jnp.logical_or(index < 0, slot * data_local + index < meta[2])

    out_bias, attn_gain, attn_shift = vec_ref[0:1, :], vec_ref[1:2, :], vec_ref[2:3, :]
    down_bias, mlp_gain, mlp_shift = vec_ref[3:4, :], vec_ref[4:5, :], vec_ref[5:6, :]
    x = jnp.where(here, xa_ref[...], xb_ref[...])
    attended = jnp.concatenate([oa_ref[...], ob_ref[...]], axis=1)
    normed_one, inverse_one = norm(x.astype(F32) + (mm(attended, wo_ref[...]) + out_bias))
    hidden = normed_one * attn_gain + attn_shift
    hidden_low = hidden.astype(BF16)
    pre = mm(hidden_low, up_ref[...]) + bias_ref[0:1, :]
    density, share = gelu_parts(pre)
    activated = (pre * share).astype(BF16)
    slope = share + pre * density
    mixed = hidden + (mm(activated, down_ref[...]) + down_bias)
    normed_two, inverse_two = norm(mixed)
    output = (normed_two * mlp_gain + mlp_shift).astype(BF16)
    cotangent = jnp.where(live, jnp.where(here, cot_a[...], cot_b[...]).astype(F32), 0.0)
    mixed_grad = norm_back(cotangent, normed_two, inverse_two, mlp_gain)
    mixed_low = mixed_grad.astype(BF16)
    pre_grad = (mm(mixed_low, down_ref[...], NT) * slope).astype(BF16)
    hidden_grad = mixed_grad + mm(pre_grad, up_ref[...], NT)
    resid_grad = norm_back(hidden_grad, normed_one, inverse_one, attn_gain)
    resid_ref[...] = resid_grad
    resid_low = resid_grad.astype(BF16)
    attended_grad = mm(resid_low, wo_ref[...], NT).astype(BF16)
    da_ref[...] = attended_grad[:, :256]
    db_ref[...] = attended_grad[:, 256:]

    up_grad = mm(hidden_low, pre_grad, TN)
    down_grad = mm(mixed_low, activated, TN)
    out_grad = mm(resid_low, attended, TN)
    for j in range(4):
        cols = slice(j * quarter, (j + 1) * quarter)
        grad_acc[j, :, :quarter] += up_grad[:, cols]
        grad_acc[j, :, quarter : 2 * quarter] += down_grad[:, cols]
        grad_acc[j, :, 2 * quarter :] += out_grad[:, head_rows(j)]
    bias_acc[...] += fold_rows(pre_grad.astype(F32))
    for place, value in enumerate(
        (
            resid_grad,
            hidden_grad * normed_one,
            hidden_grad,
            mixed_grad,
            cotangent * normed_two,
            cotangent,
        )
    ):
        vec_acc[place] += fold_rows(value)

    for j in range((prompt_local + data_local) // rows):
        split = max(0, min(rows, prompt_local - j * rows))
        for place, (prompt_ref, data_ref) in enumerate(
            ((prompt_near, data_near), (prompt_far, data_far))
        ):

            @pl.when(i == place * half + j)
            def _():
                if split:
                    prompt_ref[j * rows : j * rows + split, :] = output[:split]
                if split < rows:
                    begin = j * rows + split - prompt_local
                    data_ref[begin : begin + rows - split, :] = output[split:]

    @pl.when(i == pl.num_programs(0) - 1)
    def _():
        for place in range(6):
            sums_ref[place : place + 1, :] = jnp.sum(vec_acc[place], axis=0, keepdims=True)
        bias_grad = jnp.sum(bias_acc[...], axis=0, keepdims=True)
        per_row = bias_grad.shape[1] // 2 // quarter
        for g in range(4):
            found = jnp.zeros((1, quarter), F32)
            for j, flip in enumerate((0, 2, 1, 3)):
                piece = bias_grad[:, j * quarter : (j + 1) * quarter]
                found = jnp.where((meta[0] ^ flip) == g, piece, found)
            row, col = 6 + g // per_row, (g % per_row) * quarter
            sums_ref[row : row + 1, col : col + quarter] = found
        depth = send_ref.shape[1] - 16
        groups = send_ref.shape[0] // 4
        width, wide = sums_ref.shape[1], send_ref.shape[2]
        per = sums_ref.shape[0] * width // groups
        for g in range(groups):
            row, col = g * per // width, g * per % width
            part = jnp.pad(sums_ref[row : row + 1, col : col + per], ((0, 0), (0, wide - per)))
            high, low, _ = three_parts(part)
            extra = extra_rows([high, low], 16)
            for j, flip in enumerate((0, 2, 1, 3)):
                target = g * 4 + (meta[0] ^ flip)
                send_ref[target, :depth] = grad_acc[j, g * depth : (g + 1) * depth].astype(BF16)
                send_ref[target, depth:] = extra


def row_work(meta, xa, xb, oa, ob, cot, packs, ups, vec, sizes, groups):
    rows, width = xa.shape
    prompt_local, data_local = sizes
    step = ROW_STEP
    n = rows // step
    quarter = ups[0].shape[1]
    hidden = 4 * quarter
    wide = 2 * quarter + HEAD_DIM
    send = (4 * groups, width // groups + 16, wide)
    near = pl.BlockSpec((step, width), lambda i, meta: (jnp.minimum(i, n - 1), 0))
    far = pl.BlockSpec((step, width), lambda i, meta: (jnp.maximum(i - n, 0), 0))
    row = lambda cols: pl.BlockSpec((step, cols), lambda i, meta: (i, 0))
    return pl.pallas_call(
        partial(rows_kernel, sizes),
        out_shape=[
            jax.ShapeDtypeStruct((prompt_local, width), BF16),
            jax.ShapeDtypeStruct((data_local, width), BF16),
            jax.ShapeDtypeStruct((prompt_local, width), BF16),
            jax.ShapeDtypeStruct((data_local, width), BF16),
            jax.ShapeDtypeStruct((2 * rows, width), F32),
            jax.ShapeDtypeStruct((2 * rows, 256), BF16),
            jax.ShapeDtypeStruct((2 * rows, 256), BF16),
            jax.ShapeDtypeStruct(send, BF16),
        ],
        grid_spec=pltpu.PrefetchScalarGridSpec(
            num_scalar_prefetch=1,
            grid=(2 * n,),
            in_specs=[near, far, row(256), row(256), near, far]
            + [once(item.shape) for item in packs + ups]
            + [once(vec.shape)],
            out_specs=[
                once((prompt_local, width)),
                once((data_local, width)),
                once((prompt_local, width)),
                once((data_local, width)),
                row(width),
                row(256),
                row(256),
                once(send),
            ],
            scratch_shapes=[
                pltpu.VMEM((8, width), F32),
                pltpu.VMEM((4 * HEAD_DIM, width), BF16),
                pltpu.VMEM((width, hidden), BF16),
                pltpu.VMEM((hidden, width), BF16),
                pltpu.VMEM((8, hidden), F32),
                pltpu.VMEM((4, width, wide), F32),
                pltpu.VMEM((6, 8, width), F32),
                pltpu.VMEM((8, hidden), F32),
            ],
        ),
        compiler_params=params(),
        cost_estimate=cost(
            3 * 2 * 2 * rows * width * (width + 2 * hidden), 24 * rows * width, 4 * rows * hidden
        ),
        name="row_work",
    )(meta, xa, xb, oa, ob, *cot, *packs, *ups, vec)


def on_device(
    data_rows,
    prompt_rows,
    context_rows,
    test_rows,
    qkv_weight,
    out_bias,
    out_weight,
    attn_gain,
    attn_shift,
    up_weight,
    up_bias,
    down_weight,
    down_bias,
    mlp_gain,
    mlp_shift,
    data_cotangent,
    prompt_cotangent,
):
    data_local = data_rows.shape[1]
    prompt_local = prompt_rows.shape[0]
    width = prompt_rows.shape[1]
    quarter = up_weight.shape[1]
    sizes = (prompt_local, data_local)
    groups = lax.axis_size("ep")
    t = lax.axis_index("tp")
    mine = t >> 1
    other = 1 - mine

    def across(value):
        return lax.ppermute(value, "tp", [(i, i ^ 2) for i in range(4)])

    def beside(value):
        return lax.ppermute(value, "tp", [(i, i ^ 1) for i in range(4)])

    def pick(values, which):
        return lax.dynamic_index_in_dim(values, which, axis=0, keepdims=False)

    def stack(prompt_part, data_part):
        return jnp.concatenate([prompt_part, data_part], axis=0)

    w_far = across(qkv_weight)
    x_far = stack(prompt_rows, pick(data_rows, other))
    x = stack(prompt_rows, pick(data_rows, mine))
    x_far, x, prompt_cotangent, data_cotangent = lax.optimization_barrier(
        (x_far, x, prompt_cotangent, data_cotangent)
    )
    x_far = across(x_far)
    x_sib = beside(x)
    cot = stack(pick(prompt_cotangent, mine), pick(data_cotangent, mine))
    cot_far = stack(pick(prompt_cotangent, other), pick(data_cotangent, other))
    vec = jnp.stack(
        [out_bias, attn_gain, attn_shift, down_bias, mlp_gain, mlp_shift, mlp_shift, mlp_shift]
    ).astype(F32)
    context = pick(context_rows, mine)
    live = context + pick(test_rows, mine)
    meta = jnp.stack([t, context, live]).astype(jnp.int32)
    meta, cot, cot_far, vec = lax.optimization_barrier((meta, cot, cot_far, vec))

    qtn, qn, kn, kxn, ktn, vn, vtn, x_all, w, w_t = project(
        meta, x, x_sib, qkv_weight, w_far, sizes, 0
    )
    ptn, state, state_acc = attend_first(qtn, (kn, kxn, vtn), 512)

    bias_rows = jnp.pad(up_bias[None], ((0, 15), (0, width - quarter)))
    pack = jnp.concatenate([out_weight, down_weight, bias_rows], axis=0)
    x_far, state, pack, up_weight, cot_far = lax.optimization_barrier(
        (x_far, state, pack, up_weight, cot_far)
    )
    x_far_sib = beside(x_far)
    pack_far, up_far = across(pack), across(up_weight)
    cot_far = across(cot_far)
    pack_sib, up_sib = beside(pack), beside(up_weight)
    qtf, qf, kf, kxf, ktf, vf, vtf, x_all = project(
        meta, x_far, x_far_sib, w, w_t, sizes, 2, x_all
    )
    ptn, ptf, oa, ob, stat = attend_second(
        qtn, qtf, (kn, kxn, vtn), (kf, kxf, vtf), ptn, state, state_acc, 512
    )

    ob_send, cot_far, pack_far, up_far, pack_sib, up_sib = lax.optimization_barrier(
        (ob, cot_far, pack_far, up_far, pack_sib, up_sib)
    )
    packs = [pack, pack_far, pack_sib, beside(pack_far)]
    ups = [up_weight, up_far, up_sib, beside(up_far)]
    (prompt_near, data_near, prompt_far, data_far, resid, da, db, send) = row_work(
        meta, x, x_far, oa, beside(ob_send), (cot, cot_far), packs, ups, vec, sizes, groups
    )

    def dot(left, right, dims):
        return lax.dot_general(left, right, dims, preferred_element_type=F32)

    def exchange(parts, axes):
        return lax.all_to_all(parts, axes, 0, 0, tiled=True)

    def gather(part):
        return exchange(jnp.broadcast_to(part[None], (groups,) + part.shape), "ep")

    db = beside(db)
    send = exchange(send, ("ep", "tp"))
    prompt_back, data_back = across(prompt_far), across(data_far)

    dq, dkv = attend_back(
        da, db, oa, ob, stat, qn, qf, ptn, ptf, vn, ktn, vf, ktf, 512
    )
    send, prompt_back, data_back, dq = lax.optimization_barrier((send, prompt_back, data_back, dq))
    depth = width // groups
    total = jnp.sum(send.astype(F32), axis=0)
    part = total[depth : depth + 1] + total[depth + 1 : depth + 2]
    high = lax.optimization_barrier(part.astype(BF16))
    low = (part - high.astype(F32)).astype(BF16)
    total = jnp.concatenate(
        [total[:depth].astype(BF16), high, low, jnp.zeros((6, total.shape[1]), BF16)], axis=0
    )
    total = jnp.broadcast_to(total[None], (groups,) + total.shape)
    total, dq, dkv = lax.optimization_barrier((total, dq, dkv))
    total = exchange(total, "ep")

    slot_rows = prompt_local + data_local
    cut = 2 * slot_rows
    wq, wkv = w[:, :256], w[:, 256:]

    def rows_grad(part):
        return dot(dq[part], wq, NT) + dot(dkv[part], wkv, NT)

    grad_q, grad_kv = dot(x_all, dq, TN), dot(x_all, dkv, TN)

    def head_grad(h):
        return jnp.stack(
            [grad_q[:, head_rows(h)], grad_kv[:, head_rows(h)], grad_kv[:, head_rows(2 + h)]]
        )

    other_grad, dq, dkv = lax.optimization_barrier((head_grad(1).astype(BF16), dq, dkv))
    other_grad = across(other_grad)
    sib = rows_grad(slice(cut, None)).astype(BF16)
    sib, dq, dkv = lax.optimization_barrier((sib, dq, dkv))
    sib = beside(sib)
    own = rows_grad(slice(slot_rows, cut)) + resid[slot_rows:]
    other_grad, own = lax.optimization_barrier((other_grad, own))
    far_rows = (own + sib[slot_rows:].astype(F32)).astype(BF16)
    far_rows, dq, dkv = lax.optimization_barrier((far_rows, dq, dkv))
    far_prompt = across(far_rows[:prompt_local])
    far_data = across(far_rows[prompt_local:])
    near_rows = rows_grad(slice(0, slot_rows)) + resid[:slot_rows]
    near_rows = near_rows + sib[:slot_rows].astype(F32)
    near_data = near_rows[prompt_local:].astype(BF16)

    columns = width // HEAD_DIM
    prompt = near_rows[:prompt_local] + far_prompt.astype(F32)
    prompt = prompt.astype(BF16).reshape(groups, prompt_local // groups, width)
    prompt = jnp.concatenate([prompt[:, :, head_rows(j)] for j in range(columns)], axis=1)
    qkv = (head_grad(0) + other_grad.astype(F32)).astype(BF16).reshape(groups, -1, HEAD_DIM)
    qkv_rows = qkv.shape[1]
    last = jnp.concatenate([qkv, prompt], axis=1)
    total, last = lax.optimization_barrier((total, last))
    last = gather(jnp.sum(exchange(last, "ep").astype(F32), axis=0).astype(BF16))
    qkv = last[:, :qkv_rows].reshape(3, width, HEAD_DIM).astype(F32)
    prompt = last[:, qkv_rows:].reshape(groups, columns, prompt_local // groups, HEAD_DIM)
    prompt_grad = jnp.concatenate([prompt[:, j] for j in range(columns)], axis=2)
    prompt_grad = prompt_grad.reshape(prompt_local, width).astype(F32)

    which = lax.broadcasted_iota(jnp.int32, (2, 1, 1), 0)

    def by_episode(own, received):
        return jnp.where(which == mine, own[None], received[None])

    sums = total[:, depth : depth + 2, : 8 * width // groups].astype(F32)
    sums = (sums[:, 0] + sums[:, 1]).reshape(8, width)
    total = total[:, :depth].reshape(width, -1).astype(F32)
    bias_grad = lax.dynamic_slice_in_dim(sums[6:8].reshape(-1), t * quarter, quarter)
    return (
        by_episode(data_near, data_back),
        by_episode(prompt_near, prompt_back),
        by_episode(near_data, far_data),
        prompt_grad,
        qkv,
        sums[0],
        total[:, 2 * quarter :].T,
        sums[1],
        sums[2],
        total[:, :quarter],
        bias_grad,
        total[:, quarter : 2 * quarter].T,
        sums[3],
        sums[4],
        sums[5],
    )


def solution(mesh):
    return jax.shard_map(
        on_device,
        mesh=mesh,
        in_specs=(
            P("ep", "tp", None),
            P("tp", None),
            P("ep"),
            P("ep"),
            P(None, None, "tp"),
            P(),
            P("tp", None),
            P(),
            P(),
            P(None, "tp"),
            P("tp"),
            P("tp", None),
            P(),
            P(),
            P(),
            P("ep", "tp", None),
            P("ep", "tp", None),
        ),
        out_specs=(
            P("ep", "tp", None),
            P("ep", "tp", None),
            P("ep", "tp", None),
            P("tp", None),
            P(None, None, "tp"),
            P(),
            P("tp", None),
            P(),
            P(),
            P(None, "tp"),
            P("tp"),
            P("tp", None),
            P(),
            P(),
            P(),
        ),
        check_vma=False,
    )
```
